32 devices in a mesh: dp: 8 (over y, x, core), mp: 4 (over z).
Axes of the slice: x: 2, y: 2, z: 4, core: 2. Of those that a mesh axis runs over, the one named last changes fastest.
Arguments:
- tokens: bfloat16 [16, 1024, 768], P('dp', 'mp'), may hold values from -6 to 6
- segments: int32 [16, 1024], P('dp'), may hold values from 0 to 4, as said below
- qkv_weight: bfloat16 [2, 3, 768, 768], P(None, None, None, 'mp'), may hold values from -0.21875 to 0.21875
- out_weight: bfloat16 [2, 768, 768], P(None, 'mp'), may hold values from -1.75 to 1.75
- up_weight: bfloat16 [2, 768, 3072], P(None, None, 'mp'), may hold values from -0.21875 to 0.21875
- down_projection_weight: bfloat16 [2, 3072, 768], P(None, 'mp'), may hold values from -0.109375 to 0.109375
- norm_gain: float32 [2, 2, 768], replicated, may hold values from 0.5 to 1.5
- norm_bias: float32 [2, 2, 768], replicated, may hold values from -2 to 2
- pos_bias: float32 [2, 1024, 256], replicated, may hold values from -4 to 4
- cotangent: float32 [16, 1024, 768], P('dp', 'mp'), may hold values from -6 to 6
Outputs:
- output: bfloat16 [16, 1024, 768], P('dp', 'mp')
- grad_tokens: float32 [16, 1024, 768], P('dp', 'mp')
- grad_qkv_weight: float32 [2, 3, 768, 768], P(None, None, None, 'mp')
- grad_out_weight: float32 [2, 768, 768], P(None, 'mp')
- grad_up_weight: float32 [2, 768, 3072], P(None, None, 'mp')
- grad_down_weight: float32 [2, 3072, 768], P(None, 'mp')
- grad_norm_gain: float32 [2, 2, 768], replicated
- grad_norm_bias: float32 [2, 2, 768], replicated
- grad_pos_bias: float32 [2, 1024, 256], replicated
The draws below stay inside these ranges and needn't reach their ends.
Inputs may be any that keep to these rules, and one draw needn't show every extreme that they name: `segments`: in each sequence the document numbers start at 0, never fall and rise by at most one from one position to the next; among the 2 sequences of each index of dp, one has exactly three documents, the first and last each within 128 positions of the sequence's ends, and every other sequence ends with document number max(4, 1).
All inputs are finite; a program needn't handle non-finite values.
Results may differ from the reference program's by a relative error of at most 0.02.
Values may be sent and summed in bfloat16 or wider, within the bound.
No kernel may reach another device: no remote copies, remote signals or barrier semaphores. Data moves between devices by JAX's collectives and lax.ppermute only.
A program may use at most 192 MiB of HBM per device.

```python
import jax
import jax.numpy as jnp
from jax import lax

D = 768
FF = 3072
SEQUENCE_LENGTH = 1024
WINDOW = 256
LAYERS = 2
SEQ_DEV = 2
SEQS = 16


def draw_segments(key, part):
    key = jax.random.fold_in(key, 7)
    pick_key, break_key, front_key, back_key = jax.random.split(key, 4)
    groups = SEQS // SEQ_DEV
    chosen = jax.random.randint(pick_key, (groups,), 0, SEQ_DEV)
    member = jnp.arange(SEQS) % SEQ_DEV
    single = member == jnp.repeat(chosen, SEQ_DEV)
    count = max(SEQUENCE_LENGTH // 256, 1)
    edge = SEQUENCE_LENGTH // 8
    row_keys = jax.random.split(break_key, SEQS)
    orders = jax.vmap(lambda row_key: jax.random.permutation(row_key, SEQUENCE_LENGTH - 1))(row_keys)
    breaks = jnp.concatenate([jnp.zeros((SEQS, 1), jnp.bool_), orders < count], axis=1)
    front = jax.random.randint(front_key, (SEQS, 1), 1, edge + 1)
    back = jax.random.randint(back_key, (SEQS, 1), SEQUENCE_LENGTH - edge, SEQUENCE_LENGTH)
    places = jnp.arange(SEQUENCE_LENGTH)[None, :]
    ends = (places == front) | (places == back)
    flags = jnp.where(single[:, None], jnp.where(ends, 1, 0), jnp.where(breaks, 1, 0))
    return jnp.cumsum(flags, axis=1).astype(jnp.int32)


def block_levels(stream_key, extent, cuts, low, top_value):
    def one(dim, parts):
        steps = jax.random.uniform(jax.random.fold_in(jax.random.fold_in(stream_key, 6), dim), (parts,), jnp.float32, low / len(cuts), top_value / len(cuts))
        return jnp.repeat(jnp.exp(steps), extent[dim] // parts).reshape((-1,) + (1,) * (len(extent) - dim - 1))

    loudness = one(*cuts[0])
    for cut in cuts[1:]:
        loudness = loudness * one(*cut)
    return loudness


def bell_draw(key, dims, deviation, reach, shards=(), kind=jnp.bfloat16):
    gain = block_levels(key, dims, shards, -0.22, 0.18) if shards else 1.0
    array = jax.random.normal(key, dims, jnp.float32) * deviation * gain
    return jnp.minimum(jnp.maximum(array, -reach), reach).astype(kind)


def setup_inputs(seed: int = 0) -> dict:
    keys = jax.random.split(jax.random.key(seed), 11)
    tokens = bell_draw(keys[0], (SEQS, SEQUENCE_LENGTH, D), 1.0, 6.0, ((0, 8), (1, 4)))
    segments = draw_segments(jax.random.fold_in(keys[10], 71), 0)
    qkv_weight = bell_draw(keys[2], (LAYERS, 3, D, D), D ** -0.5, 0.21875, ((3, 4),))
    out_weight = bell_draw(keys[3], (LAYERS, D, D), (D // 64) ** -0.5, 1.75, ((1, 4),))
    up_weight = bell_draw(keys[4], (LAYERS, D, FF), D ** -0.5, 0.21875, ((2, 4),))
    down_projection_weight = bell_draw(keys[5], (LAYERS, FF, D), FF ** -0.5, 0.109375, ((1, 4),))
    norm_gain = jnp.clip(1.0 + 0.1 * jax.random.normal(keys[6], (LAYERS, 2, D), jnp.float32), 0.5, 1.5)
    norm_bias = bell_draw(keys[7], (LAYERS, 2, D), 0.3, 2.0, (), jnp.float32)
    pos_bias = bell_draw(keys[8], (LAYERS, SEQUENCE_LENGTH, WINDOW), 1.0, 4.0, (), jnp.float32)
    cotangent = bell_draw(keys[9], (SEQS, SEQUENCE_LENGTH, D), 1.0, 6.0, ((0, 8), (1, 4)), jnp.float32)
    return dict(tokens=tokens, segments=segments, qkv_weight=qkv_weight, out_weight=out_weight, up_weight=up_weight, down_projection_weight=down_projection_weight, norm_gain=norm_gain, norm_bias=norm_bias, pos_bias=pos_bias, cotangent=cotangent)


@jax.custom_vjp
def low(v):
    return lax.optimization_barrier(v.astype(jnp.bfloat16)).astype(jnp.float32)

@jax.custom_vjp
def low_back(v):
    return v

def low_keep(v):
    return (low(v), None)

def low_pass(kept, grad):
    return (grad,)

def back_keep(v):
    return (v, None)

def back_low(kept, grad):
    return (low(grad),)
low.defvjp(low_keep, low_pass)
low_back.defvjp(back_keep, back_low)

def matmul(left_op, right_op):
    return jnp.dot(left_op, right_op, precision=lax.Precision.HIGHEST, preferred_element_type=jnp.float32)

def layer_norm(values, gain_vec, shift_vec):
    center = values - lax.optimization_barrier(jnp.mean(values, axis=-1, keepdims=True))
    normal = center * lax.rsqrt(lax.optimization_barrier(jnp.mean(center * center, axis=-1, keepdims=True)) + 1e-05)
    return normal * gain_vec + shift_vec

def one_layer(stream, weights, seg_row):
    qkv_w, out_w, up_w, down_w, gain_pair, shift_pair, bias_band = weights
    normed = low(layer_norm(stream, gain_pair[0], shift_pair[0]))
    queries = low_back(matmul(normed, qkv_w[0]))
    key_rows = low_back(matmul(normed, qkv_w[1]))
    value_rows = low_back(matmul(normed, qkv_w[2]))
    key_exp = jnp.exp(key_rows)
    carried = low(key_exp * value_rows)
    weight_sum = low(key_exp)
    places = jnp.arange(SEQUENCE_LENGTH).astype(jnp.int32)
    offsets = places[:, None] - places[None, :]
    allowed = (offsets >= 0) & (offsets < WINDOW) & (seg_row[:, None] == seg_row[None, :])
    full_bias = jnp.take_along_axis(bias_band, jnp.clip(offsets, 0, WINDOW - 1).astype(jnp.int32), axis=1)
    mix_matrix = low(jnp.where(allowed, jnp.exp(full_bias), jnp.zeros_like(full_bias)))
    numerator = low_back(matmul(mix_matrix, carried))
    denominator = low_back(matmul(mix_matrix, weight_sum))
    mixed = low(jax.nn.sigmoid(queries) * numerator / denominator)
    stream = stream + low_back(matmul(mixed, out_w))
    normed_b = low(layer_norm(stream, gain_pair[1], shift_pair[1]))
    pre_act = low_back(matmul(normed_b, up_w))
    activation = low(jax.nn.gelu(pre_act, approximate=True))
    return stream + low_back(matmul(activation, down_w))

def reference(tokens, segments, qkv_weight, out_weight, up_weight, down_projection_weight, norm_gain, norm_bias, pos_bias, cotangent):
    params = (qkv_weight.astype(jnp.float32), out_weight.astype(jnp.float32), up_weight.astype(jnp.float32), down_projection_weight.astype(jnp.float32), norm_gain.astype(jnp.float32), norm_bias.astype(jnp.float32), pos_bias.astype(jnp.float32))

    def forward(weights, stream, seg_row):
        for present_rows in range(LAYERS):
            stream = one_layer(stream, tuple((member[present_rows] for member in weights)), seg_row)
        return stream

    def per_sequence(totals, inputs):
        stream, seg_row, output_gradient = inputs
        result, pullback = jax.vjp(lambda weights, entering: forward(weights, entering, seg_row), params, stream)
        grad_weights, grad_in = pullback(output_gradient)
        totals = jax.tree.map(lambda total_a, total_b: total_a + total_b, totals, grad_weights)
        return (totals, (result.astype(jnp.bfloat16), grad_in))
    zeros_tree = jax.tree.map(jnp.zeros_like, params)
    totals, (output, grad_tokens) = lax.scan(per_sequence, zeros_tree, (tokens.astype(jnp.float32), segments, cotangent.astype(jnp.float32)))
    return (output, grad_tokens, totals[0], totals[1], totals[2], totals[3], totals[4], totals[5], totals[6])
```

```python
import jax
import jax.numpy as jnp
from jax import lax
from jax.sharding import PartitionSpec as P

BF = jnp.bfloat16
F32 = jnp.float32


def layer_norm(values, gain_vec, shift_vec):
    center = values - jnp.mean(values, axis=-1, keepdims=True)
    inv_std = lax.rsqrt(jnp.mean(center * center, axis=-1, keepdims=True) + 1e-05)
    normal = center * inv_std
    return (normal * gain_vec + shift_vec, normal, inv_std)


def norm_back(output_gradient, normal, inv_std, gain_vec):
    grad_normal = output_gradient * gain_vec
    mean_one = jnp.mean(grad_normal, axis=-1, keepdims=True)
    mean_two = jnp.mean(grad_normal * normal, axis=-1, keepdims=True)
    return inv_std * (grad_normal - mean_one - normal * mean_two)


def spread_band(band_rows):
    q_rows, window = band_rows.shape
    flipped = band_rows[:, ::-1]
    padded = jnp.concatenate([flipped, jnp.zeros((q_rows, q_rows + 1), band_rows.dtype)], axis=1)
    flat = jnp.concatenate([jnp.zeros((1,), band_rows.dtype), padded.reshape(-1)])
    return flat[: q_rows * (q_rows + window)].reshape(q_rows, q_rows + window)


def fold_band(matrix):
    q_rows, columns = matrix.shape
    window = columns - q_rows
    flat = jnp.concatenate([matrix.reshape(-1)[1:], jnp.zeros((q_rows + 1,), matrix.dtype)])
    return flat.reshape(q_rows, columns + 1)[:, :window][:, ::-1]


def dot_nt(lhs, rhs):
    return lax.dot_general(lhs, rhs, (((1,), (1,)), ((), ())), preferred_element_type=F32)


def dot_nn(lhs, rhs):
    return lax.dot_general(lhs, rhs, (((1,), (0,)), ((), ())), preferred_element_type=F32)


def dot_tn(lhs, rhs):
    return lax.dot_general(lhs, rhs, (((0,), (0,)), ((), ())), preferred_element_type=F32)


class Links:
    def __init__(self, dp, mp):
        self.dp = dp
        self.mp = mp
        self.dp_bits = [1 << k for k in range(1, dp.bit_length() - 1)]

    def swap(self, value, axis, bit):
        size = self.dp if axis == "dp" else self.mp
        return lax.ppermute(value, axis, [(i, i ^ bit) for i in range(size)])

    def gather_mp(self, piece):
        parts = [piece] + [self.swap(piece, "mp", p) for p in range(1, self.mp)]
        return jnp.stack(parts, axis=0)

    def scatter_mp(self, blocks):
        total = blocks[0].astype(F32)
        for p in range(1, self.mp):
            total = total + self.swap(blocks[p], "mp", p).astype(F32)
        return total.astype(BF)

    def gather_bits(self, value, bits):
        have = []
        for bit in bits:
            place = sum(1 for other in have if other > bit)
            value = jnp.stack([value, self.swap(value, "dp", bit)], axis=place)
            have.append(bit)
        return value

    def scatter_bits(self, value, bits):
        have = sorted(bits, reverse=True)
        for bit in bits:
            place = have.index(bit)
            keep = lax.index_in_dim(value, 0, place, keepdims=False)
            send = lax.index_in_dim(value, 1, place, keepdims=False)
            value = (keep.astype(F32) + self.swap(send, "dp", bit).astype(F32)).astype(BF)
            have.remove(bit)
        return value

    def gather(self, piece_a, piece_b):
        both = self.gather_mp(jnp.concatenate([piece_a, piece_b], axis=0))
        cut = piece_a.shape[0]
        out = []
        for value, bits in ((both[:, :cut], self.dp_bits), (both[:, cut:], self.dp_bits[::-1])):
            value = self.gather_bits(value, bits)
            value = value.reshape((-1,) + value.shape[-3:])
            out.append((value, self.swap(value, "dp", 1)))
        return out

    def reduce(self, halves_a, halves_b):
        parts = []
        for halves, bits in ((halves_a, self.dp_bits[::-1]), (halves_b, self.dp_bits)):
            own, other = halves
            value = (own.astype(F32) + self.swap(other, "dp", 1).astype(F32)).astype(BF)
            value = value.reshape((2,) * len(bits) + (self.mp,) + value.shape[1:])
            parts.append(self.scatter_bits(value, bits))
        return self.scatter_mp(jnp.concatenate(parts, axis=1))

    def regather(self, piece, index):
        bits = [1] + self.dp_bits
        value = self.gather_bits(piece, self.dp_bits)
        value = jnp.stack([value, self.swap(value, "dp", 1)], axis=len(self.dp_bits))
        value = value.reshape((self.dp,) + piece.shape)
        value = jnp.take(value, jnp.bitwise_xor(jnp.arange(self.dp), index), axis=0)
        value = jnp.transpose(value, (1, 0, 2, 3))
        return value.reshape(piece.shape[0], self.dp * piece.shape[1], piece.shape[2])

    def sum_all(self, value, axis):
        size = self.dp if axis == "dp" else self.mp
        bit = 1
        while bit < size:
            value = value + self.swap(value, axis, bit)
            bit *= 2
        return value


def gelu_tanh(values):
    return jax.nn.gelu(values, approximate=True)


def make_shards(dp, mp):
    links = Links(dp, mp)

    def shards(
        tokens,
        segments,
        qkv_weight,
        out_weight,
        up_weight,
        down_projection_weight,
        norm_gain,
        norm_bias,
        pos_bias,
        cotangent,
    ):
        seqs, block, width = tokens.shape
        layers = qkv_weight.shape[0]
        window = pos_bias.shape[2]
        channels = qkv_weight.shape[-1]
        hidden = up_weight.shape[-1]
        rows = seqs * block
        dp_index = lax.axis_index("dp")
        mp_index = lax.axis_index("mp")

        def own_piece(matrix):
            size = matrix.shape[-2] // dp
            return lax.dynamic_slice_in_dim(matrix, dp_index * size, size, axis=matrix.ndim - 2)

        gathered = []
        for layer in range(layers):
            qkv_rows = jnp.transpose(qkv_weight[layer], (0, 2, 1))
            attn = own_piece(jnp.concatenate([qkv_rows, out_weight[layer][None]], axis=0))
            up = own_piece(jnp.transpose(up_weight[layer])[None])
            down = own_piece(down_projection_weight[layer][None])
            pair_a, pair_b = links.gather(attn[:2], attn[2:])
            mats = []
            for pair in (pair_a, pair_b):
                for m in range(2):
                    mats.append(
                        jnp.concatenate([half[:, m].reshape(-1, width) for half in pair], axis=0)
                    )
            up_pair, down_pair = links.gather(up, down)
            ups = [half.reshape(-1, width) for half in up_pair]
            downs = [half.reshape(-1, width) for half in down_pair]
            gathered.append((mats, ups, downs))

        seg_pad = jnp.concatenate([jnp.full((seqs, window), -1, segments.dtype), segments], axis=1)
        seg_keys = lax.dynamic_slice_in_dim(seg_pad, mp_index * block, block + window, axis=1)
        seg_own = seg_keys[:, window:]
        same_doc = seg_own[:, :, None] == seg_keys[:, None, :]

        stream = tokens.reshape(rows, width).astype(F32)
        records = []
        for layer in range(layers):
            gains = norm_gain[layer]
            shifts = norm_bias[layer]
            (wq, wk, wv, wo), ups, downs = gathered[layer]
            normed, normal_a, inv_a = layer_norm(stream, gains[0], shifts[0])
            normed_a = normed.astype(BF)
            halo = lax.ppermute(normed_a, "mp", [(i, i + 1) for i in range(mp - 1)])
            both = jnp.concatenate(
                [halo.reshape(seqs, block, width), normed_a.reshape(seqs, block, width)], axis=1
            ).reshape(seqs * (window + block), width)
            queries = dot_nt(normed_a, wq)
            keys = dot_nt(both, wk)
            value_rows = dot_nt(both, wv)
            key_exp = jnp.exp(keys)
            keyvals = jnp.concatenate(
                [(key_exp * value_rows).astype(BF), key_exp.astype(BF)], axis=-1
            ).reshape(seqs, window + block, 2 * width)
            band_own = lax.dynamic_slice_in_dim(pos_bias[layer], mp_index * block, block, axis=0)
            spread = spread_band(jnp.exp(band_own))
            masked = jnp.where(same_doc, spread[None], 0.0)
            weights = masked.astype(BF)
            sums = jnp.einsum("sqk,skc->sqc", weights, keyvals, preferred_element_type=F32)
            sums = sums.reshape(rows, 2 * width)
            mixed = (jax.nn.sigmoid(queries) * sums[:, :width] / sums[:, width:]).astype(BF)
            stream = stream + dot_nn(mixed, wo)
            normed_two, normal_b, inv_b = layer_norm(stream, gains[1], shifts[1])
            normed_b = normed_two.astype(BF)
            pres = [dot_nt(normed_b, up) for up in ups]
            acts = [gelu_tanh(pre).astype(BF) for pre in pres]
            for act, down in zip(acts, downs):
                stream = stream + dot_nn(act, down)
            records.append(
                (
                    normal_a, inv_a, normed_a, both, queries, value_rows, key_exp, keyvals,
                    masked, weights, sums, mixed, normal_b, inv_b, normed_b, pres, acts,
                )
            )
        output = stream.astype(BF).reshape(seqs, block, width)

        grad = cotangent.reshape(rows, width)
        weight_out = [None] * layers
        small_out = [None] * layers
        for layer in reversed(range(layers)):
            gains = norm_gain[layer]
            (wq, wk, wv, wo), ups, downs = gathered[layer]
            (
                normal_a, inv_a, normed_a, both, queries, value_rows, key_exp, keyvals,
                masked, weights, sums, mixed, normal_b, inv_b, normed_b, pres, acts,
            ) = records[layer]
            grad_low = grad.astype(BF)
            down_grads = [dot_tn(act, grad_low).astype(BF) for act in acts]
            pre_grads = []
            for pre, down in zip(pres, downs):
                _, pull = jax.vjp(gelu_tanh, pre)
                pre_grads.append(pull(dot_nt(grad_low, down))[0].astype(BF))
            up_grads = [dot_tn(pre_grad, normed_b).astype(BF) for pre_grad in pre_grads]
            shape = (dp // 2 * mp, 1, hidden // dp, width)
            ff_piece = links.reduce(
                [item.reshape(shape) for item in up_grads], [item.reshape(shape) for item in down_grads]
            )
            grad_normed = sum(dot_nn(pre_grad, up) for pre_grad, up in zip(pre_grads, ups))
            grad = grad + norm_back(grad_normed, normal_b, inv_b, gains[1])
            gain_b = jnp.sum(grad_normed * normal_b, axis=0)
            shift_b = jnp.sum(grad_normed, axis=0)

            grad_low = grad.astype(BF)
            out_grad = dot_tn(mixed, grad_low).astype(BF)
            grad_mixed = dot_nt(grad_low, wo)
            numerator = sums[:, :width]
            denominator = sums[:, width:]
            sig = jax.nn.sigmoid(queries)
            grad_q = (grad_mixed * (numerator / denominator) * sig * (1.0 - sig)).astype(BF)
            scaled = grad_mixed * sig
            grad_num = (scaled / denominator).astype(BF)
            grad_den = (-scaled * numerator / (denominator * denominator)).astype(BF)
            grad_sums = jnp.concatenate([grad_num, grad_den], axis=-1).reshape(seqs, block, 2 * width)
            grad_kv = jnp.einsum("sqk,sqc->skc", weights, grad_sums, preferred_element_type=F32)
            grad_weights = jnp.einsum("sqc,skc->sqk", grad_sums, keyvals, preferred_element_type=F32)
            band_grad = fold_band(jnp.sum(grad_weights * masked, axis=0))
            grad_kv = grad_kv.reshape(seqs * (window + block), 2 * width)
            grad_carried = grad_kv[:, :width]
            grad_v = (grad_carried * key_exp).astype(BF)
            grad_k = ((grad_carried * value_rows + grad_kv[:, width:]) * key_exp).astype(BF)
            grad_both = (dot_nn(grad_k, wk) + dot_nn(grad_v, wv)).reshape(seqs, window + block, width)
            back = lax.ppermute(
                grad_both[:, :window].astype(BF), "mp", [(i + 1, i) for i in range(mp - 1)]
            )
            q_grad = dot_tn(grad_q, normed_a).astype(BF)
            k_grad = dot_tn(grad_k, both).astype(BF)
            v_grad = dot_tn(grad_v, both).astype(BF)
            shape = (2, dp // 2 * mp, channels // dp, width)

            def halves(first, second):
                return [
                    jnp.stack([first.reshape(shape)[c], second.reshape(shape)[c]], axis=1)
                    for c in range(2)
                ]

            attn_piece = links.reduce(halves(q_grad, k_grad), halves(v_grad, out_grad))
            grad_normed = dot_nn(grad_q, wq) + (grad_both[:, window:] + back.astype(F32)).reshape(
                rows, width
            )
            grad = grad + norm_back(grad_normed, normal_a, inv_a, gains[0])
            gain_a = jnp.sum(grad_normed * normal_a, axis=0)
            shift_a = jnp.sum(grad_normed, axis=0)
            ff_full = links.regather(ff_piece, dp_index).astype(F32)
            attn_full = links.regather(attn_piece, dp_index).astype(F32)
            weight_out[layer] = (
                jnp.transpose(attn_full[:3], (0, 2, 1)),
                attn_full[3],
                jnp.transpose(ff_full[0]),
                ff_full[1],
            )
            norms = jnp.stack([gain_a, gain_b, shift_a, shift_b]).reshape(-1, window)
            packed = links.sum_all(jnp.concatenate([band_grad, norms], axis=0), "dp")
            spread_out = lax.all_gather(packed[:block], "mp", axis=0, tiled=True)
            norm_sum = links.sum_all(packed[block:], "mp").reshape(4, width)
            small_out[layer] = (norm_sum[:2], norm_sum[2:], spread_out)

        grad_tokens = grad.reshape(seqs, block, width)
        big = tuple(jnp.stack([weight_out[l][k] for l in range(layers)]) for k in range(4))
        small = tuple(jnp.stack([small_out[l][k] for l in range(layers)]) for k in range(3))
        return (output, grad_tokens) + big + small

    return shards


def solution(mesh):
    placed = (
        P("dp", "mp", None),
        P("dp", None),
        P(None, None, None, "mp"),
        P(None, "mp", None),
        P(None, None, "mp"),
        P(None, "mp", None),
        P(),
        P(),
        P(),
        P("dp", "mp", None),
    )
    return jax.shard_map(
        make_shards(mesh.shape["dp"], mesh.shape["mp"]),
        mesh=mesh,
        in_specs=placed,
        out_specs=(
            P("dp", "mp", None),
            P("dp", "mp", None),
            P(None, None, None, "mp"),
            P(None, "mp", None),
            P(None, None, "mp"),
            P(None, "mp", None),
            P(),
            P(),
            P(),
        ),
        check_vma=False,
    )
```

```python
import functools

import jax
import jax.numpy as jnp
from jax import lax
from jax.experimental import pallas as pl
from jax.experimental.pallas import tpu as pltpu
from jax.sharding import PartitionSpec as P

BF = jnp.bfloat16
F32 = jnp.float32
VMEM_LIMIT = 58 * 1024 * 1024
TOKEN = (8, 128)
GELU_A = 0.7978845608028654
GELU_B = 0.044715


def dot_nt(lhs, rhs):
    return lax.dot_general(lhs, rhs, (((1,), (1,)), ((), ())), preferred_element_type=F32)


def dot_nn(lhs, rhs):
    return lax.dot_general(lhs, rhs, (((1,), (0,)), ((), ())), preferred_element_type=F32)


def dot_tn(lhs, rhs):
    return lax.dot_general(lhs, rhs, (((0,), (0,)), ((), ())), preferred_element_type=F32)


def normalize(values):
    center = values - jnp.mean(values, axis=-1, keepdims=True)
    inv_std = lax.rsqrt(jnp.mean(center * center, axis=-1, keepdims=True) + 1e-05)
    return center * inv_std, inv_std


def norm_back(grad_out, normal, inv_std, gain):
    grad_normal = grad_out * gain
    mean_one = jnp.mean(grad_normal, axis=-1, keepdims=True)
    mean_two = jnp.mean(grad_normal * normal, axis=-1, keepdims=True)
    return inv_std * (grad_normal - mean_one - normal * mean_two)


def whole(shape):
    return pl.BlockSpec(shape, lambda *_: (0,) * len(shape))


def call(order, body, grid, in_specs, out_specs, out_shape, scratch=(), prefetch=0, name=None):
    first = prefetch + len(in_specs)
    second = first + 1 + len(out_specs)
    anywhere = pl.BlockSpec(memory_space=pl.ANY)

    def with_token(*refs):
        return body(*refs[:first], *refs[first + 1 : second], *refs[second + 1 :])

    kernel = pl.pallas_call(
        with_token,
        grid_spec=pltpu.PrefetchScalarGridSpec(
            num_scalar_prefetch=prefetch,
            grid=grid,
            in_specs=list(in_specs) + [anywhere],
            out_specs=list(out_specs) + [anywhere],
            scratch_shapes=list(scratch),
        ),
        out_shape=list(out_shape) + [shape_of(TOKEN, jnp.int32)],
        input_output_aliases={first: len(out_specs)},
        compiler_params=pltpu.CompilerParams(
            dimension_semantics=("arbitrary",) * len(grid), vmem_limit_bytes=VMEM_LIMIT
        ),
        cost_estimate=pl.CostEstimate(flops=0, bytes_accessed=0, transcendentals=0),
        name=name,
    )

    def run(*operands):
        *results, order.token = kernel(*operands, order.token)
        return results

    return run


def shape_of(shape, dtype):
    return jax.ShapeDtypeStruct(shape, dtype)


def tie(*arrays):
    count = len(arrays)
    return pl.pallas_call(
        lambda *refs: None,
        out_shape=[shape_of(a.shape, a.dtype) for a in arrays],
        in_specs=[pl.BlockSpec(memory_space=pl.ANY)] * count,
        out_specs=[pl.BlockSpec(memory_space=pl.ANY)] * count,
        input_output_aliases={i: i for i in range(count)},
        cost_estimate=pl.CostEstimate(flops=0, bytes_accessed=0, transcendentals=0),
        name="tie",
    )(*arrays)


def enter_kernel(order, tokens, gain, shift):
    rows, width = tokens.shape

    def body(t_ref, g_ref, s_ref, x_ref, n_ref):
        x = t_ref[...].astype(F32)
        x_ref[...] = x
        normal, _ = normalize(x)
        n_ref[...] = (normal * g_ref[...] + s_ref[...]).astype(BF)

    return call(
        order,
        body,
        (1,),
        [whole((rows, width)), whole((1, width)), whole((1, width))],
        [whole((rows, width)), whole((rows, width))],
        [shape_of((rows, width), F32), shape_of((rows, width), BF)],
        name="enter",
    )(tokens, gain, shift)


def attn_forward(order, top, x, normed, halo, weights, band_rev, seg_q, seg_k, gain, shift):
    rows, width = x.shape
    seqs, block, _ = seg_q.shape
    keys = seg_k.shape[2]
    window = keys - block
    quarter = weights[0].shape[1]
    half = 2 * quarter

    def body(top_ref, x_ref, n_ref, h_ref, oa, ob, ta, tb, band_ref, sq_ref, sk_ref, g_ref, s_ref,
             sg_ref, ratio_ref, rden_ref, v_ref, kexp_ref, mixed_ref, masked_ref, x1_ref, nb_ref, both_ref, mix):
        step = pl.program_id(0)

        @pl.when(step == 0)
        def _():
            for s in range(seqs):
                both_ref[s * keys : s * keys + window] = h_ref[s * block : (s + 1) * block]
                both_ref[s * keys + window : (s + 1) * keys] = n_ref[s * block : (s + 1) * block]
            band = jnp.concatenate([jnp.exp(band_ref[...]), jnp.zeros((block, block), F32)], axis=1)
            spread = pltpu.roll(band, 1, axis=1, stride=1, stride_axis=0)
            for s in range(seqs):
                masked = jnp.where(sq_ref[s] == sk_ref[s], spread, 0.0)
                masked_ref[s] = masked
                mix[s] = masked.astype(BF)
            x1_ref[...] = x_ref[...]

        def part(wa, wb):
            def mat(m):
                return jnp.concatenate([wa[top_ref[0] ^ m], wb[top_ref[0] ^ m]], axis=0)

            both = both_ref[...]
            q = dot_nt(n_ref[...], mat(0))
            kexp = jnp.exp(dot_nt(both, mat(1)))
            v = dot_nt(both, mat(2))
            v_ref[...] = v
            kexp_ref[...] = kexp
            carried = (kexp * v).astype(BF)
            wsum = kexp.astype(BF)
            sg = jax.nn.sigmoid(q)
            sg_ref[...] = sg
            mixed = []
            for s in range(seqs):
                num = dot_nn(mix[s], carried[s * keys : (s + 1) * keys])
                den = dot_nn(mix[s], wsum[s * keys : (s + 1) * keys])
                rden = 1.0 / den
                ratio = num * rden
                here = slice(s * block, (s + 1) * block)
                rden_ref[here] = rden
                ratio_ref[here] = ratio
                mixed.append((sg[here] * ratio).astype(BF))
            mixed = jnp.concatenate(mixed, axis=0)
            mixed_ref[...] = mixed
            x1_ref[...] += dot_nn(mixed, mat(3))

        @pl.when(step == 0)
        def _():
            part(oa, ob)

        @pl.when(step == 1)
        def _():
            part(ta, tb)
            normal, _ = normalize(x1_ref[...])
            nb_ref[...] = (normal * g_ref[...] + s_ref[...]).astype(BF)

    def col(n):
        return pl.BlockSpec((n, half), lambda i, *_: (0, i))

    return call(
        order,
        body,
        (2,),
        [whole((rows, width))] * 3
        + [whole((4, quarter, width))] * 4
        + [whole((block, window)), whole((seqs, block, 1)), whole((seqs, 1, keys)), whole((1, width)), whole((1, width))],
        [col(rows)] * 3 + [col(seqs * keys)] * 2 + [col(rows)]
        + [whole((seqs, block, keys)), whole((rows, width)), whole((rows, width)), whole((seqs * keys, width))],
        [shape_of((rows, width), F32)] * 3
        + [shape_of((seqs * keys, width), F32)] * 2
        + [
            shape_of((rows, width), BF),
            shape_of((seqs, block, keys), F32),
            shape_of((rows, width), F32),
            shape_of((rows, width), BF),
            shape_of((seqs * keys, width), BF),
        ],
        [pltpu.VMEM((seqs, block, keys), BF)],
        prefetch=1,
        name="attn_fwd",
    )(top, x, normed, halo, *weights, band_rev, seg_q, seg_k, gain, shift)


def gelu_both(pre):
    square = pre * pre
    th = jnp.tanh(GELU_A * pre * (1.0 + GELU_B * square))
    upper = 0.5 * (1.0 + th)
    slope = upper + 0.5 * GELU_A * pre * (1.0 - th * th) * (1.0 + 3.0 * GELU_B * square)
    return pre * upper, slope


def chunk_specs(chunk, width, per_half):
    own = pl.BlockSpec((chunk, width), lambda i, *_: (jnp.minimum(i, per_half - 1), 0))
    other = pl.BlockSpec((chunk, width), lambda i, *_: (jnp.maximum(i - per_half, 0), 0))
    return own, other


def ff_forward(order, x1, normed, ups, downs, gain, shift):
    rows, width = x1.shape
    half = ups[0].shape[0]
    per_half = 2
    chunk = half // per_half
    steps = 2 * per_half

    def body(x_ref, n_ref, u0, u1, d0, d1, g_ref, s_ref, act_ref, slope_ref, x2_ref, next_ref):
        step = pl.program_id(0)

        @pl.when(step == 0)
        def _():
            x2_ref[...] = x_ref[...]

        def part(u, d):
            act, slope = gelu_both(dot_nt(n_ref[...], u[...]))
            act = act.astype(BF)
            act_ref[...] = act
            slope_ref[...] = slope.astype(BF)
            x2_ref[...] += dot_nn(act, d[...])

        pl.when(step < per_half)(lambda: part(u0, d0))
        pl.when(step >= per_half)(lambda: part(u1, d1))

        @pl.when(step == steps - 1)
        def _():
            normal, _ = normalize(x2_ref[...])
            next_ref[...] = (normal * g_ref[...] + s_ref[...]).astype(BF)

    own, other = chunk_specs(chunk, width, per_half)
    col = pl.BlockSpec((rows, chunk), lambda i: (0, i))
    return call(
        order,
        body,
        (steps,),
        [whole((rows, width))] * 2 + [own, other, own, other] + [whole((1, width))] * 2,
        [col, col, whole((rows, width)), whole((rows, width))],
        [
            shape_of((rows, 2 * half), BF),
            shape_of((rows, 2 * half), BF),
            shape_of((rows, width), F32),
            shape_of((rows, width), BF),
        ],
        name="ff_fwd",
    )(x1, normed, *ups, *downs, gain, shift)


def ff_backward(order, x1, normed, ups, downs, grad, gain, saved):
    rows, width = x1.shape
    half = ups[0].shape[0]
    per_half = 2
    chunk = half // per_half
    steps = 2 * per_half
    fresh = saved is None

    def body(x_ref, n_ref, u0, u1, d0, d1, grad_ref, g_ref, *rest):
        if fresh:
            (out_ref, gu0, gu1, gd0, gd1, g1_ref, ga_ref, gg_ref, gs_ref, low, dn, x2) = rest
        else:
            (act_ref, slope_ref, gu0, gu1, gd0, gd1, g1_ref, ga_ref, gg_ref, gs_ref, low, dn) = rest
        step = pl.program_id(0)

        @pl.when(step == 0)
        def _():
            low[...] = grad_ref[...].astype(BF)
            dn[...] = jnp.zeros_like(dn)
            if fresh:
                x2[...] = x_ref[...]

        def part(u, d, gu, gd):
            if fresh:
                act, slope = gelu_both(dot_nt(n_ref[...], u[...]))
                act = act.astype(BF)
                x2[...] += dot_nn(act, d[...])
            else:
                act, slope = act_ref[...], slope_ref[...].astype(F32)
            pre_grad = (dot_nt(low[...], d[...]) * slope).astype(BF)
            dn[...] += dot_nn(pre_grad, u[...])
            gd[...] = dot_tn(act, low[...]).astype(BF)
            gu[...] = dot_tn(pre_grad, n_ref[...]).astype(BF)

        pl.when(step < per_half)(lambda: part(u0, d0, gu0, gd0))
        pl.when(step >= per_half)(lambda: part(u1, d1, gu1, gd1))

        @pl.when(step == steps - 1)
        def _():
            if fresh:
                out_ref[...] = x2[...].astype(BF)
            normal, inv = normalize(x_ref[...])
            total = dn[...]
            g1 = grad_ref[...] + norm_back(total, normal, inv, g_ref[...])
            g1_ref[...] = g1
            ga_ref[...] = g1.astype(BF)
            gg_ref[...] = jnp.sum(total * normal, axis=0, keepdims=True)
            gs_ref[...] = jnp.sum(total, axis=0, keepdims=True)

    own, other = chunk_specs(chunk, width, per_half)
    col = pl.BlockSpec((rows, chunk), lambda i: (0, i))
    out_specs = [own, other, own, other] + [whole((rows, width))] * 2 + [whole((1, width))] * 2
    out_shape = (
        [shape_of((half, width), BF)] * 4
        + [shape_of((rows, width), F32), shape_of((rows, width), BF)]
        + [shape_of((1, width), F32)] * 2
    )
    scratch = [pltpu.VMEM((rows, width), BF), pltpu.VMEM((rows, width), F32)]
    if fresh:
        out_specs = [whole((rows, width))] + out_specs
        out_shape = [shape_of((rows, width), BF)] + out_shape
        scratch.append(pltpu.VMEM((rows, width), F32))
    return call(
        order,
        body,
        (steps,),
        [whole((rows, width))] * 2 + [own, other, own, other] + [whole((rows, width)), whole((1, width))]
        + ([] if fresh else [col, col]),
        out_specs,
        out_shape,
        scratch,
        name="ff_bwd",
    )(x1, normed, *ups, *downs, grad, gain, *(() if fresh else saved))


def attn_backward(order, top, grad_low, weights, sg, ratio, rden, v, kexp, masked):
    rows, width = grad_low.shape
    seqs, block, keys = masked.shape
    window = keys - block
    quarter = weights[0].shape[1]
    half = 2 * quarter

    def body(top_ref, ga_ref, oa, ob, ta, tb, sg_ref, ratio_ref, rden_ref, v_ref, kexp_ref, masked_ref,
             gq_ref, gk_ref, gv_ref, band_ref, own_ref, halo_ref, mix_t, wgrad, dn):
        step = pl.program_id(0)

        @pl.when(step == 0)
        def _():
            for s in range(seqs):
                mix_t[s] = masked_ref[s].T.astype(BF)
            wgrad[...] = jnp.zeros_like(wgrad)
            dn[...] = jnp.zeros_like(dn)

        def part(wa, wb):
            def mat(m):
                return jnp.concatenate([wa[top_ref[0] ^ m], wb[top_ref[0] ^ m]], axis=0)

            gm = dot_nt(ga_ref[...], mat(3))
            sig = sg_ref[...]
            rat = ratio_ref[...]
            scaled = gm * sig
            gq = (scaled * rat * (1.0 - sig)).astype(BF)
            gq_ref[...] = gq
            gnum_f = scaled * rden_ref[...]
            gnum = gnum_f.astype(BF)
            gden = (-gnum_f * rat).astype(BF)
            wq, wk, wv = mat(0), mat(1), mat(2)
            dq = dot_nn(gq, wq)
            for s in range(seqs):
                here = slice(s * block, (s + 1) * block)
                there = slice(s * keys, (s + 1) * keys)
                vv = v_ref[there]
                ke = kexp_ref[there]
                gcar = dot_nn(mix_t[s], gnum[here])
                gsum = dot_nn(mix_t[s], gden[here])
                gv = (gcar * ke).astype(BF)
                gk = ((gcar * vv + gsum) * ke).astype(BF)
                gk_ref[there] = gk
                gv_ref[there] = gv
                wgrad[s] += dot_nt(gnum[here], (ke * vv).astype(BF)) + dot_nt(gden[here], ke.astype(BF))
                dkv = dot_nn(gk, wk) + dot_nn(gv, wv)
                dn[s * keys : s * keys + window] += dkv[:window]
                dn[s * keys + window : (s + 1) * keys] += dkv[window:] + dq[here]

        @pl.when(step == 0)
        def _():
            part(oa, ob)

        @pl.when(step == 1)
        def _():
            part(ta, tb)
            total = wgrad[0] * masked_ref[0]
            for s in range(1, seqs):
                total = total + wgrad[s] * masked_ref[s]
            lane_row = lax.broadcasted_iota(jnp.int32, (block, keys), 0) + 1
            bit = 1
            while bit <= block:
                rolled = pltpu.roll(total, keys - bit, axis=1)
                total = jnp.where((lane_row & bit) != 0, rolled, total)
                bit *= 2
            band_ref[...] = total[:, :window]
            for s in range(seqs):
                halo_ref[s * block : (s + 1) * block] = dn[s * keys : s * keys + window].astype(BF)
                own_ref[s * block : (s + 1) * block] = dn[s * keys + window : (s + 1) * keys]

    def col(n):
        return pl.BlockSpec((n, half), lambda i, *_: (0, i))

    return call(
        order,
        body,
        (2,),
        [whole((rows, width))]
        + [whole((4, quarter, width))] * 4
        + [col(rows)] * 3 + [col(seqs * keys)] * 2 + [whole((seqs, block, keys))],
        [col(rows), col(seqs * keys), col(seqs * keys), whole((block, window)), whole((rows, width)), whole((rows, width))],
        [
            shape_of((rows, width), BF),
            shape_of((seqs * keys, width), BF),
            shape_of((seqs * keys, width), BF),
            shape_of((block, window), F32),
            shape_of((rows, width), F32),
            shape_of((rows, width), BF),
        ],
        [
            pltpu.VMEM((seqs, keys, block), BF),
            pltpu.VMEM((seqs, block, keys), F32),
            pltpu.VMEM((seqs * keys, width), F32),
        ],
        prefetch=1,
        name="attn_bwd",
    )(top, grad_low, *weights, sg, ratio, rden, v, kexp, masked)


def attn_weight_grads(order, top, gq, gk, gv, mixed, normed, both, grad_low):
    rows, width = gq.shape
    keyrows = both.shape[0]
    half = width // 2
    quarter = half // 2

    def body(top_ref, gq_ref, gk_ref, gv_ref, mixed_ref, n_ref, b_ref, ga_ref, oa, ob, ta, tb):
        step = pl.program_id(0)
        mat = lax.rem(step, 4)

        def store(value):
            low = value.astype(BF)

            @pl.when(step < 4)
            def _():
                oa[0] = low[:quarter]
                ob[0] = low[quarter:]

            @pl.when(step >= 4)
            def _():
                ta[0] = low[:quarter]
                tb[0] = low[quarter:]

        pl.when(mat == 0)(lambda: store(dot_tn(gq_ref[...], n_ref[...])))
        pl.when(mat == 1)(lambda: store(dot_tn(gk_ref[...], b_ref[...])))
        pl.when(mat == 2)(lambda: store(dot_tn(gv_ref[...], b_ref[...])))
        pl.when(mat == 3)(lambda: store(dot_tn(mixed_ref[...], ga_ref[...])))

    def col(n):
        return pl.BlockSpec((n, half), lambda i, *_: (0, i // 4))

    own = pl.BlockSpec((1, quarter, width), lambda i, t: (jnp.minimum(i, 3) ^ t[0], 0, 0))
    other = pl.BlockSpec((1, quarter, width), lambda i, t: (jnp.maximum(i - 4, 0) ^ t[0], 0, 0))
    return call(
        order,
        body,
        (8,),
        [col(rows), col(keyrows), col(keyrows), col(rows), whole((rows, width)), whole((keyrows, width)), whole((rows, width))],
        [own, own, other, other],
        [shape_of((4, quarter, width), BF)] * 4,
        prefetch=1,
        name="attn_wgrad",
    )(top, gq, gk, gv, mixed, normed, both, grad_low)


def leave_attn(order, x, grad, own, back, gain):
    rows, width = x.shape

    def body(x_ref, g_ref, o_ref, b_ref, gain_ref, out_ref, gg_ref, gs_ref):
        normal, inv = normalize(x_ref[...])
        total = o_ref[...] + b_ref[...].astype(F32)
        out_ref[...] = g_ref[...] + norm_back(total, normal, inv, gain_ref[...])
        gg_ref[...] = jnp.sum(total * normal, axis=0, keepdims=True)
        gs_ref[...] = jnp.sum(total, axis=0, keepdims=True)

    return call(
        order,
        body,
        (1,),
        [whole((rows, width))] * 4 + [whole((1, width))],
        [whole((rows, width)), whole((1, width)), whole((1, width))],
        [shape_of((rows, width), F32)] + [shape_of((1, width), F32)] * 2,
        name="leave",
    )(x, grad, own, back, gain)


class Order:
    def __init__(self):
        self.token = jnp.zeros(TOKEN, jnp.int32)

    def pin(self, *arrays):
        *arrays, self.token = tie(*arrays, self.token)
        return arrays


class Links:
    def __init__(self, order, dp, mp):
        self.order = order
        self.dp = dp
        self.mp = mp
        bits = [1 << k for k in range(1, dp.bit_length() - 1)]
        self.routes = (bits, bits[::-1])

    def swap(self, value, axis, bit):
        size = self.dp if axis == "dp" else self.mp
        return lax.ppermute(value, axis, [(i, i ^ bit) for i in range(size)])


class Spread:
    def __init__(self, links, values):
        self.links = links
        self.values = list(values)
        self.phase = 0
        self.have = [[], []]

    def start(self):
        self.values = self.links.order.pin(*self.values)
        self.coming = [
            self.links.swap(value, "dp", route[self.phase])
            for value, route in zip(self.values, self.links.routes)
        ]

    def wait(self):
        coming = self.links.order.pin(*self.coming)
        for k in range(2):
            bit = self.links.routes[k][self.phase]
            place = sum(1 for other in self.have[k] if other > bit)
            self.values[k] = jnp.stack([self.values[k], coming[k]], axis=place)
            self.have[k].append(bit)
        self.phase += 1

    def wait_all(self):
        self.wait()
        while self.phase < len(self.links.routes[0]):
            self.start()
            self.wait()

    def start_cores(self):
        self.values = self.links.order.pin(*self.values)
        self.coming = [self.links.swap(value, "dp", 1) for value in self.values]

    def wait_cores(self):
        return self.values + self.links.order.pin(*self.coming)


class Gather(Spread):
    def __init__(self, links, piece_a, piece_b):
        super().__init__(links, ())
        self.cut = piece_a.shape[0]
        self.piece = jnp.concatenate([piece_a, piece_b], axis=0)

    def start_mp(self):
        (self.piece,) = self.links.order.pin(self.piece)
        self.coming_mp = [self.links.swap(self.piece, "mp", p) for p in range(1, self.links.mp)]

    def wait_mp(self):
        parts = [self.piece] + self.links.order.pin(*self.coming_mp)
        self.values = [
            jnp.stack([part[: self.cut] for part in parts]),
            jnp.stack([part[self.cut :] for part in parts]),
        ]


class Reduce:
    def __init__(self, links, halves):
        self.links = links
        self.halves = halves
        self.phase = 0

    def start_cores(self):
        others = self.links.order.pin(*self.halves[2:])
        self.coming = [self.links.swap(other, "dp", 1) for other in others]

    def wait_cores(self):
        coming = self.links.order.pin(*self.coming)
        mp = self.links.mp
        self.have = [sorted(route, reverse=True) for route in self.links.routes]
        self.values = []
        for own, other in zip(self.halves[:2], coming):
            total = (own.astype(F32) + other.astype(F32)).astype(BF)
            groups = self.links.dp // 2
            rows = total.size // total.shape[-1] // groups // mp
            self.values.append(total.reshape((2,) * len(self.have[0]) + (mp, rows, total.shape[-1])))

    def start(self):
        sends, self.keeps = [], []
        for k in range(2):
            place = self.have[k].index(self.links.routes[1 - k][self.phase])
            self.keeps.append(lax.index_in_dim(self.values[k], 0, place, keepdims=False))
            sends.append(lax.index_in_dim(self.values[k], 1, place, keepdims=False))
        sends = self.links.order.pin(*sends)
        self.coming = [
            self.links.swap(sends[k], "dp", self.links.routes[1 - k][self.phase]) for k in range(2)
        ]

    def wait(self):
        coming = self.links.order.pin(*self.coming)
        for k in range(2):
            self.values[k] = (self.keeps[k].astype(F32) + coming[k].astype(F32)).astype(BF)
            self.have[k].remove(self.links.routes[1 - k][self.phase])
        self.phase += 1

    def wait_all(self):
        self.wait()
        while self.phase < len(self.links.routes[0]):
            self.start()
            self.wait()

    def start_mp(self):
        blocks = [jnp.concatenate([value[p] for value in self.values], axis=0) for p in range(self.links.mp)]
        self.kept = blocks[0]
        sends = self.links.order.pin(*blocks[1:])
        self.coming = [self.links.swap(send, "mp", p + 1) for p, send in enumerate(sends)]

    def wait_mp(self):
        total = self.kept.astype(F32)
        for part in self.links.order.pin(*self.coming):
            total = total + part.astype(F32)
        return total.astype(BF)


def make_shards(dp, mp):
    def shards(
        tokens,
        segments,
        qkv_weight,
        out_weight,
        up_weight,
        down_projection_weight,
        norm_gain,
        norm_bias,
        pos_bias,
        cotangent,
    ):
        seqs, block, width = tokens.shape
        layers = qkv_weight.shape[0]
        window = pos_bias.shape[2]
        channels = qkv_weight.shape[-1]
        hidden = up_weight.shape[-1]
        rows = seqs * block
        dp_index = lax.axis_index("dp")
        mp_index = lax.axis_index("mp")
        order = Order()
        links = Links(order, dp, mp)
        attn_rows = 4 * channels // dp
        ff_rows = hidden // dp
        top = (dp_index // 2 // (dp // 8)).astype(jnp.int32).reshape(1)

        def picks(count, offset, length):
            return (
                lax.broadcasted_iota(jnp.int32, (count, length), 0) + offset
                == lax.broadcasted_iota(jnp.int32, (count, length), 1)
            ).astype(BF)

        attn_pick = picks(attn_rows, dp_index * attn_rows, 4 * channels)
        ff_pick = picks(ff_rows, dp_index * ff_rows, hidden)

        def attn_gather(layer):
            piece = jnp.einsum(
                "rmc,mdc->rd",
                attn_pick[:, : 3 * channels].reshape(attn_rows, 3, channels),
                qkv_weight[layer],
                preferred_element_type=F32,
            ) + dot_nn(attn_pick[:, 3 * channels :], out_weight[layer])
            piece = piece.astype(BF)
            return Gather(links, piece[: attn_rows // 2], piece[attn_rows // 2 :])

        def ff_gather(layer):
            return Gather(
                links,
                dot_nt(ff_pick, up_weight[layer]).astype(BF),
                dot_nn(ff_pick, down_projection_weight[layer]).astype(BF),
            )

        def attn_mats(parts):
            return [part.reshape(4, -1, width) for part in parts]

        def ff_mats(parts):
            flat = [part.reshape(-1, width) for part in parts]
            return (flat[0], flat[2]), (flat[1], flat[3])

        def forward_halo(value):
            return lax.ppermute(value, "mp", [(i, i + 1) for i in range(mp - 1)])

        def backward_halo(value):
            return lax.ppermute(value, "mp", [(i + 1, i) for i in range(mp - 1)])

        gains = norm_gain.reshape(layers, 2, 1, width)
        shifts = norm_bias.reshape(layers, 2, 1, width)

        attn0 = attn_gather(0)
        attn0.start_mp()
        ff0 = ff_gather(0)
        ff0.start_mp()
        x, normed = enter_kernel(order, tokens.reshape(rows, width), gains[0, 0], shifts[0, 0])
        (normed,) = order.pin(normed)
        halo = forward_halo(normed)
        attn0.wait_mp()
        attn0.start()
        attn1 = attn_gather(1)
        attn1.start_mp()
        ff1 = ff_gather(1)
        ff1.start_mp()

        seg_pad = jnp.concatenate([jnp.full((seqs, window), -1, segments.dtype), segments], axis=1)
        seg_keys = lax.dynamic_slice_in_dim(seg_pad, mp_index * block, block + window, axis=1)
        seg_q = seg_keys[:, window:].reshape(seqs, block, 1)
        seg_k = seg_keys.reshape(seqs, 1, block + window)
        band_rev = lax.dynamic_slice_in_dim(pos_bias, mp_index * block, block, axis=1)[:, :, ::-1]

        attn0.wait()
        attn0.start()
        ff0.wait_mp()
        ff0.start()
        attn0.wait_all()
        attn0.start_cores()
        w_attn0 = attn_mats(attn0.wait_cores())
        ff0.wait()
        ff0.start()
        (halo,) = order.pin(halo)

        def attn(layer, x, normed, halo, w_attn):
            sg, ratio, rden, v, kexp, mixed, masked, x1, normed_b, both = attn_forward(
                order, top, x, normed, halo, w_attn, band_rev[layer], seg_q, seg_k,
                gains[layer, 1], shifts[layer, 1],
            )
            return x1, normed_b, (sg, ratio, rden, v, kexp, masked), (mixed, normed, both)

        x1_0, normed_b0, saved0, rows0 = attn(0, x, normed, halo, w_attn0)
        attn1.wait_mp()
        attn1.start()
        ff0.wait_all()
        ff0.start_cores()
        ups0, downs0 = ff_mats(ff0.wait_cores())
        attn1.wait()
        attn1.start()
        act0, slope0, x2, normed2 = ff_forward(
            order, x1_0, normed_b0, ups0, downs0, gains[1, 0], shifts[1, 0]
        )
        (normed2,) = order.pin(normed2)
        halo2 = forward_halo(normed2)
        ff1.wait_mp()
        ff1.start()
        attn1.wait_all()
        attn1.start_cores()
        w_attn1 = attn_mats(attn1.wait_cores())
        ff1.wait()
        ff1.start()
        (halo2,) = order.pin(halo2)
        x1_1, normed_b1, saved1, rows1 = attn(1, x2, normed2, halo2, w_attn1)
        ff1.wait_all()
        ff1.start_cores()
        ups1, downs1 = ff_mats(ff1.wait_cores())

        output, gu0, gu1, gd0, gd1, grad1, grad1_low, gain_b1, shift_b1 = ff_backward(
            order, x1_1, normed_b1, ups1, downs1, cotangent.reshape(rows, width), gains[1, 1], None
        )
        r_ff1 = Reduce(links, [gu0, gd0, gu1, gd1])
        r_ff1.start_cores()
        r_ff1.wait_cores()
        r_ff1.start()

        def attn_back(grad_low, w_attn, saved, kept):
            gq, gk, gv, band, dn_own, dn_halo = attn_backward(order, top, grad_low, w_attn, *saved)
            (dn_halo,) = order.pin(dn_halo)
            back = backward_halo(dn_halo)
            halves = attn_weight_grads(order, top, gq, gk, gv, *kept, grad_low)
            return band, dn_own, back, Reduce(links, halves)

        band1, dn_own1, back1, r_attn1 = attn_back(grad1_low, w_attn1, saved1, rows1)
        r_attn1.start_cores()
        r_attn1.wait_cores()
        r_attn1.start()
        (back1,) = order.pin(back1)
        grad2, gain_a1, shift_a1 = leave_attn(order, x2, grad1, dn_own1, back1, gains[1, 0])
        r_ff1.wait()
        r_ff1.start()
        gu0, gu1, gd0, gd1, grad3, grad3_low, gain_b0, shift_b0 = ff_backward(
            order, x1_0, normed_b0, ups0, downs0, grad2, gains[0, 1], (act0, slope0)
        )
        r_ff0 = Reduce(links, [gu0, gd0, gu1, gd1])
        r_ff0.start_cores()
        r_attn1.wait()
        r_attn1.start()
        r_ff0.wait_cores()
        r_ff0.start()
        r_ff1.wait_all()
        band0, dn_own0, back0, r_attn0 = attn_back(grad3_low, w_attn0, saved0, rows0)
        r_ff1.start_mp()
        r_attn0.start_cores()
        r_attn0.wait_cores()
        r_attn0.start()
        r_attn1.wait_all()
        r_attn1.start_mp()
        (back0,) = order.pin(back0)
        grad4, gain_a0, shift_a0 = leave_attn(order, x, grad3, dn_own0, back0, gains[0, 0])
        norms = jnp.concatenate(
            [gain_a0, gain_b0, shift_a0, shift_b0, gain_a1, gain_b1, shift_a1, shift_b1], axis=0
        ).reshape(-1, window)
        packed = jnp.concatenate([band0, band1, norms], axis=0)
        packed = lax.psum(packed, "dp")
        r_ff0.wait()
        r_ff0.start()
        r_attn0.wait()
        r_attn0.start()

        def halves_of(*pieces):
            joined = jnp.concatenate(pieces, axis=0)
            middle = joined.shape[0] // 2
            return joined[:middle], joined[middle:]

        back_1 = Spread(links, halves_of(r_attn1.wait_mp(), r_ff1.wait_mp()))
        r_ff0.wait_all()
        r_ff0.start_mp()
        back_1.start()
        r_attn0.wait_all()
        r_attn0.start_mp()
        back_1.wait()
        back_1.start()
        (packed,) = order.pin(packed)
        packed = lax.all_gather(packed, "mp", axis=0, tiled=False)
        back_1.wait_all()
        back_1.start_cores()
        full_1 = back_1.wait_cores()
        back_0 = Spread(links, halves_of(r_ff0.wait_mp(), r_attn0.wait_mp()))
        back_0.start()

        owner = jnp.bitwise_xor(jnp.arange(dp), dp_index)

        def results(full, attn_first):
            parts = [
                jnp.concatenate(
                    [half.reshape(dp // 2, 1, -1, width) for half in (full[k], full[2 + k])], axis=1
                )
                for k in range(2)
            ]
            value = jnp.concatenate(parts, axis=2).reshape(dp, -1, width)
            if attn_first:
                attn_part, up_part, down_part = jnp.split(value, [attn_rows, attn_rows + ff_rows], axis=1)
            else:
                up_part, down_part, attn_part = jnp.split(value, [ff_rows, 2 * ff_rows], axis=1)

            def places(count):
                spots = (owner[:, None] * count + jnp.arange(count)[None, :]).reshape(-1, 1)
                return (spots == jnp.arange(dp * count)[None, :]).astype(BF)

            attn_place = places(attn_rows).reshape(-1, 4, channels)
            ff_place = places(ff_rows)
            attn_part = attn_part.reshape(-1, width)
            return (
                jnp.einsum("pd,pmc->mdc", attn_part, attn_place[:, :3], preferred_element_type=F32),
                dot_tn(attn_place[:, 3], attn_part),
                dot_tn(up_part.reshape(-1, width), ff_place),
                dot_tn(ff_place, down_part.reshape(-1, width)),
            )

        out1 = results(full_1, True)
        back_0.wait()
        back_0.start()
        back_0.wait_all()
        back_0.start_cores()
        out0 = results(back_0.wait_cores(), False)
        big = tuple(jnp.stack([out0[k], out1[k]]) for k in range(4))
        band_sum = jnp.transpose(packed[:, : layers * block].reshape(mp, layers, block, window), (1, 0, 2, 3))
        band_sum = band_sum.reshape(layers, mp * block, window)[:, :, ::-1]
        norm_sum = jnp.sum(packed[:, layers * block :], axis=0).reshape(layers, 4, width)
        return (
            (output.reshape(tokens.shape), grad4.reshape(tokens.shape))
            + big
            + (norm_sum[:, :2], norm_sum[:, 2:], band_sum)
        )

    return shards


def solution(mesh):
    placed = (
        P("dp", "mp", None),
        P("dp", None),
        P(None, None, None, "mp"),
        P(None, "mp", None),
        P(None, None, "mp"),
        P(None, "mp", None),
        P(),
        P(),
        P(),
        P("dp", "mp", None),
    )
    return jax.shard_map(
        make_shards(mesh.shape["dp"], mesh.shape["mp"]),
        mesh=mesh,
        in_specs=placed,
        out_specs=(
            P("dp", "mp", None),
            P("dp", "mp", None),
            P(None, None, None, "mp"),
            P(None, "mp", None),
            P(None, None, "mp"),
            P(None, "mp", None),
            P(),
            P(),
            P(),
        ),
        check_vma=False,
    )
```

```python
import functools

import jax
import jax.numpy as jnp
from jax import lax
from jax.experimental import pallas as pl
from jax.experimental.pallas import tpu as pltpu
from jax.sharding import PartitionSpec as P

BF = jnp.bfloat16
F32 = jnp.float32
VMEM_LIMIT = 58 * 1024 * 1024
TOKEN = (8, 128)
GELU_A = 0.7978845608028654
GELU_B = 0.044715


def dot_nt(lhs, rhs):
    return lax.dot_general(lhs, rhs, (((1,), (1,)), ((), ())), preferred_element_type=F32)


def dot_nn(lhs, rhs):
    return lax.dot_general(lhs, rhs, (((1,), (0,)), ((), ())), preferred_element_type=F32)


def dot_tn(lhs, rhs):
    return lax.dot_general(lhs, rhs, (((0,), (0,)), ((), ())), preferred_element_type=F32)


def normalize(values):
    center = values - jnp.mean(values, axis=-1, keepdims=True)
    inv_std = lax.rsqrt(jnp.mean(center * center, axis=-1, keepdims=True) + 1e-05)
    return center * inv_std, inv_std


def norm_back(grad_out, normal, inv_std, gain):
    grad_normal = grad_out * gain
    mean_one = jnp.mean(grad_normal, axis=-1, keepdims=True)
    mean_two = jnp.mean(grad_normal * normal, axis=-1, keepdims=True)
    return inv_std * (grad_normal - mean_one - normal * mean_two)


def whole(shape):
    return pl.BlockSpec(shape, lambda *_: (0,) * len(shape))


def call(order, body, grid, in_specs, out_specs, out_shape, scratch=(), prefetch=0, name=None):
    first = prefetch + len(in_specs)
    second = first + 1 + len(out_specs)
    anywhere = pl.BlockSpec(memory_space=pl.ANY)

    def with_token(*refs):
        return body(*refs[:first], *refs[first + 1 : second], *refs[second + 1 :])

    kernel = pl.pallas_call(
        with_token,
        grid_spec=pltpu.PrefetchScalarGridSpec(
            num_scalar_prefetch=prefetch,
            grid=grid,
            in_specs=list(in_specs) + [anywhere],
            out_specs=list(out_specs) + [anywhere],
            scratch_shapes=list(scratch),
        ),
        out_shape=list(out_shape) + [shape_of(TOKEN, jnp.int32)],
        input_output_aliases={first: len(out_specs)},
        compiler_params=pltpu.CompilerParams(
            dimension_semantics=("arbitrary",) * len(grid), vmem_limit_bytes=VMEM_LIMIT
        ),
        cost_estimate=pl.CostEstimate(flops=0, bytes_accessed=0, transcendentals=0),
        name=name,
    )

    def run(*operands):
        *results, order.token = kernel(*operands, order.token)
        return results

    return run


def shape_of(shape, dtype):
    return jax.ShapeDtypeStruct(shape, dtype)


def tie(*arrays):
    count = len(arrays)
    return pl.pallas_call(
        lambda *refs: None,
        out_shape=[shape_of(a.shape, a.dtype) for a in arrays],
        in_specs=[pl.BlockSpec(memory_space=pl.ANY)] * count,
        out_specs=[pl.BlockSpec(memory_space=pl.ANY)] * count,
        input_output_aliases={i: i for i in range(count)},
        cost_estimate=pl.CostEstimate(flops=0, bytes_accessed=0, transcendentals=0),
        name="tie",
    )(*arrays)


def enter_kernel(order, tokens, gain, shift):
    rows, width = tokens.shape

    def body(t_ref, g_ref, s_ref, x_ref, n_ref):
        x = t_ref[...].astype(F32)
        x_ref[...] = x
        normal, _ = normalize(x)
        n_ref[...] = (normal * g_ref[...] + s_ref[...]).astype(BF)

    return call(
        order,
        body,
        (1,),
        [whole((rows, width)), whole((1, width)), whole((1, width))],
        [whole((rows, width)), whole((rows, width))],
        [shape_of((rows, width), F32), shape_of((rows, width), BF)],
        name="enter",
    )(tokens, gain, shift)


def reverse_lanes(values):
    count = values.shape[1]
    flip = (
        lax.broadcasted_iota(jnp.int32, (count, count), 0)
        + lax.broadcasted_iota(jnp.int32, (count, count), 1)
        == count - 1
    ).astype(BF)
    high = values.astype(BF)
    rest = values - high.astype(F32)
    middle = rest.astype(BF)
    last = (rest - middle.astype(F32)).astype(BF)
    return (dot_nn(high, flip) + dot_nn(middle, flip)) + dot_nn(last, flip)


def attn_forward(order, layer, place, x, normed, halo, weights, pos_bias, seg_q, seg_k, gain, shift):
    rows, width = x.shape
    seqs, block, _ = seg_q.shape
    keys = seg_k.shape[2]
    window = keys - block
    quarter = weights[0].shape[1]
    half = 2 * quarter

    def body(place_ref, x_ref, n_ref, h_ref, oa, ob, ta, tb, band_ref, sq_ref, sk_ref, g_ref, s_ref,
             sg_ref, ratio_ref, rden_ref, v_ref, wsum_ref, car_ref, mixed_ref, masked_ref, x1_ref, nb_ref, mix):
        step = pl.program_id(0)

        @pl.when(step == 0)
        def _():
            band = reverse_lanes(jnp.exp(band_ref[0]))
            band = jnp.concatenate([band, jnp.zeros((block, block), F32)], axis=1)
            spread = pltpu.roll(band, 1, axis=1, stride=1, stride_axis=0)
            for s in range(seqs):
                masked = jnp.where(sq_ref[s] == sk_ref[s], spread, 0.0)
                masked_ref[s] = masked
                mix[s] = masked.astype(BF)
            x1_ref[...] = x_ref[...]

        def part(wa, wb):
            def mat(m):
                return jnp.concatenate([wa[place_ref[0] ^ m], wb[place_ref[0] ^ m]], axis=0)

            wq, wk, wv = mat(0), mat(1), mat(2)
            q = dot_nt(n_ref[...], wq)
            sg = jax.nn.sigmoid(q)
            sg_ref[...] = sg.astype(BF)
            carried, wsum = [], []
            for r, source in enumerate((h_ref, n_ref)):
                here = slice(r * rows, (r + 1) * rows)
                kexp = jnp.exp(dot_nt(source[...], wk))
                v = dot_nt(source[...], wv)
                v_ref[here] = v.astype(BF)
                wsum.append(kexp.astype(BF))
                carried.append((kexp * v).astype(BF))
                wsum_ref[here] = wsum[r]
                car_ref[here] = carried[r]
            mixed = []
            for s in range(seqs):
                here = slice(s * block, (s + 1) * block)
                num = dot_nn(mix[s, :, :window], carried[0][here]) + dot_nn(mix[s, :, window:], carried[1][here])
                den = dot_nn(mix[s, :, :window], wsum[0][here]) + dot_nn(mix[s, :, window:], wsum[1][here])
                rden = 1.0 / den
                ratio = num * rden
                rden_ref[here] = rden.astype(BF)
                ratio_ref[here] = ratio.astype(BF)
                mixed.append((sg[here] * ratio).astype(BF))
            mixed = jnp.concatenate(mixed, axis=0)
            mixed_ref[...] = mixed
            x1_ref[...] += dot_nn(mixed, mat(3))

        @pl.when(step == 0)
        def _():
            part(oa, ob)

        @pl.when(step == 1)
        def _():
            part(ta, tb)
            normal, _ = normalize(x1_ref[...])
            nb_ref[...] = (normal * g_ref[...] + s_ref[...]).astype(BF)

    def col(n):
        return pl.BlockSpec((n, half), lambda i, *_: (0, i))

    return call(
        order,
        body,
        (2,),
        [whole((rows, width))] * 3
        + [whole((4, quarter, width))] * 4
        + [pl.BlockSpec((1, block, window), lambda i, place: (layer, place[1], 0))]
        + [whole((seqs, block, 1)), whole((seqs, 1, keys)), whole((1, width)), whole((1, width))],
        [col(rows)] * 3 + [col(2 * rows)] * 3 + [col(rows)]
        + [whole((seqs, block, keys)), whole((rows, width)), whole((rows, width))],
        [shape_of((rows, width), BF)] * 3
        + [shape_of((2 * rows, width), BF)] * 3
        + [
            shape_of((rows, width), BF),
            shape_of((seqs, block, keys), F32),
            shape_of((rows, width), F32),
            shape_of((rows, width), BF),
        ],
        [pltpu.VMEM((seqs, block, keys), BF)],
        prefetch=1,
        name="attn_fwd",
    )(place, x, normed, halo, *weights, pos_bias, seg_q, seg_k, gain, shift)


def gelu_both(pre):
    square = pre * pre
    upper = 0.5 + 0.5 * jnp.tanh(pre * (GELU_A + (GELU_A * GELU_B) * square))
    act = pre * upper
    return act, upper + act * (1.0 - upper) * (2.0 * GELU_A + (6.0 * GELU_A * GELU_B) * square)


def chunk_specs(chunk, width, per_half):
    own = pl.BlockSpec((chunk, width), lambda i, *_: (jnp.minimum(i, per_half - 1), 0))
    other = pl.BlockSpec((chunk, width), lambda i, *_: (jnp.maximum(i - per_half, 0), 0))
    return own, other


def ff_forward(order, x1, normed, ups, downs, gain, shift):
    rows, width = x1.shape
    half = ups[0].shape[0]
    per_half = 2
    chunk = half // per_half
    steps = 2 * per_half

    def body(x_ref, n_ref, u0, u1, d0, d1, g_ref, s_ref, act_ref, slope_ref, x2_ref, next_ref):
        step = pl.program_id(0)

        @pl.when(step == 0)
        def _():
            x2_ref[...] = x_ref[...]

        def part(u, d):
            act, slope = gelu_both(dot_nt(n_ref[...], u[...]))
            act = act.astype(BF)
            act_ref[...] = act
            slope_ref[...] = slope.astype(BF)
            x2_ref[...] += dot_nn(act, d[...])

        pl.when(step < per_half)(lambda: part(u0, d0))
        pl.when(step >= per_half)(lambda: part(u1, d1))

        @pl.when(step == steps - 1)
        def _():
            normal, _ = normalize(x2_ref[...])
            next_ref[...] = (normal * g_ref[...] + s_ref[...]).astype(BF)

    own, other = chunk_specs(chunk, width, per_half)
    col = pl.BlockSpec((rows, chunk), lambda i: (0, i))
    return call(
        order,
        body,
        (steps,),
        [whole((rows, width))] * 2 + [own, other, own, other] + [whole((1, width))] * 2,
        [col, col, whole((rows, width)), whole((rows, width))],
        [
            shape_of((rows, 2 * half), BF),
            shape_of((rows, 2 * half), BF),
            shape_of((rows, width), F32),
            shape_of((rows, width), BF),
        ],
        name="ff_fwd",
    )(x1, normed, *ups, *downs, gain, shift)


def ff_backward(order, x1, normed, ups, downs, grad, gain, saved):
    rows, width = x1.shape
    half = ups[0].shape[0]
    per_half = 2
    chunk = half // per_half
    steps = 2 * per_half
    fresh = saved is None

    def body(x_ref, n_ref, u0, u1, d0, d1, grad_ref, g_ref, *rest):
        if fresh:
            (out_ref, gu0, gu1, gd0, gd1, g1_ref, ga_ref, gg_ref, gs_ref, low, dn, x2) = rest
        else:
            (act_ref, slope_ref, gu0, gu1, gd0, gd1, g1_ref, ga_ref, gg_ref, gs_ref, low, dn) = rest
        step = pl.program_id(0)

        @pl.when(step == 0)
        def _():
            low[...] = grad_ref[...].astype(BF)
            dn[...] = jnp.zeros_like(dn)
            if fresh:
                x2[...] = x_ref[...]

        def part(u, d, gu, gd):
            if fresh:
                act, slope = gelu_both(dot_nt(n_ref[...], u[...]))
                act = act.astype(BF)
                x2[...] += dot_nn(act, d[...])
            else:
                act, slope = act_ref[...], slope_ref[...].astype(F32)
            pre_grad = (dot_nt(low[...], d[...]) * slope).astype(BF)
            dn[...] += dot_nn(pre_grad, u[...])
            gd[...] = dot_tn(act, low[...]).astype(BF)
            gu[...] = dot_tn(pre_grad, n_ref[...]).astype(BF)

        pl.when(step < per_half)(lambda: part(u0, d0, gu0, gd0))
        pl.when(step >= per_half)(lambda: part(u1, d1, gu1, gd1))

        @pl.when(step == steps - 1)
        def _():
            if fresh:
                out_ref[...] = x2[...].astype(BF)
            normal, inv = normalize(x_ref[...])
            total = dn[...]
            g1 = grad_ref[...] + norm_back(total, normal, inv, g_ref[...])
            g1_ref[...] = g1
            ga_ref[...] = g1.astype(BF)
            gg_ref[...] = jnp.sum(total * normal, axis=0, keepdims=True)
            gs_ref[...] = jnp.sum(total, axis=0, keepdims=True)

    own, other = chunk_specs(chunk, width, per_half)
    col = pl.BlockSpec((rows, chunk), lambda i: (0, i))
    out_specs = [own, other, own, other] + [whole((rows, width))] * 2 + [whole((1, width))] * 2
    out_shape = (
        [shape_of((half, width), BF)] * 4
        + [shape_of((rows, width), F32), shape_of((rows, width), BF)]
        + [shape_of((1, width), F32)] * 2
    )
    scratch = [pltpu.VMEM((rows, width), BF), pltpu.VMEM((rows, width), F32)]
    if fresh:
        out_specs = [whole((rows, width))] + out_specs
        out_shape = [shape_of((rows, width), BF)] + out_shape
        scratch.append(pltpu.VMEM((rows, width), F32))
    return call(
        order,
        body,
        (steps,),
        [whole((rows, width))] * 2 + [own, other, own, other] + [whole((rows, width)), whole((1, width))]
        + ([] if fresh else [col, col]),
        out_specs,
        out_shape,
        scratch,
        name="ff_bwd",
    )(x1, normed, *ups, *downs, grad, gain, *(() if fresh else saved))


def attn_backward(order, place, grad_low, weights, sg, ratio, rden, v, wsum, carried, masked):
    rows, width = grad_low.shape
    seqs, block, keys = masked.shape
    window = keys - block
    quarter = weights[0].shape[1]
    half = 2 * quarter

    def body(place_ref, ga_ref, oa, ob, ta, tb, sg_ref, ratio_ref, rden_ref, v_ref, wsum_ref, car_ref, masked_ref,
             gq_ref, gk_ref, gv_ref, band_ref, own_ref, halo_ref, mix_t, wgrad, dn):
        step = pl.program_id(0)

        @pl.when(step == 0)
        def _():
            for s in range(seqs):
                mix_t[s] = masked_ref[s].T.astype(BF)
            wgrad[...] = jnp.zeros_like(wgrad)
            dn[...] = jnp.zeros_like(dn)

        def part(wa, wb):
            def mat(m):
                return jnp.concatenate([wa[place_ref[0] ^ m], wb[place_ref[0] ^ m]], axis=0)

            gm = dot_nt(ga_ref[...], mat(3))
            sig = sg_ref[...].astype(F32)
            rat = ratio_ref[...].astype(F32)
            scaled = gm * sig
            gq = (scaled * rat * (1.0 - sig)).astype(BF)
            gq_ref[...] = gq
            gnum_f = scaled * rden_ref[...].astype(F32)
            gnum = gnum_f.astype(BF)
            gden = (-gnum_f * rat).astype(BF)
            wq, wk, wv = mat(0), mat(1), mat(2)
            dn[rows:] += dot_nn(gq, wq)
            for r in range(2):
                for s in range(seqs):
                    here = slice(s * block, (s + 1) * block)
                    there = slice(r * rows + s * block, r * rows + (s + 1) * block)
                    cols = slice(r * window, r * window + block)
                    ke = wsum_ref[there].astype(F32)
                    gcar = dot_nn(mix_t[s, cols], gnum[here])
                    gsum = dot_nn(mix_t[s, cols], gden[here])
                    gv = (gcar * ke).astype(BF)
                    gk = ((gcar * v_ref[there].astype(F32) + gsum) * ke).astype(BF)
                    gk_ref[there] = gk
                    gv_ref[there] = gv
                    wgrad[s, :, cols] += dot_nt(gnum[here], car_ref[there]) + dot_nt(gden[here], wsum_ref[there])
                    dn[there] += dot_nn(gk, wk) + dot_nn(gv, wv)

        @pl.when(step == 0)
        def _():
            part(oa, ob)

        @pl.when(step == 1)
        def _():
            part(ta, tb)
            total = wgrad[0] * masked_ref[0]
            for s in range(1, seqs):
                total = total + wgrad[s] * masked_ref[s]
            lane_row = lax.broadcasted_iota(jnp.int32, (block, keys), 0) + 1
            bit = 1
            while bit <= block:
                rolled = pltpu.roll(total, keys - bit, axis=1)
                total = jnp.where((lane_row & bit) != 0, rolled, total)
                bit *= 2
            band_ref[...] = reverse_lanes(total[:, :window])
            halo_ref[...] = dn[:rows].astype(BF)
            own_ref[...] = dn[rows:]

    def col(n):
        return pl.BlockSpec((n, half), lambda i, *_: (0, i))

    return call(
        order,
        body,
        (2,),
        [whole((rows, width))]
        + [whole((4, quarter, width))] * 4
        + [col(rows)] * 3 + [col(2 * rows)] * 3 + [whole((seqs, block, keys))],
        [col(rows), col(2 * rows), col(2 * rows), whole((block, window)), whole((rows, width)), whole((rows, width))],
        [
            shape_of((rows, width), BF),
            shape_of((2 * rows, width), BF),
            shape_of((2 * rows, width), BF),
            shape_of((block, window), F32),
            shape_of((rows, width), F32),
            shape_of((rows, width), BF),
        ],
        [
            pltpu.VMEM((seqs, keys, block), BF),
            pltpu.VMEM((seqs, block, keys), F32),
            pltpu.VMEM((2 * rows, width), F32),
        ],
        prefetch=1,
        name="attn_bwd",
    )(place, grad_low, *weights, sg, ratio, rden, v, wsum, carried, masked)


def attn_weight_grads(order, place, gq, gk, gv, mixed, normed, halo, grad_low):
    rows, width = gq.shape
    half = width // 2
    quarter = half // 2

    def body(place_ref, gq_ref, gk_ref, gv_ref, mixed_ref, n_ref, h_ref, ga_ref, oa, ob, ta, tb):
        step = pl.program_id(0)
        mat = lax.rem(step, 4)

        def store(value):
            low = value.astype(BF)

            @pl.when(step < 4)
            def _():
                oa[0] = low[:quarter]
                ob[0] = low[quarter:]

            @pl.when(step >= 4)
            def _():
                ta[0] = low[:quarter]
                tb[0] = low[quarter:]

        def keys_grad(ref):
            return dot_tn(ref[:rows], h_ref[...]) + dot_tn(ref[rows:], n_ref[...])

        pl.when(mat == 0)(lambda: store(dot_tn(gq_ref[...], n_ref[...])))
        pl.when(mat == 1)(lambda: store(keys_grad(gk_ref)))
        pl.when(mat == 2)(lambda: store(keys_grad(gv_ref)))
        pl.when(mat == 3)(lambda: store(dot_tn(mixed_ref[...], ga_ref[...])))

    def col(n):
        return pl.BlockSpec((n, half), lambda i, *_: (0, i // 4))

    own = pl.BlockSpec((1, quarter, width), lambda i, t: (jnp.minimum(i, 3) ^ t[0], 0, 0))
    other = pl.BlockSpec((1, quarter, width), lambda i, t: (jnp.maximum(i - 4, 0) ^ t[0], 0, 0))
    return call(
        order,
        body,
        (8,),
        [col(rows), col(2 * rows), col(2 * rows), col(rows)] + [whole((rows, width))] * 3,
        [own, own, other, other],
        [shape_of((4, quarter, width), BF)] * 4,
        prefetch=1,
        name="attn_wgrad",
    )(place, gq, gk, gv, mixed, normed, halo, grad_low)


def leave_attn(order, x, grad, own, back, gain):
    rows, width = x.shape

    def body(x_ref, g_ref, o_ref, b_ref, gain_ref, out_ref, gg_ref, gs_ref):
        normal, inv = normalize(x_ref[...])
        total = o_ref[...] + b_ref[...].astype(F32)
        out_ref[...] = g_ref[...] + norm_back(total, normal, inv, gain_ref[...])
        gg_ref[...] = jnp.sum(total * normal, axis=0, keepdims=True)
        gs_ref[...] = jnp.sum(total, axis=0, keepdims=True)

    return call(
        order,
        body,
        (1,),
        [whole((rows, width))] * 4 + [whole((1, width))],
        [whole((rows, width)), whole((1, width)), whole((1, width))],
        [shape_of((rows, width), F32)] + [shape_of((1, width), F32)] * 2,
        name="leave",
    )(x, grad, own, back, gain)


def finish_layer(order, layer, layers, place, parts, channels, hidden, mp_rows, previous):
    groups, count, width = parts[0].shape
    piece = count * 2 // 3
    small = piece // 2
    total = 2 * groups * piece

    def body(place_ref, oa, ob, ta, tb, *rest):
        qkv_ref, out_ref, up_ref, down_ref, attn, up = rest[-6:]
        for core, (pa, pb) in enumerate(((oa, ob), (ta, tb))):
            for p in range(groups):
                owner = 2 * (place_ref[2] ^ p) + (place_ref[3] ^ core)
                start = pl.multiple_of(owner * piece, piece)
                up[pl.ds(start, piece)] = pa[p, :piece].astype(F32)
                down_ref[0, pl.ds(start, piece)] = pb[p, :piece].astype(F32)
                attn[pl.ds(start, small)] = pa[p, piece:].astype(F32)
                attn[pl.ds(pl.multiple_of(owner * piece + small, small), small)] = pb[p, piece:].astype(F32)
        up_ref[0] = up[...].T
        for m in range(3):
            qkv_ref[0, m] = attn[m * channels : (m + 1) * channels].T
        out_ref[0] = attn[3 * channels :]

    shapes = [
        (layers, 3, width, channels),
        (layers, channels, width),
        (layers, width, hidden),
        (layers, hidden, width),
    ]

    def here(shape):
        return pl.BlockSpec((1,) + shape[1:], lambda i, *_: (layer,) + (0,) * (len(shape) - 1))

    first = len(parts) + 1
    extra = list(previous) if previous is not None else []
    order_in = first + len(extra)
    anywhere = pl.BlockSpec(memory_space=pl.ANY)

    def with_token(*refs):
        ins = refs[: first + len(extra)]
        outs = refs[order_in + 1 : order_in + 5]
        return body(*ins[:first], *outs, *refs[order_in + 6 :])

    aliases = {first + k: k for k in range(len(extra))}
    aliases[order_in] = 4
    *results, order.token = pl.pallas_call(
        with_token,
        grid_spec=pltpu.PrefetchScalarGridSpec(
            num_scalar_prefetch=1,
            grid=(1,),
            in_specs=[whole(part.shape) for part in parts] + [anywhere] * (len(extra) + 1),
            out_specs=[here(shape) for shape in shapes] + [anywhere],
            scratch_shapes=[pltpu.VMEM((total, width), F32)] * 2,
        ),
        out_shape=[shape_of(shape, F32) for shape in shapes] + [shape_of(TOKEN, jnp.int32)],
        input_output_aliases=aliases,
        compiler_params=pltpu.CompilerParams(
            dimension_semantics=("arbitrary",), vmem_limit_bytes=VMEM_LIMIT
        ),
        cost_estimate=pl.CostEstimate(flops=0, bytes_accessed=0, transcendentals=0),
        name="finish",
    )(place, *parts, *extra, order.token)
    return results


class Order:
    def __init__(self):
        self.token = jnp.zeros(TOKEN, jnp.int32)

    def pin(self, *arrays):
        *arrays, self.token = tie(*arrays, self.token)
        return arrays


class Links:
    def __init__(self, order, dp, mp):
        self.order = order
        self.dp = dp
        self.mp = mp
        bits = [1 << k for k in range(1, dp.bit_length() - 1)]
        self.routes = (bits, bits[::-1])

    def swap(self, value, axis, bit):
        size = self.dp if axis == "dp" else self.mp
        return lax.ppermute(value, axis, [(i, i ^ bit) for i in range(size)])


class Spread:
    def __init__(self, links, values):
        self.links = links
        self.values = list(values)
        self.phase = 0
        self.have = [[], []]

    def start(self):
        self.values = self.links.order.pin(*self.values)
        self.coming = [
            self.links.swap(value, "dp", route[self.phase])
            for value, route in zip(self.values, self.links.routes)
        ]

    def wait(self):
        coming = self.links.order.pin(*self.coming)
        for k in range(2):
            bit = self.links.routes[k][self.phase]
            place = sum(1 for other in self.have[k] if other > bit)
            self.values[k] = jnp.stack([self.values[k], coming[k]], axis=place)
            self.have[k].append(bit)
        self.phase += 1

    def wait_all(self):
        self.wait()
        while self.phase < len(self.links.routes[0]):
            self.start()
            self.wait()

    def start_cores(self):
        self.values = self.links.order.pin(*self.values)
        self.coming = [self.links.swap(value, "dp", 1) for value in self.values]

    def wait_cores(self):
        return self.values + self.links.order.pin(*self.coming)


class Gather(Spread):
    def __init__(self, links, piece_a, piece_b):
        super().__init__(links, ())
        self.cut = piece_a.shape[0]
        self.piece = jnp.concatenate([piece_a, piece_b], axis=0)

    def start_mp(self):
        (self.piece,) = self.links.order.pin(self.piece)
        self.coming_mp = [self.links.swap(self.piece, "mp", p) for p in range(1, self.links.mp)]

    def wait_mp(self):
        parts = [self.piece] + self.links.order.pin(*self.coming_mp)
        self.values = [
            jnp.stack([part[: self.cut] for part in parts]),
            jnp.stack([part[self.cut :] for part in parts]),
        ]


class Reduce:
    def __init__(self, links, halves):
        self.links = links
        self.halves = halves
        self.phase = 0

    def start_cores(self):
        others = self.links.order.pin(*self.halves[2:])
        self.coming = [self.links.swap(other, "dp", 1) for other in others]

    def wait_cores(self):
        coming = self.links.order.pin(*self.coming)
        mp = self.links.mp
        self.have = [sorted(route, reverse=True) for route in self.links.routes]
        self.values = []
        for own, other in zip(self.halves[:2], coming):
            total = (own.astype(F32) + other.astype(F32)).astype(BF)
            groups = self.links.dp // 2
            rows = total.size // total.shape[-1] // groups // mp
            self.values.append(total.reshape((2,) * len(self.have[0]) + (mp, rows, total.shape[-1])))

    def start(self):
        sends, self.keeps = [], []
        for k in range(2):
            place = self.have[k].index(self.links.routes[1 - k][self.phase])
            self.keeps.append(lax.index_in_dim(self.values[k], 0, place, keepdims=False))
            sends.append(lax.index_in_dim(self.values[k], 1, place, keepdims=False))
        sends = self.links.order.pin(*sends)
        self.coming = [
            self.links.swap(sends[k], "dp", self.links.routes[1 - k][self.phase]) for k in range(2)
        ]

    def wait(self):
        coming = self.links.order.pin(*self.coming)
        for k in range(2):
            self.values[k] = (self.keeps[k].astype(F32) + coming[k].astype(F32)).astype(BF)
            self.have[k].remove(self.links.routes[1 - k][self.phase])
        self.phase += 1

    def wait_all(self):
        self.wait()
        while self.phase < len(self.links.routes[0]):
            self.start()
            self.wait()

    def start_mp(self):
        blocks = [jnp.concatenate([value[p] for value in self.values], axis=0) for p in range(self.links.mp)]
        self.kept = blocks[0]
        sends = self.links.order.pin(*blocks[1:])
        self.coming = [self.links.swap(send, "mp", p + 1) for p, send in enumerate(sends)]

    def wait_mp(self):
        total = self.kept.astype(F32)
        for part in self.links.order.pin(*self.coming):
            total = total + part.astype(F32)
        return total.astype(BF)


def make_shards(dp, mp):
    def shards(
        tokens,
        segments,
        qkv_weight,
        out_weight,
        up_weight,
        down_projection_weight,
        norm_gain,
        norm_bias,
        pos_bias,
        cotangent,
    ):
        seqs, block, width = tokens.shape
        layers = qkv_weight.shape[0]
        window = pos_bias.shape[2]
        channels = qkv_weight.shape[-1]
        hidden = up_weight.shape[-1]
        rows = seqs * block
        dp_index = lax.axis_index("dp")
        mp_index = lax.axis_index("mp")
        order = Order()
        links = Links(order, dp, mp)
        attn_rows = 4 * channels // dp
        ff_rows = hidden // dp
        group = dp_index // 2
        place = jnp.stack([group // (dp // 8), mp_index, group, dp_index % 2]).astype(jnp.int32)

        def picks(count, offset, length):
            return (
                lax.broadcasted_iota(jnp.int32, (count, length), 0) + offset
                == lax.broadcasted_iota(jnp.int32, (count, length), 1)
            ).astype(BF)

        attn_pick = picks(attn_rows, dp_index * attn_rows, 4 * channels)
        ff_pick = picks(ff_rows, dp_index * ff_rows, hidden)

        def attn_piece(layer):
            piece = jnp.einsum(
                "rmc,mdc->rd",
                attn_pick[:, : 3 * channels].reshape(attn_rows, 3, channels),
                qkv_weight[layer],
                preferred_element_type=F32,
            ) + dot_nn(attn_pick[:, 3 * channels :], out_weight[layer])
            return piece.astype(BF)

        def ff_pieces(layer):
            return (
                dot_nt(ff_pick, up_weight[layer]).astype(BF),
                dot_nn(ff_pick, down_projection_weight[layer]).astype(BF),
            )

        def attn_mats(parts):
            return [part.reshape(4, -1, width) for part in parts]

        def ff_mats(parts):
            flat = [part.reshape(-1, width) for part in parts]
            return (flat[0], flat[2]), (flat[1], flat[3])

        def relative(gathered):
            by_dp = jnp.take(gathered, jnp.bitwise_xor(jnp.arange(dp), dp_index), axis=0)
            both = jnp.take(by_dp, jnp.bitwise_xor(jnp.arange(mp), mp_index), axis=1)
            both = both.reshape((dp // 2, 2) + gathered.shape[1:])
            return both[:, 0], both[:, 1]

        def forward_halo(value):
            return lax.ppermute(value, "mp", [(i, i + 1) for i in range(mp - 1)])

        def backward_halo(value):
            return lax.ppermute(value, "mp", [(i + 1, i) for i in range(mp - 1)])

        gains = norm_gain.reshape(layers, 2, 1, width)
        shifts = norm_bias.reshape(layers, 2, 1, width)
        middle = attn_rows // 2

        piece = attn_piece(0)
        attn0 = Gather(links, piece[:middle], piece[middle:])
        attn0.start_mp()
        ff0 = Gather(links, *ff_pieces(0))
        ff0.start_mp()
        x, normed = enter_kernel(order, tokens.reshape(rows, width), gains[0, 0], shifts[0, 0])
        (normed,) = order.pin(normed)
        halo = forward_halo(normed)
        (later,) = order.pin(jnp.concatenate((attn_piece(1),) + ff_pieces(1), axis=0))
        later = lax.all_gather(later, ("dp", "mp"), axis=0, tiled=False)

        seg_pad = jnp.concatenate([jnp.full((seqs, window), -1, segments.dtype), segments], axis=1)
        seg_keys = lax.dynamic_slice_in_dim(seg_pad, mp_index * block, block + window, axis=1)
        seg_q = seg_keys[:, window:].reshape(seqs, block, 1)
        seg_k = seg_keys.reshape(seqs, 1, block + window)

        attn0.wait_mp()
        attn0.start()
        ff0.wait_mp()
        attn0.wait()
        attn0.start()
        ff0.start()
        attn0.wait_all()
        attn0.start_cores()
        ff0.wait()
        ff0.start()
        w_attn0 = attn_mats(attn0.wait_cores())
        (halo,) = order.pin(halo)

        def attn(layer, x, normed, halo, w_attn):
            sg, ratio, rden, v, wsum, carried, mixed, masked, x1, normed_b = attn_forward(
                order, layer, place, x, normed, halo, w_attn, pos_bias, seg_q, seg_k,
                gains[layer, 1], shifts[layer, 1],
            )
            return x1, normed_b, (sg, ratio, rden, v, wsum, carried, masked), (mixed, normed, halo)

        x1_0, normed_b0, saved0, rows0 = attn(0, x, normed, halo, w_attn0)
        ff0.wait_all()
        ff0.start_cores()
        ups0, downs0 = ff_mats(ff0.wait_cores())
        act0, slope0, x2, normed2 = ff_forward(
            order, x1_0, normed_b0, ups0, downs0, gains[1, 0], shifts[1, 0]
        )
        (normed2,) = order.pin(normed2)
        halo2 = forward_halo(normed2)
        (later,) = order.pin(later)
        later = later.reshape((dp, mp) + later.shape[1:])
        own, other = relative(later)
        cuts = [middle, attn_rows, attn_rows + ff_rows]
        own_a, own_b, own_up, own_down = jnp.split(own, cuts, axis=2)
        other_a, other_b, other_up, other_down = jnp.split(other, cuts, axis=2)
        w_attn1 = attn_mats([own_a, own_b, other_a, other_b])
        ups1, downs1 = ff_mats([own_up, own_down, other_up, other_down])
        (halo2,) = order.pin(halo2)
        x1_1, normed_b1, saved1, rows1 = attn(1, x2, normed2, halo2, w_attn1)

        output, gu0, gu1, gd0, gd1, grad1, grad1_low, gain_b1, shift_b1 = ff_backward(
            order, x1_1, normed_b1, ups1, downs1, cotangent.reshape(rows, width), gains[1, 1], None
        )
        r_ff1 = Reduce(links, [gu0, gd0, gu1, gd1])
        r_ff1.start_cores()
        r_ff1.wait_cores()
        r_ff1.start()
        gq, gk, gv, band1, dn_own1, back1 = attn_backward(order, place, grad1_low, w_attn1, *saved1)
        (back1,) = order.pin(back1)
        back1 = backward_halo(back1)
        r_attn1 = Reduce(links, attn_weight_grads(order, place, gq, gk, gv, *rows1, grad1_low))
        r_ff1.wait()
        r_ff1.start()
        r_attn1.start_cores()
        (back1,) = order.pin(back1)
        grad2, gain_a1, shift_a1 = leave_attn(order, x2, grad1, dn_own1, back1, gains[1, 0])
        r_attn1.wait_cores()
        r_attn1.start()
        (band1,) = order.pin(band1)
        band1 = lax.psum(band1, "dp")

        gu0, gu1, gd0, gd1, grad3, grad3_low, gain_b0, shift_b0 = ff_backward(
            order, x1_0, normed_b0, ups0, downs0, grad2, gains[0, 1], (act0, slope0)
        )
        r_ff0 = Reduce(links, [gu0, gd0, gu1, gd1])
        r_ff0.start_cores()
        r_ff1.wait_all()
        r_ff1.start_mp()
        r_attn1.wait()
        r_attn1.start()
        r_ff0.wait_cores()
        r_ff0.start()
        gq, gk, gv, band0, dn_own0, back0 = attn_backward(order, place, grad3_low, w_attn0, *saved0)
        (back0,) = order.pin(back0)
        back0 = backward_halo(back0)
        r_attn1.wait_all()
        r_attn1.start_mp()
        r_attn0 = Reduce(links, attn_weight_grads(order, place, gq, gk, gv, *rows0, grad3_low))
        r_attn0.start_cores()
        r_ff0.wait()
        r_ff0.start()
        r_attn0.wait_cores()
        r_attn0.start()
        (back0,) = order.pin(back0)
        grad4, gain_a0, shift_a0 = leave_attn(order, x, grad3, dn_own0, back0, gains[0, 0])
        norms = jnp.concatenate(
            [gain_a0, gain_b0, shift_a0, shift_b0, gain_a1, gain_b1, shift_a1, shift_b1], axis=0
        ).reshape(-1, window)
        small = jnp.concatenate([band0, norms], axis=0)

        class Small:
            def __init__(self, value):
                self.value = value
                self.bit = 1

            def start(self):
                (self.value,) = order.pin(self.value)
                self.coming = links.swap(self.value, "dp", self.bit)

            def wait(self):
                (coming,) = order.pin(self.coming)
                self.value = self.value + coming
                self.bit *= 2

        def spread_of(attn_sum, ff_sum):
            half = ff_sum.shape[0] // 2
            return Spread(
                links,
                [
                    jnp.concatenate([ff_sum[:half], attn_sum[:middle]], axis=0),
                    jnp.concatenate([ff_sum[half:], attn_sum[middle:]], axis=0),
                ],
            )

        small = Small(small)
        small.start()
        ff1_sum = r_ff1.wait_mp()
        r_ff0.wait_all()
        r_ff0.start_mp()
        small.wait()
        small.start()
        attn1_sum = r_attn1.wait_mp()
        back_1 = spread_of(attn1_sum, ff1_sum)
        back_1.start()
        r_attn0.wait()
        r_attn0.start()
        small.wait()
        while small.bit < dp:
            small.start()
            small.wait()
        (band1,) = order.pin(band1)
        (low_small,) = order.pin(jnp.concatenate([small.value, band1], axis=0).astype(BF))
        small_parts = [links.swap(low_small, "mp", p) for p in range(1, mp)]
        back_1.wait()
        back_1.start()
        r_attn0.wait_all()
        r_attn0.start_mp()
        back_1.wait_all()
        back_1.start_cores()
        ff0_sum = r_ff0.wait_mp()
        full_1 = back_1.wait_cores()
        attn0_sum = r_attn0.wait_mp()
        back_0 = spread_of(attn0_sum, ff0_sum)
        back_0.start()

        def finish(layer, full, previous):
            full = [part.reshape(dp // 2, -1, width) for part in full]
            if middle % 16 == 0:
                return finish_layer(order, layer, layers, place, full, channels, hidden, attn_rows, previous)
            owner = jnp.bitwise_xor(jnp.arange(dp), dp_index)
            part_a, part_b = [
                jnp.stack([full[k], full[2 + k]], axis=1).reshape(dp, -1, width) for k in range(2)
            ]

            def rows_of(value):
                return value.reshape(-1, width)

            def place_of(count):
                spots = (owner[:, None] * count + jnp.arange(count)[None, :]).reshape(-1, 1)
                return (spots == jnp.arange(dp * count)[None, :]).astype(BF)

            attn_part = rows_of(jnp.concatenate([part_a[:, ff_rows:], part_b[:, ff_rows:]], axis=1))
            attn_place = place_of(attn_rows).reshape(-1, 4, channels)
            ff_place = place_of(ff_rows)
            values = (
                jnp.einsum("pd,pmc->mdc", attn_part, attn_place[:, :3], preferred_element_type=F32),
                dot_tn(attn_place[:, 3], attn_part),
                dot_tn(rows_of(part_a[:, :ff_rows]), ff_place),
                dot_tn(ff_place, rows_of(part_b[:, :ff_rows])),
            )
            if previous is None:
                previous = [jnp.zeros((layers,) + value.shape, F32) for value in values]
            return [
                lax.dynamic_update_index_in_dim(kept, value, layer, 0)
                for kept, value in zip(previous, values)
            ]

        big = finish(1, full_1, None)
        back_0.wait()
        back_0.start()
        small_parts = [low_small] + order.pin(*small_parts)
        small_all = jnp.stack([part.astype(F32) for part in small_parts])
        pairs = small_all[:, block:-block]
        while pairs.shape[0] > 1:
            pairs = pairs[0::2] + pairs[1::2]
        norm_sum = pairs[0].reshape(layers, 4, width)
        bands = jnp.stack([small_all[:, :block], small_all[:, -block:]])
        band_sum = jnp.take(bands, jnp.bitwise_xor(jnp.arange(mp), mp_index), axis=1)
        band_sum = band_sum.reshape(layers, mp * block, window)
        back_0.wait_all()
        back_0.start_cores()
        big = finish(0, back_0.wait_cores(), big)
        return (
            (output.reshape(tokens.shape), grad4.reshape(tokens.shape))
            + tuple(big)
            + (norm_sum[:, :2], norm_sum[:, 2:], band_sum)
        )

    return shards


def solution(mesh):
    placed = (
        P("dp", "mp", None),
        P("dp", None),
        P(None, None, None, "mp"),
        P(None, "mp", None),
        P(None, None, "mp"),
        P(None, "mp", None),
        P(),
        P(),
        P(),
        P("dp", "mp", None),
    )
    return jax.shard_map(
        make_shards(mesh.shape["dp"], mesh.shape["mp"]),
        mesh=mesh,
        in_specs=placed,
        out_specs=(
            P("dp", "mp", None),
            P("dp", "mp", None),
            P(None, None, None, "mp"),
            P(None, "mp", None),
            P(None, None, "mp"),
            P(None, "mp", None),
            P(),
            P(),
            P(),
        ),
        check_vma=False,
    )
```

```python
import functools

import jax
import jax.numpy as jnp
from jax import lax
from jax.experimental import pallas as pl
from jax.experimental.pallas import tpu as pltpu
from jax.sharding import Mesh, PartitionSpec as P

BF = jnp.bfloat16
F32 = jnp.float32
VMEM_LIMIT = 58 * 1024 * 1024
TOKEN = (8, 128)
GELU_A = 0.7978845608028654
GELU_B = 0.044715


def dot_nt(lhs, rhs):
    return lax.dot_general(lhs, rhs, (((1,), (1,)), ((), ())), preferred_element_type=F32)


def dot_nn(lhs, rhs):
    return lax.dot_general(lhs, rhs, (((1,), (0,)), ((), ())), preferred_element_type=F32)


def dot_tn(lhs, rhs):
    return lax.dot_general(lhs, rhs, (((0,), (0,)), ((), ())), preferred_element_type=F32)


def normalize(values):
    center = values - jnp.mean(values, axis=-1, keepdims=True)
    inv_std = lax.rsqrt(jnp.mean(center * center, axis=-1, keepdims=True) + 1e-05)
    return center * inv_std, inv_std


def norm_back(grad_out, normal, inv_std, gain):
    grad_normal = grad_out * gain
    mean_one = jnp.mean(grad_normal, axis=-1, keepdims=True)
    mean_two = jnp.mean(grad_normal * normal, axis=-1, keepdims=True)
    return inv_std * (grad_normal - mean_one - normal * mean_two)


def whole(shape):
    return pl.BlockSpec(shape, lambda *_: (0,) * len(shape))


def call(order, body, grid, in_specs, out_specs, out_shape, scratch=(), prefetch=0, name=None):
    first = prefetch + len(in_specs)
    second = first + 1 + len(out_specs)
    anywhere = pl.BlockSpec(memory_space=pl.ANY)

    def with_token(*refs):
        return body(*refs[:first], *refs[first + 1 : second], *refs[second + 1 :])

    kernel = pl.pallas_call(
        with_token,
        grid_spec=pltpu.PrefetchScalarGridSpec(
            num_scalar_prefetch=prefetch,
            grid=grid,
            in_specs=list(in_specs) + [anywhere],
            out_specs=list(out_specs) + [anywhere],
            scratch_shapes=list(scratch),
        ),
        out_shape=list(out_shape) + [shape_of(TOKEN, jnp.int32)],
        input_output_aliases={first: len(out_specs)},
        compiler_params=pltpu.CompilerParams(
            dimension_semantics=("arbitrary",) * len(grid), vmem_limit_bytes=VMEM_LIMIT
        ),
        cost_estimate=pl.CostEstimate(flops=0, bytes_accessed=0, transcendentals=0),
        name=name,
    )

    def run(*operands):
        *results, order.token = kernel(*operands, order.token)
        return results

    return run


def shape_of(shape, dtype):
    return jax.ShapeDtypeStruct(shape, dtype)


def tie(*arrays):
    count = len(arrays)
    return pl.pallas_call(
        lambda *refs: None,
        out_shape=[shape_of(a.shape, a.dtype) for a in arrays],
        in_specs=[pl.BlockSpec(memory_space=pl.ANY)] * count,
        out_specs=[pl.BlockSpec(memory_space=pl.ANY)] * count,
        input_output_aliases={i: i for i in range(count)},
        cost_estimate=pl.CostEstimate(flops=0, bytes_accessed=0, transcendentals=0),
        name="tie",
    )(*arrays)


def enter_kernel(order, tokens, gain, shift):
    rows, width = tokens.shape

    def body(t_ref, g_ref, s_ref, x_ref, n_ref):
        x = t_ref[...].astype(F32)
        x_ref[...] = x
        normal, _ = normalize(x)
        n_ref[...] = (normal * g_ref[...] + s_ref[...]).astype(BF)

    return call(
        order,
        body,
        (1,),
        [whole((rows, width)), whole((1, width)), whole((1, width))],
        [whole((rows, width)), whole((rows, width))],
        [shape_of((rows, width), F32), shape_of((rows, width), BF)],
        name="enter",
    )(tokens, gain, shift)


def reverse_lanes(values):
    count = values.shape[1]
    flip = (
        lax.broadcasted_iota(jnp.int32, (count, count), 0)
        + lax.broadcasted_iota(jnp.int32, (count, count), 1)
        == count - 1
    ).astype(BF)
    high = values.astype(BF)
    rest = values - high.astype(F32)
    middle = rest.astype(BF)
    last = (rest - middle.astype(F32)).astype(BF)
    return (dot_nn(high, flip) + dot_nn(middle, flip)) + dot_nn(last, flip)


def attn_specs(weights):
    if len(weights) == 4:
        return [whole(w.shape) for w in weights]
    groups, _, mp, count, width = weights[0].shape
    return [pl.BlockSpec((groups, 1, mp, count // 3, width), lambda i, place: (0, place[3] ^ i, 0, 0, 0))]


def by_half(step, refs, place_ref, part):
    if len(refs) == 1:
        width = refs[0].shape[-1]
        part(lambda m: refs[0][m, 0].reshape(-1, width))
        return
    for half in range(2):
        wa, wb = refs[2 * half], refs[2 * half + 1]

        def mat(m, wa=wa, wb=wb):
            return jnp.concatenate([wa[place_ref[0] ^ m], wb[place_ref[0] ^ m]], axis=0)

        pl.when(step == half)(functools.partial(part, mat))


def attn_forward(order, layer, place, x, normed, halo, weights, pos_bias, seg_q, seg_k, gain, shift):
    rows, width = x.shape
    seqs, block, _ = seg_q.shape
    keys = seg_k.shape[2]
    window = keys - block
    half = width // 2

    def body(place_ref, x_ref, n_ref, h_ref, *rest):
        w_refs, rest = rest[: len(weights)], rest[len(weights) :]
        (band_ref, sq_ref, sk_ref, g_ref, s_ref, sg_ref, ratio_ref, rden_ref, v_ref, wsum_ref, car_ref, mixed_ref,
         masked_ref, x1_ref, nb_ref, mix) = rest
        step = pl.program_id(0)

        @pl.when(step == 0)
        def _():
            band = reverse_lanes(jnp.exp(band_ref[0]))
            band = jnp.concatenate([band, jnp.zeros((block, block), F32)], axis=1)
            spread = pltpu.roll(band, 1, axis=1, stride=1, stride_axis=0)
            for s in range(seqs):
                masked = jnp.where(sq_ref[s] == sk_ref[s], spread, 0.0)
                masked_ref[s] = masked
                mix[s] = masked.astype(BF)
            x1_ref[...] = x_ref[...]

        def part(mat):
            wq, wk, wv = mat(0), mat(1), mat(2)
            q = dot_nt(n_ref[...], wq)
            sg = jax.nn.sigmoid(q)
            sg_ref[...] = sg.astype(BF)
            carried, wsum = [], []
            for r, source in enumerate((h_ref, n_ref)):
                here = slice(r * rows, (r + 1) * rows)
                kexp = jnp.exp(dot_nt(source[...], wk))
                v = dot_nt(source[...], wv)
                v_ref[here] = v.astype(BF)
                wsum.append(kexp.astype(BF))
                carried.append((kexp * v).astype(BF))
                wsum_ref[here] = wsum[r]
                car_ref[here] = carried[r]
            mixed = []
            for s in range(seqs):
                here = slice(s * block, (s + 1) * block)
                num = dot_nn(mix[s, :, :window], carried[0][here]) + dot_nn(mix[s, :, window:], carried[1][here])
                den = dot_nn(mix[s, :, :window], wsum[0][here]) + dot_nn(mix[s, :, window:], wsum[1][here])
                rden = 1.0 / den
                ratio = num * rden
                rden_ref[here] = rden.astype(BF)
                ratio_ref[here] = ratio.astype(BF)
                mixed.append((sg[here] * ratio).astype(BF))
            mixed = jnp.concatenate(mixed, axis=0)
            mixed_ref[...] = mixed
            x1_ref[...] += dot_nn(mixed, mat(3))

        by_half(step, w_refs, place_ref, part)

        @pl.when(step == 1)
        def _():
            normal, _ = normalize(x1_ref[...])
            nb_ref[...] = (normal * g_ref[...] + s_ref[...]).astype(BF)

    def col(n):
        return pl.BlockSpec((n, half), lambda i, *_: (0, i))

    return call(
        order,
        body,
        (2,),
        [whole((rows, width))] * 3
        + attn_specs(weights)
        + [pl.BlockSpec((1, block, window), lambda i, place: (layer, place[1], 0))]
        + [whole((seqs, block, 1)), whole((seqs, 1, keys)), whole((1, width)), whole((1, width))],
        [col(rows)] * 3 + [col(2 * rows)] * 3 + [col(rows)]
        + [whole((seqs, block, keys)), whole((rows, width)), whole((rows, width))],
        [shape_of((rows, width), BF)] * 3
        + [shape_of((2 * rows, width), BF)] * 3
        + [
            shape_of((rows, width), BF),
            shape_of((seqs, block, keys), F32),
            shape_of((rows, width), F32),
            shape_of((rows, width), BF),
        ],
        [pltpu.VMEM((seqs, block, keys), BF)],
        prefetch=1,
        name="attn_fwd",
    )(place, x, normed, halo, *weights, pos_bias, seg_q, seg_k, gain, shift)


def gelu_both(pre):
    square = pre * pre
    upper = 0.5 + 0.5 * jnp.tanh(pre * (GELU_A + (GELU_A * GELU_B) * square))
    act = pre * upper
    return act, upper + act * (1.0 - upper) * (2.0 * GELU_A + (6.0 * GELU_A * GELU_B) * square)


def chunk_specs(chunk, width, per_half):
    own = pl.BlockSpec((chunk, width), lambda i, *_: (jnp.minimum(i, per_half - 1), 0))
    other = pl.BlockSpec((chunk, width), lambda i, *_: (jnp.maximum(i - per_half, 0), 0))
    return own, other


def ff_forward(order, x1, normed, ups, downs, gain, shift):
    rows, width = x1.shape
    half = ups[0].shape[0]
    per_half = 2
    chunk = half // per_half
    steps = 2 * per_half

    def body(x_ref, n_ref, u0, u1, d0, d1, g_ref, s_ref, act_ref, slope_ref, x2_ref, next_ref):
        step = pl.program_id(0)

        @pl.when(step == 0)
        def _():
            x2_ref[...] = x_ref[...]

        def part(u, d):
            act, slope = gelu_both(dot_nt(n_ref[...], u[...]))
            act = act.astype(BF)
            act_ref[...] = act
            slope_ref[...] = slope.astype(BF)
            x2_ref[...] += dot_nn(act, d[...])

        pl.when(step < per_half)(lambda: part(u0, d0))
        pl.when(step >= per_half)(lambda: part(u1, d1))

        @pl.when(step == steps - 1)
        def _():
            normal, _ = normalize(x2_ref[...])
            next_ref[...] = (normal * g_ref[...] + s_ref[...]).astype(BF)

    own, other = chunk_specs(chunk, width, per_half)
    col = pl.BlockSpec((rows, chunk), lambda i: (0, i))
    return call(
        order,
        body,
        (steps,),
        [whole((rows, width))] * 2 + [own, other, own, other] + [whole((1, width))] * 2,
        [col, col, whole((rows, width)), whole((rows, width))],
        [
            shape_of((rows, 2 * half), BF),
            shape_of((rows, 2 * half), BF),
            shape_of((rows, width), F32),
            shape_of((rows, width), BF),
        ],
        name="ff_fwd",
    )(x1, normed, *ups, *downs, gain, shift)


def ff_specs(weights, side, chunk):
    if len(weights) == 4:
        width = weights[0].shape[1]
        spec = pl.BlockSpec((chunk, width), lambda i, *_: (i, 0))
        return [weights[side], weights[2 + side]], [spec, spec]
    groups, _, mp, count, width = weights[0].shape
    rows = count // 3
    per = chunk // (mp * rows)

    def spec(which):
        return pl.BlockSpec((per, 1, mp, rows, width), lambda i, place: (i, place[3] ^ side, 0, which, 0))

    return [weights[0], weights[0]], [spec(1), spec(2)]


def ff_backward(order, place, x1, normed, weights, side, groups, grad, gain, saved, before):
    rows, width = x1.shape
    steps = 2
    half = 2 * width
    chunk = half // steps
    operands, w_specs = ff_specs(weights, side, chunk)
    group_rows = half // groups
    per = chunk // group_rows
    fresh = saved is None
    last = before is not None
    relative = len(weights) == 4

    def body(place_ref, x_ref, n_ref, u_ref, d_ref, grad_ref, g_ref, *rest):
        rest = list(rest)
        act_ref, slope_ref = (None, None) if fresh else (rest.pop(0), rest.pop(0))
        dn_in = rest.pop(0) if last else None
        x2_in = rest.pop(0) if last and fresh else None
        wg_ref = rest.pop(0)
        if last:
            g1_ref, ga_ref, gg_ref, gs_ref = rest[:4]
            rest = rest[4:]
            out_ref = rest.pop(0) if fresh else None
            low, dn = rest[0], rest[1]
            x2 = rest[2] if fresh else None
        else:
            dn = rest.pop(0)
            x2 = rest.pop(0) if fresh else None
            low = rest[0]
        step = pl.program_id(0)

        @pl.when(step == 0)
        def _():
            low[...] = grad_ref[...].astype(BF)
            dn[...] = dn_in[...] if last else jnp.zeros_like(dn)
            if fresh:
                x2[...] = x2_in[...] if last else x_ref[...]

        u = u_ref[...].reshape(chunk, width)
        d = d_ref[...].reshape(chunk, width)
        if fresh:
            act, slope = gelu_both(dot_nt(n_ref[...], u))
            act = act.astype(BF)
            x2[...] += dot_nn(act, d)
        else:
            act, slope = act_ref[...], slope_ref[...].astype(F32)
        pre_grad = (dot_nt(low[...], d) * slope).astype(BF)
        dn[...] += dot_nn(pre_grad, u)
        for which, value in ((0, dot_tn(pre_grad, n_ref[...])), (1, dot_tn(act, low[...]))):
            value = value.astype(BF)
            for k in range(per):
                spot = (place_ref[5] ^ k) if relative else k
                wg_ref[spot, which] = value[k * group_rows : (k + 1) * group_rows]

        if last:

            @pl.when(step == steps - 1)
            def _():
                if fresh:
                    out_ref[...] = x2[...].astype(BF)
                normal, inv = normalize(x_ref[...])
                total = dn[...]
                g1 = grad_ref[...] + norm_back(total, normal, inv, g_ref[...])
                g1_ref[...] = g1
                ga_ref[...] = g1.astype(BF)
                gg_ref[...] = jnp.sum(total * normal, axis=0, keepdims=True)
                gs_ref[...] = jnp.sum(total, axis=0, keepdims=True)

    full = whole((rows, width))
    col = pl.BlockSpec((rows, chunk), lambda i, *_: (0, steps * side + i))
    wg = pl.BlockSpec((per, 2, group_rows, width), lambda i, place: ((place[4] ^ i) if relative else i, 0, 0, 0))
    in_specs = [full, full] + w_specs + [full, whole((1, width))]
    operands = [x1, normed] + operands + [grad, gain]
    if not fresh:
        in_specs += [col, col]
        operands += list(saved)
    out_specs, out_shape = [wg], [shape_of((groups, 2, group_rows, width), BF)]
    scratch = [pltpu.VMEM((rows, width), BF)]
    sums = [shape_of((rows, width), F32)] * (2 if fresh else 1)
    if last:
        in_specs += [full] * len(sums)
        operands += list(before)
        out_specs += [full, full, whole((1, width)), whole((1, width))]
        out_shape += [shape_of((rows, width), F32), shape_of((rows, width), BF)] + [shape_of((1, width), F32)] * 2
        if fresh:
            out_specs.append(full)
            out_shape.append(shape_of((rows, width), BF))
        scratch += [pltpu.VMEM((rows, width), F32)] * len(sums)
    else:
        out_specs += [full] * len(sums)
        out_shape += sums
    return call(
        order, body, (steps,), in_specs, out_specs, out_shape, scratch, prefetch=1, name="ff_bwd"
    )(place, *operands)


def attn_backward(order, place, grad_low, weights, sg, ratio, rden, v, wsum, carried, masked):
    rows, width = grad_low.shape
    seqs, block, keys = masked.shape
    window = keys - block
    half = width // 2

    def body(place_ref, ga_ref, *rest):
        w_refs, rest = rest[: len(weights)], rest[len(weights) :]
        (sg_ref, ratio_ref, rden_ref, v_ref, wsum_ref, car_ref, masked_ref,
         gq_ref, gk_ref, gv_ref, band_ref, own_ref, halo_ref, mix_t, wgrad, dn) = rest
        step = pl.program_id(0)

        @pl.when(step == 0)
        def _():
            for s in range(seqs):
                mix_t[s] = masked_ref[s].T.astype(BF)
            wgrad[...] = jnp.zeros_like(wgrad)
            dn[...] = jnp.zeros_like(dn)

        def part(mat):
            gm = dot_nt(ga_ref[...], mat(3))
            sig = sg_ref[...].astype(F32)
            rat = ratio_ref[...].astype(F32)
            scaled = gm * sig
            gq = (scaled * rat * (1.0 - sig)).astype(BF)
            gq_ref[...] = gq
            gnum_f = scaled * rden_ref[...].astype(F32)
            gnum = gnum_f.astype(BF)
            gden = (-gnum_f * rat).astype(BF)
            wq, wk, wv = mat(0), mat(1), mat(2)
            dn[rows:] += dot_nn(gq, wq)
            for r in range(2):
                for s in range(seqs):
                    here = slice(s * block, (s + 1) * block)
                    there = slice(r * rows + s * block, r * rows + (s + 1) * block)
                    cols = slice(r * window, r * window + block)
                    ke = wsum_ref[there].astype(F32)
                    gcar = dot_nn(mix_t[s, cols], gnum[here])
                    gsum = dot_nn(mix_t[s, cols], gden[here])
                    gv = (gcar * ke).astype(BF)
                    gk = ((gcar * v_ref[there].astype(F32) + gsum) * ke).astype(BF)
                    gk_ref[there] = gk
                    gv_ref[there] = gv
                    wgrad[s, :, cols] += dot_nt(gnum[here], car_ref[there]) + dot_nt(gden[here], wsum_ref[there])
                    dn[there] += dot_nn(gk, wk) + dot_nn(gv, wv)

        by_half(step, w_refs, place_ref, part)

        @pl.when(step == 1)
        def _():
            total = wgrad[0] * masked_ref[0]
            for s in range(1, seqs):
                total = total + wgrad[s] * masked_ref[s]
            lane_row = lax.broadcasted_iota(jnp.int32, (block, keys), 0) + 1
            bit = 1
            while bit <= block:
                rolled = pltpu.roll(total, keys - bit, axis=1)
                total = jnp.where((lane_row & bit) != 0, rolled, total)
                bit *= 2
            band_ref[...] = reverse_lanes(total[:, :window])
            halo_ref[...] = dn[:rows].astype(BF)
            own_ref[...] = dn[rows:]

    def col(n):
        return pl.BlockSpec((n, half), lambda i, *_: (0, i))

    return call(
        order,
        body,
        (2,),
        [whole((rows, width))]
        + attn_specs(weights)
        + [col(rows)] * 3 + [col(2 * rows)] * 3 + [whole((seqs, block, keys))],
        [col(rows), col(2 * rows), col(2 * rows), whole((block, window)), whole((rows, width)), whole((rows, width))],
        [
            shape_of((rows, width), BF),
            shape_of((2 * rows, width), BF),
            shape_of((2 * rows, width), BF),
            shape_of((block, window), F32),
            shape_of((rows, width), F32),
            shape_of((rows, width), BF),
        ],
        [
            pltpu.VMEM((seqs, keys, block), BF),
            pltpu.VMEM((seqs, block, keys), F32),
            pltpu.VMEM((2 * rows, width), F32),
        ],
        prefetch=1,
        name="attn_bwd",
    )(place, grad_low, *weights, sg, ratio, rden, v, wsum, carried, masked)


def attn_weight_grads(order, place, gq, gk, gv, mixed, normed, halo, grad_low, mp, mixed_rows):
    rows, width = gq.shape
    half = width // 2
    quarter = half // 2

    def body(place_ref, gq_ref, gk_ref, gv_ref, mixed_ref, n_ref, h_ref, ga_ref, oa, ob, ta, tb):
        step = pl.program_id(0)
        mat = lax.rem(step, 4)

        def store(value):
            low = value.astype(BF)

            def put(a_ref, b_ref):
                if not mixed_rows:
                    a_ref[0] = low[:quarter]
                    b_ref[0] = low[quarter:]
                    return
                piece = quarter // mp
                for z in range(mp):
                    a_ref[0, z * piece : (z + 1) * piece] = low[2 * z * piece : (2 * z + 1) * piece]
                    b_ref[0, z * piece : (z + 1) * piece] = low[(2 * z + 1) * piece : (2 * z + 2) * piece]

            pl.when(step < 4)(lambda: put(oa, ob))
            pl.when(step >= 4)(lambda: put(ta, tb))

        def keys_grad(ref):
            return dot_tn(ref[:rows], h_ref[...]) + dot_tn(ref[rows:], n_ref[...])

        pl.when(mat == 0)(lambda: store(dot_tn(gq_ref[...], n_ref[...])))
        pl.when(mat == 1)(lambda: store(keys_grad(gk_ref)))
        pl.when(mat == 2)(lambda: store(keys_grad(gv_ref)))
        pl.when(mat == 3)(lambda: store(dot_tn(mixed_ref[...], ga_ref[...])))

    def col(n):
        return pl.BlockSpec((n, half), lambda i, *_: (0, i // 4))

    own = pl.BlockSpec((1, quarter, width), lambda i, t: (jnp.minimum(i, 3) ^ t[0], 0, 0))
    other = pl.BlockSpec((1, quarter, width), lambda i, t: (jnp.maximum(i - 4, 0) ^ t[0], 0, 0))
    return call(
        order,
        body,
        (8,),
        [col(rows), col(2 * rows), col(2 * rows), col(rows)] + [whole((rows, width))] * 3,
        [own, own, other, other],
        [shape_of((4, quarter, width), BF)] * 4,
        prefetch=1,
        name="attn_wgrad",
    )(place, gq, gk, gv, mixed, normed, halo, grad_low)


def leave_attn(order, x, grad, own, back, gain):
    rows, width = x.shape

    def body(x_ref, g_ref, o_ref, b_ref, gain_ref, out_ref, gg_ref, gs_ref):
        normal, inv = normalize(x_ref[...])
        total = o_ref[...] + b_ref[...].astype(F32)
        out_ref[...] = g_ref[...] + norm_back(total, normal, inv, gain_ref[...])
        gg_ref[...] = jnp.sum(total * normal, axis=0, keepdims=True)
        gs_ref[...] = jnp.sum(total, axis=0, keepdims=True)

    return call(
        order,
        body,
        (1,),
        [whole((rows, width))] * 4 + [whole((1, width))],
        [whole((rows, width)), whole((1, width)), whole((1, width))],
        [shape_of((rows, width), F32)] + [shape_of((1, width), F32)] * 2,
        name="leave",
    )(x, grad, own, back, gain)


def finish_layer(order, layer, layers, place, parts, channels, hidden, mp_rows, previous):
    width = parts[0].shape[-1]
    piece = mp_rows
    small = piece // 2
    total = 4 * channels

    def body(place_ref, *rest):
        p_refs, (qkv_ref, out_ref, up_ref, down_ref, up) = rest[: len(parts)], rest[len(parts) :]

        def put(owner, count, shift, value):
            start = owner * piece + shift
            mat = start // channels
            inner = pl.multiple_of(start - mat * channels, small)

            @pl.when(mat < 3)
            def _():
                qkv_ref[0, jnp.minimum(mat, 2), pl.ds(inner, count)] = value

            @pl.when(mat == 3)
            def _():
                out_ref[0, pl.ds(inner, count)] = value

        if len(parts) == 1:
            for owner in range(total // piece):
                here = slice(owner * piece, (owner + 1) * piece)
                mat = owner * piece // channels
                inner = slice(owner * piece - mat * channels, owner * piece - mat * channels + piece)
                value = p_refs[0][owner, :piece].astype(F32)
                if mat < 3:
                    qkv_ref[0, mat, inner] = value
                else:
                    out_ref[0, inner] = value
                up[here] = p_refs[0][owner, piece : 2 * piece].astype(F32)
                down_ref[0, here] = p_refs[0][owner, 2 * piece :].astype(F32)
        else:
            for core in range(2):
                pa, pb = p_refs[2 * core], p_refs[2 * core + 1]
                for p in range(pa.shape[0]):
                    owner = 2 * (place_ref[2] ^ p) + (place_ref[3] ^ core)
                    start = pl.multiple_of(owner * piece, piece)
                    up[pl.ds(start, piece)] = pa[p, :piece].astype(F32)
                    down_ref[0, pl.ds(start, piece)] = pb[p, :piece].astype(F32)
                    put(owner, small, 0, pa[p, piece:].astype(F32))
                    put(owner, small, small, pb[p, piece:].astype(F32))
        up_ref[0] = up[...].T

    shapes = [
        (layers, 3, channels, width),
        (layers, channels, width),
        (layers, width, hidden),
        (layers, hidden, width),
    ]

    def here(shape):
        return pl.BlockSpec((1,) + shape[1:], lambda i, *_: (layer,) + (0,) * (len(shape) - 1))

    first = len(parts) + 1
    extra = list(previous) if previous is not None else []
    order_in = first + len(extra)
    anywhere = pl.BlockSpec(memory_space=pl.ANY)

    def with_token(*refs):
        ins = refs[: first + len(extra)]
        outs = refs[order_in + 1 : order_in + 5]
        return body(*ins[:first], *outs, *refs[order_in + 6 :])

    aliases = {first + k: k for k in range(len(extra))}
    aliases[order_in] = 4
    *results, order.token = pl.pallas_call(
        with_token,
        grid_spec=pltpu.PrefetchScalarGridSpec(
            num_scalar_prefetch=1,
            grid=(1,),
            in_specs=[whole(part.shape) for part in parts] + [anywhere] * (len(extra) + 1),
            out_specs=[here(shape) for shape in shapes] + [anywhere],
            scratch_shapes=[pltpu.VMEM((total, width), F32)],
        ),
        out_shape=[shape_of(shape, F32) for shape in shapes] + [shape_of(TOKEN, jnp.int32)],
        input_output_aliases=aliases,
        compiler_params=pltpu.CompilerParams(
            dimension_semantics=("arbitrary",), vmem_limit_bytes=VMEM_LIMIT
        ),
        cost_estimate=pl.CostEstimate(flops=0, bytes_accessed=0, transcendentals=0),
        name="finish",
    )(place, *parts, *extra, order.token)
    return results


DP = ("g", "c")


class Order:
    def __init__(self):
        self.token = jnp.zeros(TOKEN, jnp.int32)

    def pin(self, *arrays):
        *arrays, self.token = tie(*arrays, self.token)
        return arrays


class Links:
    def __init__(self, order, dp, mp):
        self.order = order
        self.dp = dp
        self.mp = mp
        bits = [1 << k for k in range(1, dp.bit_length() - 1)]
        self.routes = (bits, bits[::-1])

    def swap(self, value, axis, bit):
        size = self.dp if axis == DP else self.mp
        return lax.ppermute(value, axis, [(i, i ^ bit) for i in range(size)])


class Spread:
    def __init__(self, links, values):
        self.links = links
        self.values = list(values)
        self.phase = 0
        self.have = [[], []]

    def start(self):
        self.values = self.links.order.pin(*self.values)
        self.coming = [
            self.links.swap(value, DP, route[self.phase])
            for value, route in zip(self.values, self.links.routes)
        ]

    def wait(self):
        coming = self.links.order.pin(*self.coming)
        for k in range(2):
            bit = self.links.routes[k][self.phase]
            place = sum(1 for other in self.have[k] if other > bit)
            self.values[k] = jnp.stack([self.values[k], coming[k]], axis=place)
            self.have[k].append(bit)
        self.phase += 1

    def wait_all(self):
        self.wait()
        while self.phase < len(self.links.routes[0]):
            self.start()
            self.wait()

    def start_cores(self):
        self.values = self.links.order.pin(*self.values)
        self.coming = [self.links.swap(value, DP, 1) for value in self.values]

    def wait_cores(self):
        return self.values + self.links.order.pin(*self.coming)


class Gather(Spread):
    def __init__(self, links, piece_a, piece_b):
        super().__init__(links, ())
        self.cut = piece_a.shape[0]
        self.piece = jnp.concatenate([piece_a, piece_b], axis=0)

    def start_mp(self):
        (self.piece,) = self.links.order.pin(self.piece)
        self.coming_mp = [self.links.swap(self.piece, "mp", p) for p in range(1, self.links.mp)]

    def wait_mp(self):
        parts = [self.piece] + self.links.order.pin(*self.coming_mp)
        self.values = [
            jnp.stack([part[: self.cut] for part in parts]),
            jnp.stack([part[self.cut :] for part in parts]),
        ]


class Reduce:
    def __init__(self, links, halves):
        self.links = links
        self.halves = halves
        self.phase = 0

    def start_cores(self):
        others = self.links.order.pin(*self.halves[2:])
        self.coming = [self.links.swap(other, DP, 1) for other in others]

    def wait_cores(self):
        coming = self.links.order.pin(*self.coming)
        mp = self.links.mp
        self.have = [sorted(route, reverse=True) for route in self.links.routes]
        self.values = []
        for own, other in zip(self.halves[:2], coming):
            total = (own.astype(F32) + other.astype(F32)).astype(BF)
            groups = self.links.dp // 2
            rows = total.size // total.shape[-1] // groups // mp
            self.values.append(total.reshape((2,) * len(self.have[0]) + (mp, rows, total.shape[-1])))

    def start(self):
        sends, self.keeps = [], []
        for k in range(2):
            place = self.have[k].index(self.links.routes[1 - k][self.phase])
            self.keeps.append(lax.index_in_dim(self.values[k], 0, place, keepdims=False))
            sends.append(lax.index_in_dim(self.values[k], 1, place, keepdims=False))
        sends = self.links.order.pin(*sends)
        self.coming = [
            self.links.swap(sends[k], DP, self.links.routes[1 - k][self.phase]) for k in range(2)
        ]

    def wait(self):
        coming = self.links.order.pin(*self.coming)
        for k in range(2):
            self.values[k] = (self.keeps[k].astype(F32) + coming[k].astype(F32)).astype(BF)
            self.have[k].remove(self.links.routes[1 - k][self.phase])
        self.phase += 1

    def wait_all(self):
        self.wait()
        while self.phase < len(self.links.routes[0]):
            self.start()
            self.wait()
        return self.values


class ReduceWide:
    def __init__(self, links, own, other):
        self.links = links
        self.own = own
        self.other = other

    def start_cores(self):
        (self.other,) = self.links.order.pin(self.other)
        self.coming = self.links.swap(self.other, DP, 1)

    def wait_cores(self):
        (coming,) = self.links.order.pin(self.coming)
        total = (self.own.astype(F32) + coming.astype(F32)).astype(BF)
        (total,) = self.links.order.pin(total)
        self.sums = lax.psum_scatter(total, "g", scatter_dimension=0, tiled=True)

    def wait(self):
        (sums,) = self.links.order.pin(self.sums)
        return sums.reshape(2, self.links.mp, -1, sums.shape[-1])


class ReduceMp:
    def __init__(self, links, arrays, index):
        self.links = links
        joined = jnp.concatenate(arrays, axis=1)
        if index is None:
            blocks = [joined[p] for p in range(links.mp)]
        else:
            blocks = [
                lax.dynamic_index_in_dim(joined, jnp.bitwise_xor(index, p), 0, keepdims=False)
                for p in range(links.mp)
            ]
        self.kept, *sends = links.order.pin(*blocks)
        self.coming = [links.swap(send, "mp", p + 1) for p, send in enumerate(sends)]

    def wait(self):
        total = self.kept.astype(F32)
        for part in self.links.order.pin(*self.coming):
            total = total + part.astype(F32)
        return total.astype(BF)


def make_shards(dp, mp):
    def shards(
        tokens,
        segments,
        qkv_weight,
        out_weight,
        up_weight,
        down_projection_weight,
        norm_gain,
        norm_bias,
        pos_bias,
        cotangent,
    ):
        seqs, block, width = tokens.shape
        layers = qkv_weight.shape[0]
        window = pos_bias.shape[2]
        channels = qkv_weight.shape[-1]
        hidden = up_weight.shape[-1]
        rows = seqs * block
        group = lax.axis_index("g")
        core = lax.axis_index("c")
        dp_index = group * 2 + core
        mp_index = lax.axis_index("mp")
        order = Order()
        links = Links(order, dp, mp)
        attn_rows = 4 * channels // dp
        ff_rows = hidden // dp
        groups = dp // 2
        per = max(1, width // (mp * ff_rows))
        place = jnp.stack([group // (groups // 4), mp_index, group, core, group // per, group % per]).astype(jnp.int32)

        def picks(count, offset, length):
            return (
                lax.broadcasted_iota(jnp.int32, (count, length), 0) + offset
                == lax.broadcasted_iota(jnp.int32, (count, length), 1)
            ).astype(BF)

        ff_pick = picks(ff_rows, dp_index * ff_rows, hidden)

        def attn_piece(layer):
            by_channel = jnp.transpose(qkv_weight[layer], (0, 2, 1)).reshape(3 * channels, width)
            start = dp_index * attn_rows
            inner = start - 3 * channels
            return jnp.where(
                inner < 0,
                lax.dynamic_slice_in_dim(by_channel, jnp.minimum(start, 3 * channels - attn_rows), attn_rows),
                lax.dynamic_slice_in_dim(out_weight[layer], jnp.maximum(inner, 0), attn_rows),
            )

        def ff_pieces(layer):
            return (
                dot_nt(ff_pick, up_weight[layer]).astype(BF),
                dot_nn(ff_pick, down_projection_weight[layer]).astype(BF),
            )

        def attn_mats(parts):
            return [part.reshape(4, -1, width) for part in parts]

        def ff_mats(parts):
            flat = [part.reshape(-1, width) for part in parts]
            return (flat[0], flat[2]), (flat[1], flat[3])

        def relative(gathered):
            by_dp = jnp.take(gathered, jnp.bitwise_xor(jnp.arange(dp), dp_index), axis=0)
            both = jnp.take(by_dp, jnp.bitwise_xor(jnp.arange(mp), mp_index), axis=1)
            both = both.reshape((dp // 2, 2) + gathered.shape[1:])
            return both[:, 0], both[:, 1]

        def forward_halo(value):
            return lax.ppermute(value, "mp", [(i, i + 1) for i in range(mp - 1)])

        def backward_halo(value):
            return lax.ppermute(value, "mp", [(i + 1, i) for i in range(mp - 1)])

        gains = norm_gain.reshape(layers, 2, 1, width)
        shifts = norm_bias.reshape(layers, 2, 1, width)
        middle = attn_rows // 2
        in_blocks = middle % 16 == 0

        piece = attn_piece(0)
        attn0 = Gather(links, piece[:middle], piece[middle:])
        attn0.start_mp()
        x, normed = enter_kernel(order, tokens.reshape(rows, width), gains[0, 0], shifts[0, 0])
        (normed,) = order.pin(normed)
        halo = forward_halo(normed)
        ff0 = Gather(links, *ff_pieces(0))
        ff0.start_mp()
        later = jnp.concatenate((attn_piece(1),) + ff_pieces(1), axis=0)

        seg_pad = jnp.concatenate([jnp.full((seqs, window), -1, segments.dtype), segments], axis=1)
        seg_keys = lax.dynamic_slice_in_dim(seg_pad, mp_index * block, block + window, axis=1)
        seg_q = seg_keys[:, window:].reshape(seqs, block, 1)
        seg_k = seg_keys.reshape(seqs, 1, block + window)

        attn0.wait_mp()
        attn0.start()
        (later,) = order.pin(later)
        later = lax.all_gather(later, ("g", "c", "mp"), axis=0, tiled=False)
        attn0.wait()
        attn0.start()
        ff0.wait_mp()
        ff0.start()
        attn0.wait_all()
        attn0.start_cores()
        ff0.wait()
        ff0.start()
        w_attn0 = attn_mats(attn0.wait_cores())
        (halo,) = order.pin(halo)

        def attn(layer, x, normed, halo, w_attn):
            sg, ratio, rden, v, wsum, carried, mixed, masked, x1, normed_b = attn_forward(
                order, layer, place, x, normed, halo, w_attn, pos_bias, seg_q, seg_k,
                gains[layer, 1], shifts[layer, 1],
            )
            return x1, normed_b, (sg, ratio, rden, v, wsum, carried, masked), (mixed, normed, halo)

        x1_0, normed_b0, saved0, rows0 = attn(0, x, normed, halo, w_attn0)
        ff0.wait_all()
        ff0.start_cores()
        ups0, downs0 = ff_mats(ff0.wait_cores())
        act0, slope0, x2, normed2 = ff_forward(
            order, x1_0, normed_b0, ups0, downs0, gains[1, 0], shifts[1, 0]
        )
        (normed2,) = order.pin(normed2)
        halo2 = forward_halo(normed2)
        (later,) = order.pin(later)
        if in_blocks:
            w_attn1 = w_ff1 = [later.reshape((groups, 2, mp) + later.shape[1:])]
        else:
            own, other = relative(later.reshape((dp, mp) + later.shape[1:]))
            cuts = [middle, attn_rows, attn_rows + ff_rows]
            own_a, own_b, own_up, own_down = jnp.split(own, cuts, axis=2)
            other_a, other_b, other_up, other_down = jnp.split(other, cuts, axis=2)
            w_attn1 = attn_mats([own_a, own_b, other_a, other_b])
            w_ff1 = sum(ff_mats([own_up, own_down, other_up, other_down]), ())
        (halo2,) = order.pin(halo2)
        x1_1, normed_b1, saved1, rows1 = attn(1, x2, normed2, halo2, w_attn1)

        def ff_back(layer, x1, normed_b, weights, grad, saved):
            args = (order, place, x1, normed_b, weights)
            kept = (groups, grad, gains[layer, 1], saved)
            wg_other, *before = ff_backward(*args, 1, *kept, None)
            wide = ReduceWide(links, None, wg_other)
            wide.start_cores()
            wide.own, *rest = ff_backward(*args, 0, *kept, before)
            return wide, rest

        wide1, (grad1, grad1_low, gain_b1, shift_b1, output) = ff_back(
            1, x1_1, normed_b1, w_ff1, cotangent.reshape(rows, width), None
        )
        wide1.wait_cores()
        gq, gk, gv, band1, dn_own1, back1 = attn_backward(order, place, grad1_low, w_attn1, *saved1)
        (back1,) = order.pin(back1)
        back1 = backward_halo(back1)
        r_attn1 = Reduce(
            links, attn_weight_grads(order, place, gq, gk, gv, *rows1, grad1_low, mp, in_blocks)
        )
        (back1,) = order.pin(back1)
        r_attn1.start_cores()
        grad2, gain_a1, shift_a1 = leave_attn(order, x2, grad1, dn_own1, back1, gains[1, 0])
        r_attn1.wait_cores()
        r_attn1.start()
        wide0, (grad3, grad3_low, gain_b0, shift_b0) = ff_back(
            0, x1_0, normed_b0, ups0 + downs0, grad2, (act0, slope0)
        )
        wide0.wait_cores()
        r_attn1.wait()
        r_attn1.start()
        gq, gk, gv, band0, dn_own0, back0 = attn_backward(order, place, grad3_low, w_attn0, *saved0)
        attn1_sum = r_attn1.wait_all()
        (back0,) = order.pin(back0)
        back0 = backward_halo(back0)
        r_attn0 = Reduce(
            links, attn_weight_grads(order, place, gq, gk, gv, *rows0, grad3_low, mp, False)
        )
        r_attn0.start_cores()
        up1, down1 = wide1.wait()
        mp1 = ReduceMp(links, attn1_sum + [up1, down1], mp_index if in_blocks else None)
        r_attn0.wait_cores()
        r_attn0.start()
        (back0,) = order.pin(back0)
        grad4, gain_a0, shift_a0 = leave_attn(order, x, grad3, dn_own0, back0, gains[0, 0])
        norms = jnp.concatenate(
            [gain_a0, gain_b0, shift_a0, shift_b0, gain_a1, gain_b1, shift_a1, shift_b1], axis=0
        ).reshape(-1, window)
        small = jnp.concatenate([band0, band1, norms], axis=0).astype(BF)

        def small_start(bit):
            (here,) = order.pin(small)
            return here, links.swap(here, DP, bit)

        def small_wait(pair):
            (coming,) = order.pin(pair[1])
            return (pair[0].astype(F32) + coming.astype(F32)).astype(BF)

        bits = [1 << k for k in range(dp.bit_length() - 1)]
        pair = small_start(bits[0])
        r_attn0.wait()
        small = small_wait(pair)
        r_attn0.start()
        pair = small_start(bits[1])
        sum1 = mp1.wait()
        (sum1,) = order.pin(sum1)
        full1 = lax.all_gather(sum1, DP, axis=0, tiled=False)
        attn0_sum = r_attn0.wait_all()
        small = small_wait(pair)
        for bit in bits[2:]:
            small = small_wait(small_start(bit))
        up0, down0 = wide0.wait()
        mp0 = ReduceMp(links, attn0_sum + [up0, down0], None)
        (small,) = order.pin(small)
        small_parts = [links.swap(small, "mp", p) for p in range(1, mp)]
        (full1,) = order.pin(full1)

        def finish(layer, full, previous):
            if in_blocks:
                return finish_layer(order, layer, layers, place, full, channels, hidden, attn_rows, previous)
            if len(full) == 1:
                owner = jnp.arange(dp)
                attn_part, up_part, down_part = jnp.split(full[0], [attn_rows, attn_rows + ff_rows], axis=1)
            else:
                owner = jnp.bitwise_xor(jnp.arange(dp), dp_index)
                part_a, part_b = [
                    jnp.stack([full[k], full[2 + k]], axis=1).reshape(dp, -1, width) for k in range(2)
                ]
                attn_part = jnp.concatenate([part_a[:, ff_rows:], part_b[:, ff_rows:]], axis=1)
                up_part, down_part = part_a[:, :ff_rows], part_b[:, :ff_rows]

            def rows_of(value):
                return value.reshape(-1, width)

            def place_of(count):
                spots = (owner[:, None] * count + jnp.arange(count)[None, :]).reshape(-1, 1)
                return (spots == jnp.arange(dp * count)[None, :]).astype(BF)

            attn_place = place_of(attn_rows).reshape(-1, 4, channels)
            ff_place = place_of(ff_rows)
            values = (
                jnp.einsum("pd,pmc->mcd", rows_of(attn_part), attn_place[:, :3], preferred_element_type=F32),
                dot_tn(attn_place[:, 3], rows_of(attn_part)),
                dot_tn(rows_of(up_part), ff_place),
                dot_tn(ff_place, rows_of(down_part)),
            )
            if previous is None:
                previous = [jnp.zeros((layers,) + value.shape, F32) for value in values]
            return [
                lax.dynamic_update_index_in_dim(kept, value, layer, 0)
                for kept, value in zip(previous, values)
            ]

        big = finish(1, [full1], None)
        sum0 = mp0.wait()
        spread0 = Spread(
            links,
            [
                jnp.concatenate([sum0[attn_rows : attn_rows + ff_rows], sum0[:middle]], axis=0),
                jnp.concatenate([sum0[attn_rows + ff_rows :], sum0[middle:attn_rows]], axis=0),
            ],
        )
        spread0.start()
        small_parts = [small] + order.pin(*small_parts)
        spread0.wait()
        spread0.start()
        small_all = jnp.stack(small_parts)
        pairs = small_all[:, 2 * block :].astype(F32)
        while pairs.shape[0] > 1:
            pairs = pairs[0::2] + pairs[1::2]
        norm_sum = pairs[0].reshape(layers, 4, width)
        bands = jnp.take(
            small_all[:, : 2 * block].astype(F32), jnp.bitwise_xor(jnp.arange(mp), mp_index), axis=0
        ).reshape(mp, layers, block, window)
        band_sum = jnp.transpose(bands, (1, 0, 2, 3)).reshape(layers, mp * block, window)
        spread0.wait_all()
        spread0.start_cores()
        full0 = [part.reshape(groups, -1, width) for part in spread0.wait_cores()]
        qkv_out, out_out, up_out, down_out = finish(0, full0, big)
        return (
            output.reshape(tokens.shape),
            grad4.reshape(tokens.shape),
            jnp.transpose(qkv_out, (0, 1, 3, 2)),
            out_out,
            up_out,
            down_out,
            norm_sum[:, :2],
            norm_sum[:, 2:],
            band_sum,
        )

    return shards


def solution(mesh):
    dp, mp = mesh.shape["dp"], mesh.shape["mp"]
    inner = Mesh(mesh.devices.reshape(dp // 2, 2, mp), DP + ("mp",))
    placed = (
        P(DP, "mp", None),
        P(DP, None),
        P(None, None, None, "mp"),
        P(None, "mp", None),
        P(None, None, "mp"),
        P(None, "mp", None),
        P(),
        P(),
        P(),
        P(DP, "mp", None),
    )
    return jax.shard_map(
        make_shards(dp, mp),
        mesh=inner,
        in_specs=placed,
        out_specs=(
            P(DP, "mp", None),
            P(DP, "mp", None),
            P(None, None, None, "mp"),
            P(None, "mp", None),
            P(None, None, "mp"),
            P(None, "mp", None),
            P(),
            P(),
            P(),
        ),
        check_vma=False,
    )
```

```python
import functools

import jax
import jax.numpy as jnp
from jax import lax
from jax.experimental import pallas as pl
from jax.experimental.pallas import tpu as pltpu
from jax.sharding import Mesh, PartitionSpec as P

BF = jnp.bfloat16
F32 = jnp.float32
VMEM_LIMIT = 58 * 1024 * 1024
TOKEN = (8, 128)
GELU_A = 0.7978845608028654
GELU_B = 0.044715


def dot_nt(lhs, rhs):
    return lax.dot_general(lhs, rhs, (((1,), (1,)), ((), ())), preferred_element_type=F32)


def dot_nn(lhs, rhs):
    return lax.dot_general(lhs, rhs, (((1,), (0,)), ((), ())), preferred_element_type=F32)


def dot_tn(lhs, rhs):
    return lax.dot_general(lhs, rhs, (((0,), (0,)), ((), ())), preferred_element_type=F32)


def normalize(values):
    center = values - jnp.mean(values, axis=-1, keepdims=True)
    inv_std = lax.rsqrt(jnp.mean(center * center, axis=-1, keepdims=True) + 1e-05)
    return center * inv_std, inv_std


def norm_back(grad_out, normal, inv_std, gain):
    grad_normal = grad_out * gain
    mean_one = jnp.mean(grad_normal, axis=-1, keepdims=True)
    mean_two = jnp.mean(grad_normal * normal, axis=-1, keepdims=True)
    return inv_std * (grad_normal - mean_one - normal * mean_two)


def whole(shape):
    return pl.BlockSpec(shape, lambda *_: (0,) * len(shape))


def call(order, body, grid, in_specs, out_specs, out_shape, scratch=(), prefetch=0, name=None):
    first = prefetch + len(in_specs)
    second = first + 1 + len(out_specs)
    anywhere = pl.BlockSpec(memory_space=pl.ANY)

    def with_token(*refs):
        return body(*refs[:first], *refs[first + 1 : second], *refs[second + 1 :])

    kernel = pl.pallas_call(
        with_token,
        grid_spec=pltpu.PrefetchScalarGridSpec(
            num_scalar_prefetch=prefetch,
            grid=grid,
            in_specs=list(in_specs) + [anywhere],
            out_specs=list(out_specs) + [anywhere],
            scratch_shapes=list(scratch),
        ),
        out_shape=list(out_shape) + [shape_of(TOKEN, jnp.int32)],
        input_output_aliases={first: len(out_specs)},
        compiler_params=pltpu.CompilerParams(
            dimension_semantics=("arbitrary",) * len(grid), vmem_limit_bytes=VMEM_LIMIT
        ),
        cost_estimate=pl.CostEstimate(flops=0, bytes_accessed=0, transcendentals=0),
        name=name,
    )

    def run(*operands):
        *results, order.token = kernel(*operands, order.token)
        return results

    return run


def shape_of(shape, dtype):
    return jax.ShapeDtypeStruct(shape, dtype)


def tie(*arrays):
    count = len(arrays)
    return pl.pallas_call(
        lambda *refs: None,
        out_shape=[shape_of(a.shape, a.dtype) for a in arrays],
        in_specs=[pl.BlockSpec(memory_space=pl.ANY)] * count,
        out_specs=[pl.BlockSpec(memory_space=pl.ANY)] * count,
        input_output_aliases={i: i for i in range(count)},
        cost_estimate=pl.CostEstimate(flops=0, bytes_accessed=0, transcendentals=0),
        name="tie",
    )(*arrays)


def enter_kernel(order, tokens, gain, shift):
    rows, width = tokens.shape

    def body(t_ref, g_ref, s_ref, x_ref, n_ref):
        x = t_ref[...].astype(F32)
        x_ref[...] = x
        normal, _ = normalize(x)
        n_ref[...] = (normal * g_ref[...] + s_ref[...]).astype(BF)

    return call(
        order,
        body,
        (1,),
        [whole((rows, width)), whole((1, width)), whole((1, width))],
        [whole((rows, width)), whole((rows, width))],
        [shape_of((rows, width), F32), shape_of((rows, width), BF)],
        name="enter",
    )(tokens, gain, shift)


def reverse_lanes(values):
    count = values.shape[1]
    flip = (
        lax.broadcasted_iota(jnp.int32, (count, count), 0)
        + lax.broadcasted_iota(jnp.int32, (count, count), 1)
        == count - 1
    ).astype(BF)
    high = values.astype(BF)
    rest = values - high.astype(F32)
    middle = rest.astype(BF)
    last = (rest - middle.astype(F32)).astype(BF)
    return (dot_nn(high, flip) + dot_nn(middle, flip)) + dot_nn(last, flip)


def attn_specs(weights):
    if len(weights) == 4:
        return [whole(w.shape) for w in weights]
    groups, _, mp, count, width = weights[0].shape
    return [pl.BlockSpec((groups, 1, mp, count // 3, width), lambda i, place: (0, place[3] ^ i, 0, 0, 0))]


def by_half(step, refs, place_ref, part):
    if len(refs) == 1:
        width = refs[0].shape[-1]
        part(lambda m: refs[0][m, 0].reshape(-1, width))
        return
    for half in range(2):
        wa, wb = refs[2 * half], refs[2 * half + 1]

        def mat(m, wa=wa, wb=wb):
            return jnp.concatenate([wa[place_ref[0] ^ m], wb[place_ref[0] ^ m]], axis=0)

        pl.when(step == half)(functools.partial(part, mat))


def attn_forward(order, layer, place, x, normed, halo, weights, pos_bias, seg_q, seg_k, gain, shift):
    rows, width = x.shape
    seqs, block, _ = seg_q.shape
    keys = seg_k.shape[2]
    window = keys - block
    half = width // 2

    def body(place_ref, x_ref, n_ref, h_ref, *rest):
        w_refs, rest = rest[: len(weights)], rest[len(weights) :]
        (band_ref, sq_ref, sk_ref, g_ref, s_ref, sg_ref, ratio_ref, rden_ref, v_ref, wsum_ref, car_ref, mixed_ref,
         masked_ref, x1_ref, nb_ref, mix) = rest
        step = pl.program_id(0)

        @pl.when(step == 0)
        def _():
            band = reverse_lanes(jnp.exp(band_ref[0]))
            band = jnp.concatenate([band, jnp.zeros((block, block), F32)], axis=1)
            spread = pltpu.roll(band, 1, axis=1, stride=1, stride_axis=0)
            for s in range(seqs):
                masked = jnp.where(sq_ref[s] == sk_ref[s], spread, 0.0)
                masked_ref[s] = masked
                mix[s] = masked.astype(BF)
            x1_ref[...] = x_ref[...]

        def part(mat):
            wq, wk, wv = mat(0), mat(1), mat(2)
            q = dot_nt(n_ref[...], wq)
            sg = jax.nn.sigmoid(q)
            sg_ref[...] = sg.astype(BF)
            carried, wsum = [], []
            for r, source in enumerate((h_ref, n_ref)):
                here = slice(r * rows, (r + 1) * rows)
                kexp = jnp.exp(dot_nt(source[...], wk))
                v = dot_nt(source[...], wv)
                v_ref[here] = v.astype(BF)
                wsum.append(kexp.astype(BF))
                carried.append((kexp * v).astype(BF))
                wsum_ref[here] = wsum[r]
                car_ref[here] = carried[r]
            mixed = []
            for s in range(seqs):
                here = slice(s * block, (s + 1) * block)
                num = dot_nn(mix[s, :, :window], carried[0][here]) + dot_nn(mix[s, :, window:], carried[1][here])
                den = dot_nn(mix[s, :, :window], wsum[0][here]) + dot_nn(mix[s, :, window:], wsum[1][here])
                rden = 1.0 / den
                ratio = num * rden
                rden_ref[here] = rden.astype(BF)
                ratio_ref[here] = ratio.astype(BF)
                mixed.append((sg[here] * ratio).astype(BF))
            mixed = jnp.concatenate(mixed, axis=0)
            mixed_ref[...] = mixed
            x1_ref[...] += dot_nn(mixed, mat(3))

        by_half(step, w_refs, place_ref, part)

        @pl.when(step == 1)
        def _():
            normal, _ = normalize(x1_ref[...])
            nb_ref[...] = (normal * g_ref[...] + s_ref[...]).astype(BF)

    def col(n):
        return pl.BlockSpec((n, half), lambda i, *_: (0, i))

    return call(
        order,
        body,
        (2,),
        [whole((rows, width))] * 3
        + attn_specs(weights)
        + [pl.BlockSpec((1, block, window), lambda i, place: (layer, place[1], 0))]
        + [whole((seqs, block, 1)), whole((seqs, 1, keys)), whole((1, width)), whole((1, width))],
        [col(rows)] * 3 + [col(2 * rows)] * 3 + [col(rows)]
        + [whole((seqs, block, keys)), whole((rows, width)), whole((rows, width))],
        [shape_of((rows, width), BF)] * 3
        + [shape_of((2 * rows, width), BF)] * 3
        + [
            shape_of((rows, width), BF),
            shape_of((seqs, block, keys), F32),
            shape_of((rows, width), F32),
            shape_of((rows, width), BF),
        ],
        [pltpu.VMEM((seqs, block, keys), BF)],
        prefetch=1,
        name="attn_fwd",
    )(place, x, normed, halo, *weights, pos_bias, seg_q, seg_k, gain, shift)


def gelu_both(pre):
    square = pre * pre
    upper = 0.5 + 0.5 * jnp.tanh(pre * (GELU_A + (GELU_A * GELU_B) * square))
    act = pre * upper
    return act, upper + act * (1.0 - upper) * (2.0 * GELU_A + (6.0 * GELU_A * GELU_B) * square)


def chunk_specs(chunk, width, per_half):
    own = pl.BlockSpec((chunk, width), lambda i, *_: (jnp.minimum(i, per_half - 1), 0))
    other = pl.BlockSpec((chunk, width), lambda i, *_: (jnp.maximum(i - per_half, 0), 0))
    return own, other


def ff_forward(order, x1, normed, ups, downs, gain, shift):
    rows, width = x1.shape
    half = ups[0].shape[0]
    per_half = 2
    chunk = half // per_half
    steps = 2 * per_half

    def body(x_ref, n_ref, u0, u1, d0, d1, g_ref, s_ref, act_ref, slope_ref, x2_ref, next_ref):
        step = pl.program_id(0)

        @pl.when(step == 0)
        def _():
            x2_ref[...] = x_ref[...]

        def part(u, d):
            act, slope = gelu_both(dot_nt(n_ref[...], u[...]))
            act = act.astype(BF)
            act_ref[...] = act
            slope_ref[...] = slope.astype(BF)
            x2_ref[...] += dot_nn(act, d[...])

        pl.when(step < per_half)(lambda: part(u0, d0))
        pl.when(step >= per_half)(lambda: part(u1, d1))

        @pl.when(step == steps - 1)
        def _():
            normal, _ = normalize(x2_ref[...])
            next_ref[...] = (normal * g_ref[...] + s_ref[...]).astype(BF)

    own, other = chunk_specs(chunk, width, per_half)
    col = pl.BlockSpec((rows, chunk), lambda i: (0, i))
    return call(
        order,
        body,
        (steps,),
        [whole((rows, width))] * 2 + [own, other, own, other] + [whole((1, width))] * 2,
        [col, col, whole((rows, width)), whole((rows, width))],
        [
            shape_of((rows, 2 * half), BF),
            shape_of((rows, 2 * half), BF),
            shape_of((rows, width), F32),
            shape_of((rows, width), BF),
        ],
        name="ff_fwd",
    )(x1, normed, *ups, *downs, gain, shift)


def ff_specs(weights, chunk):
    if len(weights) == 4:
        half, width = weights[0].shape
        own, other = chunk_specs(chunk, width, half // chunk)
        return list(weights), [own, other, own, other]
    groups, _, mp, count, width = weights[0].shape
    rows = count // 3
    per = chunk // (mp * rows)
    steps = groups // per

    def spec(which):
        return pl.BlockSpec(
            (per, 1, mp, rows, width), lambda i, place: (i % steps, place[3] ^ (i // steps), 0, which, 0)
        )

    return [weights[0], weights[0]], [spec(1), spec(2)]


def ff_backward(order, place, x1, normed, weights, groups, grad, gain, saved):
    rows, width = x1.shape
    chunk = width
    half = 2 * width
    per_half = half // chunk
    steps = 2 * per_half
    operands, w_specs = ff_specs(weights, chunk)
    group_rows = half // groups
    per = chunk // group_rows
    fresh = saved is None
    relative = len(weights) == 4

    def body(place_ref, x_ref, n_ref, *rest):
        rest = list(rest)
        w_refs = [rest.pop(0) for _ in operands]
        grad_ref, g_ref = rest.pop(0), rest.pop(0)
        act_ref, slope_ref = (None, None) if fresh else (rest.pop(0), rest.pop(0))
        wg_ref, g1_ref, ga_ref, gg_ref, gs_ref = rest[:5]
        out_ref, (low, dn, x2) = (rest[5], rest[6:]) if fresh else (None, (rest[5], rest[6], None))
        step = pl.program_id(0)

        @pl.when(step == 0)
        def _():
            low[...] = grad_ref[...].astype(BF)
            dn[...] = jnp.zeros_like(dn)
            if fresh:
                x2[...] = x_ref[...]

        def part(u_ref, d_ref):
            u = u_ref[...].reshape(chunk, width)
            d = d_ref[...].reshape(chunk, width)
            if fresh:
                act, slope = gelu_both(dot_nt(n_ref[...], u))
                act = act.astype(BF)
                x2[...] += dot_nn(act, d)
            else:
                act, slope = act_ref[...], slope_ref[...].astype(F32)
            pre_grad = (dot_nt(low[...], d) * slope).astype(BF)
            dn[...] += dot_nn(pre_grad, u)
            for which, value in ((0, dot_tn(pre_grad, n_ref[...])), (1, dot_tn(act, low[...]))):
                value = value.astype(BF)
                for k in range(per):
                    spot = (place_ref[5] ^ k) if relative else k
                    wg_ref[spot, 0, which] = value[k * group_rows : (k + 1) * group_rows]

        if relative:
            pl.when(step < per_half)(lambda: part(w_refs[0], w_refs[2]))
            pl.when(step >= per_half)(lambda: part(w_refs[1], w_refs[3]))
        else:
            part(*w_refs)

        @pl.when(step == steps - 1)
        def _():
            if fresh:
                out_ref[...] = x2[...].astype(BF)
            normal, inv = normalize(x_ref[...])
            total = dn[...]
            g1 = grad_ref[...] + norm_back(total, normal, inv, g_ref[...])
            g1_ref[...] = g1
            ga_ref[...] = g1.astype(BF)
            gg_ref[...] = jnp.sum(total * normal, axis=0, keepdims=True)
            gs_ref[...] = jnp.sum(total, axis=0, keepdims=True)

    full = whole((rows, width))
    col = pl.BlockSpec((rows, chunk), lambda i, *_: (0, i))
    wg = pl.BlockSpec(
        (per, 1, 2, group_rows, width),
        lambda i, place: (
            (place[4] ^ (i % per_half)) if relative else i % per_half, place[3] ^ (i // per_half), 0, 0, 0,
        ),
    )
    return call(
        order,
        body,
        (steps,),
        [full, full] + w_specs + [full, whole((1, width))] + ([] if fresh else [col, col]),
        [wg, full, full, whole((1, width)), whole((1, width))] + ([full] if fresh else []),
        [
            shape_of((groups, 2, 2, group_rows, width), BF),
            shape_of((rows, width), F32),
            shape_of((rows, width), BF),
            shape_of((1, width), F32),
            shape_of((1, width), F32),
        ]
        + ([shape_of((rows, width), BF)] if fresh else []),
        [pltpu.VMEM((rows, width), BF), pltpu.VMEM((rows, width), F32)]
        + ([pltpu.VMEM((rows, width), F32)] if fresh else []),
        prefetch=1,
        name="ff_bwd",
    )(place, x1, normed, *operands, grad, gain, *(() if fresh else saved))


def attn_backward(order, place, grad_low, weights, sg, ratio, rden, v, wsum, carried, masked):
    rows, width = grad_low.shape
    seqs, block, keys = masked.shape
    window = keys - block
    half = width // 2

    def body(place_ref, ga_ref, *rest):
        w_refs, rest = rest[: len(weights)], rest[len(weights) :]
        (sg_ref, ratio_ref, rden_ref, v_ref, wsum_ref, car_ref, masked_ref,
         gq_ref, gk_ref, gv_ref, band_ref, own_ref, halo_ref, mix_t, wgrad, dn) = rest
        step = pl.program_id(0)

        @pl.when(step == 0)
        def _():
            for s in range(seqs):
                mix_t[s] = masked_ref[s].T.astype(BF)
            wgrad[...] = jnp.zeros_like(wgrad)
            dn[...] = jnp.zeros_like(dn)

        def part(mat):
            gm = dot_nt(ga_ref[...], mat(3))
            sig = sg_ref[...].astype(F32)
            rat = ratio_ref[...].astype(F32)
            scaled = gm * sig
            gq = (scaled * rat * (1.0 - sig)).astype(BF)
            gq_ref[...] = gq
            gnum_f = scaled * rden_ref[...].astype(F32)
            gnum = gnum_f.astype(BF)
            gden = (-gnum_f * rat).astype(BF)
            wq, wk, wv = mat(0), mat(1), mat(2)
            dn[rows:] += dot_nn(gq, wq)
            for r in range(2):
                for s in range(seqs):
                    here = slice(s * block, (s + 1) * block)
                    there = slice(r * rows + s * block, r * rows + (s + 1) * block)
                    cols = slice(r * window, r * window + block)
                    ke = wsum_ref[there].astype(F32)
                    gcar = dot_nn(mix_t[s, cols], gnum[here])
                    gsum = dot_nn(mix_t[s, cols], gden[here])
                    gv = (gcar * ke).astype(BF)
                    gk = ((gcar * v_ref[there].astype(F32) + gsum) * ke).astype(BF)
                    gk_ref[there] = gk
                    gv_ref[there] = gv
                    wgrad[s, :, cols] += dot_nt(gnum[here], car_ref[there]) + dot_nt(gden[here], wsum_ref[there])
                    dn[there] += dot_nn(gk, wk) + dot_nn(gv, wv)

        by_half(step, w_refs, place_ref, part)

        @pl.when(step == 1)
        def _():
            total = wgrad[0] * masked_ref[0]
            for s in range(1, seqs):
                total = total + wgrad[s] * masked_ref[s]
            lane_row = lax.broadcasted_iota(jnp.int32, (block, keys), 0) + 1
            bit = 1
            while bit <= block:
                rolled = pltpu.roll(total, keys - bit, axis=1)
                total = jnp.where((lane_row & bit) != 0, rolled, total)
                bit *= 2
            band_ref[...] = reverse_lanes(total[:, :window])
            halo_ref[...] = dn[:rows].astype(BF)
            own_ref[...] = dn[rows:]

    def col(n):
        return pl.BlockSpec((n, half), lambda i, *_: (0, i))

    return call(
        order,
        body,
        (2,),
        [whole((rows, width))]
        + attn_specs(weights)
        + [col(rows)] * 3 + [col(2 * rows)] * 3 + [whole((seqs, block, keys))],
        [col(rows), col(2 * rows), col(2 * rows), whole((block, window)), whole((rows, width)), whole((rows, width))],
        [
            shape_of((rows, width), BF),
            shape_of((2 * rows, width), BF),
            shape_of((2 * rows, width), BF),
            shape_of((block, window), F32),
            shape_of((rows, width), F32),
            shape_of((rows, width), BF),
        ],
        [
            pltpu.VMEM((seqs, keys, block), BF),
            pltpu.VMEM((seqs, block, keys), F32),
            pltpu.VMEM((2 * rows, width), F32),
        ],
        prefetch=1,
        name="attn_bwd",
    )(place, grad_low, *weights, sg, ratio, rden, v, wsum, carried, masked)


def attn_weight_grads(order, place, gq, gk, gv, mixed, normed, halo, grad_low, mp, mixed_rows):
    rows, width = gq.shape
    half = width // 2
    quarter = half // 2

    def body(place_ref, gq_ref, gk_ref, gv_ref, mixed_ref, n_ref, h_ref, ga_ref, oa, ob, ta, tb):
        step = pl.program_id(0)
        mat = lax.rem(step, 4)

        def store(value):
            low = value.astype(BF)

            def put(a_ref, b_ref):
                if not mixed_rows:
                    a_ref[0] = low[:quarter]
                    b_ref[0] = low[quarter:]
                    return
                piece = quarter // mp
                for z in range(mp):
                    a_ref[0, z * piece : (z + 1) * piece] = low[2 * z * piece : (2 * z + 1) * piece]
                    b_ref[0, z * piece : (z + 1) * piece] = low[(2 * z + 1) * piece : (2 * z + 2) * piece]

            pl.when(step < 4)(lambda: put(oa, ob))
            pl.when(step >= 4)(lambda: put(ta, tb))

        def keys_grad(ref):
            return dot_tn(ref[:rows], h_ref[...]) + dot_tn(ref[rows:], n_ref[...])

        pl.when(mat == 0)(lambda: store(dot_tn(gq_ref[...], n_ref[...])))
        pl.when(mat == 1)(lambda: store(keys_grad(gk_ref)))
        pl.when(mat == 2)(lambda: store(keys_grad(gv_ref)))
        pl.when(mat == 3)(lambda: store(dot_tn(mixed_ref[...], ga_ref[...])))

    def col(n):
        return pl.BlockSpec((n, half), lambda i, *_: (0, i // 4))

    own = pl.BlockSpec((1, quarter, width), lambda i, t: (jnp.minimum(i, 3) ^ t[0], 0, 0))
    other = pl.BlockSpec((1, quarter, width), lambda i, t: (jnp.maximum(i - 4, 0) ^ t[0], 0, 0))
    return call(
        order,
        body,
        (8,),
        [col(rows), col(2 * rows), col(2 * rows), col(rows)] + [whole((rows, width))] * 3,
        [own, own, other, other],
        [shape_of((4, quarter, width), BF)] * 4,
        prefetch=1,
        name="attn_wgrad",
    )(place, gq, gk, gv, mixed, normed, halo, grad_low)


def leave_attn(order, x, grad, own, back, gain):
    rows, width = x.shape

    def body(x_ref, g_ref, o_ref, b_ref, gain_ref, out_ref, gg_ref, gs_ref):
        normal, inv = normalize(x_ref[...])
        total = o_ref[...] + b_ref[...].astype(F32)
        out_ref[...] = g_ref[...] + norm_back(total, normal, inv, gain_ref[...])
        gg_ref[...] = jnp.sum(total * normal, axis=0, keepdims=True)
        gs_ref[...] = jnp.sum(total, axis=0, keepdims=True)

    return call(
        order,
        body,
        (1,),
        [whole((rows, width))] * 4 + [whole((1, width))],
        [whole((rows, width)), whole((1, width)), whole((1, width))],
        [shape_of((rows, width), F32)] + [shape_of((1, width), F32)] * 2,
        name="leave",
    )(x, grad, own, back, gain)


def finish_layer(order, layer, layers, place, parts, channels, hidden, mp_rows, previous):
    width = parts[0].shape[-1]
    piece = mp_rows
    small = piece // 2
    total = 4 * channels

    def body(place_ref, *rest):
        p_refs, (qkv_ref, out_ref, up_ref, down_ref, up) = rest[: len(parts)], rest[len(parts) :]

        def put(owner, count, shift, value):
            start = owner * piece + shift
            mat = start // channels
            inner = pl.multiple_of(start - mat * channels, small)

            @pl.when(mat < 3)
            def _():
                qkv_ref[0, jnp.minimum(mat, 2), pl.ds(inner, count)] = value

            @pl.when(mat == 3)
            def _():
                out_ref[0, pl.ds(inner, count)] = value

        if len(parts) == 1:
            for owner in range(total // piece):
                here = slice(owner * piece, (owner + 1) * piece)
                mat = owner * piece // channels
                inner = slice(owner * piece - mat * channels, owner * piece - mat * channels + piece)
                value = p_refs[0][owner, :piece].astype(F32)
                if mat < 3:
                    qkv_ref[0, mat, inner] = value
                else:
                    out_ref[0, inner] = value
                up[here] = p_refs[0][owner, piece : 2 * piece].astype(F32)
                down_ref[0, here] = p_refs[0][owner, 2 * piece :].astype(F32)
        else:
            for core in range(2):
                pa, pb = p_refs[2 * core], p_refs[2 * core + 1]
                for p in range(pa.shape[0]):
                    owner = 2 * (place_ref[2] ^ p) + (place_ref[3] ^ core)
                    start = pl.multiple_of(owner * piece, piece)
                    up[pl.ds(start, piece)] = pa[p, :piece].astype(F32)
                    down_ref[0, pl.ds(start, piece)] = pb[p, :piece].astype(F32)
                    put(owner, small, 0, pa[p, piece:].astype(F32))
                    put(owner, small, small, pb[p, piece:].astype(F32))
        up_ref[0] = up[...].T

    shapes = [
        (layers, 3, channels, width),
        (layers, channels, width),
        (layers, width, hidden),
        (layers, hidden, width),
    ]

    def here(shape):
        return pl.BlockSpec((1,) + shape[1:], lambda i, *_: (layer,) + (0,) * (len(shape) - 1))

    first = len(parts) + 1
    extra = list(previous) if previous is not None else []
    order_in = first + len(extra)
    anywhere = pl.BlockSpec(memory_space=pl.ANY)

    def with_token(*refs):
        ins = refs[: first + len(extra)]
        outs = refs[order_in + 1 : order_in + 5]
        return body(*ins[:first], *outs, *refs[order_in + 6 :])

    aliases = {first + k: k for k in range(len(extra))}
    aliases[order_in] = 4
    *results, order.token = pl.pallas_call(
        with_token,
        grid_spec=pltpu.PrefetchScalarGridSpec(
            num_scalar_prefetch=1,
            grid=(1,),
            in_specs=[whole(part.shape) for part in parts] + [anywhere] * (len(extra) + 1),
            out_specs=[here(shape) for shape in shapes] + [anywhere],
            scratch_shapes=[pltpu.VMEM((total, width), F32)],
        ),
        out_shape=[shape_of(shape, F32) for shape in shapes] + [shape_of(TOKEN, jnp.int32)],
        input_output_aliases=aliases,
        compiler_params=pltpu.CompilerParams(
            dimension_semantics=("arbitrary",), vmem_limit_bytes=VMEM_LIMIT
        ),
        cost_estimate=pl.CostEstimate(flops=0, bytes_accessed=0, transcendentals=0),
        name="finish",
    )(place, *parts, *extra, order.token)
    return results


DP = ("g", "c")


class Order:
    def __init__(self):
        self.token = jnp.zeros(TOKEN, jnp.int32)

    def pin(self, *arrays):
        *arrays, self.token = tie(*arrays, self.token)
        return arrays


class Links:
    def __init__(self, order, dp, mp):
        self.order = order
        self.dp = dp
        self.mp = mp
        bits = [1 << k for k in range(1, dp.bit_length() - 1)]
        self.routes = (bits, bits[::-1])

    def swap(self, value, axis, bit):
        size = self.dp if axis == DP else self.mp
        return lax.ppermute(value, axis, [(i, i ^ bit) for i in range(size)])


class Spread:
    def __init__(self, links, values):
        self.links = links
        self.values = list(values)
        self.phase = 0
        self.have = [[], []]

    def start(self):
        self.values = self.links.order.pin(*self.values)
        self.coming = [
            self.links.swap(value, DP, route[self.phase])
            for value, route in zip(self.values, self.links.routes)
        ]

    def wait(self):
        coming = self.links.order.pin(*self.coming)
        for k in range(2):
            bit = self.links.routes[k][self.phase]
            place = sum(1 for other in self.have[k] if other > bit)
            self.values[k] = jnp.stack([self.values[k], coming[k]], axis=place)
            self.have[k].append(bit)
        self.phase += 1

    def wait_all(self):
        self.wait()
        while self.phase < len(self.links.routes[0]):
            self.start()
            self.wait()

    def start_cores(self):
        self.values = self.links.order.pin(*self.values)
        self.coming = [self.links.swap(value, DP, 1) for value in self.values]

    def wait_cores(self):
        return self.values + self.links.order.pin(*self.coming)


class Gather(Spread):
    def __init__(self, links, piece_a, piece_b):
        super().__init__(links, ())
        self.cut = piece_a.shape[0]
        self.piece = jnp.concatenate([piece_a, piece_b], axis=0)

    def start_mp(self):
        (self.piece,) = self.links.order.pin(self.piece)
        self.coming_mp = [self.links.swap(self.piece, "mp", p) for p in range(1, self.links.mp)]

    def wait_mp(self):
        parts = [self.piece] + self.links.order.pin(*self.coming_mp)
        self.values = [
            jnp.stack([part[: self.cut] for part in parts]),
            jnp.stack([part[self.cut :] for part in parts]),
        ]


class Reduce:
    def __init__(self, links, halves):
        self.links = links
        self.halves = halves
        self.phase = 0

    def start_cores(self):
        others = self.links.order.pin(*self.halves[2:])
        self.coming = [self.links.swap(other, DP, 1) for other in others]

    def wait_cores(self):
        coming = self.links.order.pin(*self.coming)
        mp = self.links.mp
        self.have = [sorted(route, reverse=True) for route in self.links.routes]
        self.values = []
        for own, other in zip(self.halves[:2], coming):
            total = (own.astype(F32) + other.astype(F32)).astype(BF)
            groups = self.links.dp // 2
            rows = total.size // total.shape[-1] // groups // mp
            self.values.append(total.reshape((2,) * len(self.have[0]) + (mp, rows, total.shape[-1])))

    def start(self):
        sends, self.keeps = [], []
        for k in range(2):
            place = self.have[k].index(self.links.routes[1 - k][self.phase])
            self.keeps.append(lax.index_in_dim(self.values[k], 0, place, keepdims=False))
            sends.append(lax.index_in_dim(self.values[k], 1, place, keepdims=False))
        sends = self.links.order.pin(*sends)
        self.coming = [
            self.links.swap(sends[k], DP, self.links.routes[1 - k][self.phase]) for k in range(2)
        ]

    def wait(self):
        coming = self.links.order.pin(*self.coming)
        for k in range(2):
            self.values[k] = (self.keeps[k].astype(F32) + coming[k].astype(F32)).astype(BF)
            self.have[k].remove(self.links.routes[1 - k][self.phase])
        self.phase += 1

    def wait_all(self):
        self.wait()
        while self.phase < len(self.links.routes[0]):
            self.start()
            self.wait()
        return self.values


class ReduceWide:
    def __init__(self, links, grads):
        self.links = links
        (grads,) = links.order.pin(grads.reshape((links.dp,) + grads.shape[2:]))
        self.sums = lax.psum_scatter(grads, DP, scatter_dimension=0, tiled=True)

    def wait(self):
        (sums,) = self.links.order.pin(self.sums)
        return sums.reshape(2, self.links.mp, -1, sums.shape[-1])


class ReduceMp:
    def __init__(self, links, arrays, index):
        self.links = links
        joined = jnp.concatenate(arrays, axis=1)
        if index is None:
            blocks = [joined[p] for p in range(links.mp)]
        else:
            blocks = [
                lax.dynamic_index_in_dim(joined, jnp.bitwise_xor(index, p), 0, keepdims=False)
                for p in range(links.mp)
            ]
        self.kept, *sends = links.order.pin(*blocks)
        self.coming = [links.swap(send, "mp", p + 1) for p, send in enumerate(sends)]

    def wait(self):
        total = self.kept.astype(F32)
        for part in self.links.order.pin(*self.coming):
            total = total + part.astype(F32)
        return total.astype(BF)


def make_shards(dp, mp):
    def shards(
        tokens,
        segments,
        qkv_weight,
        out_weight,
        up_weight,
        down_projection_weight,
        norm_gain,
        norm_bias,
        pos_bias,
        cotangent,
    ):
        seqs, block, width = tokens.shape
        layers = qkv_weight.shape[0]
        window = pos_bias.shape[2]
        channels = qkv_weight.shape[-1]
        hidden = up_weight.shape[-1]
        rows = seqs * block
        group = lax.axis_index("g")
        core = lax.axis_index("c")
        dp_index = group * 2 + core
        mp_index = lax.axis_index("mp")
        order = Order()
        links = Links(order, dp, mp)
        attn_rows = 4 * channels // dp
        ff_rows = hidden // dp
        groups = dp // 2
        per = max(1, width // (mp * ff_rows))
        place = jnp.stack([group // (groups // 4), mp_index, group, core, group // per, group % per]).astype(jnp.int32)

        def picks(count, offset, length):
            return (
                lax.broadcasted_iota(jnp.int32, (count, length), 0) + offset
                == lax.broadcasted_iota(jnp.int32, (count, length), 1)
            ).astype(BF)

        ff_pick = picks(ff_rows, dp_index * ff_rows, hidden)

        def attn_piece(layer):
            by_channel = jnp.transpose(qkv_weight[layer], (0, 2, 1)).reshape(3 * channels, width)
            start = dp_index * attn_rows
            inner = start - 3 * channels
            return jnp.where(
                inner < 0,
                lax.dynamic_slice_in_dim(by_channel, jnp.minimum(start, 3 * channels - attn_rows), attn_rows),
                lax.dynamic_slice_in_dim(out_weight[layer], jnp.maximum(inner, 0), attn_rows),
            )

        def ff_pieces(layer):
            return (
                dot_nt(ff_pick, up_weight[layer]).astype(BF),
                dot_nn(ff_pick, down_projection_weight[layer]).astype(BF),
            )

        def attn_mats(parts):
            return [part.reshape(4, -1, width) for part in parts]

        def ff_mats(parts):
            flat = [part.reshape(-1, width) for part in parts]
            return (flat[0], flat[2]), (flat[1], flat[3])

        def relative(gathered):
            by_dp = jnp.take(gathered, jnp.bitwise_xor(jnp.arange(dp), dp_index), axis=0)
            both = jnp.take(by_dp, jnp.bitwise_xor(jnp.arange(mp), mp_index), axis=1)
            both = both.reshape((dp // 2, 2) + gathered.shape[1:])
            return both[:, 0], both[:, 1]

        def forward_halo(value):
            return lax.ppermute(value, "mp", [(i, i + 1) for i in range(mp - 1)])

        def backward_halo(value):
            return lax.ppermute(value, "mp", [(i + 1, i) for i in range(mp - 1)])

        gains = norm_gain.reshape(layers, 2, 1, width)
        shifts = norm_bias.reshape(layers, 2, 1, width)
        middle = attn_rows // 2
        in_blocks = middle % 16 == 0

        piece = attn_piece(0)
        attn0 = Gather(links, piece[:middle], piece[middle:])
        attn0.start_mp()
        (later,) = order.pin(jnp.concatenate((attn_piece(1),) + ff_pieces(1), axis=0))
        later = lax.all_gather(later, ("g", "c", "mp"), axis=0, tiled=False)
        ff0 = Gather(links, *ff_pieces(0))
        ff0.start_mp()
        x, normed = enter_kernel(order, tokens.reshape(rows, width), gains[0, 0], shifts[0, 0])

        seg_pad = jnp.concatenate([jnp.full((seqs, window), -1, segments.dtype), segments], axis=1)
        seg_keys = lax.dynamic_slice_in_dim(seg_pad, mp_index * block, block + window, axis=1)
        seg_q = seg_keys[:, window:].reshape(seqs, block, 1)
        seg_k = seg_keys.reshape(seqs, 1, block + window)

        attn0.wait_mp()
        attn0.start()
        attn0.wait()
        attn0.start()
        ff0.wait_mp()
        ff0.start()
        (normed,) = order.pin(normed)
        halo = forward_halo(normed)
        attn0.wait_all()
        attn0.start_cores()
        ff0.wait()
        ff0.start()
        w_attn0 = attn_mats(attn0.wait_cores())
        (halo,) = order.pin(halo)

        def attn(layer, x, normed, halo, w_attn):
            sg, ratio, rden, v, wsum, carried, mixed, masked, x1, normed_b = attn_forward(
                order, layer, place, x, normed, halo, w_attn, pos_bias, seg_q, seg_k,
                gains[layer, 1], shifts[layer, 1],
            )
            return x1, normed_b, (sg, ratio, rden, v, wsum, carried, masked), (mixed, normed, halo)

        x1_0, normed_b0, saved0, rows0 = attn(0, x, normed, halo, w_attn0)
        ff0.wait_all()
        ff0.start_cores()
        ups0, downs0 = ff_mats(ff0.wait_cores())
        act0, slope0, x2, normed2 = ff_forward(
            order, x1_0, normed_b0, ups0, downs0, gains[1, 0], shifts[1, 0]
        )
        (normed2,) = order.pin(normed2)
        halo2 = forward_halo(normed2)
        (later,) = order.pin(later)
        if in_blocks:
            w_attn1 = w_ff1 = [later.reshape((groups, 2, mp) + later.shape[1:])]
        else:
            own, other = relative(later.reshape((dp, mp) + later.shape[1:]))
            cuts = [middle, attn_rows, attn_rows + ff_rows]
            own_a, own_b, own_up, own_down = jnp.split(own, cuts, axis=2)
            other_a, other_b, other_up, other_down = jnp.split(other, cuts, axis=2)
            w_attn1 = attn_mats([own_a, own_b, other_a, other_b])
            w_ff1 = sum(ff_mats([own_up, own_down, other_up, other_down]), ())
        (halo2,) = order.pin(halo2)
        x1_1, normed_b1, saved1, rows1 = attn(1, x2, normed2, halo2, w_attn1)

        def ff_back(layer, x1, normed_b, weights, grad, saved):
            grads, *rest = ff_backward(
                order, place, x1, normed_b, weights, groups, grad, gains[layer, 1], saved
            )
            return grads, rest

        ff_grads1, (grad1, grad1_low, gain_b1, shift_b1, output) = ff_back(
            1, x1_1, normed_b1, w_ff1, cotangent.reshape(rows, width), None
        )
        wide1 = ReduceWide(links, ff_grads1)
        gq, gk, gv, band1, dn_own1, back1 = attn_backward(order, place, grad1_low, w_attn1, *saved1)
        (back1,) = order.pin(back1)
        back1 = backward_halo(back1)
        r_attn1 = Reduce(
            links, attn_weight_grads(order, place, gq, gk, gv, *rows1, grad1_low, mp, in_blocks)
        )
        (back1,) = order.pin(back1)
        r_attn1.start_cores()
        grad2, gain_a1, shift_a1 = leave_attn(order, x2, grad1, dn_own1, back1, gains[1, 0])
        r_attn1.wait_cores()
        r_attn1.start()
        ff_grads0, (grad3, grad3_low, gain_b0, shift_b0) = ff_back(
            0, x1_0, normed_b0, ups0 + downs0, grad2, (act0, slope0)
        )
        r_attn1.wait()
        wide0 = ReduceWide(links, ff_grads0)
        r_attn1.start()
        up1, down1 = wide1.wait()
        attn1_sum = r_attn1.wait_all()
        mp1 = ReduceMp(links, attn1_sum + [up1, down1], mp_index if in_blocks else None)
        gq, gk, gv, band0, dn_own0, back0 = attn_backward(order, place, grad3_low, w_attn0, *saved0)
        r_attn0 = Reduce(
            links, attn_weight_grads(order, place, gq, gk, gv, *rows0, grad3_low, mp, False)
        )
        sum1 = mp1.wait()
        r_attn0.start_cores()
        (back0,) = order.pin(back0)
        back0 = backward_halo(back0)
        (sum1,) = order.pin(sum1)
        full1 = lax.all_gather(sum1, DP, axis=0, tiled=False)
        r_attn0.wait_cores()
        r_attn0.start()
        (back0,) = order.pin(back0)
        grad4, gain_a0, shift_a0 = leave_attn(order, x, grad3, dn_own0, back0, gains[0, 0])
        norms = jnp.concatenate(
            [gain_a0, gain_b0, shift_a0, shift_b0, gain_a1, gain_b1, shift_a1, shift_b1], axis=0
        ).reshape(-1, window)
        small = jnp.concatenate([band0, band1, norms], axis=0).astype(BF)

        def small_start(bit):
            (here,) = order.pin(small)
            return here, links.swap(here, DP, bit)

        def small_wait(pair):
            (coming,) = order.pin(pair[1])
            return (pair[0].astype(F32) + coming.astype(F32)).astype(BF)

        bits = [1 << k for k in range(dp.bit_length() - 1)]
        r_attn0.wait()
        r_attn0.start()
        pair = small_start(bits[0])
        attn0_sum = r_attn0.wait_all()
        small = small_wait(pair)
        up0, down0 = wide0.wait()
        mp0 = ReduceMp(links, attn0_sum + [up0, down0], None)
        for bit in bits[1:]:
            small = small_wait(small_start(bit))
        (small,) = order.pin(small)
        small_parts = [links.swap(small, "mp", p) for p in range(1, mp)]
        (full1,) = order.pin(full1)

        def finish(layer, full, previous):
            if in_blocks:
                return finish_layer(order, layer, layers, place, full, channels, hidden, attn_rows, previous)
            if len(full) == 1:
                owner = jnp.arange(dp)
                attn_part, up_part, down_part = jnp.split(full[0], [attn_rows, attn_rows + ff_rows], axis=1)
            else:
                owner = jnp.bitwise_xor(jnp.arange(dp), dp_index)
                part_a, part_b = [
                    jnp.stack([full[k], full[2 + k]], axis=1).reshape(dp, -1, width) for k in range(2)
                ]
                attn_part = jnp.concatenate([part_a[:, ff_rows:], part_b[:, ff_rows:]], axis=1)
                up_part, down_part = part_a[:, :ff_rows], part_b[:, :ff_rows]

            def rows_of(value):
                return value.reshape(-1, width)

            def place_of(count):
                spots = (owner[:, None] * count + jnp.arange(count)[None, :]).reshape(-1, 1)
                return (spots == jnp.arange(dp * count)[None, :]).astype(BF)

            attn_place = place_of(attn_rows).reshape(-1, 4, channels)
            ff_place = place_of(ff_rows)
            values = (
                jnp.einsum("pd,pmc->mcd", rows_of(attn_part), attn_place[:, :3], preferred_element_type=F32),
                dot_tn(attn_place[:, 3], rows_of(attn_part)),
                dot_tn(rows_of(up_part), ff_place),
                dot_tn(ff_place, rows_of(down_part)),
            )
            if previous is None:
                previous = [jnp.zeros((layers,) + value.shape, F32) for value in values]
            return [
                lax.dynamic_update_index_in_dim(kept, value, layer, 0)
                for kept, value in zip(previous, values)
            ]

        big = finish(1, [full1], None)
        sum0 = mp0.wait()
        spread0 = Spread(
            links,
            [
                jnp.concatenate([sum0[attn_rows : attn_rows + ff_rows], sum0[:middle]], axis=0),
                jnp.concatenate([sum0[attn_rows + ff_rows :], sum0[middle:attn_rows]], axis=0),
            ],
        )
        spread0.start()
        small_parts = [small] + order.pin(*small_parts)
        spread0.wait()
        spread0.start()
        small_all = jnp.stack(small_parts)
        pairs = small_all[:, 2 * block :].astype(F32)
        while pairs.shape[0] > 1:
            pairs = pairs[0::2] + pairs[1::2]
        norm_sum = pairs[0].reshape(layers, 4, width)
        bands = jnp.take(
            small_all[:, : 2 * block].astype(F32), jnp.bitwise_xor(jnp.arange(mp), mp_index), axis=0
        ).reshape(mp, layers, block, window)
        band_sum = jnp.transpose(bands, (1, 0, 2, 3)).reshape(layers, mp * block, window)
        spread0.wait_all()
        spread0.start_cores()
        full0 = [part.reshape(groups, -1, width) for part in spread0.wait_cores()]
        qkv_out, out_out, up_out, down_out = finish(0, full0, big)
        return (
            output.reshape(tokens.shape),
            grad4.reshape(tokens.shape),
            jnp.transpose(qkv_out, (0, 1, 3, 2)),
            out_out,
            up_out,
            down_out,
            norm_sum[:, :2],
            norm_sum[:, 2:],
            band_sum,
        )

    return shards


def solution(mesh):
    dp, mp = mesh.shape["dp"], mesh.shape["mp"]
    inner = Mesh(mesh.devices.reshape(dp // 2, 2, mp), DP + ("mp",))
    placed = (
        P(DP, "mp", None),
        P(DP, None),
        P(None, None, None, "mp"),
        P(None, "mp", None),
        P(None, None, "mp"),
        P(None, "mp", None),
        P(),
        P(),
        P(),
        P(DP, "mp", None),
    )
    return jax.shard_map(
        make_shards(dp, mp),
        mesh=inner,
        in_specs=placed,
        out_specs=(
            P(DP, "mp", None),
            P(DP, "mp", None),
            P(None, None, None, "mp"),
            P(None, "mp", None),
            P(None, None, "mp"),
            P(None, "mp", None),
            P(),
            P(),
            P(),
        ),
        check_vma=False,
    )
```

```python
import functools

import jax
import jax.numpy as jnp
from jax import lax
from jax.experimental import pallas as pl
from jax.experimental.pallas import tpu as pltpu
from jax.sharding import Mesh, PartitionSpec as P

BF = jnp.bfloat16
F32 = jnp.float32
VMEM_LIMIT = 58 * 1024 * 1024
TOKEN = (8, 128)
GELU_A = 0.7978845608028654
GELU_B = 0.044715


def dot_nt(lhs, rhs):
    return lax.dot_general(lhs, rhs, (((1,), (1,)), ((), ())), preferred_element_type=F32)


def dot_nn(lhs, rhs):
    return lax.dot_general(lhs, rhs, (((1,), (0,)), ((), ())), preferred_element_type=F32)


def dot_tn(lhs, rhs):
    return lax.dot_general(lhs, rhs, (((0,), (0,)), ((), ())), preferred_element_type=F32)


def normalize(values):
    center = values - jnp.mean(values, axis=-1, keepdims=True)
    inv_std = lax.rsqrt(jnp.mean(center * center, axis=-1, keepdims=True) + 1e-05)
    return center * inv_std, inv_std


def norm_back(grad_out, normal, inv_std, gain):
    grad_normal = grad_out * gain
    mean_one = jnp.mean(grad_normal, axis=-1, keepdims=True)
    mean_two = jnp.mean(grad_normal * normal, axis=-1, keepdims=True)
    return inv_std * (grad_normal - mean_one - normal * mean_two)


def whole(shape):
    return pl.BlockSpec(shape, lambda *_: (0,) * len(shape))


def call(order, body, grid, in_specs, out_specs, out_shape, scratch=(), prefetch=0, name=None):
    first = prefetch + len(in_specs)
    second = first + 1 + len(out_specs)
    anywhere = pl.BlockSpec(memory_space=pl.ANY)

    def with_token(*refs):
        return body(*refs[:first], *refs[first + 1 : second], *refs[second + 1 :])

    kernel = pl.pallas_call(
        with_token,
        grid_spec=pltpu.PrefetchScalarGridSpec(
            num_scalar_prefetch=prefetch,
            grid=grid,
            in_specs=list(in_specs) + [anywhere],
            out_specs=list(out_specs) + [anywhere],
            scratch_shapes=list(scratch),
        ),
        out_shape=list(out_shape) + [shape_of(TOKEN, jnp.int32)],
        input_output_aliases={first: len(out_specs)},
        compiler_params=pltpu.CompilerParams(
            dimension_semantics=("arbitrary",) * len(grid), vmem_limit_bytes=VMEM_LIMIT
        ),
        cost_estimate=pl.CostEstimate(flops=0, bytes_accessed=0, transcendentals=0),
        name=name,
    )

    def run(*operands):
        *results, order.token = kernel(*operands, order.token)
        return results

    return run


def shape_of(shape, dtype):
    return jax.ShapeDtypeStruct(shape, dtype)


def tie(*arrays):
    count = len(arrays)
    return pl.pallas_call(
        lambda *refs: None,
        out_shape=[shape_of(a.shape, a.dtype) for a in arrays],
        in_specs=[pl.BlockSpec(memory_space=pl.ANY)] * count,
        out_specs=[pl.BlockSpec(memory_space=pl.ANY)] * count,
        input_output_aliases={i: i for i in range(count)},
        cost_estimate=pl.CostEstimate(flops=0, bytes_accessed=0, transcendentals=0),
        name="tie",
    )(*arrays)


def enter_kernel(order, tokens, gain, shift):
    rows, width = tokens.shape

    def body(t_ref, g_ref, s_ref, x_ref, n_ref):
        x = t_ref[...].astype(F32)
        x_ref[...] = x
        normal, _ = normalize(x)
        n_ref[...] = (normal * g_ref[...] + s_ref[...]).astype(BF)

    return call(
        order,
        body,
        (1,),
        [whole((rows, width)), whole((1, width)), whole((1, width))],
        [whole((rows, width)), whole((rows, width))],
        [shape_of((rows, width), F32), shape_of((rows, width), BF)],
        name="enter",
    )(tokens, gain, shift)


def reverse_lanes(values):
    count = values.shape[1]
    flip = (
        lax.broadcasted_iota(jnp.int32, (count, count), 0)
        + lax.broadcasted_iota(jnp.int32, (count, count), 1)
        == count - 1
    ).astype(BF)
    high = values.astype(BF)
    rest = values - high.astype(F32)
    middle = rest.astype(BF)
    last = (rest - middle.astype(F32)).astype(BF)
    return (dot_nn(high, flip) + dot_nn(middle, flip)) + dot_nn(last, flip)


def attn_specs(weights):
    if len(weights) == 4:
        return [whole(w.shape) for w in weights]
    groups, _, mp, count, width = weights[0].shape
    return [pl.BlockSpec((groups, 1, mp, count // 3, width), lambda i, place: (0, place[3] ^ i, 0, 0, 0))]


def by_half(step, refs, place_ref, part):
    if len(refs) == 1:
        width = refs[0].shape[-1]
        part(lambda m: refs[0][m, 0].reshape(-1, width))
        return
    for half in range(2):
        wa, wb = refs[2 * half], refs[2 * half + 1]

        def mat(m, wa=wa, wb=wb):
            return jnp.concatenate([wa[place_ref[0] ^ m], wb[place_ref[0] ^ m]], axis=0)

        pl.when(step == half)(functools.partial(part, mat))


def attn_forward(order, layer, place, x, normed, halo, weights, pos_bias, seg_q, seg_k, gain, shift):
    rows, width = x.shape
    seqs, block, _ = seg_q.shape
    keys = seg_k.shape[2]
    window = keys - block
    half = width // 2

    def body(place_ref, x_ref, n_ref, h_ref, *rest):
        w_refs, rest = rest[: len(weights)], rest[len(weights) :]
        (band_ref, sq_ref, sk_ref, g_ref, s_ref, sg_ref, ratio_ref, rden_ref, v_ref, wsum_ref, car_ref, mixed_ref,
         masked_ref, x1_ref, nb_ref, mix) = rest
        step = pl.program_id(0)

        @pl.when(step == 0)
        def _():
            band = reverse_lanes(jnp.exp(band_ref[0]))
            band = jnp.concatenate([band, jnp.zeros((block, block), F32)], axis=1)
            spread = pltpu.roll(band, 1, axis=1, stride=1, stride_axis=0)
            for s in range(seqs):
                masked = jnp.where(sq_ref[s] == sk_ref[s], spread, 0.0)
                masked_ref[s] = masked
                mix[s] = masked.astype(BF)
            x1_ref[...] = x_ref[...]

        def part(mat):
            wq, wk, wv = mat(0), mat(1), mat(2)
            q = dot_nt(n_ref[...], wq)
            sg = jax.nn.sigmoid(q)
            sg_ref[...] = sg.astype(BF)
            carried, wsum = [], []
            for r, source in enumerate((h_ref, n_ref)):
                here = slice(r * rows, (r + 1) * rows)
                kexp = jnp.exp(dot_nt(source[...], wk))
                v = dot_nt(source[...], wv)
                v_ref[here] = v.astype(BF)
                wsum.append(kexp.astype(BF))
                carried.append((kexp * v).astype(BF))
                wsum_ref[here] = wsum[r]
                car_ref[here] = carried[r]
            mixed = []
            for s in range(seqs):
                here = slice(s * block, (s + 1) * block)
                num = dot_nn(mix[s, :, :window], carried[0][here]) + dot_nn(mix[s, :, window:], carried[1][here])
                den = dot_nn(mix[s, :, :window], wsum[0][here]) + dot_nn(mix[s, :, window:], wsum[1][here])
                rden = 1.0 / den
                ratio = num * rden
                rden_ref[here] = rden.astype(BF)
                ratio_ref[here] = ratio.astype(BF)
                mixed.append((sg[here] * ratio).astype(BF))
            mixed = jnp.concatenate(mixed, axis=0)
            mixed_ref[...] = mixed
            x1_ref[...] += dot_nn(mixed, mat(3))

        by_half(step, w_refs, place_ref, part)

        @pl.when(step == 1)
        def _():
            normal, _ = normalize(x1_ref[...])
            nb_ref[...] = (normal * g_ref[...] + s_ref[...]).astype(BF)

    def col(n):
        return pl.BlockSpec((n, half), lambda i, *_: (0, i))

    return call(
        order,
        body,
        (2,),
        [whole((rows, width))] * 3
        + attn_specs(weights)
        + [pl.BlockSpec((1, block, window), lambda i, place: (layer, place[1], 0))]
        + [whole((seqs, block, 1)), whole((seqs, 1, keys)), whole((1, width)), whole((1, width))],
        [col(rows)] * 3 + [col(2 * rows)] * 3 + [col(rows)]
        + [whole((seqs, block, keys)), whole((rows, width)), whole((rows, width))],
        [shape_of((rows, width), BF)] * 3
        + [shape_of((2 * rows, width), BF)] * 3
        + [
            shape_of((rows, width), BF),
            shape_of((seqs, block, keys), F32),
            shape_of((rows, width), F32),
            shape_of((rows, width), BF),
        ],
        [pltpu.VMEM((seqs, block, keys), BF)],
        prefetch=1,
        name="attn_fwd",
    )(place, x, normed, halo, *weights, pos_bias, seg_q, seg_k, gain, shift)


def gelu_both(pre):
    square = pre * pre
    upper = 0.5 + 0.5 * jnp.tanh(pre * (GELU_A + (GELU_A * GELU_B) * square))
    act = pre * upper
    return act, upper + act * (1.0 - upper) * (2.0 * GELU_A + (6.0 * GELU_A * GELU_B) * square)


def chunk_specs(chunk, width, per_half):
    own = pl.BlockSpec((chunk, width), lambda i, *_: (jnp.minimum(i, per_half - 1), 0))
    other = pl.BlockSpec((chunk, width), lambda i, *_: (jnp.maximum(i - per_half, 0), 0))
    return own, other


def ff_forward(order, x1, normed, ups, downs, gain, shift):
    rows, width = x1.shape
    half = ups[0].shape[0]
    per_half = 2
    chunk = half // per_half
    steps = 2 * per_half

    def body(x_ref, n_ref, u0, u1, d0, d1, g_ref, s_ref, act_ref, slope_ref, x2_ref, next_ref):
        step = pl.program_id(0)

        @pl.when(step == 0)
        def _():
            x2_ref[...] = x_ref[...]

        def part(u, d):
            act, slope = gelu_both(dot_nt(n_ref[...], u[...]))
            act = act.astype(BF)
            act_ref[...] = act
            slope_ref[...] = slope.astype(BF)
            x2_ref[...] += dot_nn(act, d[...])

        pl.when(step < per_half)(lambda: part(u0, d0))
        pl.when(step >= per_half)(lambda: part(u1, d1))

        @pl.when(step == steps - 1)
        def _():
            normal, _ = normalize(x2_ref[...])
            next_ref[...] = (normal * g_ref[...] + s_ref[...]).astype(BF)

    own, other = chunk_specs(chunk, width, per_half)
    col = pl.BlockSpec((rows, chunk), lambda i: (0, i))
    return call(
        order,
        body,
        (steps,),
        [whole((rows, width))] * 2 + [own, other, own, other] + [whole((1, width))] * 2,
        [col, col, whole((rows, width)), whole((rows, width))],
        [
            shape_of((rows, 2 * half), BF),
            shape_of((rows, 2 * half), BF),
            shape_of((rows, width), F32),
            shape_of((rows, width), BF),
        ],
        name="ff_fwd",
    )(x1, normed, *ups, *downs, gain, shift)


def ff_specs(weights, chunk):
    if len(weights) == 4:
        half, width = weights[0].shape
        own, other = chunk_specs(chunk, width, half // chunk)
        return list(weights), [own, other, own, other]
    groups, _, mp, count, width = weights[0].shape
    rows = count // 3
    per = chunk // (mp * rows)
    steps = groups // per

    def spec(which):
        return pl.BlockSpec(
            (per, 1, mp, rows, width), lambda i, place: (i % steps, place[3] ^ (i // steps), 0, which, 0)
        )

    return [weights[0], weights[0]], [spec(1), spec(2)]


def ff_backward(order, place, x1, normed, weights, groups, grad, gain, saved):
    rows, width = x1.shape
    chunk = width
    half = 2 * width
    per_half = half // chunk
    steps = 2 * per_half
    operands, w_specs = ff_specs(weights, chunk)
    group_rows = half // groups
    per = chunk // group_rows
    fresh = saved is None
    relative = len(weights) == 4

    def body(place_ref, x_ref, n_ref, *rest):
        rest = list(rest)
        w_refs = [rest.pop(0) for _ in operands]
        grad_ref, g_ref = rest.pop(0), rest.pop(0)
        act_ref, slope_ref = (None, None) if fresh else (rest.pop(0), rest.pop(0))
        wg_ref, g1_ref, ga_ref, gg_ref, gs_ref = rest[:5]
        out_ref, (low, dn, x2) = (rest[5], rest[6:]) if fresh else (None, (rest[5], rest[6], None))
        step = pl.program_id(0)

        @pl.when(step == 0)
        def _():
            low[...] = grad_ref[...].astype(BF)
            dn[...] = jnp.zeros_like(dn)
            if fresh:
                x2[...] = x_ref[...]

        def part(u_ref, d_ref):
            u = u_ref[...].reshape(chunk, width)
            d = d_ref[...].reshape(chunk, width)
            if fresh:
                act, slope = gelu_both(dot_nt(n_ref[...], u))
                act = act.astype(BF)
                x2[...] += dot_nn(act, d)
            else:
                act, slope = act_ref[...], slope_ref[...].astype(F32)
            pre_grad = (dot_nt(low[...], d) * slope).astype(BF)
            dn[...] += dot_nn(pre_grad, u)
            for which, value in ((0, dot_tn(pre_grad, n_ref[...])), (1, dot_tn(act, low[...]))):
                value = value.astype(BF)
                for k in range(per):
                    spot = (place_ref[5] ^ k) if relative else k
                    wg_ref[spot, 0, which] = value[k * group_rows : (k + 1) * group_rows]

        if relative:
            pl.when(step < per_half)(lambda: part(w_refs[0], w_refs[2]))
            pl.when(step >= per_half)(lambda: part(w_refs[1], w_refs[3]))
        else:
            part(*w_refs)

        @pl.when(step == steps - 1)
        def _():
            if fresh:
                out_ref[...] = x2[...].astype(BF)
            normal, inv = normalize(x_ref[...])
            total = dn[...]
            g1 = grad_ref[...] + norm_back(total, normal, inv, g_ref[...])
            g1_ref[...] = g1
            ga_ref[...] = g1.astype(BF)
            gg_ref[...] = jnp.sum(total * normal, axis=0, keepdims=True)
            gs_ref[...] = jnp.sum(total, axis=0, keepdims=True)

    full = whole((rows, width))
    col = pl.BlockSpec((rows, chunk), lambda i, *_: (0, i))
    wg = pl.BlockSpec(
        (per, 1, 2, group_rows, width),
        lambda i, place: (
            (place[4] ^ (i % per_half)) if relative else i % per_half, place[3] ^ (i // per_half), 0, 0, 0,
        ),
    )
    return call(
        order,
        body,
        (steps,),
        [full, full] + w_specs + [full, whole((1, width))] + ([] if fresh else [col, col]),
        [wg, full, full, whole((1, width)), whole((1, width))] + ([full] if fresh else []),
        [
            shape_of((groups, 2, 2, group_rows, width), BF),
            shape_of((rows, width), F32),
            shape_of((rows, width), BF),
            shape_of((1, width), F32),
            shape_of((1, width), F32),
        ]
        + ([shape_of((rows, width), BF)] if fresh else []),
        [pltpu.VMEM((rows, width), BF), pltpu.VMEM((rows, width), F32)]
        + ([pltpu.VMEM((rows, width), F32)] if fresh else []),
        prefetch=1,
        name="ff_bwd",
    )(place, x1, normed, *operands, grad, gain, *(() if fresh else saved))


def attn_backward(order, place, grad_low, weights, sg, ratio, rden, v, wsum, carried, masked):
    rows, width = grad_low.shape
    seqs, block, keys = masked.shape
    window = keys - block
    half = width // 2

    def body(place_ref, ga_ref, *rest):
        w_refs, rest = rest[: len(weights)], rest[len(weights) :]
        (sg_ref, ratio_ref, rden_ref, v_ref, wsum_ref, car_ref, masked_ref,
         gq_ref, gk_ref, gv_ref, band_ref, own_ref, halo_ref, mix_t, wgrad, dn) = rest
        step = pl.program_id(0)

        @pl.when(step == 0)
        def _():
            for s in range(seqs):
                mix_t[s] = masked_ref[s].T.astype(BF)
            wgrad[...] = jnp.zeros_like(wgrad)
            dn[...] = jnp.zeros_like(dn)

        def part(mat):
            gm = dot_nt(ga_ref[...], mat(3))
            sig = sg_ref[...].astype(F32)
            rat = ratio_ref[...].astype(F32)
            scaled = gm * sig
            gq = (scaled * rat * (1.0 - sig)).astype(BF)
            gq_ref[...] = gq
            gnum_f = scaled * rden_ref[...].astype(F32)
            gnum = gnum_f.astype(BF)
            gden = (-gnum_f * rat).astype(BF)
            wq, wk, wv = mat(0), mat(1), mat(2)
            dn[rows:] += dot_nn(gq, wq)
            for r in range(2):
                for s in range(seqs):
                    here = slice(s * block, (s + 1) * block)
                    there = slice(r * rows + s * block, r * rows + (s + 1) * block)
                    cols = slice(r * window, r * window + block)
                    ke = wsum_ref[there].astype(F32)
                    gcar = dot_nn(mix_t[s, cols], gnum[here])
                    gsum = dot_nn(mix_t[s, cols], gden[here])
                    gv = (gcar * ke).astype(BF)
                    gk = ((gcar * v_ref[there].astype(F32) + gsum) * ke).astype(BF)
                    gk_ref[there] = gk
                    gv_ref[there] = gv
                    wgrad[s, :, cols] += dot_nt(gnum[here], car_ref[there]) + dot_nt(gden[here], wsum_ref[there])
                    dn[there] += dot_nn(gk, wk) + dot_nn(gv, wv)

        by_half(step, w_refs, place_ref, part)

        @pl.when(step == 1)
        def _():
            total = wgrad[0] * masked_ref[0]
            for s in range(1, seqs):
                total = total + wgrad[s] * masked_ref[s]
            lane_row = lax.broadcasted_iota(jnp.int32, (block, keys), 0) + 1
            bit = 1
            while bit <= block:
                rolled = pltpu.roll(total, keys - bit, axis=1)
                total = jnp.where((lane_row & bit) != 0, rolled, total)
                bit *= 2
            band_ref[...] = reverse_lanes(total[:, :window])
            halo_ref[...] = dn[:rows].astype(BF)
            own_ref[...] = dn[rows:]

    def col(n):
        return pl.BlockSpec((n, half), lambda i, *_: (0, i))

    return call(
        order,
        body,
        (2,),
        [whole((rows, width))]
        + attn_specs(weights)
        + [col(rows)] * 3 + [col(2 * rows)] * 3 + [whole((seqs, block, keys))],
        [col(rows), col(2 * rows), col(2 * rows), whole((block, window)), whole((rows, width)), whole((rows, width))],
        [
            shape_of((rows, width), BF),
            shape_of((2 * rows, width), BF),
            shape_of((2 * rows, width), BF),
            shape_of((block, window), F32),
            shape_of((rows, width), F32),
            shape_of((rows, width), BF),
        ],
        [
            pltpu.VMEM((seqs, keys, block), BF),
            pltpu.VMEM((seqs, block, keys), F32),
            pltpu.VMEM((2 * rows, width), F32),
        ],
        prefetch=1,
        name="attn_bwd",
    )(place, grad_low, *weights, sg, ratio, rden, v, wsum, carried, masked)


def attn_weight_grads(order, place, gq, gk, gv, mixed, normed, halo, grad_low, mp, mixed_rows):
    rows, width = gq.shape
    half = width // 2
    quarter = half // 2

    def body(place_ref, gq_ref, gk_ref, gv_ref, mixed_ref, n_ref, h_ref, ga_ref, oa, ob, ta, tb):
        step = pl.program_id(0)
        mat = lax.rem(step, 4)

        def store(value):
            low = value.astype(BF)

            def put(a_ref, b_ref):
                if not mixed_rows:
                    a_ref[0] = low[:quarter]
                    b_ref[0] = low[quarter:]
                    return
                piece = quarter // mp
                for z in range(mp):
                    a_ref[0, z * piece : (z + 1) * piece] = low[2 * z * piece : (2 * z + 1) * piece]
                    b_ref[0, z * piece : (z + 1) * piece] = low[(2 * z + 1) * piece : (2 * z + 2) * piece]

            pl.when(step < 4)(lambda: put(oa, ob))
            pl.when(step >= 4)(lambda: put(ta, tb))

        def keys_grad(ref):
            return dot_tn(ref[:rows], h_ref[...]) + dot_tn(ref[rows:], n_ref[...])

        pl.when(mat == 0)(lambda: store(dot_tn(gq_ref[...], n_ref[...])))
        pl.when(mat == 1)(lambda: store(keys_grad(gk_ref)))
        pl.when(mat == 2)(lambda: store(keys_grad(gv_ref)))
        pl.when(mat == 3)(lambda: store(dot_tn(mixed_ref[...], ga_ref[...])))

    def col(n):
        return pl.BlockSpec((n, half), lambda i, *_: (0, i // 4))

    own = pl.BlockSpec((1, quarter, width), lambda i, t: (jnp.minimum(i, 3) ^ t[0], 0, 0))
    other = pl.BlockSpec((1, quarter, width), lambda i, t: (jnp.maximum(i - 4, 0) ^ t[0], 0, 0))
    return call(
        order,
        body,
        (8,),
        [col(rows), col(2 * rows), col(2 * rows), col(rows)] + [whole((rows, width))] * 3,
        [own, own, other, other],
        [shape_of((4, quarter, width), BF)] * 4,
        prefetch=1,
        name="attn_wgrad",
    )(place, gq, gk, gv, mixed, normed, halo, grad_low)


def leave_attn(order, x, grad, own, back, gain):
    rows, width = x.shape

    def body(x_ref, g_ref, o_ref, b_ref, gain_ref, out_ref, gg_ref, gs_ref):
        normal, inv = normalize(x_ref[...])
        total = o_ref[...] + b_ref[...].astype(F32)
        out_ref[...] = g_ref[...] + norm_back(total, normal, inv, gain_ref[...])
        gg_ref[...] = jnp.sum(total * normal, axis=0, keepdims=True)
        gs_ref[...] = jnp.sum(total, axis=0, keepdims=True)

    return call(
        order,
        body,
        (1,),
        [whole((rows, width))] * 4 + [whole((1, width))],
        [whole((rows, width)), whole((1, width)), whole((1, width))],
        [shape_of((rows, width), F32)] + [shape_of((1, width), F32)] * 2,
        name="leave",
    )(x, grad, own, back, gain)


def finish_layer(order, layer, layers, place, parts, channels, hidden, mp_rows, previous):
    width = parts[0].shape[-1]
    piece = mp_rows
    small = piece // 2
    total = 4 * channels

    def body(place_ref, *rest):
        p_refs, (qkv_ref, out_ref, up_ref, down_ref, up) = rest[: len(parts)], rest[len(parts) :]

        def put(owner, count, shift, value):
            start = owner * piece + shift
            mat = start // channels
            inner = pl.multiple_of(start - mat * channels, small)

            @pl.when(mat < 3)
            def _():
                qkv_ref[0, jnp.minimum(mat, 2), pl.ds(inner, count)] = value

            @pl.when(mat == 3)
            def _():
                out_ref[0, pl.ds(inner, count)] = value

        if len(parts) == 1:
            for owner in range(total // piece):
                here = slice(owner * piece, (owner + 1) * piece)
                mat = owner * piece // channels
                inner = slice(owner * piece - mat * channels, owner * piece - mat * channels + piece)
                value = p_refs[0][owner, :piece].astype(F32)
                if mat < 3:
                    qkv_ref[0, mat, inner] = value
                else:
                    out_ref[0, inner] = value
                up[here] = p_refs[0][owner, piece : 2 * piece].astype(F32)
                down_ref[0, here] = p_refs[0][owner, 2 * piece :].astype(F32)
        else:
            for core in range(2):
                pa, pb = p_refs[2 * core], p_refs[2 * core + 1]
                for p in range(pa.shape[0]):
                    owner = 2 * (place_ref[2] ^ p) + (place_ref[3] ^ core)
                    start = pl.multiple_of(owner * piece, piece)
                    up[pl.ds(start, piece)] = pa[p, :piece].astype(F32)
                    down_ref[0, pl.ds(start, piece)] = pb[p, :piece].astype(F32)
                    put(owner, small, 0, pa[p, piece:].astype(F32))
                    put(owner, small, small, pb[p, piece:].astype(F32))
        up_ref[0] = up[...].T

    shapes = [
        (layers, 3, channels, width),
        (layers, channels, width),
        (layers, width, hidden),
        (layers, hidden, width),
    ]

    def here(shape):
        return pl.BlockSpec((1,) + shape[1:], lambda i, *_: (layer,) + (0,) * (len(shape) - 1))

    first = len(parts) + 1
    extra = list(previous) if previous is not None else []
    order_in = first + len(extra)
    anywhere = pl.BlockSpec(memory_space=pl.ANY)

    def with_token(*refs):
        ins = refs[: first + len(extra)]
        outs = refs[order_in + 1 : order_in + 5]
        return body(*ins[:first], *outs, *refs[order_in + 6 :])

    aliases = {first + k: k for k in range(len(extra))}
    aliases[order_in] = 4
    *results, order.token = pl.pallas_call(
        with_token,
        grid_spec=pltpu.PrefetchScalarGridSpec(
            num_scalar_prefetch=1,
            grid=(1,),
            in_specs=[whole(part.shape) for part in parts] + [anywhere] * (len(extra) + 1),
            out_specs=[here(shape) for shape in shapes] + [anywhere],
            scratch_shapes=[pltpu.VMEM((total, width), F32)],
        ),
        out_shape=[shape_of(shape, F32) for shape in shapes] + [shape_of(TOKEN, jnp.int32)],
        input_output_aliases=aliases,
        compiler_params=pltpu.CompilerParams(
            dimension_semantics=("arbitrary",), vmem_limit_bytes=VMEM_LIMIT
        ),
        cost_estimate=pl.CostEstimate(flops=0, bytes_accessed=0, transcendentals=0),
        name="finish",
    )(place, *parts, *extra, order.token)
    return results


DP = ("g", "c")


class Order:
    def __init__(self):
        self.token = jnp.zeros(TOKEN, jnp.int32)

    def pin(self, *arrays):
        *arrays, self.token = tie(*arrays, self.token)
        return arrays


class Links:
    def __init__(self, order, dp, mp):
        self.order = order
        self.dp = dp
        self.mp = mp
        bits = [1 << k for k in range(1, dp.bit_length() - 1)]
        self.routes = (bits, bits[::-1])

    def swap(self, value, axis, bit):
        size = self.dp if axis == DP else self.mp
        return lax.ppermute(value, axis, [(i, i ^ bit) for i in range(size)])


class Spread:
    def __init__(self, links, values):
        self.links = links
        self.values = list(values)
        self.phase = 0
        self.have = [[], []]

    def start(self):
        self.values = self.links.order.pin(*self.values)
        self.coming = [
            self.links.swap(value, DP, route[self.phase])
            for value, route in zip(self.values, self.links.routes)
        ]

    def wait(self):
        coming = self.links.order.pin(*self.coming)
        for k in range(2):
            bit = self.links.routes[k][self.phase]
            place = sum(1 for other in self.have[k] if other > bit)
            self.values[k] = jnp.stack([self.values[k], coming[k]], axis=place)
            self.have[k].append(bit)
        self.phase += 1

    def wait_all(self):
        self.wait()
        while self.phase < len(self.links.routes[0]):
            self.start()
            self.wait()

    def start_cores(self):
        self.values = self.links.order.pin(*self.values)
        self.coming = [self.links.swap(value, DP, 1) for value in self.values]

    def wait_cores(self):
        return self.values + self.links.order.pin(*self.coming)


class Gather(Spread):
    def __init__(self, links, piece_a, piece_b):
        super().__init__(links, ())
        self.cut = piece_a.shape[0]
        self.piece = jnp.concatenate([piece_a, piece_b], axis=0)

    def start_mp(self):
        (self.piece,) = self.links.order.pin(self.piece)
        self.coming_mp = [self.links.swap(self.piece, "mp", p) for p in range(1, self.links.mp)]

    def wait_mp(self):
        parts = [self.piece] + self.links.order.pin(*self.coming_mp)
        self.values = [
            jnp.stack([part[: self.cut] for part in parts]),
            jnp.stack([part[self.cut :] for part in parts]),
        ]


class Reduce:
    def __init__(self, links, halves):
        self.links = links
        self.halves = halves
        self.phase = 0

    def start_cores(self):
        others = self.links.order.pin(*self.halves[2:])
        self.coming = [self.links.swap(other, DP, 1) for other in others]

    def wait_cores(self):
        coming = self.links.order.pin(*self.coming)
        mp = self.links.mp
        self.have = [sorted(route, reverse=True) for route in self.links.routes]
        self.values = []
        for own, other in zip(self.halves[:2], coming):
            total = (own.astype(F32) + other.astype(F32)).astype(BF)
            groups = self.links.dp // 2
            rows = total.size // total.shape[-1] // groups // mp
            self.values.append(total.reshape((2,) * len(self.have[0]) + (mp, rows, total.shape[-1])))

    def start(self):
        sends, self.keeps = [], []
        for k in range(2):
            place = self.have[k].index(self.links.routes[1 - k][self.phase])
            self.keeps.append(lax.index_in_dim(self.values[k], 0, place, keepdims=False))
            sends.append(lax.index_in_dim(self.values[k], 1, place, keepdims=False))
        sends = self.links.order.pin(*sends)
        self.coming = [
            self.links.swap(sends[k], DP, self.links.routes[1 - k][self.phase]) for k in range(2)
        ]

    def wait(self):
        coming = self.links.order.pin(*self.coming)
        for k in range(2):
            self.values[k] = (self.keeps[k].astype(F32) + coming[k].astype(F32)).astype(BF)
            self.have[k].remove(self.links.routes[1 - k][self.phase])
        self.phase += 1

    def wait_all(self):
        self.wait()
        while self.phase < len(self.links.routes[0]):
            self.start()
            self.wait()
        return self.values


class ReduceWide:
    def __init__(self, links, grads):
        self.links = links
        (grads,) = links.order.pin(grads.reshape((links.dp,) + grads.shape[2:]))
        self.sums = lax.psum_scatter(grads, DP, scatter_dimension=0, tiled=True)

    def wait(self):
        (sums,) = self.links.order.pin(self.sums)
        return sums.reshape(2, self.links.mp, -1, sums.shape[-1])


class ReduceMp:
    def __init__(self, links, arrays, index):
        self.links = links
        joined = jnp.concatenate(arrays, axis=1)
        if index is None:
            blocks = [joined[p] for p in range(links.mp)]
        else:
            blocks = [
                lax.dynamic_index_in_dim(joined, jnp.bitwise_xor(index, p), 0, keepdims=False)
                for p in range(links.mp)
            ]
        self.kept, *sends = links.order.pin(*blocks)
        self.coming = [links.swap(send, "mp", p + 1) for p, send in enumerate(sends)]

    def wait(self):
        total = self.kept.astype(F32)
        for part in self.links.order.pin(*self.coming):
            total = total + part.astype(F32)
        return total.astype(BF)


def make_shards(dp, mp):
    def shards(
        tokens,
        segments,
        qkv_weight,
        out_weight,
        up_weight,
        down_projection_weight,
        norm_gain,
        norm_bias,
        pos_bias,
        cotangent,
    ):
        seqs, block, width = tokens.shape
        layers = qkv_weight.shape[0]
        window = pos_bias.shape[2]
        channels = qkv_weight.shape[-1]
        hidden = up_weight.shape[-1]
        rows = seqs * block
        group = lax.axis_index("g")
        core = lax.axis_index("c")
        dp_index = group * 2 + core
        mp_index = lax.axis_index("mp")
        order = Order()
        links = Links(order, dp, mp)
        attn_rows = 4 * channels // dp
        ff_rows = hidden // dp
        groups = dp // 2
        per = max(1, width // (mp * ff_rows))
        place = jnp.stack([group // (groups // 4), mp_index, group, core, group // per, group % per]).astype(jnp.int32)

        def picks(count, offset, length):
            return (
                lax.broadcasted_iota(jnp.int32, (count, length), 0) + offset
                == lax.broadcasted_iota(jnp.int32, (count, length), 1)
            ).astype(BF)

        ff_pick = picks(ff_rows, dp_index * ff_rows, hidden)

        def attn_piece(layer):
            by_channel = jnp.transpose(qkv_weight[layer], (0, 2, 1)).reshape(3 * channels, width)
            start = dp_index * attn_rows
            inner = start - 3 * channels
            return jnp.where(
                inner < 0,
                lax.dynamic_slice_in_dim(by_channel, jnp.minimum(start, 3 * channels - attn_rows), attn_rows),
                lax.dynamic_slice_in_dim(out_weight[layer], jnp.maximum(inner, 0), attn_rows),
            )

        def ff_pieces(layer):
            return (
                dot_nt(ff_pick, up_weight[layer]).astype(BF),
                dot_nn(ff_pick, down_projection_weight[layer]).astype(BF),
            )

        def attn_mats(parts):
            return [part.reshape(4, -1, width) for part in parts]

        def ff_mats(parts):
            flat = [part.reshape(-1, width) for part in parts]
            return (flat[0], flat[2]), (flat[1], flat[3])

        def relative(gathered):
            by_dp = jnp.take(gathered, jnp.bitwise_xor(jnp.arange(dp), dp_index), axis=0)
            both = jnp.take(by_dp, jnp.bitwise_xor(jnp.arange(mp), mp_index), axis=1)
            both = both.reshape((dp // 2, 2) + gathered.shape[1:])
            return both[:, 0], both[:, 1]

        def forward_halo(value):
            return lax.ppermute(value, "mp", [(i, i + 1) for i in range(mp - 1)])

        def backward_halo(value):
            return lax.ppermute(value, "mp", [(i + 1, i) for i in range(mp - 1)])

        gains = norm_gain.reshape(layers, 2, 1, width)
        shifts = norm_bias.reshape(layers, 2, 1, width)
        middle = attn_rows // 2
        in_blocks = middle % 16 == 0

        piece = attn_piece(0)
        attn0 = Gather(links, piece[:middle], piece[middle:])
        attn0.start_mp()
        ff0 = Gather(links, *ff_pieces(0))
        ff0.start_mp()
        later = jnp.concatenate((attn_piece(1),) + ff_pieces(1), axis=0)
        x, normed = enter_kernel(order, tokens.reshape(rows, width), gains[0, 0], shifts[0, 0])

        seg_pad = jnp.concatenate([jnp.full((seqs, window), -1, segments.dtype), segments], axis=1)
        seg_keys = lax.dynamic_slice_in_dim(seg_pad, mp_index * block, block + window, axis=1)
        seg_q = seg_keys[:, window:].reshape(seqs, block, 1)
        seg_k = seg_keys.reshape(seqs, 1, block + window)

        attn0.wait_mp()
        attn0.start()
        attn0.wait()
        attn0.start()
        ff0.wait_mp()
        ff0.start()
        (later,) = order.pin(later)
        later = lax.all_gather(later, ("g", "c", "mp"), axis=0, tiled=False)
        (normed,) = order.pin(normed)
        halo = forward_halo(normed)
        attn0.wait_all()
        attn0.start_cores()
        ff0.wait()
        ff0.start()
        w_attn0 = attn_mats(attn0.wait_cores())
        (halo,) = order.pin(halo)

        def attn(layer, x, normed, halo, w_attn):
            sg, ratio, rden, v, wsum, carried, mixed, masked, x1, normed_b = attn_forward(
                order, layer, place, x, normed, halo, w_attn, pos_bias, seg_q, seg_k,
                gains[layer, 1], shifts[layer, 1],
            )
            return x1, normed_b, (sg, ratio, rden, v, wsum, carried, masked), (mixed, normed, halo)

        x1_0, normed_b0, saved0, rows0 = attn(0, x, normed, halo, w_attn0)
        ff0.wait_all()
        ff0.start_cores()
        ups0, downs0 = ff_mats(ff0.wait_cores())
        act0, slope0, x2, normed2 = ff_forward(
            order, x1_0, normed_b0, ups0, downs0, gains[1, 0], shifts[1, 0]
        )
        (normed2,) = order.pin(normed2)
        halo2 = forward_halo(normed2)
        (later,) = order.pin(later)
        if in_blocks:
            w_attn1 = w_ff1 = [later.reshape((groups, 2, mp) + later.shape[1:])]
        else:
            own, other = relative(later.reshape((dp, mp) + later.shape[1:]))
            cuts = [middle, attn_rows, attn_rows + ff_rows]
            own_a, own_b, own_up, own_down = jnp.split(own, cuts, axis=2)
            other_a, other_b, other_up, other_down = jnp.split(other, cuts, axis=2)
            w_attn1 = attn_mats([own_a, own_b, other_a, other_b])
            w_ff1 = sum(ff_mats([own_up, own_down, other_up, other_down]), ())
        (halo2,) = order.pin(halo2)
        x1_1, normed_b1, saved1, rows1 = attn(1, x2, normed2, halo2, w_attn1)

        def ff_back(layer, x1, normed_b, weights, grad, saved):
            grads, *rest = ff_backward(
                order, place, x1, normed_b, weights, groups, grad, gains[layer, 1], saved
            )
            return grads, rest

        ff_grads1, (grad1, grad1_low, gain_b1, shift_b1, output) = ff_back(
            1, x1_1, normed_b1, w_ff1, cotangent.reshape(rows, width), None
        )
        wide1 = ReduceWide(links, ff_grads1)
        gq, gk, gv, band1, dn_own1, back1 = attn_backward(order, place, grad1_low, w_attn1, *saved1)
        (back1,) = order.pin(back1)
        back1 = backward_halo(back1)
        r_attn1 = Reduce(
            links, attn_weight_grads(order, place, gq, gk, gv, *rows1, grad1_low, mp, in_blocks)
        )
        (back1,) = order.pin(back1)
        r_attn1.start_cores()
        grad2, gain_a1, shift_a1 = leave_attn(order, x2, grad1, dn_own1, back1, gains[1, 0])
        r_attn1.wait_cores()
        r_attn1.start()
        ff_grads0, (grad3, grad3_low, gain_b0, shift_b0) = ff_back(
            0, x1_0, normed_b0, ups0 + downs0, grad2, (act0, slope0)
        )
        r_attn1.wait()
        wide0 = ReduceWide(links, ff_grads0)
        r_attn1.start()
        up1, down1 = wide1.wait()
        attn1_sum = r_attn1.wait_all()
        mp1 = ReduceMp(links, attn1_sum + [up1, down1], mp_index if in_blocks else None)
        gq, gk, gv, band0, dn_own0, back0 = attn_backward(order, place, grad3_low, w_attn0, *saved0)
        r_attn0 = Reduce(
            links, attn_weight_grads(order, place, gq, gk, gv, *rows0, grad3_low, mp, False)
        )
        sum1 = mp1.wait()
        r_attn0.start_cores()
        (back0,) = order.pin(back0)
        back0 = backward_halo(back0)
        (sum1,) = order.pin(sum1)
        full1 = lax.all_gather(sum1, DP, axis=0, tiled=False)
        r_attn0.wait_cores()
        r_attn0.start()
        (back0,) = order.pin(back0)
        grad4, gain_a0, shift_a0 = leave_attn(order, x, grad3, dn_own0, back0, gains[0, 0])
        norms = jnp.concatenate(
            [gain_a0, gain_b0, shift_a0, shift_b0, gain_a1, gain_b1, shift_a1, shift_b1], axis=0
        ).reshape(-1, window)
        small = jnp.concatenate([band0, band1, norms], axis=0).astype(BF)

        def small_start(bit):
            (here,) = order.pin(small)
            return here, links.swap(here, DP, bit)

        def small_wait(pair):
            (coming,) = order.pin(pair[1])
            return (pair[0].astype(F32) + coming.astype(F32)).astype(BF)

        bits = [1 << k for k in range(dp.bit_length() - 1)]
        pair = small_start(bits[0])
        r_attn0.wait()
        small = small_wait(pair)
        r_attn0.start()
        for bit in bits[1:-1]:
            pair = small_start(bit)
            small = small_wait(pair)
        attn0_sum = r_attn0.wait_all()
        pair = small_start(bits[-1])
        small = small_wait(pair)
        up0, down0 = wide0.wait()
        mp0 = ReduceMp(links, attn0_sum + [up0, down0], None)
        (small,) = order.pin(small)
        small_parts = [links.swap(small, "mp", p) for p in range(1, mp)]
        (full1,) = order.pin(full1)

        def finish(layer, full, previous):
            if in_blocks:
                return finish_layer(order, layer, layers, place, full, channels, hidden, attn_rows, previous)
            if len(full) == 1:
                owner = jnp.arange(dp)
                attn_part, up_part, down_part = jnp.split(full[0], [attn_rows, attn_rows + ff_rows], axis=1)
            else:
                owner = jnp.bitwise_xor(jnp.arange(dp), dp_index)
                part_a, part_b = [
                    jnp.stack([full[k], full[2 + k]], axis=1).reshape(dp, -1, width) for k in range(2)
                ]
                attn_part = jnp.concatenate([part_a[:, ff_rows:], part_b[:, ff_rows:]], axis=1)
                up_part, down_part = part_a[:, :ff_rows], part_b[:, :ff_rows]

            def rows_of(value):
                return value.reshape(-1, width)

            def place_of(count):
                spots = (owner[:, None] * count + jnp.arange(count)[None, :]).reshape(-1, 1)
                return (spots == jnp.arange(dp * count)[None, :]).astype(BF)

            attn_place = place_of(attn_rows).reshape(-1, 4, channels)
            ff_place = place_of(ff_rows)
            values = (
                jnp.einsum("pd,pmc->mcd", rows_of(attn_part), attn_place[:, :3], preferred_element_type=F32),
                dot_tn(attn_place[:, 3], rows_of(attn_part)),
                dot_tn(rows_of(up_part), ff_place),
                dot_tn(ff_place, rows_of(down_part)),
            )
            if previous is None:
                previous = [jnp.zeros((layers,) + value.shape, F32) for value in values]
            return [
                lax.dynamic_update_index_in_dim(kept, value, layer, 0)
                for kept, value in zip(previous, values)
            ]

        big = finish(1, [full1], None)
        sum0 = mp0.wait()
        spread0 = Spread(
            links,
            [
                jnp.concatenate([sum0[attn_rows : attn_rows + ff_rows], sum0[:middle]], axis=0),
                jnp.concatenate([sum0[attn_rows + ff_rows :], sum0[middle:attn_rows]], axis=0),
            ],
        )
        spread0.start()
        small_parts = [small] + order.pin(*small_parts)
        spread0.wait()
        spread0.start()
        small_all = jnp.stack(small_parts)
        pairs = small_all[:, 2 * block :].astype(F32)
        while pairs.shape[0] > 1:
            pairs = pairs[0::2] + pairs[1::2]
        norm_sum = pairs[0].reshape(layers, 4, width)
        bands = jnp.take(
            small_all[:, : 2 * block].astype(F32), jnp.bitwise_xor(jnp.arange(mp), mp_index), axis=0
        ).reshape(mp, layers, block, window)
        band_sum = jnp.transpose(bands, (1, 0, 2, 3)).reshape(layers, mp * block, window)
        spread0.wait_all()
        spread0.start_cores()
        full0 = [part.reshape(groups, -1, width) for part in spread0.wait_cores()]
        qkv_out, out_out, up_out, down_out = finish(0, full0, big)
        return (
            output.reshape(tokens.shape),
            grad4.reshape(tokens.shape),
            jnp.transpose(qkv_out, (0, 1, 3, 2)),
            out_out,
            up_out,
            down_out,
            norm_sum[:, :2],
            norm_sum[:, 2:],
            band_sum,
        )

    return shards


def solution(mesh):
    dp, mp = mesh.shape["dp"], mesh.shape["mp"]
    inner = Mesh(mesh.devices.reshape(dp // 2, 2, mp), DP + ("mp",))
    placed = (
        P(DP, "mp", None),
        P(DP, None),
        P(None, None, None, "mp"),
        P(None, "mp", None),
        P(None, None, "mp"),
        P(None, "mp", None),
        P(),
        P(),
        P(),
        P(DP, "mp", None),
    )
    return jax.shard_map(
        make_shards(dp, mp),
        mesh=inner,
        in_specs=placed,
        out_specs=(
            P(DP, "mp", None),
            P(DP, "mp", None),
            P(None, None, None, "mp"),
            P(None, "mp", None),
            P(None, None, "mp"),
            P(None, "mp", None),
            P(),
            P(),
            P(),
        ),
        check_vma=False,
    )
```

```python
import functools

import jax
import jax.numpy as jnp
from jax import lax
from jax.experimental import pallas as pl
from jax.experimental.pallas import tpu as pltpu
from jax.sharding import Mesh, PartitionSpec as P

BF = jnp.bfloat16
F32 = jnp.float32
VMEM_LIMIT = 58 * 1024 * 1024
TOKEN = (8, 128)
SUB = 256
RIDERS = 16
GELU_A = 0.7978845608028654
GELU_B = 0.044715


def dot_nt(lhs, rhs):
    return lax.dot_general(lhs, rhs, (((1,), (1,)), ((), ())), preferred_element_type=F32)


def dot_nn(lhs, rhs):
    return lax.dot_general(lhs, rhs, (((1,), (0,)), ((), ())), preferred_element_type=F32)


def dot_tn(lhs, rhs):
    return lax.dot_general(lhs, rhs, (((0,), (0,)), ((), ())), preferred_element_type=F32)


def normalize(values):
    center = values - jnp.mean(values, axis=-1, keepdims=True)
    inv_std = lax.rsqrt(jnp.mean(center * center, axis=-1, keepdims=True) + 1e-05)
    return center * inv_std, inv_std


def norm_back(grad_out, normal, inv_std, gain):
    grad_normal = grad_out * gain
    mean_one = jnp.mean(grad_normal, axis=-1, keepdims=True)
    mean_two = jnp.mean(grad_normal * normal, axis=-1, keepdims=True)
    return inv_std * (grad_normal - mean_one - normal * mean_two)


def whole(shape):
    return pl.BlockSpec(shape, lambda *_: (0,) * len(shape))


def call(order, body, grid, in_specs, out_specs, out_shape, scratch=(), prefetch=0, name=None, aliases=None):
    first = prefetch + len(in_specs)
    second = first + 1 + len(out_specs)
    anywhere = pl.BlockSpec(memory_space=pl.ANY)

    def with_token(*refs):
        return body(*refs[:first], *refs[first + 1 : second], *refs[second + 1 :])

    kernel = pl.pallas_call(
        with_token,
        grid_spec=pltpu.PrefetchScalarGridSpec(
            num_scalar_prefetch=prefetch,
            grid=grid,
            in_specs=list(in_specs) + [anywhere],
            out_specs=list(out_specs) + [anywhere],
            scratch_shapes=list(scratch),
        ),
        out_shape=list(out_shape) + [shape_of(TOKEN, jnp.int32)],
        input_output_aliases={**(aliases or {}), first: len(out_specs)},
        compiler_params=pltpu.CompilerParams(
            dimension_semantics=("arbitrary",) * len(grid), vmem_limit_bytes=VMEM_LIMIT
        ),
        cost_estimate=pl.CostEstimate(flops=0, bytes_accessed=0, transcendentals=0),
        name=name,
    )

    def run(*operands):
        *results, order.token = kernel(*operands, order.token)
        return results

    return run


def shape_of(shape, dtype):
    return jax.ShapeDtypeStruct(shape, dtype)


def tie(*arrays):
    count = len(arrays)
    return pl.pallas_call(
        lambda *refs: None,
        out_shape=[shape_of(a.shape, a.dtype) for a in arrays],
        in_specs=[pl.BlockSpec(memory_space=pl.ANY)] * count,
        out_specs=[pl.BlockSpec(memory_space=pl.ANY)] * count,
        input_output_aliases={i: i for i in range(count)},
        cost_estimate=pl.CostEstimate(flops=0, bytes_accessed=0, transcendentals=0),
        name="tie",
    )(*arrays)


def enter_kernel(order, tokens, gain, shift):
    rows, width = tokens.shape

    def body(t_ref, g_ref, s_ref, x_ref, n_ref):
        x = t_ref[...].astype(F32)
        x_ref[...] = x
        normal, _ = normalize(x)
        n_ref[...] = (normal * g_ref[...] + s_ref[...]).astype(BF)

    return call(
        order,
        body,
        (1,),
        [whole((rows, width)), whole((1, width)), whole((1, width))],
        [whole((rows, width)), whole((rows, width))],
        [shape_of((rows, width), F32), shape_of((rows, width), BF)],
        name="enter",
    )(tokens, gain, shift)


def reverse_lanes(values):
    count = values.shape[1]
    flip = (
        lax.broadcasted_iota(jnp.int32, (count, count), 0)
        + lax.broadcasted_iota(jnp.int32, (count, count), 1)
        == count - 1
    ).astype(BF)
    high = values.astype(BF)
    rest = values - high.astype(F32)
    middle = rest.astype(BF)
    last = (rest - middle.astype(F32)).astype(BF)
    return (dot_nn(high, flip) + dot_nn(middle, flip)) + dot_nn(last, flip)


def attn_specs(weights):
    if len(weights) == 4:
        return [whole(w.shape) for w in weights]
    groups, _, mp, count, width = weights[0].shape
    return [pl.BlockSpec((groups, 1, mp, count // 3, width), lambda i, place: (0, place[3] ^ i, 0, 0, 0))]


def by_half(step, refs, place_ref, part):
    if len(refs) == 1:
        width = refs[0].shape[-1]
        part(lambda m: refs[0][m, 0].reshape(-1, width))
        return
    for half in range(2):
        wa, wb = refs[2 * half], refs[2 * half + 1]

        def mat(m, wa=wa, wb=wb):
            return jnp.concatenate([wa[place_ref[0] ^ m], wb[place_ref[0] ^ m]], axis=0)

        pl.when(step == half)(functools.partial(part, mat))


def attn_forward(order, layer, place, x, normed, halo, weights, pos_bias, seg_q, seg_k, gain, shift):
    rows, width = x.shape
    seqs, block, _ = seg_q.shape
    keys = seg_k.shape[2]
    window = keys - block
    half = width // 2

    def body(place_ref, x_ref, n_ref, h_ref, *rest):
        w_refs, rest = rest[: len(weights)], rest[len(weights) :]
        (band_ref, sq_ref, sk_ref, g_ref, s_ref, sg_ref, ratio_ref, rden_ref, v_ref, wsum_ref, car_ref, mixed_ref,
         masked_ref, x1_ref, nb_ref, mix) = rest
        step = pl.program_id(0)

        @pl.when(step == 0)
        def _():
            band = reverse_lanes(jnp.exp(band_ref[0]))
            band = jnp.concatenate([band, jnp.zeros((block, block), F32)], axis=1)
            spread = pltpu.roll(band, 1, axis=1, stride=1, stride_axis=0)
            for s in range(seqs):
                masked = jnp.where(sq_ref[s] == sk_ref[s], spread, 0.0)
                masked_ref[s] = masked
                mix[s] = masked.astype(BF)
            x1_ref[...] = x_ref[...]

        def part(mat):
            wq, wk, wv = mat(0), mat(1), mat(2)
            q = dot_nt(n_ref[...], wq)
            sg = jax.nn.sigmoid(q)
            sg_ref[...] = sg.astype(BF)
            carried, wsum = [], []
            for r, source in enumerate((h_ref, n_ref)):
                here = slice(r * rows, (r + 1) * rows)
                kexp = jnp.exp(dot_nt(source[...], wk))
                v = dot_nt(source[...], wv)
                v_ref[here] = v.astype(BF)
                wsum.append(kexp.astype(BF))
                carried.append((kexp * v).astype(BF))
                wsum_ref[here] = wsum[r]
                car_ref[here] = carried[r]
            mixed = []
            for s in range(seqs):
                here = slice(s * block, (s + 1) * block)
                num = dot_nn(mix[s, :, :window], carried[0][here]) + dot_nn(mix[s, :, window:], carried[1][here])
                den = dot_nn(mix[s, :, :window], wsum[0][here]) + dot_nn(mix[s, :, window:], wsum[1][here])
                rden = 1.0 / den
                ratio = num * rden
                rden_ref[here] = rden.astype(BF)
                ratio_ref[here] = ratio.astype(BF)
                mixed.append((sg[here] * ratio).astype(BF))
            mixed = jnp.concatenate(mixed, axis=0)
            mixed_ref[...] = mixed
            x1_ref[...] += dot_nn(mixed, mat(3))

        by_half(step, w_refs, place_ref, part)

        @pl.when(step == 1)
        def _():
            normal, _ = normalize(x1_ref[...])
            nb_ref[...] = (normal * g_ref[...] + s_ref[...]).astype(BF)

    def col(n):
        return pl.BlockSpec((n, half), lambda i, *_: (0, i))

    return call(
        order,
        body,
        (2,),
        [whole((rows, width))] * 3
        + attn_specs(weights)
        + [pl.BlockSpec((1, block, window), lambda i, place: (layer, place[1], 0))]
        + [whole((seqs, block, 1)), whole((seqs, 1, keys)), whole((1, width)), whole((1, width))],
        [col(rows)] * 3 + [col(2 * rows)] * 3 + [col(rows)]
        + [whole((seqs, block, keys)), whole((rows, width)), whole((rows, width))],
        [shape_of((rows, width), BF)] * 3
        + [shape_of((2 * rows, width), BF)] * 3
        + [
            shape_of((rows, width), BF),
            shape_of((seqs, block, keys), F32),
            shape_of((rows, width), F32),
            shape_of((rows, width), BF),
        ],
        [pltpu.VMEM((seqs, block, keys), BF)],
        prefetch=1,
        name="attn_fwd",
    )(place, x, normed, halo, *weights, pos_bias, seg_q, seg_k, gain, shift)


def gelu_both(pre):
    square = pre * pre
    upper = 0.5 + 0.5 * jnp.tanh(pre * (GELU_A + (GELU_A * GELU_B) * square))
    act = pre * upper
    return act, upper + act * (1.0 - upper) * (2.0 * GELU_A + (6.0 * GELU_A * GELU_B) * square)


def chunk_specs(chunk, width, per_half):
    own = pl.BlockSpec((chunk, width), lambda i, *_: (jnp.minimum(i, per_half - 1), 0))
    other = pl.BlockSpec((chunk, width), lambda i, *_: (jnp.maximum(i - per_half, 0), 0))
    return own, other


def ff_forward(order, x1, normed, up, down, gain, shift):
    rows, width = x1.shape
    half = up.shape[0]
    chunk = width
    steps = half // chunk
    last = gain is not None

    def body(x_ref, n_ref, u, d, *rest):
        if last:
            g_ref, s_ref, act_ref, slope_ref, x2_ref, next_ref = rest
        else:
            act_ref, slope_ref, x2_ref = rest
        step = pl.program_id(0)

        @pl.when(step == 0)
        def _():
            x2_ref[...] = x_ref[...]

        for k in range(chunk // SUB):
            here = slice(k * SUB, (k + 1) * SUB)
            act, slope = gelu_both(dot_nt(n_ref[...], u[here]))
            act_ref[:, here] = act.astype(BF)
            slope_ref[:, here] = slope.astype(BF)
        x2_ref[...] += dot_nn(act_ref[...], d[...])

        if last:

            @pl.when(step == steps - 1)
            def _():
                normal, _ = normalize(x2_ref[...])
                next_ref[...] = (normal * g_ref[...] + s_ref[...]).astype(BF)

    full = whole((rows, width))
    weight = pl.BlockSpec((chunk, width), lambda i: (i, 0))
    col = pl.BlockSpec((rows, chunk), lambda i: (0, i))
    return call(
        order,
        body,
        (steps,),
        [full, full, weight, weight] + [whole((1, width))] * (2 if last else 0),
        [col, col, full] + ([full] if last else []),
        [shape_of((rows, half), BF)] * 2 + [shape_of((rows, width), F32)] + ([shape_of((rows, width), BF)] if last else []),
        name="ff_fwd",
    )(x1, normed, up, down, *((gain, shift) if last else ()))


def ff_specs(weights, chunk):
    if len(weights) == 4:
        half, width = weights[0].shape
        own, other = chunk_specs(chunk, width, half // chunk)
        return list(weights), [own, other, own, other]
    groups, _, mp, count, width = weights[0].shape
    rows = count // 3
    per = chunk // (mp * rows)
    steps = groups // per

    def spec(which):
        return pl.BlockSpec(
            (per, 1, mp, rows, width), lambda i, place: (i % steps, place[3] ^ (i // steps), 0, which, 0)
        )

    return [weights[0], weights[0]], [spec(1), spec(2)]


def ff_backward(order, place, x1, normed, weights, groups, grad, gain, saved):
    rows, width = x1.shape
    chunk = width
    half = 2 * width
    per_half = half // chunk
    steps = 2 * per_half
    operands, w_specs = ff_specs(weights, chunk)
    group_rows = half // groups
    per = chunk // group_rows
    fresh = saved is None
    relative = len(weights) == 4

    def body(place_ref, x_ref, n_ref, *rest):
        rest = list(rest)
        w_refs = [rest.pop(0) for _ in operands]
        grad_ref, g_ref = rest.pop(0), rest.pop(0)
        kept = [] if fresh else [rest.pop(0) for _ in range(4)]
        wg_ref = rest.pop(0)
        g1_ref, ga_ref, gg_ref, gs_ref = rest[:4]
        out_ref = rest[4] if fresh else None
        low, dn, pre_grads = rest[5:8] if fresh else rest[4:7]
        acts, x2 = rest[8:] if fresh else (None, None)
        step = pl.program_id(0)

        @pl.when(step == 0)
        def _():
            low[...] = grad_ref[...].astype(BF)
            dn[...] = jnp.zeros_like(dn)
            if fresh:
                x2[...] = x_ref[...]

        def part(u_ref, d_ref, act_ref, slope_ref):
            u = u_ref[...].reshape(chunk, width)
            d = d_ref[...].reshape(chunk, width)
            for k in range(chunk // SUB):
                here = slice(k * SUB, (k + 1) * SUB)
                if fresh:
                    act, slope = gelu_both(dot_nt(n_ref[...], u[here]))
                    acts[:, here] = act.astype(BF)
                else:
                    slope = slope_ref[:, here].astype(F32)
                pre_grads[:, here] = (dot_nt(low[...], d[here]) * slope).astype(BF)
            pre_grad = pre_grads[...]
            act = acts[...] if fresh else act_ref[...]
            if fresh:
                x2[...] += dot_nn(act, d)
            dn[...] += dot_nn(pre_grad, u)
            for which, value in ((0, dot_tn(pre_grad, n_ref[...])), (1, dot_tn(act, low[...]))):
                value = value.astype(BF)
                for k in range(per):
                    spot = (place_ref[5] ^ k) if relative else k
                    wg_ref[spot, 0, which] = value[k * group_rows : (k + 1) * group_rows]

        own_w, other_w = (w_refs[::2], w_refs[1::2]) if relative else (w_refs, w_refs)
        if fresh:
            pl.when(step < per_half)(lambda: part(*own_w, None, None))
            pl.when(step >= per_half)(lambda: part(*other_w, None, None))
        else:
            pl.when(step < per_half)(lambda: part(*own_w, *kept[:2]))
            pl.when(step >= per_half)(lambda: part(*other_w, *kept[2:]))

        @pl.when(step == steps - 1)
        def _():
            if fresh:
                out_ref[...] = x2[...].astype(BF)
            normal, inv = normalize(x_ref[...])
            total = dn[...]
            g1 = grad_ref[...] + norm_back(total, normal, inv, g_ref[...])
            g1_ref[...] = g1
            ga_ref[...] = g1.astype(BF)
            gg_ref[...] = jnp.sum(total * normal, axis=0, keepdims=True)
            gs_ref[...] = jnp.sum(total, axis=0, keepdims=True)

    full = whole((rows, width))
    def own_index(i):
        return jnp.minimum(i, per_half - 1)

    def other_index(i):
        return jnp.maximum(i - per_half, 0)

    wg_specs = [
        pl.BlockSpec(
            (per, 1, 2, group_rows, width),
            lambda i, place: (
                (place[4] ^ (i % per_half)) if relative else i % per_half, place[3] ^ (i // per_half), 0, 0, 0,
            ),
        )
    ]
    wg_shapes = [shape_of((groups, 2, 2, group_rows, width), BF)]
    kept_specs = [
        pl.BlockSpec((rows, chunk), lambda i, *_, index=index: (0, index(i)))
        for index in (() if fresh else (own_index, own_index, other_index, other_index))
    ]
    return call(
        order,
        body,
        (steps,),
        [full, full] + w_specs + [full, whole((1, width))] + kept_specs,
        wg_specs + [full, full, whole((1, width)), whole((1, width))] + ([full] if fresh else []),
        wg_shapes
        + [
            shape_of((rows, width), F32),
            shape_of((rows, width), BF),
            shape_of((1, width), F32),
            shape_of((1, width), F32),
        ]
        + ([shape_of((rows, width), BF)] if fresh else []),
        [pltpu.VMEM((rows, width), BF), pltpu.VMEM((rows, width), F32), pltpu.VMEM((rows, chunk), BF)]
        + ([pltpu.VMEM((rows, chunk), BF), pltpu.VMEM((rows, width), F32)] if fresh else []),
        prefetch=1,
        name="ff_bwd",
    )(place, x1, normed, *operands, grad, gain, *(() if fresh else saved))


def attn_backward(order, place, grad_low, weights, sg, ratio, rden, v, wsum, carried, masked):
    rows, width = grad_low.shape
    seqs, block, keys = masked.shape
    window = keys - block
    half = width // 2

    def body(place_ref, ga_ref, *rest):
        w_refs, rest = rest[: len(weights)], rest[len(weights) :]
        (sg_ref, ratio_ref, rden_ref, v_ref, wsum_ref, car_ref, masked_ref,
         gq_ref, gk_ref, gv_ref, band_ref, own_ref, halo_ref, mix_t, wgrad, dn) = rest
        step = pl.program_id(0)

        @pl.when(step == 0)
        def _():
            for s in range(seqs):
                mix_t[s] = masked_ref[s].T.astype(BF)
            wgrad[...] = jnp.zeros_like(wgrad)
            dn[...] = jnp.zeros_like(dn)

        def part(mat):
            gm = dot_nt(ga_ref[...], mat(3))
            sig = sg_ref[...].astype(F32)
            rat = ratio_ref[...].astype(F32)
            scaled = gm * sig
            gq = (scaled * rat * (1.0 - sig)).astype(BF)
            gq_ref[...] = gq
            gnum_f = scaled * rden_ref[...].astype(F32)
            gnum = gnum_f.astype(BF)
            gden = (-gnum_f * rat).astype(BF)
            wq, wk, wv = mat(0), mat(1), mat(2)
            dn[rows:] += dot_nn(gq, wq)
            for r in range(2):
                for s in range(seqs):
                    here = slice(s * block, (s + 1) * block)
                    there = slice(r * rows + s * block, r * rows + (s + 1) * block)
                    cols = slice(r * window, r * window + block)
                    ke = wsum_ref[there].astype(F32)
                    gcar = dot_nn(mix_t[s, cols], gnum[here])
                    gsum = dot_nn(mix_t[s, cols], gden[here])
                    gv = (gcar * ke).astype(BF)
                    gk = ((gcar * v_ref[there].astype(F32) + gsum) * ke).astype(BF)
                    gk_ref[there] = gk
                    gv_ref[there] = gv
                    wgrad[s, :, cols] += dot_nt(gnum[here], car_ref[there]) + dot_nt(gden[here], wsum_ref[there])
                    dn[there] += dot_nn(gk, wk) + dot_nn(gv, wv)

        by_half(step, w_refs, place_ref, part)

        @pl.when(step == 1)
        def _():
            total = wgrad[0] * masked_ref[0]
            for s in range(1, seqs):
                total = total + wgrad[s] * masked_ref[s]
            lane_row = lax.broadcasted_iota(jnp.int32, (block, keys), 0) + 1
            bit = 1
            while bit <= block:
                rolled = pltpu.roll(total, keys - bit, axis=1)
                total = jnp.where((lane_row & bit) != 0, rolled, total)
                bit *= 2
            band_ref[...] = reverse_lanes(total[:, :window])
            halo_ref[...] = dn[:rows].astype(BF)
            own_ref[...] = dn[rows:]

    def col(n):
        return pl.BlockSpec((n, half), lambda i, *_: (0, i))

    return call(
        order,
        body,
        (2,),
        [whole((rows, width))]
        + attn_specs(weights)
        + [col(rows)] * 3 + [col(2 * rows)] * 3 + [whole((seqs, block, keys))],
        [col(rows), col(2 * rows), col(2 * rows), whole((block, window)), whole((rows, width)), whole((rows, width))],
        [
            shape_of((rows, width), BF),
            shape_of((2 * rows, width), BF),
            shape_of((2 * rows, width), BF),
            shape_of((block, window), F32),
            shape_of((rows, width), F32),
            shape_of((rows, width), BF),
        ],
        [
            pltpu.VMEM((seqs, keys, block), BF),
            pltpu.VMEM((seqs, block, keys), F32),
            pltpu.VMEM((2 * rows, width), F32),
        ],
        prefetch=1,
        name="attn_bwd",
    )(place, grad_low, *weights, sg, ratio, rden, v, wsum, carried, masked)


def attn_weight_grads(order, place, gq, gk, gv, mixed, normed, halo, grad_low, band, mp, mixed_rows, riding):
    rows, width = gq.shape
    half = width // 2
    quarter = half // 2
    piece = quarter // mp
    window = band.shape[1]
    share = 2 * RIDERS
    def body(place_ref, gq_ref, gk_ref, gv_ref, mixed_ref, n_ref, h_ref, ga_ref, band_ref, *out_refs):
        def part(outs, core):
            if riding:
                for p in range(4):
                    owner = 2 * (place_ref[2] ^ p) + (place_ref[3] ^ core)
                    start = pl.multiple_of(owner * share, share)
                    rows_here = band_ref[pl.ds(start, share)].astype(BF)
                    outs[0][p, quarter:] = jnp.concatenate(
                        [rows_here[:RIDERS], rows_here[RIDERS:], jnp.zeros((RIDERS, width - 2 * window), BF)], axis=1
                    )

            def put(m, value):
                low = value.astype(BF)
                spot = place_ref[0] ^ m
                if not mixed_rows:
                    outs[0][spot, :quarter] = low[:quarter]
                    outs[1][spot] = low[quarter:]
                    return
                for z in range(mp):
                    for k in range(2):
                        outs[k][spot, z * piece : (z + 1) * piece] = low[
                            (2 * z + k) * piece : (2 * z + k + 1) * piece
                        ]

            put(0, dot_tn(gq_ref[...], n_ref[...]))
            for m, ref in ((1, gk_ref), (2, gv_ref)):
                put(m, dot_tn(ref[:rows], h_ref[...]) + dot_tn(ref[rows:], n_ref[...]))
            put(3, dot_tn(mixed_ref[...], ga_ref[...]))

        pl.when(pl.program_id(0) == 0)(lambda: part(out_refs[:2], 0))
        pl.when(pl.program_id(0) == 1)(lambda: part(out_refs[2:], 1))

    def col(n):
        return pl.BlockSpec((n, half), lambda i, *_: (0, i))

    shapes = [(4, quarter + (RIDERS if riding else 0), width), (4, quarter, width)] * 2
    return call(
        order,
        body,
        (2,),
        [col(rows), col(2 * rows), col(2 * rows), col(rows)] + [whole((rows, width))] * 3 + [whole(band.shape)],
        [whole(shape) for shape in shapes],
        [shape_of(shape, BF) for shape in shapes],
        prefetch=1,
        name="attn_wgrad",
    )(place, gq, gk, gv, mixed, normed, halo, grad_low, band)


def leave_attn(order, x, grad, own, back, gain):
    rows, width = x.shape

    def body(x_ref, g_ref, o_ref, b_ref, gain_ref, out_ref, gg_ref, gs_ref):
        normal, inv = normalize(x_ref[...])
        total = o_ref[...] + b_ref[...].astype(F32)
        out_ref[...] = g_ref[...] + norm_back(total, normal, inv, gain_ref[...])
        gg_ref[...] = jnp.sum(total * normal, axis=0, keepdims=True)
        gs_ref[...] = jnp.sum(total, axis=0, keepdims=True)

    return call(
        order,
        body,
        (1,),
        [whole((rows, width))] * 4 + [whole((1, width))],
        [whole((rows, width)), whole((1, width)), whole((1, width))],
        [shape_of((rows, width), F32)] + [shape_of((1, width), F32)] * 2,
        name="leave",
    )(x, grad, own, back, gain)


def finish_layer(order, layer, layers, place, parts, channels, hidden, mp, window, norm_rows, previous):
    width = parts[0].shape[-1]
    total = 4 * channels
    single = len(parts) == 1
    groups = len(parts) // 2
    dp = parts[0].shape[0] if single else len(parts)
    piece = total // dp
    share = 2 * RIDERS
    block = dp * share

    def body(place_ref, *rest):
        p_refs, rest = rest[: len(parts)], rest[len(parts) :]
        qkv_ref, out_ref, up_ref, down_ref, band_ref = rest[:5]
        up = rest[-1]

        def put(owner, rows_of):
            start = pl.multiple_of(owner * piece, piece)
            mat = owner * piece // channels
            inner = pl.multiple_of(owner * piece - mat * channels, piece)
            value = rows_of(0, piece).astype(F32)

            @pl.when(mat < 3)
            def _():
                qkv_ref[0, jnp.minimum(mat, 2), pl.ds(inner, piece)] = value

            @pl.when(mat == 3)
            def _():
                out_ref[0, pl.ds(inner, piece)] = value

            up[pl.ds(start, piece)] = rows_of(piece, piece).astype(F32)
            down_ref[0, pl.ds(start, piece)] = rows_of(2 * piece, piece).astype(F32)
            for p in range(mp):
                band = rows_of(3 * piece + norm_rows + p * RIDERS, RIDERS).astype(F32)
                first = pl.multiple_of((place_ref[1] ^ p) * block + owner * share, share)
                band_ref[0, pl.ds(first, RIDERS)] = band[:, :window]
                band_ref[0, pl.ds(first + RIDERS, RIDERS)] = band[:, window : 2 * window]

        if single:
            for owner in range(dp):
                put(jnp.int32(owner), lambda start, count, owner=owner: p_refs[0][owner, start : start + count])
        else:
            for core in range(2):
                for p in range(groups):
                    ref = p_refs[core * groups + p]
                    owner = 2 * (place_ref[2] ^ p) + (place_ref[3] ^ core)
                    put(owner, lambda start, count, ref=ref: ref[start : start + count])
        up_ref[0] = up[...].T
        if norm_rows:
            half = norm_rows // 2
            sums = []
            for p in range(groups):
                for core in range(2):
                    rows = p_refs[core * groups + p][3 * piece : 3 * piece + norm_rows].astype(F32)
                    sums.append(rows[:half] + rows[half:])
            while len(sums) > 1:
                sums = [sums[k] + sums[k + 1] for k in range(0, len(sums), 2)]
            rest[5][...] = sums[0]

    shapes = [
        (layers, 3, channels, width),
        (layers, channels, width),
        (layers, width, hidden),
        (layers, hidden, width),
        (layers, mp * block, window),
    ]

    def here(shape):
        return pl.BlockSpec((1,) + shape[1:], lambda i, *_: (layer,) + (0,) * (len(shape) - 1))

    extra = list(previous) if previous is not None else []
    anywhere = pl.BlockSpec(memory_space=pl.ANY)
    return call(
        order,
        lambda *refs: body(*refs[: 1 + len(parts)], *refs[1 + len(parts) + len(extra) :]),
        (1,),
        [whole(part.shape) for part in parts] + [anywhere] * len(extra),
        [here(shape) for shape in shapes] + ([whole((norm_rows // 2, width))] if norm_rows else []),
        [shape_of(shape, F32) for shape in shapes]
        + ([shape_of((norm_rows // 2, width), F32)] if norm_rows else []),
        [pltpu.VMEM((total, width), F32)],
        prefetch=1,
        name="finish",
        aliases={1 + len(parts) + k: k for k in range(len(extra))},
    )(place, *parts, *extra)


DP = ("g", "c")


class Order:
    def __init__(self):
        self.token = jnp.zeros(TOKEN, jnp.int32)

    def pin(self, *arrays):
        *arrays, self.token = tie(*arrays, self.token)
        return arrays


class Links:
    def __init__(self, order, dp, mp):
        self.order = order
        self.dp = dp
        self.mp = mp
        bits = [1 << k for k in range(1, dp.bit_length() - 1)]
        self.routes = (bits, bits[::-1])

    def swap(self, value, axis, bit):
        size = self.dp if axis == DP else self.mp
        return lax.ppermute(value, axis, [(i, i ^ bit) for i in range(size)])


class Spread:
    def __init__(self, links, values):
        self.links = links
        self.values = list(values)
        self.phase = 0
        self.have = [[], []]

    def start(self):
        self.values = self.links.order.pin(*self.values)
        self.coming = [
            self.links.swap(value, DP, route[self.phase])
            for value, route in zip(self.values, self.links.routes)
        ]

    def wait(self):
        coming = self.links.order.pin(*self.coming)
        for k in range(2):
            bit = self.links.routes[k][self.phase]
            place = sum(1 for other in self.have[k] if other > bit)
            self.values[k] = jnp.stack([self.values[k], coming[k]], axis=place)
            self.have[k].append(bit)
        self.phase += 1

    def wait_all(self):
        self.wait()
        while self.phase < len(self.links.routes[0]):
            self.start()
            self.wait()

    def start_cores(self):
        self.values = self.links.order.pin(*self.values)
        self.coming = [self.links.swap(value, DP, 1) for value in self.values]

    def wait_cores(self):
        return self.values + self.links.order.pin(*self.coming)


class Gather(Spread):
    def __init__(self, links, piece_a, piece_b):
        super().__init__(links, ())
        self.cut = piece_a.shape[0]
        self.piece = jnp.concatenate([piece_a, piece_b], axis=0)

    def start_mp(self):
        (self.piece,) = self.links.order.pin(self.piece)
        self.coming_mp = [self.links.swap(self.piece, "mp", p) for p in range(1, self.links.mp)]

    def wait_mp(self):
        parts = [self.piece] + self.links.order.pin(*self.coming_mp)
        self.values = [
            jnp.stack([part[: self.cut] for part in parts]),
            jnp.stack([part[self.cut :] for part in parts]),
        ]


class Reduce:
    def __init__(self, links, halves):
        self.links = links
        self.halves = halves
        self.phase = 0

    def start_cores(self):
        others = self.links.order.pin(*self.halves[2:])
        self.coming = [self.links.swap(other, DP, 1) for other in others]

    def wait_cores(self):
        coming = self.links.order.pin(*self.coming)
        mp = self.links.mp
        self.have = [sorted(route, reverse=True) for route in self.links.routes]
        lead = (2,) * len(self.have[0])
        self.terms = []
        for own, other in zip(self.halves[:2], coming):
            shape = lead + (-1, own.shape[-1])
            self.terms.append([own.reshape(shape), other.reshape(shape)])

    def start(self):
        sends = []
        for k in range(2):
            place = self.have[k].index(self.links.routes[1 - k][self.phase])
            sends.append(
                sum(lax.index_in_dim(term, 1, place, keepdims=False).astype(F32) for term in self.terms[k]).astype(BF)
            )
            self.terms[k] = [lax.index_in_dim(term, 0, place, keepdims=False) for term in self.terms[k]]
        sends = self.links.order.pin(*sends)
        self.coming = [
            self.links.swap(sends[k], DP, self.links.routes[1 - k][self.phase]) for k in range(2)
        ]

    def wait(self):
        coming = self.links.order.pin(*self.coming)
        for k in range(2):
            self.terms[k].append(coming[k])
            self.have[k].remove(self.links.routes[1 - k][self.phase])
        self.phase += 1

    def wait_all(self):
        self.wait()
        while self.phase < len(self.links.routes[0]):
            self.start()
            self.wait()
        sums = [sum(term.astype(F32) for term in terms).astype(BF) for terms in self.terms]
        count = sums[1].shape[0]
        mp = self.links.mp
        riders = sums[0][count:]
        return [value[:count].reshape(mp, count // mp, -1) for value in sums], riders


class ReduceWide:
    def __init__(self, links, grads):
        self.links = links
        (grads,) = links.order.pin(grads.reshape((links.dp,) + grads.shape[2:]))
        self.sums = lax.psum_scatter(grads, DP, scatter_dimension=0, tiled=True)

    def wait(self):
        (sums,) = self.links.order.pin(self.sums)
        sums = sums.reshape(2, self.links.mp, -1, sums.shape[-1])
        return [sums[0], sums[1]]


class ReduceMp:
    def __init__(self, links, arrays, index, riders):
        self.links = links
        joined = jnp.concatenate(arrays, axis=1)
        self.count = joined.shape[1]
        if index is None:
            blocks = [joined[p] for p in range(links.mp)]
        else:
            blocks = [
                lax.dynamic_index_in_dim(joined, jnp.bitwise_xor(index, p), 0, keepdims=False)
                for p in range(links.mp)
            ]
        if riders is not None:
            blocks = [jnp.concatenate([block, riders], axis=0) for block in blocks]
        self.kept, *sends = links.order.pin(*blocks)
        self.coming = [links.swap(send, "mp", p + 1) for p, send in enumerate(sends)]

    def wait(self):
        parts = [self.kept] + self.links.order.pin(*self.coming)
        total = sum(part[: self.count].astype(F32) for part in parts)
        return total.astype(BF), [part[self.count :] for part in parts]


def make_shards(dp, mp):
    def shards(
        tokens,
        segments,
        qkv_weight,
        out_weight,
        up_weight,
        down_projection_weight,
        norm_gain,
        norm_bias,
        pos_bias,
        cotangent,
    ):
        seqs, block, width = tokens.shape
        layers = qkv_weight.shape[0]
        window = pos_bias.shape[2]
        channels = qkv_weight.shape[-1]
        hidden = up_weight.shape[-1]
        rows = seqs * block
        group = lax.axis_index("g")
        core = lax.axis_index("c")
        dp_index = group * 2 + core
        mp_index = lax.axis_index("mp")
        order = Order()
        links = Links(order, dp, mp)
        attn_rows = 4 * channels // dp
        ff_rows = hidden // dp
        groups = dp // 2
        per = max(1, width // (mp * ff_rows))
        place = jnp.stack([group // (groups // 4), mp_index, group, core, group // per, group % per]).astype(jnp.int32)

        def picks(count, offset, length):
            return (
                lax.broadcasted_iota(jnp.int32, (count, length), 0) + offset
                == lax.broadcasted_iota(jnp.int32, (count, length), 1)
            ).astype(BF)

        ff_pick = picks(ff_rows, dp_index * ff_rows, hidden)

        def attn_piece(layer):
            by_channel = jnp.transpose(qkv_weight[layer], (0, 2, 1)).reshape(3 * channels, width)
            start = dp_index * attn_rows
            inner = start - 3 * channels
            return jnp.where(
                inner < 0,
                lax.dynamic_slice_in_dim(by_channel, jnp.minimum(start, 3 * channels - attn_rows), attn_rows),
                lax.dynamic_slice_in_dim(out_weight[layer], jnp.maximum(inner, 0), attn_rows),
            )

        def ff_pieces(layer):
            return (
                dot_nt(ff_pick, up_weight[layer]).astype(BF),
                dot_nn(ff_pick, down_projection_weight[layer]).astype(BF),
            )

        def attn_mats(parts):
            return [part.reshape(4, -1, width) for part in parts]

        def ff_mats(parts):
            flat = [part.reshape(-1, width) for part in parts]
            return (flat[0], flat[2]), (flat[1], flat[3])

        def relative(gathered):
            by_dp = jnp.take(gathered, jnp.bitwise_xor(jnp.arange(dp), dp_index), axis=0)
            both = jnp.take(by_dp, jnp.bitwise_xor(jnp.arange(mp), mp_index), axis=1)
            both = both.reshape((dp // 2, 2) + gathered.shape[1:])
            return both[:, 0], both[:, 1]

        def forward_halo(value):
            return lax.ppermute(value, "mp", [(i, i + 1) for i in range(mp - 1)])

        def backward_halo(value):
            return lax.ppermute(value, "mp", [(i + 1, i) for i in range(mp - 1)])

        gains = norm_gain.reshape(layers, 2, 1, width)
        shifts = norm_bias.reshape(layers, 2, 1, width)
        middle = attn_rows // 2
        in_blocks = (
            middle % 16 == 0 and groups == 4 and block == 2 * RIDERS * dp and width == 3 * window
        )

        piece = attn_piece(0)
        attn0 = Gather(links, piece[:middle], piece[middle:])
        attn0.start_mp()
        ff0 = Gather(links, *ff_pieces(0))
        ff0.start_mp()
        later = jnp.concatenate((attn_piece(1),) + ff_pieces(1), axis=0)
        x, normed = enter_kernel(order, tokens.reshape(rows, width), gains[0, 0], shifts[0, 0])
        (normed,) = order.pin(normed)
        halo = forward_halo(normed)

        seg_pad = jnp.concatenate([jnp.full((seqs, window), -1, segments.dtype), segments], axis=1)
        seg_keys = lax.dynamic_slice_in_dim(seg_pad, mp_index * block, block + window, axis=1)
        seg_q = seg_keys[:, window:].reshape(seqs, block, 1)
        seg_k = seg_keys.reshape(seqs, 1, block + window)

        attn0.wait_mp()
        attn0.start()
        attn0.wait()
        attn0.start()
        ff0.wait_mp()
        ff0.start()
        (later,) = order.pin(later)
        later = lax.all_gather(later, ("g", "c", "mp"), axis=0, tiled=False)
        (halo,) = order.pin(halo)
        attn0.wait_all()
        ff0.wait()
        ff0.start()
        attn0.start_cores()
        w_attn0 = attn_mats(attn0.wait_cores())

        def attn(layer, x, normed, halo, w_attn):
            sg, ratio, rden, v, wsum, carried, mixed, masked, x1, normed_b = attn_forward(
                order, layer, place, x, normed, halo, w_attn, pos_bias, seg_q, seg_k,
                gains[layer, 1], shifts[layer, 1],
            )
            return x1, normed_b, (sg, ratio, rden, v, wsum, carried, masked), (mixed, normed, halo)

        x1_0, normed_b0, saved0, rows0 = attn(0, x, normed, halo, w_attn0)
        ff0.wait_all()
        ff0.start_cores()
        own_up, own_down = [value.reshape(-1, width) for value in ff0.values]
        act0, slope0, x_half = ff_forward(order, x1_0, normed_b0, own_up, own_down, None, None)
        ups0, downs0 = ff_mats(ff0.wait_cores())
        act0o, slope0o, x2, normed2 = ff_forward(
            order, x_half, normed_b0, ups0[1], downs0[1], gains[1, 0], shifts[1, 0]
        )
        (normed2,) = order.pin(normed2)
        halo2 = forward_halo(normed2)
        (later,) = order.pin(later)
        if in_blocks:
            w_attn1 = w_ff1 = [later.reshape((groups, 2, mp) + later.shape[1:])]
        else:
            own, other = relative(later.reshape((dp, mp) + later.shape[1:]))
            cuts = [middle, attn_rows, attn_rows + ff_rows]
            own_a, own_b, own_up, own_down = jnp.split(own, cuts, axis=2)
            other_a, other_b, other_up, other_down = jnp.split(other, cuts, axis=2)
            w_attn1 = attn_mats([own_a, own_b, other_a, other_b])
            w_ff1 = sum(ff_mats([own_up, own_down, other_up, other_down]), ())
        (halo2,) = order.pin(halo2)
        x1_1, normed_b1, saved1, rows1 = attn(1, x2, normed2, halo2, w_attn1)

        wide1, grad1, grad1_low, gain_b1, shift_b1, output = ff_backward(
            order, place, x1_1, normed_b1, w_ff1, groups, cotangent.reshape(rows, width), gains[1, 1], None
        )
        wide1 = ReduceWide(links, wide1)
        gq, gk, gv, band1, dn_own1, back1 = attn_backward(order, place, grad1_low, w_attn1, *saved1)
        (back1,) = order.pin(back1)
        back1 = backward_halo(back1)
        r_attn1 = Reduce(
            links, attn_weight_grads(order, place, gq, gk, gv, *rows1, grad1_low, band1, mp, in_blocks, in_blocks)
        )
        (back1,) = order.pin(back1)
        r_attn1.start_cores()
        grad2, gain_a1, shift_a1 = leave_attn(order, x2, grad1, dn_own1, back1, gains[1, 0])
        r_attn1.wait_cores()
        r_attn1.start()
        wide0, grad3, grad3_low, gain_b0, shift_b0 = ff_backward(
            order, place, x1_0, normed_b0, ups0 + downs0, groups, grad2, gains[0, 1],
            (act0, slope0, act0o, slope0o),
        )
        r_attn1.wait()
        wide0 = ReduceWide(links, wide0)
        r_attn1.start()
        z_of_1 = mp_index if in_blocks else None
        attn1_sum, riders1 = r_attn1.wait_all()
        z_ff1 = ReduceMp(links, wide1.wait(), z_of_1, None)
        gq, gk, gv, band0, dn_own0, back0 = attn_backward(order, place, grad3_low, w_attn0, *saved0)
        r_attn0 = Reduce(
            links, attn_weight_grads(order, place, gq, gk, gv, *rows0, grad3_low, band0, mp, False, in_blocks)
        )
        sum1_ff, _ = z_ff1.wait()
        r_attn0.start_cores()
        r_attn0.wait_cores()
        r_attn0.start()
        (back0,) = order.pin(back0)
        back0 = backward_halo(back0)
        r_attn0.wait()
        (back0,) = order.pin(back0)
        r_attn0.start()
        z_attn1 = ReduceMp(links, attn1_sum, z_of_1, riders1)
        grad4, gain_a0, shift_a0 = leave_attn(order, x, grad3, dn_own0, back0, gains[0, 0])
        norms = jnp.concatenate(
            [gain_a0, gain_b0, shift_a0, shift_b0, gain_a1, gain_b1, shift_a1, shift_b1], axis=0
        )

        def two_parts(value):
            high = value.astype(BF)
            return jnp.concatenate([high, (value - high.astype(F32)).astype(BF)], axis=0)

        def one_part(value):
            count = value.shape[0] // 2
            return value[:count].astype(F32) + value[count:].astype(F32)

        attn0_sum, riders0 = r_attn0.wait_all()
        sum1_attn, riders1 = z_attn1.wait()
        (full1,) = order.pin(jnp.concatenate([sum1_attn, sum1_ff] + riders1, axis=0))
        full1 = lax.all_gather(full1, DP, axis=0, tiled=False)
        z_0 = ReduceMp(
            links, attn0_sum + wide0.wait(), None, jnp.concatenate([two_parts(norms), riders0], axis=0)
        )
        (full1,) = order.pin(full1)

        cut = 2 * norms.shape[0]

        def finish(layer, full, previous):
            if in_blocks:
                norm_rows = 0 if len(full) == 1 else cut
                return finish_layer(
                    order, layer, layers, place, full, channels, hidden, mp, window, norm_rows, previous
                )
            if len(full) == 1:
                owner = jnp.arange(dp)
                joined = full[0]
            else:
                owner = jnp.bitwise_xor(jnp.arange(dp), dp_index)
                joined = jnp.stack(full).reshape(2, groups, -1, width)
                joined = jnp.swapaxes(joined, 0, 1).reshape(dp, -1, width)
            joined = joined[:, : attn_rows + 2 * ff_rows]
            attn_part, up_part, down_part = jnp.split(joined, [attn_rows, attn_rows + ff_rows], axis=1)

            def rows_of(value):
                return value.reshape(-1, width)

            def place_of(count):
                spots = (owner[:, None] * count + jnp.arange(count)[None, :]).reshape(-1, 1)
                return (spots == jnp.arange(dp * count)[None, :]).astype(BF)

            attn_place = place_of(attn_rows).reshape(-1, 4, channels)
            ff_place = place_of(ff_rows)
            values = (
                jnp.einsum("pd,pmc->mcd", rows_of(attn_part), attn_place[:, :3], preferred_element_type=F32),
                dot_tn(attn_place[:, 3], rows_of(attn_part)),
                dot_tn(rows_of(up_part), ff_place),
                dot_tn(ff_place, rows_of(down_part)),
            )
            if previous is None:
                previous = [jnp.zeros((layers,) + value.shape, F32) for value in values]
            return [
                lax.dynamic_update_index_in_dim(kept, value, layer, 0)
                for kept, value in zip(previous, values)
            ]

        big = finish(1, [full1], None)
        sum0, riders0 = z_0.wait()
        norms = [one_part(part[:cut]) for part in riders0]
        while len(norms) > 1:
            norms = [norms[k] + norms[k + 1] for k in range(0, len(norms), 2)]
        (sum0,) = order.pin(
            jnp.concatenate([sum0, two_parts(norms[0])] + [part[cut:] for part in riders0], axis=0)
        )
        full0 = [sum0] + [links.swap(sum0, DP, 2 * p) for p in range(1, groups)]
        others = [links.swap(sum0, DP, 1)]
        others[0], *full0[1:] = order.pin(others[0], *full0[1:])
        full0[1:] = order.pin(*full0[1:])
        others += [links.swap(part, DP, 1) for part in full0[1:]]
        others[1:] = order.pin(*others[1:])
        qkv_out, out_out, up_out, down_out, *small = finish(0, full0 + others, big)
        if in_blocks:
            band_sum, norm_sum = small
        else:
            count = attn_rows + 2 * ff_rows
            sums = [one_part(part[count : count + cut]) for pair in zip(full0, others) for part in pair]
            while len(sums) > 1:
                sums = [sums[k] + sums[k + 1] for k in range(0, len(sums), 2)]
            norm_sum = sums[0]
            band_sum = lax.all_gather(
                lax.psum(jnp.stack([band0, band1]), DP), "mp", axis=1, tiled=True
            )
        norm_sum = norm_sum.reshape(layers, 4, width)
        return (
            output.reshape(tokens.shape),
            grad4.reshape(tokens.shape),
            jnp.transpose(qkv_out, (0, 1, 3, 2)),
            out_out,
            up_out,
            down_out,
            norm_sum[:, :2],
            norm_sum[:, 2:],
            band_sum,
        )

    return shards


def solution(mesh):
    dp, mp = mesh.shape["dp"], mesh.shape["mp"]
    inner = Mesh(mesh.devices.reshape(dp // 2, 2, mp), DP + ("mp",))
    placed = (
        P(DP, "mp", None),
        P(DP, None),
        P(None, None, None, "mp"),
        P(None, "mp", None),
        P(None, None, "mp"),
        P(None, "mp", None),
        P(),
        P(),
        P(),
        P(DP, "mp", None),
    )
    return jax.shard_map(
        make_shards(dp, mp),
        mesh=inner,
        in_specs=placed,
        out_specs=(
            P(DP, "mp", None),
            P(DP, "mp", None),
            P(None, None, None, "mp"),
            P(None, "mp", None),
            P(None, None, "mp"),
            P(None, "mp", None),
            P(),
            P(),
            P(),
        ),
        check_vma=False,
    )
```

```python
import functools

import jax
import jax.numpy as jnp
from jax import lax
from jax.experimental import pallas as pl
from jax.experimental.pallas import tpu as pltpu
from jax.sharding import Mesh, PartitionSpec as P

BF = jnp.bfloat16
F32 = jnp.float32
VMEM_LIMIT = 58 * 1024 * 1024
TOKEN = (8, 128)
SUB = 256
RIDERS = 16
GELU_A = 0.7978845608028654
GELU_B = 0.044715


def dot_nt(lhs, rhs):
    return lax.dot_general(lhs, rhs, (((1,), (1,)), ((), ())), preferred_element_type=F32)


def dot_nn(lhs, rhs):
    return lax.dot_general(lhs, rhs, (((1,), (0,)), ((), ())), preferred_element_type=F32)


def dot_tn(lhs, rhs):
    return lax.dot_general(lhs, rhs, (((0,), (0,)), ((), ())), preferred_element_type=F32)


def normalize(values):
    center = values - jnp.mean(values, axis=-1, keepdims=True)
    inv_std = lax.rsqrt(jnp.mean(center * center, axis=-1, keepdims=True) + 1e-05)
    return center * inv_std, inv_std


def norm_back(grad_out, normal, inv_std, gain):
    grad_normal = grad_out * gain
    mean_one = jnp.mean(grad_normal, axis=-1, keepdims=True)
    mean_two = jnp.mean(grad_normal * normal, axis=-1, keepdims=True)
    return inv_std * (grad_normal - mean_one - normal * mean_two)


def whole(shape):
    return pl.BlockSpec(shape, lambda *_: (0,) * len(shape))


def call(order, body, grid, in_specs, out_specs, out_shape, scratch=(), prefetch=0, name=None, aliases=None):
    first = prefetch + len(in_specs)
    second = first + 1 + len(out_specs)
    anywhere = pl.BlockSpec(memory_space=pl.ANY)

    def with_token(*refs):
        return body(*refs[:first], *refs[first + 1 : second], *refs[second + 1 :])

    kernel = pl.pallas_call(
        with_token,
        grid_spec=pltpu.PrefetchScalarGridSpec(
            num_scalar_prefetch=prefetch,
            grid=grid,
            in_specs=list(in_specs) + [anywhere],
            out_specs=list(out_specs) + [anywhere],
            scratch_shapes=list(scratch),
        ),
        out_shape=list(out_shape) + [shape_of(TOKEN, jnp.int32)],
        input_output_aliases={**(aliases or {}), first: len(out_specs)},
        compiler_params=pltpu.CompilerParams(
            dimension_semantics=("arbitrary",) * len(grid), vmem_limit_bytes=VMEM_LIMIT
        ),
        cost_estimate=pl.CostEstimate(flops=0, bytes_accessed=0, transcendentals=0),
        name=name,
    )

    def run(*operands):
        *results, order.token = kernel(*operands, order.token)
        return results

    return run


def shape_of(shape, dtype):
    return jax.ShapeDtypeStruct(shape, dtype)


def tie(*arrays):
    count = len(arrays)
    return pl.pallas_call(
        lambda *refs: None,
        out_shape=[shape_of(a.shape, a.dtype) for a in arrays],
        in_specs=[pl.BlockSpec(memory_space=pl.ANY)] * count,
        out_specs=[pl.BlockSpec(memory_space=pl.ANY)] * count,
        input_output_aliases={i: i for i in range(count)},
        cost_estimate=pl.CostEstimate(flops=0, bytes_accessed=0, transcendentals=0),
        name="tie",
    )(*arrays)


def enter_kernel(order, tokens, gain, shift):
    rows, width = tokens.shape

    def body(t_ref, g_ref, s_ref, x_ref, n_ref):
        x = t_ref[...].astype(F32)
        x_ref[...] = x
        normal, _ = normalize(x)
        n_ref[...] = (normal * g_ref[...] + s_ref[...]).astype(BF)

    return call(
        order,
        body,
        (1,),
        [whole((rows, width)), whole((1, width)), whole((1, width))],
        [whole((rows, width)), whole((rows, width))],
        [shape_of((rows, width), F32), shape_of((rows, width), BF)],
        name="enter",
    )(tokens, gain, shift)


def reverse_lanes(values):
    count = values.shape[1]
    flip = (
        lax.broadcasted_iota(jnp.int32, (count, count), 0)
        + lax.broadcasted_iota(jnp.int32, (count, count), 1)
        == count - 1
    ).astype(BF)
    high = values.astype(BF)
    rest = values - high.astype(F32)
    middle = rest.astype(BF)
    last = (rest - middle.astype(F32)).astype(BF)
    return (dot_nn(high, flip) + dot_nn(middle, flip)) + dot_nn(last, flip)


def attn_specs(weights):
    if len(weights) == 4:
        return [whole(w.shape) for w in weights]
    groups, _, mp, count, width = weights[0].shape
    return [pl.BlockSpec((groups, 1, mp, count // 3, width), lambda i, place: (0, place[3] ^ i, 0, 0, 0))]


def by_half(step, refs, place_ref, part):
    if len(refs) == 1:
        width = refs[0].shape[-1]
        part(lambda m: refs[0][m, 0].reshape(-1, width))
        return
    for half in range(2):
        wa, wb = refs[2 * half], refs[2 * half + 1]

        def mat(m, wa=wa, wb=wb):
            return jnp.concatenate([wa[place_ref[0] ^ m], wb[place_ref[0] ^ m]], axis=0)

        pl.when(step == half)(functools.partial(part, mat))


def attn_forward(order, layer, place, x, normed, halo, weights, pos_bias, seg_q, seg_k, gain, shift):
    rows, width = x.shape
    seqs, block, _ = seg_q.shape
    keys = seg_k.shape[2]
    window = keys - block
    half = width // 2

    def body(place_ref, x_ref, n_ref, h_ref, *rest):
        w_refs, rest = rest[: len(weights)], rest[len(weights) :]
        (band_ref, sq_ref, sk_ref, g_ref, s_ref, sg_ref, ratio_ref, rden_ref, v_ref, wsum_ref, car_ref, mixed_ref,
         masked_ref, x1_ref, nb_ref, mix) = rest
        step = pl.program_id(0)

        @pl.when(step == 0)
        def _():
            band = reverse_lanes(jnp.exp(band_ref[0]))
            band = jnp.concatenate([band, jnp.zeros((block, block), F32)], axis=1)
            spread = pltpu.roll(band, 1, axis=1, stride=1, stride_axis=0)
            for s in range(seqs):
                masked = jnp.where(sq_ref[s] == sk_ref[s], spread, 0.0)
                masked_ref[s] = masked
                mix[s] = masked.astype(BF)
            x1_ref[...] = x_ref[...]

        def part(mat):
            wq, wk, wv = mat(0), mat(1), mat(2)
            q = dot_nt(n_ref[...], wq)
            sg = jax.nn.sigmoid(q)
            sg_ref[...] = sg.astype(BF)
            carried, wsum = [], []
            for r, source in enumerate((h_ref, n_ref)):
                here = slice(r * rows, (r + 1) * rows)
                kexp = jnp.exp(dot_nt(source[...], wk))
                v = dot_nt(source[...], wv)
                v_ref[here] = v.astype(BF)
                wsum.append(kexp.astype(BF))
                carried.append((kexp * v).astype(BF))
                wsum_ref[here] = wsum[r]
                car_ref[here] = carried[r]
            mixed = []
            for s in range(seqs):
                here = slice(s * block, (s + 1) * block)
                num = dot_nn(mix[s, :, :window], carried[0][here]) + dot_nn(mix[s, :, window:], carried[1][here])
                den = dot_nn(mix[s, :, :window], wsum[0][here]) + dot_nn(mix[s, :, window:], wsum[1][here])
                rden = 1.0 / den
                ratio = num * rden
                rden_ref[here] = rden.astype(BF)
                ratio_ref[here] = ratio.astype(BF)
                mixed.append((sg[here] * ratio).astype(BF))
            mixed = jnp.concatenate(mixed, axis=0)
            mixed_ref[...] = mixed
            x1_ref[...] += dot_nn(mixed, mat(3))

        by_half(step, w_refs, place_ref, part)

        @pl.when(step == 1)
        def _():
            normal, _ = normalize(x1_ref[...])
            nb_ref[...] = (normal * g_ref[...] + s_ref[...]).astype(BF)

    def col(n):
        return pl.BlockSpec((n, half), lambda i, *_: (0, i))

    return call(
        order,
        body,
        (2,),
        [whole((rows, width))] * 3
        + attn_specs(weights)
        + [pl.BlockSpec((1, block, window), lambda i, place: (layer, place[1], 0))]
        + [whole((seqs, block, 1)), whole((seqs, 1, keys)), whole((1, width)), whole((1, width))],
        [col(rows)] * 3 + [col(2 * rows)] * 3 + [col(rows)]
        + [whole((seqs, block, keys)), whole((rows, width)), whole((rows, width))],
        [shape_of((rows, width), BF)] * 3
        + [shape_of((2 * rows, width), BF)] * 3
        + [
            shape_of((rows, width), BF),
            shape_of((seqs, block, keys), F32),
            shape_of((rows, width), F32),
            shape_of((rows, width), BF),
        ],
        [pltpu.VMEM((seqs, block, keys), BF)],
        prefetch=1,
        name="attn_fwd",
    )(place, x, normed, halo, *weights, pos_bias, seg_q, seg_k, gain, shift)


def gelu_both(pre):
    square = pre * pre
    upper = 0.5 + 0.5 * jnp.tanh(pre * (GELU_A + (GELU_A * GELU_B) * square))
    act = pre * upper
    return act, upper + act * (1.0 - upper) * (2.0 * GELU_A + (6.0 * GELU_A * GELU_B) * square)


def chunk_specs(chunk, width, per_half):
    own = pl.BlockSpec((chunk, width), lambda i, *_: (jnp.minimum(i, per_half - 1), 0))
    other = pl.BlockSpec((chunk, width), lambda i, *_: (jnp.maximum(i - per_half, 0), 0))
    return own, other


def ff_forward(order, x1, normed, up, down, gain, shift):
    rows, width = x1.shape
    half = up.shape[0]
    chunk = width
    steps = half // chunk
    last = gain is not None

    def body(x_ref, n_ref, u, d, *rest):
        if last:
            g_ref, s_ref, act_ref, slope_ref, x2_ref, next_ref = rest
        else:
            act_ref, slope_ref, x2_ref = rest
        step = pl.program_id(0)

        @pl.when(step == 0)
        def _():
            x2_ref[...] = x_ref[...]

        for k in range(chunk // SUB):
            here = slice(k * SUB, (k + 1) * SUB)
            act, slope = gelu_both(dot_nt(n_ref[...], u[here]))
            act_ref[:, here] = act.astype(BF)
            slope_ref[:, here] = slope.astype(BF)
        x2_ref[...] += dot_nn(act_ref[...], d[...])

        if last:

            @pl.when(step == steps - 1)
            def _():
                normal, _ = normalize(x2_ref[...])
                next_ref[...] = (normal * g_ref[...] + s_ref[...]).astype(BF)

    full = whole((rows, width))
    weight = pl.BlockSpec((chunk, width), lambda i: (i, 0))
    col = pl.BlockSpec((rows, chunk), lambda i: (0, i))
    return call(
        order,
        body,
        (steps,),
        [full, full, weight, weight] + [whole((1, width))] * (2 if last else 0),
        [col, col, full] + ([full] if last else []),
        [shape_of((rows, half), BF)] * 2 + [shape_of((rows, width), F32)] + ([shape_of((rows, width), BF)] if last else []),
        name="ff_fwd",
    )(x1, normed, up, down, *((gain, shift) if last else ()))


def ff_specs(weights, chunk):
    if len(weights) == 4:
        half, width = weights[0].shape
        own, other = chunk_specs(chunk, width, half // chunk)
        return list(weights), [own, other, own, other]
    groups, _, mp, count, width = weights[0].shape
    rows = count // 3
    per = chunk // (mp * rows)
    steps = groups // per

    def spec(which):
        return pl.BlockSpec(
            (per, 1, mp, rows, width), lambda i, place: (i % steps, place[3] ^ (i // steps), 0, which, 0)
        )

    return [weights[0], weights[0]], [spec(1), spec(2)]


def ff_backward(order, place, x1, normed, weights, groups, grad, gain, saved):
    rows, width = x1.shape
    chunk = width
    half = 2 * width
    per_half = half // chunk
    steps = 2 * per_half
    operands, w_specs = ff_specs(weights, chunk)
    group_rows = half // groups
    per = chunk // group_rows
    fresh = saved is None
    relative = len(weights) == 4

    def body(place_ref, x_ref, n_ref, *rest):
        rest = list(rest)
        w_refs = [rest.pop(0) for _ in operands]
        grad_ref, g_ref = rest.pop(0), rest.pop(0)
        kept = [] if fresh else [rest.pop(0) for _ in range(4)]
        wg_ref = rest.pop(0)
        g1_ref, ga_ref, gg_ref, gs_ref = rest[:4]
        out_ref = rest[4] if fresh else None
        low, dn, pre_grads = rest[5:8] if fresh else rest[4:7]
        acts, x2 = rest[8:] if fresh else (None, None)
        step = pl.program_id(0)

        @pl.when(step == 0)
        def _():
            low[...] = grad_ref[...].astype(BF)
            dn[...] = jnp.zeros_like(dn)
            if fresh:
                x2[...] = x_ref[...]

        def part(u_ref, d_ref, act_ref, slope_ref):
            u = u_ref[...].reshape(chunk, width)
            d = d_ref[...].reshape(chunk, width)
            for k in range(chunk // SUB):
                here = slice(k * SUB, (k + 1) * SUB)
                if fresh:
                    act, slope = gelu_both(dot_nt(n_ref[...], u[here]))
                    acts[:, here] = act.astype(BF)
                else:
                    slope = slope_ref[:, here].astype(F32)
                pre_grads[:, here] = (dot_nt(low[...], d[here]) * slope).astype(BF)
            pre_grad = pre_grads[...]
            act = acts[...] if fresh else act_ref[...]
            if fresh:
                x2[...] += dot_nn(act, d)
            dn[...] += dot_nn(pre_grad, u)
            for which, value in ((0, dot_tn(pre_grad, n_ref[...])), (1, dot_tn(act, low[...]))):
                value = value.astype(BF)
                for k in range(per):
                    spot = (place_ref[5] ^ k) if relative else k
                    wg_ref[spot, 0, which] = value[k * group_rows : (k + 1) * group_rows]

        own_w, other_w = (w_refs[::2], w_refs[1::2]) if relative else (w_refs, w_refs)
        if fresh:
            pl.when(step < per_half)(lambda: part(*own_w, None, None))
            pl.when(step >= per_half)(lambda: part(*other_w, None, None))
        else:
            pl.when(step < per_half)(lambda: part(*own_w, *kept[:2]))
            pl.when(step >= per_half)(lambda: part(*other_w, *kept[2:]))

        @pl.when(step == steps - 1)
        def _():
            if fresh:
                out_ref[...] = x2[...].astype(BF)
            normal, inv = normalize(x_ref[...])
            total = dn[...]
            g1 = grad_ref[...] + norm_back(total, normal, inv, g_ref[...])
            g1_ref[...] = g1
            ga_ref[...] = g1.astype(BF)
            gg_ref[...] = jnp.sum(total * normal, axis=0, keepdims=True)
            gs_ref[...] = jnp.sum(total, axis=0, keepdims=True)

    full = whole((rows, width))
    def own_index(i):
        return jnp.minimum(i, per_half - 1)

    def other_index(i):
        return jnp.maximum(i - per_half, 0)

    wg_specs = [
        pl.BlockSpec(
            (per, 1, 2, group_rows, width),
            lambda i, place: (
                (place[4] ^ (i % per_half)) if relative else i % per_half, place[3] ^ (i // per_half), 0, 0, 0,
            ),
        )
    ]
    wg_shapes = [shape_of((groups, 2, 2, group_rows, width), BF)]
    kept_specs = [
        pl.BlockSpec((rows, chunk), lambda i, *_, index=index: (0, index(i)))
        for index in (() if fresh else (own_index, own_index, other_index, other_index))
    ]
    return call(
        order,
        body,
        (steps,),
        [full, full] + w_specs + [full, whole((1, width))] + kept_specs,
        wg_specs + [full, full, whole((1, width)), whole((1, width))] + ([full] if fresh else []),
        wg_shapes
        + [
            shape_of((rows, width), F32),
            shape_of((rows, width), BF),
            shape_of((1, width), F32),
            shape_of((1, width), F32),
        ]
        + ([shape_of((rows, width), BF)] if fresh else []),
        [pltpu.VMEM((rows, width), BF), pltpu.VMEM((rows, width), F32), pltpu.VMEM((rows, chunk), BF)]
        + ([pltpu.VMEM((rows, chunk), BF), pltpu.VMEM((rows, width), F32)] if fresh else []),
        prefetch=1,
        name="ff_bwd",
    )(place, x1, normed, *operands, grad, gain, *(() if fresh else saved))


def attn_backward(order, place, grad_low, weights, sg, ratio, rden, v, wsum, carried, masked):
    rows, width = grad_low.shape
    seqs, block, keys = masked.shape
    window = keys - block
    half = width // 2

    def body(place_ref, ga_ref, *rest):
        w_refs, rest = rest[: len(weights)], rest[len(weights) :]
        (sg_ref, ratio_ref, rden_ref, v_ref, wsum_ref, car_ref, masked_ref,
         gq_ref, gk_ref, gv_ref, band_ref, own_ref, halo_ref, mix_t, wgrad, dn) = rest
        step = pl.program_id(0)

        @pl.when(step == 0)
        def _():
            for s in range(seqs):
                mix_t[s] = masked_ref[s].T.astype(BF)
            wgrad[...] = jnp.zeros_like(wgrad)
            dn[...] = jnp.zeros_like(dn)

        def part(mat):
            gm = dot_nt(ga_ref[...], mat(3))
            sig = sg_ref[...].astype(F32)
            rat = ratio_ref[...].astype(F32)
            scaled = gm * sig
            gq = (scaled * rat * (1.0 - sig)).astype(BF)
            gq_ref[...] = gq
            gnum_f = scaled * rden_ref[...].astype(F32)
            gnum = gnum_f.astype(BF)
            gden = (-gnum_f * rat).astype(BF)
            wq, wk, wv = mat(0), mat(1), mat(2)
            dn[rows:] += dot_nn(gq, wq)
            for r in range(2):
                for s in range(seqs):
                    here = slice(s * block, (s + 1) * block)
                    there = slice(r * rows + s * block, r * rows + (s + 1) * block)
                    cols = slice(r * window, r * window + block)
                    ke = wsum_ref[there].astype(F32)
                    gcar = dot_nn(mix_t[s, cols], gnum[here])
                    gsum = dot_nn(mix_t[s, cols], gden[here])
                    gv = (gcar * ke).astype(BF)
                    gk = ((gcar * v_ref[there].astype(F32) + gsum) * ke).astype(BF)
                    gk_ref[there] = gk
                    gv_ref[there] = gv
                    wgrad[s, :, cols] += dot_nt(gnum[here], car_ref[there]) + dot_nt(gden[here], wsum_ref[there])
                    dn[there] += dot_nn(gk, wk) + dot_nn(gv, wv)

        by_half(step, w_refs, place_ref, part)

        @pl.when(step == 1)
        def _():
            total = wgrad[0] * masked_ref[0]
            for s in range(1, seqs):
                total = total + wgrad[s] * masked_ref[s]
            lane_row = lax.broadcasted_iota(jnp.int32, (block, keys), 0) + 1
            bit = 1
            while bit <= block:
                rolled = pltpu.roll(total, keys - bit, axis=1)
                total = jnp.where((lane_row & bit) != 0, rolled, total)
                bit *= 2
            band_ref[...] = reverse_lanes(total[:, :window])
            halo_ref[...] = dn[:rows].astype(BF)
            own_ref[...] = dn[rows:]

    def col(n):
        return pl.BlockSpec((n, half), lambda i, *_: (0, i))

    return call(
        order,
        body,
        (2,),
        [whole((rows, width))]
        + attn_specs(weights)
        + [col(rows)] * 3 + [col(2 * rows)] * 3 + [whole((seqs, block, keys))],
        [col(rows), col(2 * rows), col(2 * rows), whole((block, window)), whole((rows, width)), whole((rows, width))],
        [
            shape_of((rows, width), BF),
            shape_of((2 * rows, width), BF),
            shape_of((2 * rows, width), BF),
            shape_of((block, window), F32),
            shape_of((rows, width), F32),
            shape_of((rows, width), BF),
        ],
        [
            pltpu.VMEM((seqs, keys, block), BF),
            pltpu.VMEM((seqs, block, keys), F32),
            pltpu.VMEM((2 * rows, width), F32),
        ],
        prefetch=1,
        name="attn_bwd",
    )(place, grad_low, *weights, sg, ratio, rden, v, wsum, carried, masked)


def attn_weight_grads(order, place, gq, gk, gv, mixed, normed, halo, grad_low, band, mp, mixed_rows, riding):
    rows, width = gq.shape
    half = width // 2
    quarter = half // 2
    piece = quarter // mp
    window = band.shape[1]
    share = 2 * RIDERS
    def body(place_ref, gq_ref, gk_ref, gv_ref, mixed_ref, n_ref, h_ref, ga_ref, band_ref, *out_refs):
        def part(outs, core):
            if riding:
                for p in range(4):
                    owner = 2 * (place_ref[2] ^ p) + (place_ref[3] ^ core)
                    start = pl.multiple_of(owner * share, share)
                    rows_here = band_ref[pl.ds(start, share)].astype(BF)
                    outs[0][p, quarter:] = jnp.concatenate(
                        [rows_here[:RIDERS], rows_here[RIDERS:], jnp.zeros((RIDERS, width - 2 * window), BF)], axis=1
                    )

            def put(m, value):
                low = value.astype(BF)
                spot = place_ref[0] ^ m
                if not mixed_rows:
                    outs[0][spot, :quarter] = low[:quarter]
                    outs[1][spot] = low[quarter:]
                    return
                for z in range(mp):
                    for k in range(2):
                        outs[k][spot, z * piece : (z + 1) * piece] = low[
                            (2 * z + k) * piece : (2 * z + k + 1) * piece
                        ]

            put(0, dot_tn(gq_ref[...], n_ref[...]))
            for m, ref in ((1, gk_ref), (2, gv_ref)):
                put(m, dot_tn(ref[:rows], h_ref[...]) + dot_tn(ref[rows:], n_ref[...]))
            put(3, dot_tn(mixed_ref[...], ga_ref[...]))

        pl.when(pl.program_id(0) == 0)(lambda: part(out_refs[:2], 0))
        pl.when(pl.program_id(0) == 1)(lambda: part(out_refs[2:], 1))

    def col(n):
        return pl.BlockSpec((n, half), lambda i, *_: (0, i))

    shapes = [(4, quarter + (RIDERS if riding else 0), width), (4, quarter, width)] * 2
    return call(
        order,
        body,
        (2,),
        [col(rows), col(2 * rows), col(2 * rows), col(rows)] + [whole((rows, width))] * 3 + [whole(band.shape)],
        [whole(shape) for shape in shapes],
        [shape_of(shape, BF) for shape in shapes],
        prefetch=1,
        name="attn_wgrad",
    )(place, gq, gk, gv, mixed, normed, halo, grad_low, band)


def leave_attn(order, x, grad, own, back, gain):
    rows, width = x.shape

    def body(x_ref, g_ref, o_ref, b_ref, gain_ref, out_ref, gg_ref, gs_ref):
        normal, inv = normalize(x_ref[...])
        total = o_ref[...] + b_ref[...].astype(F32)
        out_ref[...] = g_ref[...] + norm_back(total, normal, inv, gain_ref[...])
        gg_ref[...] = jnp.sum(total * normal, axis=0, keepdims=True)
        gs_ref[...] = jnp.sum(total, axis=0, keepdims=True)

    return call(
        order,
        body,
        (1,),
        [whole((rows, width))] * 4 + [whole((1, width))],
        [whole((rows, width)), whole((1, width)), whole((1, width))],
        [shape_of((rows, width), F32)] + [shape_of((1, width), F32)] * 2,
        name="leave",
    )(x, grad, own, back, gain)


def finish_layer(order, layer, layers, place, parts, channels, hidden, mp, window, norm_rows, previous):
    width = parts[0].shape[-1]
    total = 4 * channels
    single = len(parts) == 1
    groups = len(parts) // 4
    dp = parts[0].shape[0] if single else 2 * groups
    piece = total // dp
    share = 2 * RIDERS
    block = dp * share

    def body(place_ref, *rest):
        p_refs, rest = rest[: len(parts)], rest[len(parts) :]
        qkv_ref, out_ref, up_ref, down_ref, band_ref = rest[:5]
        up = rest[-1]

        def put(owner, rows_of, ff_rows_of, bands):
            start = pl.multiple_of(owner * piece, piece)
            mat = owner * piece // channels
            inner = pl.multiple_of(owner * piece - mat * channels, piece)
            value = rows_of(0, piece).astype(F32)

            @pl.when(mat < 3)
            def _():
                qkv_ref[0, jnp.minimum(mat, 2), pl.ds(inner, piece)] = value

            @pl.when(mat == 3)
            def _():
                out_ref[0, pl.ds(inner, piece)] = value

            up[pl.ds(start, piece)] = ff_rows_of(0, piece).astype(F32)
            down_ref[0, pl.ds(start, piece)] = ff_rows_of(piece, piece).astype(F32)
            for p in range(mp):
                band = rows_of(bands + p * RIDERS, RIDERS).astype(F32)
                first = pl.multiple_of((place_ref[1] ^ p) * block + owner * share, share)
                band_ref[0, pl.ds(first, RIDERS)] = band[:, :window]
                band_ref[0, pl.ds(first + RIDERS, RIDERS)] = band[:, window : 2 * window]

        if single:
            for owner in range(dp):
                put(
                    jnp.int32(owner),
                    lambda start, count, owner=owner: p_refs[0][owner, start : start + count],
                    lambda start, count, owner=owner: p_refs[0][owner, piece + start : piece + start + count],
                    3 * piece,
                )
        else:
            for core in range(2):
                for p in range(groups):
                    ref, ff_ref = p_refs[core * groups + p], p_refs[(2 + core) * groups + p]
                    owner = 2 * (place_ref[2] ^ p) + (place_ref[3] ^ core)
                    put(
                        owner,
                        lambda start, count, ref=ref: ref[start : start + count],
                        lambda start, count, ref=ff_ref: ref[start : start + count],
                        piece + norm_rows,
                    )
        up_ref[0] = up[...].T
        if norm_rows:
            half = norm_rows // 2
            sums = []
            for p in range(groups):
                for core in range(2):
                    rows = p_refs[core * groups + p][piece : piece + norm_rows].astype(F32)
                    sums.append(rows[:half] + rows[half:])
            while len(sums) > 1:
                sums = [sums[k] + sums[k + 1] for k in range(0, len(sums), 2)]
            rest[5][...] = sums[0]

    shapes = [
        (layers, 3, channels, width),
        (layers, channels, width),
        (layers, width, hidden),
        (layers, hidden, width),
        (layers, mp * block, window),
    ]

    def here(shape):
        return pl.BlockSpec((1,) + shape[1:], lambda i, *_: (layer,) + (0,) * (len(shape) - 1))

    extra = list(previous) if previous is not None else []
    anywhere = pl.BlockSpec(memory_space=pl.ANY)
    return call(
        order,
        lambda *refs: body(*refs[: 1 + len(parts)], *refs[1 + len(parts) + len(extra) :]),
        (1,),
        [whole(part.shape) for part in parts] + [anywhere] * len(extra),
        [here(shape) for shape in shapes] + ([whole((norm_rows // 2, width))] if norm_rows else []),
        [shape_of(shape, F32) for shape in shapes]
        + ([shape_of((norm_rows // 2, width), F32)] if norm_rows else []),
        [pltpu.VMEM((total, width), F32)],
        prefetch=1,
        name="finish",
        aliases={1 + len(parts) + k: k for k in range(len(extra))},
    )(place, *parts, *extra)


DP = ("g", "c")


class Order:
    def __init__(self):
        self.token = jnp.zeros(TOKEN, jnp.int32)

    def pin(self, *arrays):
        *arrays, self.token = tie(*arrays, self.token)
        return arrays


class Links:
    def __init__(self, order, dp, mp):
        self.order = order
        self.dp = dp
        self.mp = mp
        bits = [1 << k for k in range(1, dp.bit_length() - 1)]
        self.routes = (bits, bits[::-1])

    def swap(self, value, axis, bit):
        size = self.dp if axis == DP else self.mp
        return lax.ppermute(value, axis, [(i, i ^ bit) for i in range(size)])


class Spread:
    def __init__(self, links, values):
        self.links = links
        self.values = list(values)
        self.phase = 0
        self.have = [[], []]

    def start(self):
        self.values = self.links.order.pin(*self.values)
        self.coming = [
            self.links.swap(value, DP, route[self.phase])
            for value, route in zip(self.values, self.links.routes)
        ]

    def wait(self):
        coming = self.links.order.pin(*self.coming)
        for k in range(2):
            bit = self.links.routes[k][self.phase]
            place = sum(1 for other in self.have[k] if other > bit)
            self.values[k] = jnp.stack([self.values[k], coming[k]], axis=place)
            self.have[k].append(bit)
        self.phase += 1

    def wait_all(self):
        self.wait()
        while self.phase < len(self.links.routes[0]):
            self.start()
            self.wait()

    def start_cores(self):
        self.values = self.links.order.pin(*self.values)
        self.coming = [self.links.swap(value, DP, 1) for value in self.values]

    def wait_cores(self):
        return self.values + self.links.order.pin(*self.coming)


class Gather(Spread):
    def __init__(self, links, piece_a, piece_b):
        super().__init__(links, ())
        self.cut = piece_a.shape[0]
        self.piece = jnp.concatenate([piece_a, piece_b], axis=0)

    def start_mp(self):
        (self.piece,) = self.links.order.pin(self.piece)
        self.coming_mp = [self.links.swap(self.piece, "mp", p) for p in range(1, self.links.mp)]

    def wait_mp(self):
        parts = [self.piece] + self.links.order.pin(*self.coming_mp)
        self.values = [
            jnp.stack([part[: self.cut] for part in parts]),
            jnp.stack([part[self.cut :] for part in parts]),
        ]


class Reduce:
    def __init__(self, links, halves):
        self.links = links
        self.halves = halves
        self.phase = 0

    def start_cores(self):
        others = self.links.order.pin(*self.halves[2:])
        self.coming = [self.links.swap(other, DP, 1) for other in others]

    def wait_cores(self):
        coming = self.links.order.pin(*self.coming)
        mp = self.links.mp
        self.have = [sorted(route, reverse=True) for route in self.links.routes]
        lead = (2,) * len(self.have[0])
        self.terms = []
        for own, other in zip(self.halves[:2], coming):
            shape = lead + (-1, own.shape[-1])
            self.terms.append([own.reshape(shape), other.reshape(shape)])

    def start(self):
        sends = []
        for k in range(2):
            place = self.have[k].index(self.links.routes[1 - k][self.phase])
            sends.append(
                sum(lax.index_in_dim(term, 1, place, keepdims=False).astype(F32) for term in self.terms[k]).astype(BF)
            )
            self.terms[k] = [lax.index_in_dim(term, 0, place, keepdims=False) for term in self.terms[k]]
        sends = self.links.order.pin(*sends)
        self.coming = [
            self.links.swap(sends[k], DP, self.links.routes[1 - k][self.phase]) for k in range(2)
        ]

    def wait(self):
        coming = self.links.order.pin(*self.coming)
        for k in range(2):
            self.terms[k].append(coming[k])
            self.have[k].remove(self.links.routes[1 - k][self.phase])
        self.phase += 1

    def wait_all(self):
        self.wait()
        while self.phase < len(self.links.routes[0]):
            self.start()
            self.wait()
        sums = [sum(term.astype(F32) for term in terms).astype(BF) for terms in self.terms]
        count = sums[1].shape[0]
        mp = self.links.mp
        riders = sums[0][count:]
        return [value[:count].reshape(mp, count // mp, -1) for value in sums], riders


class ReduceWide:
    def __init__(self, links, grads):
        self.links = links
        (grads,) = links.order.pin(grads.reshape((links.dp,) + grads.shape[2:]))
        self.sums = lax.psum_scatter(grads, DP, scatter_dimension=0, tiled=True)

    def wait(self):
        (sums,) = self.links.order.pin(self.sums)
        sums = sums.reshape(2, self.links.mp, -1, sums.shape[-1])
        return [sums[0], sums[1]]


class ReduceMp:
    def __init__(self, links, arrays, index, riders):
        self.links = links
        joined = jnp.concatenate(arrays, axis=1)
        self.count = joined.shape[1]
        if index is None:
            blocks = [joined[p] for p in range(links.mp)]
        else:
            blocks = [
                lax.dynamic_index_in_dim(joined, jnp.bitwise_xor(index, p), 0, keepdims=False)
                for p in range(links.mp)
            ]
        if riders is not None:
            blocks = [jnp.concatenate([block, riders], axis=0) for block in blocks]
        self.kept, *sends = links.order.pin(*blocks)
        self.coming = [links.swap(send, "mp", p + 1) for p, send in enumerate(sends)]

    def wait(self):
        parts = [self.kept] + self.links.order.pin(*self.coming)
        total = sum(part[: self.count].astype(F32) for part in parts)
        return total.astype(BF), [part[self.count :] for part in parts]


def make_shards(dp, mp):
    def shards(
        tokens,
        segments,
        qkv_weight,
        out_weight,
        up_weight,
        down_projection_weight,
        norm_gain,
        norm_bias,
        pos_bias,
        cotangent,
    ):
        seqs, block, width = tokens.shape
        layers = qkv_weight.shape[0]
        window = pos_bias.shape[2]
        channels = qkv_weight.shape[-1]
        hidden = up_weight.shape[-1]
        rows = seqs * block
        group = lax.axis_index("g")
        core = lax.axis_index("c")
        dp_index = group * 2 + core
        mp_index = lax.axis_index("mp")
        order = Order()
        links = Links(order, dp, mp)
        attn_rows = 4 * channels // dp
        ff_rows = hidden // dp
        groups = dp // 2
        per = max(1, width // (mp * ff_rows))
        place = jnp.stack([group // (groups // 4), mp_index, group, core, group // per, group % per]).astype(jnp.int32)

        def picks(count, offset, length):
            return (
                lax.broadcasted_iota(jnp.int32, (count, length), 0) + offset
                == lax.broadcasted_iota(jnp.int32, (count, length), 1)
            ).astype(BF)

        ff_pick = picks(ff_rows, dp_index * ff_rows, hidden)

        def attn_piece(layer):
            by_channel = jnp.transpose(qkv_weight[layer], (0, 2, 1)).reshape(3 * channels, width)
            start = dp_index * attn_rows
            inner = start - 3 * channels
            return jnp.where(
                inner < 0,
                lax.dynamic_slice_in_dim(by_channel, jnp.minimum(start, 3 * channels - attn_rows), attn_rows),
                lax.dynamic_slice_in_dim(out_weight[layer], jnp.maximum(inner, 0), attn_rows),
            )

        def ff_pieces(layer):
            return (
                dot_nt(ff_pick, up_weight[layer]).astype(BF),
                dot_nn(ff_pick, down_projection_weight[layer]).astype(BF),
            )

        def attn_mats(parts):
            return [part.reshape(4, -1, width) for part in parts]

        def ff_mats(parts):
            flat = [part.reshape(-1, width) for part in parts]
            return (flat[0], flat[2]), (flat[1], flat[3])

        def relative(gathered):
            by_dp = jnp.take(gathered, jnp.bitwise_xor(jnp.arange(dp), dp_index), axis=0)
            both = jnp.take(by_dp, jnp.bitwise_xor(jnp.arange(mp), mp_index), axis=1)
            both = both.reshape((dp // 2, 2) + gathered.shape[1:])
            return both[:, 0], both[:, 1]

        def forward_halo(value):
            return lax.ppermute(value, "mp", [(i, i + 1) for i in range(mp - 1)])

        def backward_halo(value):
            return lax.ppermute(value, "mp", [(i + 1, i) for i in range(mp - 1)])

        gains = norm_gain.reshape(layers, 2, 1, width)
        shifts = norm_bias.reshape(layers, 2, 1, width)
        middle = attn_rows // 2
        in_blocks = (
            middle % 16 == 0 and groups == 4 and block == 2 * RIDERS * dp and width == 3 * window
        )

        piece = attn_piece(0)
        attn0 = Gather(links, piece[:middle], piece[middle:])
        attn0.start_mp()
        ff0 = Gather(links, *ff_pieces(0))
        ff0.start_mp()
        later = jnp.concatenate((attn_piece(1),) + ff_pieces(1), axis=0)
        x, normed = enter_kernel(order, tokens.reshape(rows, width), gains[0, 0], shifts[0, 0])
        (normed,) = order.pin(normed)
        halo = forward_halo(normed)

        seg_pad = jnp.concatenate([jnp.full((seqs, window), -1, segments.dtype), segments], axis=1)
        seg_keys = lax.dynamic_slice_in_dim(seg_pad, mp_index * block, block + window, axis=1)
        seg_q = seg_keys[:, window:].reshape(seqs, block, 1)
        seg_k = seg_keys.reshape(seqs, 1, block + window)

        attn0.wait_mp()
        attn0.start()
        attn0.wait()
        attn0.start()
        ff0.wait_mp()
        ff0.start()
        (later,) = order.pin(later)
        later = lax.all_gather(later, ("g", "c", "mp"), axis=0, tiled=False)
        (halo,) = order.pin(halo)
        attn0.wait_all()
        ff0.wait()
        ff0.start()
        attn0.start_cores()
        w_attn0 = attn_mats(attn0.wait_cores())

        def attn(layer, x, normed, halo, w_attn):
            sg, ratio, rden, v, wsum, carried, mixed, masked, x1, normed_b = attn_forward(
                order, layer, place, x, normed, halo, w_attn, pos_bias, seg_q, seg_k,
                gains[layer, 1], shifts[layer, 1],
            )
            return x1, normed_b, (sg, ratio, rden, v, wsum, carried, masked), (mixed, normed, halo)

        x1_0, normed_b0, saved0, rows0 = attn(0, x, normed, halo, w_attn0)
        ff0.wait_all()
        ff0.start_cores()
        own_up, own_down = [value.reshape(-1, width) for value in ff0.values]
        act0, slope0, x_half = ff_forward(order, x1_0, normed_b0, own_up, own_down, None, None)
        ups0, downs0 = ff_mats(ff0.wait_cores())
        act0o, slope0o, x2, normed2 = ff_forward(
            order, x_half, normed_b0, ups0[1], downs0[1], gains[1, 0], shifts[1, 0]
        )
        (normed2,) = order.pin(normed2)
        halo2 = forward_halo(normed2)
        (later,) = order.pin(later)
        if in_blocks:
            w_attn1 = w_ff1 = [later.reshape((groups, 2, mp) + later.shape[1:])]
        else:
            own, other = relative(later.reshape((dp, mp) + later.shape[1:]))
            cuts = [middle, attn_rows, attn_rows + ff_rows]
            own_a, own_b, own_up, own_down = jnp.split(own, cuts, axis=2)
            other_a, other_b, other_up, other_down = jnp.split(other, cuts, axis=2)
            w_attn1 = attn_mats([own_a, own_b, other_a, other_b])
            w_ff1 = sum(ff_mats([own_up, own_down, other_up, other_down]), ())
        (halo2,) = order.pin(halo2)
        x1_1, normed_b1, saved1, rows1 = attn(1, x2, normed2, halo2, w_attn1)

        wide1, grad1, grad1_low, gain_b1, shift_b1, output = ff_backward(
            order, place, x1_1, normed_b1, w_ff1, groups, cotangent.reshape(rows, width), gains[1, 1], None
        )
        wide1 = ReduceWide(links, wide1)
        gq, gk, gv, band1, dn_own1, back1 = attn_backward(order, place, grad1_low, w_attn1, *saved1)
        (back1,) = order.pin(back1)
        back1 = backward_halo(back1)
        r_attn1 = Reduce(
            links, attn_weight_grads(order, place, gq, gk, gv, *rows1, grad1_low, band1, mp, in_blocks, in_blocks)
        )
        (back1,) = order.pin(back1)
        r_attn1.start_cores()
        grad2, gain_a1, shift_a1 = leave_attn(order, x2, grad1, dn_own1, back1, gains[1, 0])
        r_attn1.wait_cores()
        r_attn1.start()
        wide0, grad3, grad3_low, gain_b0, shift_b0 = ff_backward(
            order, place, x1_0, normed_b0, ups0 + downs0, groups, grad2, gains[0, 1],
            (act0, slope0, act0o, slope0o),
        )
        r_attn1.wait()
        wide0 = ReduceWide(links, wide0)
        r_attn1.start()
        z_of_1 = mp_index if in_blocks else None
        attn1_sum, riders1 = r_attn1.wait_all()
        z_1 = ReduceMp(links, attn1_sum + wide1.wait(), z_of_1, riders1)
        gq, gk, gv, band0, dn_own0, back0 = attn_backward(order, place, grad3_low, w_attn0, *saved0)
        r_attn0 = Reduce(
            links, attn_weight_grads(order, place, gq, gk, gv, *rows0, grad3_low, band0, mp, False, in_blocks)
        )
        sum1, riders1 = z_1.wait()
        r_attn0.start_cores()
        r_attn0.wait_cores()
        r_attn0.start()
        (back0,) = order.pin(back0)
        back0 = backward_halo(back0)
        r_attn0.wait()
        (back0,) = order.pin(back0)
        ff0_sum = wide0.wait()
        r_attn0.start()
        z_ff0 = ReduceMp(links, ff0_sum, None, None)
        (full1,) = order.pin(jnp.concatenate([sum1] + riders1, axis=0))
        full1 = lax.all_gather(full1, DP, axis=0, tiled=False)
        grad4, gain_a0, shift_a0 = leave_attn(order, x, grad3, dn_own0, back0, gains[0, 0])
        norms = jnp.concatenate(
            [gain_a0, gain_b0, shift_a0, shift_b0, gain_a1, gain_b1, shift_a1, shift_b1], axis=0
        )

        def two_parts(value):
            high = value.astype(BF)
            return jnp.concatenate([high, (value - high.astype(F32)).astype(BF)], axis=0)

        def one_part(value):
            count = value.shape[0] // 2
            return value[:count].astype(F32) + value[count:].astype(F32)

        attn0_sum, riders0 = r_attn0.wait_all()

        def regather(value):
            (value,) = order.pin(value)
            return [value] + [links.swap(value, DP, 2 * p) for p in range(1, groups)], [links.swap(value, DP, 1)]

        def regather_cores(parts):
            same, other = parts
            other[0], *same[1:] = order.pin(other[0], *same[1:])
            same[1:] = order.pin(*same[1:])
            return same, other + [links.swap(part, DP, 1) for part in same[1:]]

        def regather_wait(parts):
            same, other = parts
            return same + other[:1] + order.pin(*other[1:])

        ff0_sum, _ = z_ff0.wait()
        z_attn0 = ReduceMp(links, attn0_sum, None, jnp.concatenate([two_parts(norms), riders0], axis=0))
        ff0_parts = regather(ff0_sum)
        (full1,) = order.pin(full1)

        cut = 2 * norms.shape[0]

        def finish(layer, full, previous):
            if in_blocks:
                norm_rows = 0 if layer else cut
                return finish_layer(
                    order, layer, layers, place, full, channels, hidden, mp, window, norm_rows, previous
                )
            if len(full) == 1:
                owner = jnp.arange(dp)
                joined = full[0]
            else:
                owner = jnp.bitwise_xor(jnp.arange(dp), dp_index)
                joined = jnp.concatenate(
                    [jnp.stack(full[: 2 * groups])[:, :attn_rows], jnp.stack(full[2 * groups :])], axis=1
                ).reshape(2, groups, -1, width)
                joined = jnp.swapaxes(joined, 0, 1).reshape(dp, -1, width)
            joined = joined[:, : attn_rows + 2 * ff_rows]
            attn_part, up_part, down_part = jnp.split(joined, [attn_rows, attn_rows + ff_rows], axis=1)

            def rows_of(value):
                return value.reshape(-1, width)

            def place_of(count):
                spots = (owner[:, None] * count + jnp.arange(count)[None, :]).reshape(-1, 1)
                return (spots == jnp.arange(dp * count)[None, :]).astype(BF)

            attn_place = place_of(attn_rows).reshape(-1, 4, channels)
            ff_place = place_of(ff_rows)
            values = (
                jnp.einsum("pd,pmc->mcd", rows_of(attn_part), attn_place[:, :3], preferred_element_type=F32),
                dot_tn(attn_place[:, 3], rows_of(attn_part)),
                dot_tn(rows_of(up_part), ff_place),
                dot_tn(ff_place, rows_of(down_part)),
            )
            if previous is None:
                previous = [jnp.zeros((layers,) + value.shape, F32) for value in values]
            return [
                lax.dynamic_update_index_in_dim(kept, value, layer, 0)
                for kept, value in zip(previous, values)
            ]

        big = finish(1, [full1], None)
        sum0, riders0 = z_attn0.wait()
        norms = [one_part(part[:cut]) for part in riders0]
        while len(norms) > 1:
            norms = [norms[k] + norms[k + 1] for k in range(0, len(norms), 2)]
        sum0 = jnp.concatenate([sum0, two_parts(norms[0])] + [part[cut:] for part in riders0], axis=0)
        ff0_parts = regather_cores(ff0_parts)
        attn0_parts = regather(sum0)
        ff0_parts = regather_wait(ff0_parts)
        attn0_parts = regather_wait(regather_cores(attn0_parts))
        qkv_out, out_out, up_out, down_out, *small = finish(0, attn0_parts + ff0_parts, big)
        if in_blocks:
            band_sum, norm_sum = small
        else:
            sums = [one_part(attn0_parts[p + k][attn_rows : attn_rows + cut]) for p in range(groups) for k in (0, groups)]
            while len(sums) > 1:
                sums = [sums[k] + sums[k + 1] for k in range(0, len(sums), 2)]
            norm_sum = sums[0]
            band_sum = lax.all_gather(
                lax.psum(jnp.stack([band0, band1]), DP), "mp", axis=1, tiled=True
            )
        norm_sum = norm_sum.reshape(layers, 4, width)
        return (
            output.reshape(tokens.shape),
            grad4.reshape(tokens.shape),
            jnp.transpose(qkv_out, (0, 1, 3, 2)),
            out_out,
            up_out,
            down_out,
            norm_sum[:, :2],
            norm_sum[:, 2:],
            band_sum,
        )

    return shards


def solution(mesh):
    dp, mp = mesh.shape["dp"], mesh.shape["mp"]
    inner = Mesh(mesh.devices.reshape(dp // 2, 2, mp), DP + ("mp",))
    placed = (
        P(DP, "mp", None),
        P(DP, None),
        P(None, None, None, "mp"),
        P(None, "mp", None),
        P(None, None, "mp"),
        P(None, "mp", None),
        P(),
        P(),
        P(),
        P(DP, "mp", None),
    )
    return jax.shard_map(
        make_shards(dp, mp),
        mesh=inner,
        in_specs=placed,
        out_specs=(
            P(DP, "mp", None),
            P(DP, "mp", None),
            P(None, None, None, "mp"),
            P(None, "mp", None),
            P(None, None, "mp"),
            P(None, "mp", None),
            P(),
            P(),
            P(),
        ),
        check_vma=False,
    )
```

```python
import functools

import jax
import jax.numpy as jnp
from jax import lax
from jax.experimental import pallas as pl
from jax.experimental.pallas import tpu as pltpu
from jax.sharding import Mesh, PartitionSpec as P

BF = jnp.bfloat16
F32 = jnp.float32
VMEM_LIMIT = 58 * 1024 * 1024
TOKEN = (8, 128)
SUB = 256
RIDERS = 16
GELU_A = 0.7978845608028654
GELU_B = 0.044715


def dot_nt(lhs, rhs):
    return lax.dot_general(lhs, rhs, (((1,), (1,)), ((), ())), preferred_element_type=F32)


def dot_nn(lhs, rhs):
    return lax.dot_general(lhs, rhs, (((1,), (0,)), ((), ())), preferred_element_type=F32)


def dot_tn(lhs, rhs):
    return lax.dot_general(lhs, rhs, (((0,), (0,)), ((), ())), preferred_element_type=F32)


def normalize(values):
    center = values - jnp.mean(values, axis=-1, keepdims=True)
    inv_std = lax.rsqrt(jnp.mean(center * center, axis=-1, keepdims=True) + 1e-05)
    return center * inv_std, inv_std


def norm_back(grad_out, normal, inv_std, gain):
    grad_normal = grad_out * gain
    mean_one = jnp.mean(grad_normal, axis=-1, keepdims=True)
    mean_two = jnp.mean(grad_normal * normal, axis=-1, keepdims=True)
    return inv_std * (grad_normal - mean_one - normal * mean_two)


def whole(shape):
    return pl.BlockSpec(shape, lambda *_: (0,) * len(shape))


def call(
    order, body, grid, in_specs, out_specs, out_shape, scratch=(), prefetch=0, name=None, aliases=None,
    limit=None, near_in=(), near_out=(),
):
    first = prefetch + len(in_specs)
    second = first + 1 + len(out_specs)
    anywhere = pl.BlockSpec(memory_space=pl.ANY)

    def with_token(*refs):
        return body(*refs[:first], *refs[first + 1 : second], *refs[second + 1 :])

    kernel = pl.pallas_call(
        with_token,
        grid_spec=pltpu.PrefetchScalarGridSpec(
            num_scalar_prefetch=prefetch,
            grid=grid,
            in_specs=list(in_specs) + [anywhere],
            out_specs=list(out_specs) + [anywhere],
            scratch_shapes=list(scratch),
        ),
        out_shape=[
            shape if limit is None or k in near_out else pltpu.HBM(shape.shape, shape.dtype)
            for k, shape in enumerate(out_shape)
        ]
        + [shape_of(TOKEN, jnp.int32)],
        input_output_aliases={**(aliases or {}), first: len(out_specs)},
        compiler_params=pltpu.CompilerParams(
            dimension_semantics=("arbitrary",) * len(grid), vmem_limit_bytes=limit or VMEM_LIMIT
        ),
        cost_estimate=pl.CostEstimate(flops=0, bytes_accessed=0, transcendentals=0),
        name=name,
    )

    def run(*operands):
        placed = [
            operand
            if limit is None or k < prefetch or k - prefetch in near_in
            else pltpu.with_memory_space_constraint(operand, pltpu.HBM)
            for k, operand in enumerate(operands)
        ]
        *results, order.token = kernel(*placed, order.token)
        return results

    return run


def shape_of(shape, dtype):
    return jax.ShapeDtypeStruct(shape, dtype)


def tie(*arrays):
    count = len(arrays)
    return pl.pallas_call(
        lambda *refs: None,
        out_shape=[shape_of(a.shape, a.dtype) for a in arrays],
        in_specs=[pl.BlockSpec(memory_space=pl.ANY)] * count,
        out_specs=[pl.BlockSpec(memory_space=pl.ANY)] * count,
        input_output_aliases={i: i for i in range(count)},
        cost_estimate=pl.CostEstimate(flops=0, bytes_accessed=0, transcendentals=0),
        name="tie",
    )(*arrays)


def enter_kernel(order, tokens, gain, shift):
    rows, width = tokens.shape

    def body(t_ref, g_ref, s_ref, x_ref, n_ref):
        x = t_ref[...].astype(F32)
        x_ref[...] = x
        normal, _ = normalize(x)
        n_ref[...] = (normal * g_ref[...] + s_ref[...]).astype(BF)

    return call(
        order,
        body,
        (1,),
        [whole((rows, width)), whole((1, width)), whole((1, width))],
        [whole((rows, width)), whole((rows, width))],
        [shape_of((rows, width), F32), shape_of((rows, width), BF)],
        name="enter",
    )(tokens, gain, shift)


def reverse_lanes(values):
    count = values.shape[1]
    flip = (
        lax.broadcasted_iota(jnp.int32, (count, count), 0)
        + lax.broadcasted_iota(jnp.int32, (count, count), 1)
        == count - 1
    ).astype(BF)
    high = values.astype(BF)
    rest = values - high.astype(F32)
    middle = rest.astype(BF)
    last = (rest - middle.astype(F32)).astype(BF)
    return (dot_nn(high, flip) + dot_nn(middle, flip)) + dot_nn(last, flip)


THIRDS = 3


def attn_specs(weights):
    if len(weights) == 4:
        return [whole(w.shape) for w in weights]
    groups, two, mp, count, width = weights[0].shape
    return [pl.BlockSpec((groups, two, mp, count // 3, width), lambda i, place: (0, 0, 0, 0, 0))]


def by_third(step, refs, place_ref, part):
    def pieces(m):
        if len(refs) == 4:
            for ref in refs:
                yield lambda here, ref=ref: ref[place_ref[0] ^ m, here], ref.shape[1]
            return
        for half in range(2):
            for z in range(refs[0].shape[2]):
                yield lambda here, half=half, z=z: refs[0][m, place_ref[3] ^ half, z, here], refs[0].shape[3]

    def mat(m, third):
        count = sum(length for _, length in pieces(m)) // THIRDS
        first, last, at, out = third * count, (third + 1) * count, 0, []
        for read, length in pieces(m):
            low, high = max(first - at, 0), min(last - at, length)
            if low < high:
                out.append(read(slice(low, high)))
            at += length
        return jnp.concatenate(out, axis=0)

    for third in range(THIRDS):
        pl.when(step == third)(functools.partial(part, functools.partial(mat, third=third)))


def attn_forward(order, layer, place, x, normed, halo, weights, pos_bias, seg_q, seg_k, gain, shift):
    rows, width = x.shape
    seqs, block, _ = seg_q.shape
    keys = seg_k.shape[2]
    window = keys - block
    third = width // THIRDS

    def body(place_ref, x_ref, n_ref, h_ref, *rest):
        w_refs, rest = rest[: len(weights)], rest[len(weights) :]
        (band_ref, sq_ref, sk_ref, g_ref, s_ref, sg_ref, ratio_ref, rden_ref, v_ref, wsum_ref, car_ref, mixed_ref,
         masked_ref, x1_ref, nb_ref, mix) = rest
        step = pl.program_id(0)

        @pl.when(step == 0)
        def _():
            band = reverse_lanes(jnp.exp(band_ref[0]))
            band = jnp.concatenate([band, jnp.zeros((block, block), F32)], axis=1)
            spread = pltpu.roll(band, 1, axis=1, stride=1, stride_axis=0)
            for s in range(seqs):
                masked = jnp.where(sq_ref[s] == sk_ref[s], spread, 0.0)
                masked_ref[s] = masked
                mix[s] = masked.astype(BF)
            x1_ref[...] = x_ref[...]

        def part(mat):
            wq, wk, wv = mat(0), mat(1), mat(2)
            q = dot_nt(n_ref[...], wq)
            sg = jax.nn.sigmoid(q)
            sg_ref[...] = sg.astype(BF)
            carried, wsum = [], []
            for r, source in enumerate((h_ref, n_ref)):
                here = slice(r * rows, (r + 1) * rows)
                kexp = jnp.exp(dot_nt(source[...], wk))
                v = dot_nt(source[...], wv)
                v_ref[here] = v.astype(BF)
                wsum.append(kexp.astype(BF))
                carried.append((kexp * v).astype(BF))
                wsum_ref[here] = wsum[r]
                car_ref[here] = carried[r]
            mixed = []
            for s in range(seqs):
                here = slice(s * block, (s + 1) * block)
                num = dot_nn(mix[s, :, :window], carried[0][here]) + dot_nn(mix[s, :, window:], carried[1][here])
                den = dot_nn(mix[s, :, :window], wsum[0][here]) + dot_nn(mix[s, :, window:], wsum[1][here])
                rden = 1.0 / den
                ratio = num * rden
                rden_ref[here] = rden.astype(BF)
                ratio_ref[here] = ratio.astype(BF)
                mixed.append((sg[here] * ratio).astype(BF))
            mixed = jnp.concatenate(mixed, axis=0)
            mixed_ref[...] = mixed
            x1_ref[...] += dot_nn(mixed, mat(3))

        by_third(step, w_refs, place_ref, part)

        @pl.when(step == THIRDS - 1)
        def _():
            normal, _ = normalize(x1_ref[...])
            nb_ref[...] = (normal * g_ref[...] + s_ref[...]).astype(BF)

    def col(n):
        return pl.BlockSpec((n, third), lambda i, *_: (0, i))

    return call(
        order,
        body,
        (THIRDS,),
        [whole((rows, width))] * 3
        + attn_specs(weights)
        + [pl.BlockSpec((1, block, window), lambda i, place: (layer, place[1], 0))]
        + [whole((seqs, block, 1)), whole((seqs, 1, keys)), whole((1, width)), whole((1, width))],
        [col(rows)] * 3 + [col(2 * rows)] * 3 + [col(rows)]
        + [whole((seqs, block, keys)), whole((rows, width)), whole((rows, width))],
        [shape_of((rows, width), BF)] * 3
        + [shape_of((2 * rows, width), BF)] * 3
        + [
            shape_of((rows, width), BF),
            shape_of((seqs, block, keys), F32),
            shape_of((rows, width), F32),
            shape_of((rows, width), BF),
        ],
        [pltpu.VMEM((seqs, block, keys), BF)],
        prefetch=1,
        name="attn_fwd",
    )(place, x, normed, halo, *weights, pos_bias, seg_q, seg_k, gain, shift)


def gelu_both(pre):
    square = pre * pre
    upper = 0.5 + 0.5 * jnp.tanh(pre * (GELU_A + (GELU_A * GELU_B) * square))
    act = pre * upper
    return act, upper + act * (1.0 - upper) * (2.0 * GELU_A + (6.0 * GELU_A * GELU_B) * square)


def chunk_specs(chunk, width, per_half):
    own = pl.BlockSpec((chunk, width), lambda i, *_: (jnp.minimum(i, per_half - 1), 0))
    other = pl.BlockSpec((chunk, width), lambda i, *_: (jnp.maximum(i - per_half, 0), 0))
    return own, other


def ff_forward(order, x1, normed, up, down, gain, shift):
    rows, width = x1.shape
    half = up.shape[0]
    chunk = width
    steps = half // chunk
    last = gain is not None

    def body(x_ref, n_ref, u, d, *rest):
        if last:
            g_ref, s_ref, act_ref, slope_ref, x2_ref, next_ref = rest
        else:
            act_ref, slope_ref, x2_ref = rest
        step = pl.program_id(0)

        @pl.when(step == 0)
        def _():
            x2_ref[...] = x_ref[...]

        for k in range(chunk // SUB):
            here = slice(k * SUB, (k + 1) * SUB)
            act, slope = gelu_both(dot_nt(n_ref[...], u[here]))
            act_ref[:, here] = act.astype(BF)
            slope_ref[:, here] = slope.astype(BF)
        x2_ref[...] += dot_nn(act_ref[...], d[...])

        if last:

            @pl.when(step == steps - 1)
            def _():
                normal, _ = normalize(x2_ref[...])
                next_ref[...] = (normal * g_ref[...] + s_ref[...]).astype(BF)

    full = whole((rows, width))
    weight = pl.BlockSpec((chunk, width), lambda i: (i, 0))
    col = pl.BlockSpec((rows, chunk), lambda i: (0, i))
    return call(
        order,
        body,
        (steps,),
        [full, full, weight, weight] + [whole((1, width))] * (2 if last else 0),
        [col, col, full] + ([full] if last else []),
        [shape_of((rows, half), BF)] * 2 + [shape_of((rows, width), F32)] + ([shape_of((rows, width), BF)] if last else []),
        name="ff_fwd",
    )(x1, normed, up, down, *((gain, shift) if last else ()))


def ff_specs(weights, chunk):
    if len(weights) == 4:
        half, width = weights[0].shape
        own, other = chunk_specs(chunk, width, half // chunk)
        return list(weights), [own, other, own, other]
    groups, _, mp, count, width = weights[0].shape
    rows = count // 3
    per = chunk // (mp * rows)
    steps = groups // per

    def spec(which):
        return pl.BlockSpec(
            (per, 1, mp, rows, width), lambda i, place: (i % steps, place[3] ^ (i // steps), 0, which, 0)
        )

    return [weights[0], weights[0]], [spec(1), spec(2)]


def ff_backward(order, place, x1, normed, weights, groups, grad, gain, saved):
    rows, width = x1.shape
    chunk = width
    half = 2 * width
    per_half = half // chunk
    steps = 2 * per_half
    operands, w_specs = ff_specs(weights, chunk)
    group_rows = half // groups
    per = chunk // group_rows
    fresh = saved is None
    relative = len(weights) == 4

    def body(place_ref, x_ref, n_ref, *rest):
        rest = list(rest)
        w_refs = [rest.pop(0) for _ in operands]
        grad_ref, g_ref = rest.pop(0), rest.pop(0)
        kept = [] if fresh else [rest.pop(0) for _ in range(4)]
        wg_ref = rest.pop(0)
        g1_ref, ga_ref, gg_ref, gs_ref = rest[:4]
        out_ref = rest[4] if fresh else None
        low, dn, pre_grads = rest[5:8] if fresh else rest[4:7]
        acts, x2 = rest[8:] if fresh else (None, None)
        step = pl.program_id(0)

        @pl.when(step == 0)
        def _():
            low[...] = grad_ref[...].astype(BF)
            dn[...] = jnp.zeros_like(dn)
            if fresh:
                x2[...] = x_ref[...]

        def part(u_ref, d_ref, act_ref, slope_ref):
            u = u_ref[...].reshape(chunk, width)
            d = d_ref[...].reshape(chunk, width)
            for k in range(chunk // SUB):
                here = slice(k * SUB, (k + 1) * SUB)
                if fresh:
                    act, slope = gelu_both(dot_nt(n_ref[...], u[here]))
                    acts[:, here] = act.astype(BF)
                else:
                    slope = slope_ref[:, here].astype(F32)
                pre_grads[:, here] = (dot_nt(low[...], d[here]) * slope).astype(BF)
            pre_grad = pre_grads[...]
            act = acts[...] if fresh else act_ref[...]
            if fresh:
                x2[...] += dot_nn(act, d)
            dn[...] += dot_nn(pre_grad, u)
            for which, value in ((0, dot_tn(pre_grad, n_ref[...])), (1, dot_tn(act, low[...]))):
                value = value.astype(BF)
                for k in range(per):
                    spot = (place_ref[5] ^ k) if relative else k
                    wg_ref[spot, 0, which] = value[k * group_rows : (k + 1) * group_rows]

        own_w, other_w = (w_refs[::2], w_refs[1::2]) if relative else (w_refs, w_refs)
        if fresh:
            pl.when(step < per_half)(lambda: part(*own_w, None, None))
            pl.when(step >= per_half)(lambda: part(*other_w, None, None))
        else:
            pl.when(step < per_half)(lambda: part(*own_w, *kept[:2]))
            pl.when(step >= per_half)(lambda: part(*other_w, *kept[2:]))

        @pl.when(step == steps - 1)
        def _():
            if fresh:
                out_ref[...] = x2[...].astype(BF)
            normal, inv = normalize(x_ref[...])
            total = dn[...]
            g1 = grad_ref[...] + norm_back(total, normal, inv, g_ref[...])
            g1_ref[...] = g1
            ga_ref[...] = g1.astype(BF)
            gg_ref[...] = jnp.sum(total * normal, axis=0, keepdims=True)
            gs_ref[...] = jnp.sum(total, axis=0, keepdims=True)

    full = whole((rows, width))
    def own_index(i):
        return jnp.minimum(i, per_half - 1)

    def other_index(i):
        return jnp.maximum(i - per_half, 0)

    wg_specs = [
        pl.BlockSpec(
            (per, 1, 2, group_rows, width),
            lambda i, place: (
                (place[4] ^ (i % per_half)) if relative else i % per_half, place[3] ^ (i // per_half), 0, 0, 0,
            ),
        )
    ]
    wg_shapes = [shape_of((groups, 2, 2, group_rows, width), BF)]
    kept_specs = [
        pl.BlockSpec((rows, chunk), lambda i, *_, index=index: (0, index(i)))
        for index in (() if fresh else (own_index, own_index, other_index, other_index))
    ]
    return call(
        order,
        body,
        (steps,),
        [full, full] + w_specs + [full, whole((1, width))] + kept_specs,
        wg_specs + [full, full, whole((1, width)), whole((1, width))] + ([full] if fresh else []),
        wg_shapes
        + [
            shape_of((rows, width), F32),
            shape_of((rows, width), BF),
            shape_of((1, width), F32),
            shape_of((1, width), F32),
        ]
        + ([shape_of((rows, width), BF)] if fresh else []),
        [pltpu.VMEM((rows, width), BF), pltpu.VMEM((rows, width), F32), pltpu.VMEM((rows, chunk), BF)]
        + ([pltpu.VMEM((rows, chunk), BF), pltpu.VMEM((rows, width), F32)] if fresh else []),
        prefetch=1,
        name="ff_bwd",
    )(place, x1, normed, *operands, grad, gain, *(() if fresh else saved))


def attn_backward(order, place, grad_low, weights, sg, ratio, rden, v, wsum, carried, masked):
    rows, width = grad_low.shape
    seqs, block, keys = masked.shape
    window = keys - block
    third = width // THIRDS

    def body(place_ref, ga_ref, *rest):
        w_refs, rest = rest[: len(weights)], rest[len(weights) :]
        (sg_ref, ratio_ref, rden_ref, v_ref, wsum_ref, car_ref, masked_ref,
         gq_ref, gk_ref, gv_ref, band_ref, own_ref, halo_ref, mix_t, wgrad, dn) = rest
        step = pl.program_id(0)

        @pl.when(step == 0)
        def _():
            for s in range(seqs):
                mix_t[s] = masked_ref[s].T.astype(BF)
            wgrad[...] = jnp.zeros_like(wgrad)
            dn[...] = jnp.zeros_like(dn)

        def part(mat):
            gm = dot_nt(ga_ref[...], mat(3))
            sig = sg_ref[...].astype(F32)
            rat = ratio_ref[...].astype(F32)
            scaled = gm * sig
            gq = (scaled * rat * (1.0 - sig)).astype(BF)
            gq_ref[...] = gq
            gnum_f = scaled * rden_ref[...].astype(F32)
            gnum = gnum_f.astype(BF)
            gden = (-gnum_f * rat).astype(BF)
            wq, wk, wv = mat(0), mat(1), mat(2)
            dn[rows:] += dot_nn(gq, wq)
            for r in range(2):
                for s in range(seqs):
                    here = slice(s * block, (s + 1) * block)
                    there = slice(r * rows + s * block, r * rows + (s + 1) * block)
                    cols = slice(r * window, r * window + block)
                    ke = wsum_ref[there].astype(F32)
                    gcar = dot_nn(mix_t[s, cols], gnum[here])
                    gsum = dot_nn(mix_t[s, cols], gden[here])
                    gv = (gcar * ke).astype(BF)
                    gk = ((gcar * v_ref[there].astype(F32) + gsum) * ke).astype(BF)
                    gk_ref[there] = gk
                    gv_ref[there] = gv
                    wgrad[s, :, cols] += dot_nt(gnum[here], car_ref[there]) + dot_nt(gden[here], wsum_ref[there])
                    dn[there] += dot_nn(gk, wk) + dot_nn(gv, wv)

        by_third(step, w_refs, place_ref, part)

        @pl.when(step == THIRDS - 1)
        def _():
            total = wgrad[0] * masked_ref[0]
            for s in range(1, seqs):
                total = total + wgrad[s] * masked_ref[s]
            lane_row = lax.broadcasted_iota(jnp.int32, (block, keys), 0) + 1
            bit = 1
            while bit <= block:
                rolled = pltpu.roll(total, keys - bit, axis=1)
                total = jnp.where((lane_row & bit) != 0, rolled, total)
                bit *= 2
            band_ref[...] = reverse_lanes(total[:, :window])
            halo_ref[...] = dn[:rows].astype(BF)
            own_ref[...] = dn[rows:]

    def col(n):
        return pl.BlockSpec((n, third), lambda i, *_: (0, i))

    return call(
        order,
        body,
        (THIRDS,),
        [whole((rows, width))]
        + attn_specs(weights)
        + [col(rows)] * 3 + [col(2 * rows)] * 3 + [whole((seqs, block, keys))],
        [col(rows), col(2 * rows), col(2 * rows), whole((block, window)), whole((rows, width)), whole((rows, width))],
        [
            shape_of((rows, width), BF),
            shape_of((2 * rows, width), BF),
            shape_of((2 * rows, width), BF),
            shape_of((block, window), F32),
            shape_of((rows, width), F32),
            shape_of((rows, width), BF),
        ],
        [
            pltpu.VMEM((seqs, keys, block), BF),
            pltpu.VMEM((seqs, block, keys), F32),
            pltpu.VMEM((2 * rows, width), F32),
        ],
        prefetch=1,
        name="attn_bwd",
        limit=46 * 1024 * 1024,
        near_in=(0,),
        near_out=(0, 1, 2, 3, 4, 5),
    )(place, grad_low, *weights, sg, ratio, rden, v, wsum, carried, masked)


def attn_weight_grads(order, place, gq, gk, gv, mixed, normed, halo, grad_low, band, mp, mixed_rows, riding):
    rows, width = gq.shape
    half = width // 2
    quarter = half // 2
    piece = quarter // mp
    window = band.shape[1]
    share = 2 * RIDERS
    def body(place_ref, gq_ref, gk_ref, gv_ref, mixed_ref, n_ref, h_ref, ga_ref, band_ref, *out_refs):
        def part(outs, core):
            if riding:
                for p in range(4):
                    owner = 2 * (place_ref[2] ^ p) + (place_ref[3] ^ core)
                    start = pl.multiple_of(owner * share, share)
                    rows_here = band_ref[pl.ds(start, share)].astype(BF)
                    outs[0][p, quarter:] = jnp.concatenate(
                        [rows_here[:RIDERS], rows_here[RIDERS:], jnp.zeros((RIDERS, width - 2 * window), BF)], axis=1
                    )

            def put(m, value):
                low = value.astype(BF)
                spot = place_ref[0] ^ m
                if not mixed_rows:
                    outs[0][spot, :quarter] = low[:quarter]
                    outs[1][spot] = low[quarter:]
                    return
                for z in range(mp):
                    for k in range(2):
                        outs[k][spot, z * piece : (z + 1) * piece] = low[
                            (2 * z + k) * piece : (2 * z + k + 1) * piece
                        ]

            put(0, dot_tn(gq_ref[...], n_ref[...]))
            for m, ref in ((1, gk_ref), (2, gv_ref)):
                put(m, dot_tn(ref[:rows], h_ref[...]) + dot_tn(ref[rows:], n_ref[...]))
            put(3, dot_tn(mixed_ref[...], ga_ref[...]))

        pl.when(pl.program_id(0) == 0)(lambda: part(out_refs[:2], 0))
        pl.when(pl.program_id(0) == 1)(lambda: part(out_refs[2:], 1))

    def col(n):
        return pl.BlockSpec((n, half), lambda i, *_: (0, i))

    shapes = [(4, quarter + (RIDERS if riding else 0), width), (4, quarter, width)] * 2
    return call(
        order,
        body,
        (2,),
        [col(rows), col(2 * rows), col(2 * rows), col(rows)] + [whole((rows, width))] * 3 + [whole(band.shape)],
        [whole(shape) for shape in shapes],
        [shape_of(shape, BF) for shape in shapes],
        prefetch=1,
        name="attn_wgrad",
        limit=36 * 1024 * 1024,
        near_in=(0, 1, 2, 6, 7),
    )(place, gq, gk, gv, mixed, normed, halo, grad_low, band)


def leave_attn(order, x, grad, own, back, gain):
    rows, width = x.shape

    def body(x_ref, g_ref, o_ref, b_ref, gain_ref, out_ref, gg_ref, gs_ref):
        normal, inv = normalize(x_ref[...])
        total = o_ref[...] + b_ref[...].astype(F32)
        out_ref[...] = g_ref[...] + norm_back(total, normal, inv, gain_ref[...])
        gg_ref[...] = jnp.sum(total * normal, axis=0, keepdims=True)
        gs_ref[...] = jnp.sum(total, axis=0, keepdims=True)

    return call(
        order,
        body,
        (1,),
        [whole((rows, width))] * 4 + [whole((1, width))],
        [whole((rows, width)), whole((1, width)), whole((1, width))],
        [shape_of((rows, width), F32)] + [shape_of((1, width), F32)] * 2,
        name="leave",
    )(x, grad, own, back, gain)


def finish_layer(order, layer, layers, place, parts, channels, hidden, mp, window, norm_rows, previous):
    width = parts[0].shape[-1]
    total = 4 * channels
    single = len(parts) == 1
    groups = len(parts) // 4
    dp = parts[0].shape[0] if single else 2 * groups
    piece = total // dp
    share = 2 * RIDERS
    block = dp * share

    def body(place_ref, *rest):
        p_refs, rest = rest[: len(parts)], rest[len(parts) :]
        qkv_ref, out_ref, up_ref, down_ref, band_ref = rest[:5]
        up = rest[-1]

        def put(owner, rows_of, ff_rows_of, bands):
            start = pl.multiple_of(owner * piece, piece)
            mat = owner * piece // channels
            inner = pl.multiple_of(owner * piece - mat * channels, piece)
            value = rows_of(0, piece).astype(F32)

            @pl.when(mat < 3)
            def _():
                qkv_ref[0, jnp.minimum(mat, 2), pl.ds(inner, piece)] = value

            @pl.when(mat == 3)
            def _():
                out_ref[0, pl.ds(inner, piece)] = value

            up[pl.ds(start, piece)] = ff_rows_of(0, piece).astype(F32)
            down_ref[0, pl.ds(start, piece)] = ff_rows_of(piece, piece).astype(F32)
            for p in range(mp):
                band = rows_of(bands + p * RIDERS, RIDERS).astype(F32)
                first = pl.multiple_of((place_ref[1] ^ p) * block + owner * share, share)
                band_ref[0, pl.ds(first, RIDERS)] = band[:, :window]
                band_ref[0, pl.ds(first + RIDERS, RIDERS)] = band[:, window : 2 * window]

        if single:
            for owner in range(dp):
                put(
                    jnp.int32(owner),
                    lambda start, count, owner=owner: p_refs[0][owner, start : start + count],
                    lambda start, count, owner=owner: p_refs[0][owner, piece + start : piece + start + count],
                    3 * piece,
                )
        else:
            for core in range(2):
                for p in range(groups):
                    ref, ff_ref = p_refs[core * groups + p], p_refs[(2 + core) * groups + p]
                    owner = 2 * (place_ref[2] ^ p) + (place_ref[3] ^ core)
                    put(
                        owner,
                        lambda start, count, ref=ref: ref[start : start + count],
                        lambda start, count, ref=ff_ref: ref[start : start + count],
                        piece + norm_rows,
                    )
        up_ref[0] = up[...].T
        if norm_rows:
            half = norm_rows // 2
            sums = []
            for p in range(groups):
                for core in range(2):
                    rows = p_refs[core * groups + p][piece : piece + norm_rows].astype(F32)
                    sums.append(rows[:half] + rows[half:])
            while len(sums) > 1:
                sums = [sums[k] + sums[k + 1] for k in range(0, len(sums), 2)]
            rest[5][...] = sums[0]

    shapes = [
        (layers, 3, channels, width),
        (layers, channels, width),
        (layers, width, hidden),
        (layers, hidden, width),
        (layers, mp * block, window),
    ]

    def here(shape):
        return pl.BlockSpec((1,) + shape[1:], lambda i, *_: (layer,) + (0,) * (len(shape) - 1))

    extra = list(previous) if previous is not None else []
    anywhere = pl.BlockSpec(memory_space=pl.ANY)
    return call(
        order,
        lambda *refs: body(*refs[: 1 + len(parts)], *refs[1 + len(parts) + len(extra) :]),
        (1,),
        [whole(part.shape) for part in parts] + [anywhere] * len(extra),
        [here(shape) for shape in shapes] + ([whole((norm_rows // 2, width))] if norm_rows else []),
        [shape_of(shape, F32) for shape in shapes]
        + ([shape_of((norm_rows // 2, width), F32)] if norm_rows else []),
        [pltpu.VMEM((total, width), F32)],
        prefetch=1,
        name="finish",
        aliases={1 + len(parts) + k: k for k in range(len(extra))},
    )(place, *parts, *extra)


DP = ("g", "c")


class Order:
    def __init__(self):
        self.token = jnp.zeros(TOKEN, jnp.int32)

    def pin(self, *arrays):
        *arrays, self.token = tie(*arrays, self.token)
        return arrays


class Links:
    def __init__(self, order, dp, mp):
        self.order = order
        self.dp = dp
        self.mp = mp
        bits = [1 << k for k in range(1, dp.bit_length() - 1)]
        self.routes = (bits, bits[::-1])

    def swap(self, value, axis, bit):
        size = self.dp if axis == DP else self.mp
        return lax.ppermute(value, axis, [(i, i ^ bit) for i in range(size)])


class Spread:
    def __init__(self, links, values):
        self.links = links
        self.values = list(values)
        self.phase = 0
        self.have = [[], []]

    def start(self):
        self.values = self.links.order.pin(*self.values)
        self.coming = [
            self.links.swap(value, DP, route[self.phase])
            for value, route in zip(self.values, self.links.routes)
        ]

    def wait(self):
        coming = self.links.order.pin(*self.coming)
        for k in range(2):
            bit = self.links.routes[k][self.phase]
            place = sum(1 for other in self.have[k] if other > bit)
            self.values[k] = jnp.stack([self.values[k], coming[k]], axis=place)
            self.have[k].append(bit)
        self.phase += 1

    def wait_all(self):
        self.wait()
        while self.phase < len(self.links.routes[0]):
            self.start()
            self.wait()

    def start_cores(self):
        self.values = self.links.order.pin(*self.values)
        self.coming = [self.links.swap(value, DP, 1) for value in self.values]

    def wait_cores(self):
        return self.values + self.links.order.pin(*self.coming)


class Gather(Spread):
    def __init__(self, links, piece_a, piece_b):
        super().__init__(links, ())
        self.cut = piece_a.shape[0]
        self.piece = jnp.concatenate([piece_a, piece_b], axis=0)

    def start_mp(self):
        (self.piece,) = self.links.order.pin(self.piece)
        self.coming_mp = [self.links.swap(self.piece, "mp", p) for p in range(1, self.links.mp)]

    def wait_mp(self):
        parts = [self.piece] + self.links.order.pin(*self.coming_mp)
        self.values = [
            jnp.stack([part[: self.cut] for part in parts]),
            jnp.stack([part[self.cut :] for part in parts]),
        ]


class Reduce:
    def __init__(self, links, halves):
        self.links = links
        self.halves = halves
        self.phase = 0

    def start_cores(self):
        others = self.links.order.pin(*self.halves[2:])
        self.coming = [self.links.swap(other, DP, 1) for other in others]

    def wait_cores(self):
        coming = self.links.order.pin(*self.coming)
        mp = self.links.mp
        self.have = [sorted(route, reverse=True) for route in self.links.routes]
        lead = (2,) * len(self.have[0])
        self.terms = []
        for own, other in zip(self.halves[:2], coming):
            shape = lead + (-1, own.shape[-1])
            self.terms.append([own.reshape(shape), other.reshape(shape)])

    def start(self):
        sends = []
        for k in range(2):
            place = self.have[k].index(self.links.routes[1 - k][self.phase])
            sends.append(
                sum(lax.index_in_dim(term, 1, place, keepdims=False).astype(F32) for term in self.terms[k]).astype(BF)
            )
            self.terms[k] = [lax.index_in_dim(term, 0, place, keepdims=False) for term in self.terms[k]]
        sends = self.links.order.pin(*sends)
        self.coming = [
            self.links.swap(sends[k], DP, self.links.routes[1 - k][self.phase]) for k in range(2)
        ]

    def wait(self):
        coming = self.links.order.pin(*self.coming)
        for k in range(2):
            self.terms[k].append(coming[k])
            self.have[k].remove(self.links.routes[1 - k][self.phase])
        self.phase += 1

    def wait_all(self):
        self.wait()
        while self.phase < len(self.links.routes[0]):
            self.start()
            self.wait()
        sums = [sum(term.astype(F32) for term in terms).astype(BF) for terms in self.terms]
        count = sums[1].shape[0]
        mp = self.links.mp
        riders = sums[0][count:]
        return [value[:count].reshape(mp, count // mp, -1) for value in sums], riders


class ReduceWide:
    def __init__(self, links, grads):
        self.links = links
        (grads,) = links.order.pin(grads.reshape((links.dp,) + grads.shape[2:]))
        self.sums = lax.psum_scatter(grads, DP, scatter_dimension=0, tiled=True)

    def wait(self):
        (sums,) = self.links.order.pin(self.sums)
        sums = sums.reshape(2, self.links.mp, -1, sums.shape[-1])
        return [sums[0], sums[1]]


class ReduceMp:
    def __init__(self, links, arrays, index, riders):
        self.links = links
        joined = jnp.concatenate(arrays, axis=1)
        self.count = joined.shape[1]
        if index is None:
            blocks = [joined[p] for p in range(links.mp)]
        else:
            blocks = [
                lax.dynamic_index_in_dim(joined, jnp.bitwise_xor(index, p), 0, keepdims=False)
                for p in range(links.mp)
            ]
        if riders is not None:
            blocks = [jnp.concatenate([block, riders], axis=0) for block in blocks]
        self.kept, *sends = links.order.pin(*blocks)
        self.coming = [links.swap(send, "mp", p + 1) for p, send in enumerate(sends)]

    def wait(self):
        parts = [self.kept] + self.links.order.pin(*self.coming)
        total = sum(part[: self.count].astype(F32) for part in parts)
        return total.astype(BF), [part[self.count :] for part in parts]


def make_shards(dp, mp):
    def shards(
        tokens,
        segments,
        qkv_weight,
        out_weight,
        up_weight,
        down_projection_weight,
        norm_gain,
        norm_bias,
        pos_bias,
        cotangent,
    ):
        seqs, block, width = tokens.shape
        layers = qkv_weight.shape[0]
        window = pos_bias.shape[2]
        channels = qkv_weight.shape[-1]
        hidden = up_weight.shape[-1]
        rows = seqs * block
        group = lax.axis_index("g")
        core = lax.axis_index("c")
        dp_index = group * 2 + core
        mp_index = lax.axis_index("mp")
        order = Order()
        links = Links(order, dp, mp)
        attn_rows = 4 * channels // dp
        ff_rows = hidden // dp
        groups = dp // 2
        per = max(1, width // (mp * ff_rows))
        place = jnp.stack([group // (groups // 4), mp_index, group, core, group // per, group % per]).astype(jnp.int32)

        def picks(count, offset, length):
            return (
                lax.broadcasted_iota(jnp.int32, (count, length), 0) + offset
                == lax.broadcasted_iota(jnp.int32, (count, length), 1)
            ).astype(BF)

        ff_pick = picks(ff_rows, dp_index * ff_rows, hidden)

        def attn_piece(layer):
            by_channel = jnp.transpose(qkv_weight[layer], (0, 2, 1)).reshape(3 * channels, width)
            start = dp_index * attn_rows
            inner = start - 3 * channels
            return jnp.where(
                inner < 0,
                lax.dynamic_slice_in_dim(by_channel, jnp.minimum(start, 3 * channels - attn_rows), attn_rows),
                lax.dynamic_slice_in_dim(out_weight[layer], jnp.maximum(inner, 0), attn_rows),
            )

        def ff_pieces(layer):
            return (
                dot_nt(ff_pick, up_weight[layer]).astype(BF),
                dot_nn(ff_pick, down_projection_weight[layer]).astype(BF),
            )

        def attn_mats(parts):
            return [part.reshape(4, -1, width) for part in parts]

        def ff_mats(parts):
            flat = [part.reshape(-1, width) for part in parts]
            return (flat[0], flat[2]), (flat[1], flat[3])

        def relative(gathered):
            by_dp = jnp.take(gathered, jnp.bitwise_xor(jnp.arange(dp), dp_index), axis=0)
            both = jnp.take(by_dp, jnp.bitwise_xor(jnp.arange(mp), mp_index), axis=1)
            both = both.reshape((dp // 2, 2) + gathered.shape[1:])
            return both[:, 0], both[:, 1]

        def forward_halo(value):
            return lax.ppermute(value, "mp", [(i, i + 1) for i in range(mp - 1)])

        def backward_halo(value):
            return lax.ppermute(value, "mp", [(i + 1, i) for i in range(mp - 1)])

        gains = norm_gain.reshape(layers, 2, 1, width)
        shifts = norm_bias.reshape(layers, 2, 1, width)
        middle = attn_rows // 2
        in_blocks = (
            middle % 16 == 0 and groups == 4 and block == 2 * RIDERS * dp and width == 3 * window
        )

        piece = attn_piece(0)
        attn0 = Gather(links, piece[:middle], piece[middle:])
        attn0.start_mp()
        ff0 = Gather(links, *ff_pieces(0))
        ff0.start_mp()
        later = jnp.concatenate((attn_piece(1),) + ff_pieces(1), axis=0)
        x, normed = enter_kernel(order, tokens.reshape(rows, width), gains[0, 0], shifts[0, 0])
        (normed,) = order.pin(normed)
        halo = forward_halo(normed)

        seg_pad = jnp.concatenate([jnp.full((seqs, window), -1, segments.dtype), segments], axis=1)
        seg_keys = lax.dynamic_slice_in_dim(seg_pad, mp_index * block, block + window, axis=1)
        seg_q = seg_keys[:, window:].reshape(seqs, block, 1)
        seg_k = seg_keys.reshape(seqs, 1, block + window)

        attn0.wait_mp()
        attn0.start()
        attn0.wait()
        attn0.start()
        ff0.wait_mp()
        ff0.start()
        (later,) = order.pin(later)
        later = lax.all_gather(later, ("g", "c", "mp"), axis=0, tiled=False)
        (halo,) = order.pin(halo)
        attn0.wait_all()
        ff0.wait()
        ff0.start()
        attn0.start_cores()
        w_attn0 = attn_mats(attn0.wait_cores())

        def attn(layer, x, normed, halo, w_attn):
            sg, ratio, rden, v, wsum, carried, mixed, masked, x1, normed_b = attn_forward(
                order, layer, place, x, normed, halo, w_attn, pos_bias, seg_q, seg_k,
                gains[layer, 1], shifts[layer, 1],
            )
            return x1, normed_b, (sg, ratio, rden, v, wsum, carried, masked), (mixed, normed, halo)

        x1_0, normed_b0, saved0, rows0 = attn(0, x, normed, halo, w_attn0)
        ff0.wait_all()
        ff0.start_cores()
        own_up, own_down = [value.reshape(-1, width) for value in ff0.values]
        act0, slope0, x_half = ff_forward(order, x1_0, normed_b0, own_up, own_down, None, None)
        ups0, downs0 = ff_mats(ff0.wait_cores())
        act0o, slope0o, x2, normed2 = ff_forward(
            order, x_half, normed_b0, ups0[1], downs0[1], gains[1, 0], shifts[1, 0]
        )
        (normed2,) = order.pin(normed2)
        halo2 = forward_halo(normed2)
        (later,) = order.pin(later)
        if in_blocks:
            w_attn1 = w_ff1 = [later.reshape((groups, 2, mp) + later.shape[1:])]
        else:
            own, other = relative(later.reshape((dp, mp) + later.shape[1:]))
            cuts = [middle, attn_rows, attn_rows + ff_rows]
            own_a, own_b, own_up, own_down = jnp.split(own, cuts, axis=2)
            other_a, other_b, other_up, other_down = jnp.split(other, cuts, axis=2)
            w_attn1 = attn_mats([own_a, own_b, other_a, other_b])
            w_ff1 = sum(ff_mats([own_up, own_down, other_up, other_down]), ())
        (halo2,) = order.pin(halo2)
        x1_1, normed_b1, saved1, rows1 = attn(1, x2, normed2, halo2, w_attn1)

        wide1, grad1, grad1_low, gain_b1, shift_b1, output = ff_backward(
            order, place, x1_1, normed_b1, w_ff1, groups, cotangent.reshape(rows, width), gains[1, 1], None
        )
        wide1 = ReduceWide(links, wide1)
        gq, gk, gv, band1, dn_own1, back1 = attn_backward(order, place, grad1_low, w_attn1, *saved1)
        (back1,) = order.pin(back1)
        back1 = backward_halo(back1)
        r_attn1 = Reduce(
            links, attn_weight_grads(order, place, gq, gk, gv, *rows1, grad1_low, band1, mp, in_blocks, in_blocks)
        )
        (back1,) = order.pin(back1)
        r_attn1.start_cores()
        grad2, gain_a1, shift_a1 = leave_attn(order, x2, grad1, dn_own1, back1, gains[1, 0])
        r_attn1.wait_cores()
        r_attn1.start()
        wide0, grad3, grad3_low, gain_b0, shift_b0 = ff_backward(
            order, place, x1_0, normed_b0, ups0 + downs0, groups, grad2, gains[0, 1],
            (act0, slope0, act0o, slope0o),
        )
        r_attn1.wait()
        wide0 = ReduceWide(links, wide0)
        r_attn1.start()
        z_of_1 = mp_index if in_blocks else None
        attn1_sum, riders1 = r_attn1.wait_all()
        z_ff1 = ReduceMp(links, wide1.wait(), z_of_1, None)
        gq, gk, gv, band0, dn_own0, back0 = attn_backward(order, place, grad3_low, w_attn0, *saved0)
        r_attn0 = Reduce(
            links, attn_weight_grads(order, place, gq, gk, gv, *rows0, grad3_low, band0, mp, False, in_blocks)
        )
        sum1_ff, _ = z_ff1.wait()
        r_attn0.start_cores()
        z_attn1 = ReduceMp(links, attn1_sum, z_of_1, riders1)
        r_attn0.wait_cores()
        sum1, riders1 = z_attn1.wait()
        r_attn0.start()
        (back0,) = order.pin(back0)
        back0 = backward_halo(back0)
        (full1,) = order.pin(jnp.concatenate([sum1, sum1_ff] + riders1, axis=0))
        full1 = lax.all_gather(full1, DP, axis=0, tiled=False)
        r_attn0.wait()
        (back0,) = order.pin(back0)
        ff0_sum = wide0.wait()
        r_attn0.start()
        z_ff0 = ReduceMp(links, ff0_sum, None, None)
        grad4, gain_a0, shift_a0 = leave_attn(order, x, grad3, dn_own0, back0, gains[0, 0])
        norms = jnp.concatenate(
            [gain_a0, gain_b0, shift_a0, shift_b0, gain_a1, gain_b1, shift_a1, shift_b1], axis=0
        )

        def two_parts(value):
            high = value.astype(BF)
            return jnp.concatenate([high, (value - high.astype(F32)).astype(BF)], axis=0)

        def one_part(value):
            count = value.shape[0] // 2
            return value[:count].astype(F32) + value[count:].astype(F32)

        attn0_sum, riders0 = r_attn0.wait_all()

        def regather(value):
            (value,) = order.pin(value)
            return [value] + [links.swap(value, DP, 2 * p) for p in range(1, groups)], [links.swap(value, DP, 1)]

        def regather_cores(parts):
            same, other = parts
            other[0], *same[1:] = order.pin(other[0], *same[1:])
            same[1:] = order.pin(*same[1:])
            return same, other + [links.swap(part, DP, 1) for part in same[1:]]

        def regather_wait(parts):
            same, other = parts
            return same + other[:1] + order.pin(*other[1:])

        ff0_sum, _ = z_ff0.wait()
        z_attn0 = ReduceMp(links, attn0_sum, None, jnp.concatenate([two_parts(norms), riders0], axis=0))
        ff0_parts = regather(ff0_sum)
        (full1,) = order.pin(full1)

        cut = 2 * norms.shape[0]

        def finish(layer, full, previous):
            if in_blocks:
                norm_rows = 0 if layer else cut
                return finish_layer(
                    order, layer, layers, place, full, channels, hidden, mp, window, norm_rows, previous
                )
            if len(full) == 1:
                owner = jnp.arange(dp)
                joined = full[0]
            else:
                owner = jnp.bitwise_xor(jnp.arange(dp), dp_index)
                joined = jnp.concatenate(
                    [jnp.stack(full[: 2 * groups])[:, :attn_rows], jnp.stack(full[2 * groups :])], axis=1
                ).reshape(2, groups, -1, width)
                joined = jnp.swapaxes(joined, 0, 1).reshape(dp, -1, width)
            joined = joined[:, : attn_rows + 2 * ff_rows]
            attn_part, up_part, down_part = jnp.split(joined, [attn_rows, attn_rows + ff_rows], axis=1)

            def rows_of(value):
                return value.reshape(-1, width)

            def place_of(count):
                spots = (owner[:, None] * count + jnp.arange(count)[None, :]).reshape(-1, 1)
                return (spots == jnp.arange(dp * count)[None, :]).astype(BF)

            attn_place = place_of(attn_rows).reshape(-1, 4, channels)
            ff_place = place_of(ff_rows)
            values = (
                jnp.einsum("pd,pmc->mcd", rows_of(attn_part), attn_place[:, :3], preferred_element_type=F32),
                dot_tn(attn_place[:, 3], rows_of(attn_part)),
                dot_tn(rows_of(up_part), ff_place),
                dot_tn(ff_place, rows_of(down_part)),
            )
            if previous is None:
                previous = [jnp.zeros((layers,) + value.shape, F32) for value in values]
            return [
                lax.dynamic_update_index_in_dim(kept, value, layer, 0)
                for kept, value in zip(previous, values)
            ]

        big = finish(1, [full1], None)
        sum0, riders0 = z_attn0.wait()
        norms = [one_part(part[:cut]) for part in riders0]
        while len(norms) > 1:
            norms = [norms[k] + norms[k + 1] for k in range(0, len(norms), 2)]
        sum0 = jnp.concatenate([sum0, two_parts(norms[0])] + [part[cut:] for part in riders0], axis=0)
        ff0_parts = regather_cores(ff0_parts)
        attn0_parts = regather(sum0)
        ff0_parts = regather_wait(ff0_parts)
        attn0_parts = regather_wait(regather_cores(attn0_parts))
        qkv_out, out_out, up_out, down_out, *small = finish(0, attn0_parts + ff0_parts, big)
        if in_blocks:
            band_sum, norm_sum = small
        else:
            sums = [one_part(attn0_parts[p + k][attn_rows : attn_rows + cut]) for p in range(groups) for k in (0, groups)]
            while len(sums) > 1:
                sums = [sums[k] + sums[k + 1] for k in range(0, len(sums), 2)]
            norm_sum = sums[0]
            band_sum = lax.all_gather(
                lax.psum(jnp.stack([band0, band1]), DP), "mp", axis=1, tiled=True
            )
        norm_sum = norm_sum.reshape(layers, 4, width)
        return (
            output.reshape(tokens.shape),
            grad4.reshape(tokens.shape),
            jnp.transpose(qkv_out, (0, 1, 3, 2)),
            out_out,
            up_out,
            down_out,
            norm_sum[:, :2],
            norm_sum[:, 2:],
            band_sum,
        )

    return shards


def solution(mesh):
    dp, mp = mesh.shape["dp"], mesh.shape["mp"]
    inner = Mesh(mesh.devices.reshape(dp // 2, 2, mp), DP + ("mp",))
    placed = (
        P(DP, "mp", None),
        P(DP, None),
        P(None, None, None, "mp"),
        P(None, "mp", None),
        P(None, None, "mp"),
        P(None, "mp", None),
        P(),
        P(),
        P(),
        P(DP, "mp", None),
    )
    return jax.shard_map(
        make_shards(dp, mp),
        mesh=inner,
        in_specs=placed,
        out_specs=(
            P(DP, "mp", None),
            P(DP, "mp", None),
            P(None, None, None, "mp"),
            P(None, "mp", None),
            P(None, None, "mp"),
            P(None, "mp", None),
            P(),
            P(),
            P(),
        ),
        check_vma=False,
    )
```

```python
import functools

import jax
import jax.numpy as jnp
from jax import lax
from jax.experimental import pallas as pl
from jax.experimental.pallas import tpu as pltpu
from jax.sharding import Mesh, PartitionSpec as P

BF = jnp.bfloat16
F32 = jnp.float32
VMEM_LIMIT = 58 * 1024 * 1024
TOKEN = (8, 128)
SUB = 256
RIDERS = 16
GELU_A = 0.7978845608028654
GELU_B = 0.044715


def dot_nt(lhs, rhs):
    return lax.dot_general(lhs, rhs, (((1,), (1,)), ((), ())), preferred_element_type=F32)


def dot_nn(lhs, rhs):
    return lax.dot_general(lhs, rhs, (((1,), (0,)), ((), ())), preferred_element_type=F32)


def dot_tn(lhs, rhs):
    return lax.dot_general(lhs, rhs, (((0,), (0,)), ((), ())), preferred_element_type=F32)


def normalize(values):
    center = values - jnp.mean(values, axis=-1, keepdims=True)
    inv_std = lax.rsqrt(jnp.mean(center * center, axis=-1, keepdims=True) + 1e-05)
    return center * inv_std, inv_std


def norm_back(grad_out, normal, inv_std, gain):
    grad_normal = grad_out * gain
    mean_one = jnp.mean(grad_normal, axis=-1, keepdims=True)
    mean_two = jnp.mean(grad_normal * normal, axis=-1, keepdims=True)
    return inv_std * (grad_normal - mean_one - normal * mean_two)


def whole(shape):
    return pl.BlockSpec(shape, lambda *_: (0,) * len(shape))


def call(
    order, body, grid, in_specs, out_specs, out_shape, scratch=(), prefetch=0, name=None, aliases=None,
    limit=None, near_in=(), near_out=(),
):
    first = prefetch + len(in_specs)
    second = first + 1 + len(out_specs)
    anywhere = pl.BlockSpec(memory_space=pl.ANY)

    def with_token(*refs):
        return body(*refs[:first], *refs[first + 1 : second], *refs[second + 1 :])

    kernel = pl.pallas_call(
        with_token,
        grid_spec=pltpu.PrefetchScalarGridSpec(
            num_scalar_prefetch=prefetch,
            grid=grid,
            in_specs=list(in_specs) + [anywhere],
            out_specs=list(out_specs) + [anywhere],
            scratch_shapes=list(scratch),
        ),
        out_shape=[
            shape if limit is None or k in near_out else pltpu.HBM(shape.shape, shape.dtype)
            for k, shape in enumerate(out_shape)
        ]
        + [shape_of(TOKEN, jnp.int32)],
        input_output_aliases={**(aliases or {}), first: len(out_specs)},
        compiler_params=pltpu.CompilerParams(
            dimension_semantics=("arbitrary",) * len(grid), vmem_limit_bytes=limit or VMEM_LIMIT
        ),
        cost_estimate=pl.CostEstimate(flops=0, bytes_accessed=0, transcendentals=0),
        name=name,
    )

    def run(*operands):
        placed = [
            operand
            if limit is None or k < prefetch or k - prefetch in near_in
            else pltpu.with_memory_space_constraint(operand, pltpu.HBM)
            for k, operand in enumerate(operands)
        ]
        *results, order.token = kernel(*placed, order.token)
        return results

    return run


def shape_of(shape, dtype):
    return jax.ShapeDtypeStruct(shape, dtype)


def tie(*arrays):
    count = len(arrays)
    return pl.pallas_call(
        lambda *refs: None,
        out_shape=[shape_of(a.shape, a.dtype) for a in arrays],
        in_specs=[pl.BlockSpec(memory_space=pl.ANY)] * count,
        out_specs=[pl.BlockSpec(memory_space=pl.ANY)] * count,
        input_output_aliases={i: i for i in range(count)},
        cost_estimate=pl.CostEstimate(flops=0, bytes_accessed=0, transcendentals=0),
        name="tie",
    )(*arrays)


def enter_kernel(order, tokens, gain, shift):
    rows, width = tokens.shape

    def body(t_ref, g_ref, s_ref, x_ref, n_ref):
        x = t_ref[...].astype(F32)
        x_ref[...] = x
        normal, _ = normalize(x)
        n_ref[...] = (normal * g_ref[...] + s_ref[...]).astype(BF)

    return call(
        order,
        body,
        (1,),
        [whole((rows, width)), whole((1, width)), whole((1, width))],
        [whole((rows, width)), whole((rows, width))],
        [shape_of((rows, width), F32), shape_of((rows, width), BF)],
        name="enter",
    )(tokens, gain, shift)


def reverse_lanes(values):
    count = values.shape[1]
    flip = (
        lax.broadcasted_iota(jnp.int32, (count, count), 0)
        + lax.broadcasted_iota(jnp.int32, (count, count), 1)
        == count - 1
    ).astype(BF)
    high = values.astype(BF)
    rest = values - high.astype(F32)
    middle = rest.astype(BF)
    last = (rest - middle.astype(F32)).astype(BF)
    return (dot_nn(high, flip) + dot_nn(middle, flip)) + dot_nn(last, flip)


THIRDS = 3


def attn_specs(weights):
    if len(weights) == 4:
        return [whole(w.shape) for w in weights]
    groups, two, mp, count, width = weights[0].shape
    return [pl.BlockSpec((groups, two, mp, count // 3, width), lambda i, place: (0, 0, 0, 0, 0))]


def by_third(step, refs, place_ref, part):
    def pieces(m):
        if len(refs) == 4:
            for ref in refs:
                yield lambda here, ref=ref: ref[place_ref[0] ^ m, here], ref.shape[1]
            return
        for half in range(2):
            for z in range(refs[0].shape[2]):
                yield lambda here, half=half, z=z: refs[0][m, place_ref[3] ^ half, z, here], refs[0].shape[3]

    def mat(m, third):
        count = sum(length for _, length in pieces(m)) // THIRDS
        first, last, at, out = third * count, (third + 1) * count, 0, []
        for read, length in pieces(m):
            low, high = max(first - at, 0), min(last - at, length)
            if low < high:
                out.append(read(slice(low, high)))
            at += length
        return jnp.concatenate(out, axis=0)

    for third in range(THIRDS):
        pl.when(step == third)(functools.partial(part, functools.partial(mat, third=third)))


def attn_forward(order, layer, place, x, normed, halo, weights, pos_bias, seg_q, seg_k, gain, shift):
    rows, width = x.shape
    seqs, block, _ = seg_q.shape
    keys = seg_k.shape[2]
    window = keys - block
    third = width // THIRDS

    def body(place_ref, x_ref, n_ref, h_ref, *rest):
        w_refs, rest = rest[: len(weights)], rest[len(weights) :]
        (band_ref, sq_ref, sk_ref, g_ref, s_ref, sg_ref, ratio_ref, rden_ref, v_ref, wsum_ref, car_ref, mixed_ref,
         masked_ref, x1_ref, nb_ref, mix) = rest
        step = pl.program_id(0)

        @pl.when(step == 0)
        def _():
            band = reverse_lanes(jnp.exp(band_ref[0]))
            band = jnp.concatenate([band, jnp.zeros((block, block), F32)], axis=1)
            spread = pltpu.roll(band, 1, axis=1, stride=1, stride_axis=0)
            for s in range(seqs):
                masked = jnp.where(sq_ref[s] == sk_ref[s], spread, 0.0)
                masked_ref[s] = masked
                mix[s] = masked.astype(BF)
            x1_ref[...] = x_ref[...]

        def part(mat):
            wq, wk, wv = mat(0), mat(1), mat(2)
            q = dot_nt(n_ref[...], wq)
            sg = jax.nn.sigmoid(q)
            sg_ref[...] = sg.astype(BF)
            carried, wsum = [], []
            for r, source in enumerate((h_ref, n_ref)):
                here = slice(r * rows, (r + 1) * rows)
                kexp = jnp.exp(dot_nt(source[...], wk))
                v = dot_nt(source[...], wv)
                v_ref[here] = v.astype(BF)
                wsum.append(kexp.astype(BF))
                carried.append((kexp * v).astype(BF))
                wsum_ref[here] = wsum[r]
                car_ref[here] = carried[r]
            mixed = []
            for s in range(seqs):
                here = slice(s * block, (s + 1) * block)
                num = dot_nn(mix[s, :, :window], carried[0][here]) + dot_nn(mix[s, :, window:], carried[1][here])
                den = dot_nn(mix[s, :, :window], wsum[0][here]) + dot_nn(mix[s, :, window:], wsum[1][here])
                rden = 1.0 / den
                ratio = num / den
                rden_ref[here] = rden.astype(BF)
                ratio_ref[here] = ratio.astype(BF)
                mixed.append((sg[here] * ratio).astype(BF))
            mixed = jnp.concatenate(mixed, axis=0)
            mixed_ref[...] = mixed
            x1_ref[...] += dot_nn(mixed, mat(3))

        by_third(step, w_refs, place_ref, part)

        @pl.when(step == THIRDS - 1)
        def _():
            normal, _ = normalize(x1_ref[...])
            nb_ref[...] = (normal * g_ref[...] + s_ref[...]).astype(BF)

    def col(n):
        return pl.BlockSpec((n, third), lambda i, *_: (0, i))

    return call(
        order,
        body,
        (THIRDS,),
        [whole((rows, width))] * 3
        + attn_specs(weights)
        + [pl.BlockSpec((1, block, window), lambda i, place: (layer, place[1], 0))]
        + [whole((seqs, block, 1)), whole((seqs, 1, keys)), whole((1, width)), whole((1, width))],
        [col(rows)] * 3 + [col(2 * rows)] * 3 + [col(rows)]
        + [whole((seqs, block, keys)), whole((rows, width)), whole((rows, width))],
        [shape_of((rows, width), BF)] * 3
        + [shape_of((2 * rows, width), BF)] * 3
        + [
            shape_of((rows, width), BF),
            shape_of((seqs, block, keys), F32),
            shape_of((rows, width), F32),
            shape_of((rows, width), BF),
        ],
        [pltpu.VMEM((seqs, block, keys), BF)],
        prefetch=1,
        name="attn_fwd",
    )(place, x, normed, halo, *weights, pos_bias, seg_q, seg_k, gain, shift)


def gelu_both(pre):
    square = pre * pre
    upper = 0.5 + 0.5 * jnp.tanh(pre * (GELU_A + (GELU_A * GELU_B) * square))
    act = pre * upper
    return act, upper + act * (1.0 - upper) * (2.0 * GELU_A + (6.0 * GELU_A * GELU_B) * square)


def chunk_specs(chunk, width, per_half):
    own = pl.BlockSpec((chunk, width), lambda i, *_: (jnp.minimum(i, per_half - 1), 0))
    other = pl.BlockSpec((chunk, width), lambda i, *_: (jnp.maximum(i - per_half, 0), 0))
    return own, other


def ff_forward(order, x1, normed, up, down, gain, shift):
    rows, width = x1.shape
    half = up.shape[0]
    chunk = width
    steps = half // chunk
    last = gain is not None

    def body(x_ref, n_ref, u, d, *rest):
        if last:
            g_ref, s_ref, act_ref, slope_ref, x2_ref, next_ref = rest
        else:
            act_ref, slope_ref, x2_ref = rest
        step = pl.program_id(0)

        @pl.when(step == 0)
        def _():
            x2_ref[...] = x_ref[...]

        for k in range(chunk // SUB):
            here = slice(k * SUB, (k + 1) * SUB)
            act, slope = gelu_both(dot_nt(n_ref[...], u[here]))
            act_ref[:, here] = act.astype(BF)
            slope_ref[:, here] = slope.astype(BF)
        x2_ref[...] += dot_nn(act_ref[...], d[...])

        if last:

            @pl.when(step == steps - 1)
            def _():
                normal, _ = normalize(x2_ref[...])
                next_ref[...] = (normal * g_ref[...] + s_ref[...]).astype(BF)

    full = whole((rows, width))
    weight = pl.BlockSpec((chunk, width), lambda i: (i, 0))
    col = pl.BlockSpec((rows, chunk), lambda i: (0, i))
    return call(
        order,
        body,
        (steps,),
        [full, full, weight, weight] + [whole((1, width))] * (2 if last else 0),
        [col, col, full] + ([full] if last else []),
        [shape_of((rows, half), BF)] * 2 + [shape_of((rows, width), F32)] + ([shape_of((rows, width), BF)] if last else []),
        name="ff_fwd",
    )(x1, normed, up, down, *((gain, shift) if last else ()))


def ff_specs(weights, chunk):
    if len(weights) == 4:
        half, width = weights[0].shape
        own, other = chunk_specs(chunk, width, half // chunk)
        return list(weights), [own, other, own, other]
    groups, _, mp, count, width = weights[0].shape
    rows = count // 3
    per = chunk // (mp * rows)
    steps = groups // per

    def spec(which):
        return pl.BlockSpec(
            (per, 1, mp, rows, width), lambda i, place: (i % steps, place[3] ^ (i // steps), 0, which, 0)
        )

    return [weights[0], weights[0]], [spec(1), spec(2)]


def ff_backward(order, place, x1, normed, weights, groups, grad, gain, saved):
    rows, width = x1.shape
    chunk = width
    half = 2 * width
    per_half = half // chunk
    steps = 2 * per_half
    operands, w_specs = ff_specs(weights, chunk)
    group_rows = half // groups
    per = chunk // group_rows
    fresh = saved is None
    relative = len(weights) == 4

    def body(place_ref, x_ref, n_ref, *rest):
        rest = list(rest)
        w_refs = [rest.pop(0) for _ in operands]
        grad_ref, g_ref = rest.pop(0), rest.pop(0)
        kept = [] if fresh else [rest.pop(0) for _ in range(4)]
        wg_ref = rest.pop(0)
        g1_ref, ga_ref, gg_ref, gs_ref = rest[:4]
        out_ref = rest[4] if fresh else None
        low, dn, pre_grads = rest[5:8] if fresh else rest[4:7]
        acts, x2 = rest[8:] if fresh else (None, None)
        step = pl.program_id(0)

        @pl.when(step == 0)
        def _():
            low[...] = grad_ref[...].astype(BF)
            dn[...] = jnp.zeros_like(dn)
            if fresh:
                x2[...] = x_ref[...]

        def part(u_ref, d_ref, act_ref, slope_ref):
            u = u_ref[...].reshape(chunk, width)
            d = d_ref[...].reshape(chunk, width)
            for k in range(chunk // SUB):
                here = slice(k * SUB, (k + 1) * SUB)
                if fresh:
                    act, slope = gelu_both(dot_nt(n_ref[...], u[here]))
                    acts[:, here] = act.astype(BF)
                else:
                    slope = slope_ref[:, here].astype(F32)
                pre_grads[:, here] = (dot_nt(low[...], d[here]) * slope).astype(BF)
            pre_grad = pre_grads[...]
            act = acts[...] if fresh else act_ref[...]
            if fresh:
                x2[...] += dot_nn(act, d)
            dn[...] += dot_nn(pre_grad, u)
            for which, value in ((0, dot_tn(pre_grad, n_ref[...])), (1, dot_tn(act, low[...]))):
                value = value.astype(BF)
                for k in range(per):
                    spot = (place_ref[5] ^ k) if relative else k
                    wg_ref[spot, 0, which] = value[k * group_rows : (k + 1) * group_rows]

        own_w, other_w = (w_refs[::2], w_refs[1::2]) if relative else (w_refs, w_refs)
        if fresh:
            pl.when(step < per_half)(lambda: part(*own_w, None, None))
            pl.when(step >= per_half)(lambda: part(*other_w, None, None))
        else:
            pl.when(step < per_half)(lambda: part(*own_w, *kept[:2]))
            pl.when(step >= per_half)(lambda: part(*other_w, *kept[2:]))

        @pl.when(step == steps - 1)
        def _():
            if fresh:
                out_ref[...] = x2[...].astype(BF)
            normal, inv = normalize(x_ref[...])
            total = dn[...]
            g1 = grad_ref[...] + norm_back(total, normal, inv, g_ref[...])
            g1_ref[...] = g1
            ga_ref[...] = g1.astype(BF)
            gg_ref[...] = jnp.sum(total * normal, axis=0, keepdims=True)
            gs_ref[...] = jnp.sum(total, axis=0, keepdims=True)

    full = whole((rows, width))
    def own_index(i):
        return jnp.minimum(i, per_half - 1)

    def other_index(i):
        return jnp.maximum(i - per_half, 0)

    wg_specs = [
        pl.BlockSpec(
            (per, 1, 2, group_rows, width),
            lambda i, place: (
                (place[4] ^ (i % per_half)) if relative else i % per_half, place[3] ^ (i // per_half), 0, 0, 0,
            ),
        )
    ]
    wg_shapes = [shape_of((groups, 2, 2, group_rows, width), BF)]
    kept_specs = [
        pl.BlockSpec((rows, chunk), lambda i, *_, index=index: (0, index(i)))
        for index in (() if fresh else (own_index, own_index, other_index, other_index))
    ]
    return call(
        order,
        body,
        (steps,),
        [full, full] + w_specs + [full, whole((1, width))] + kept_specs,
        wg_specs + [full, full, whole((1, width)), whole((1, width))] + ([full] if fresh else []),
        wg_shapes
        + [
            shape_of((rows, width), F32),
            shape_of((rows, width), BF),
            shape_of((1, width), F32),
            shape_of((1, width), F32),
        ]
        + ([shape_of((rows, width), BF)] if fresh else []),
        [pltpu.VMEM((rows, width), BF), pltpu.VMEM((rows, width), F32), pltpu.VMEM((rows, chunk), BF)]
        + ([pltpu.VMEM((rows, chunk), BF), pltpu.VMEM((rows, width), F32)] if fresh else []),
        prefetch=1,
        name="ff_bwd",
    )(place, x1, normed, *operands, grad, gain, *(() if fresh else saved))


def attn_backward(order, place, grad_low, weights, sg, ratio, rden, v, wsum, carried, masked):
    rows, width = grad_low.shape
    seqs, block, keys = masked.shape
    window = keys - block
    third = width // THIRDS

    def body(place_ref, ga_ref, *rest):
        w_refs, rest = rest[: len(weights)], rest[len(weights) :]
        (sg_ref, ratio_ref, rden_ref, v_ref, wsum_ref, car_ref, masked_ref,
         gq_ref, gk_ref, gv_ref, band_ref, own_ref, halo_ref, mix_t, wgrad, dn) = rest
        step = pl.program_id(0)

        @pl.when(step == 0)
        def _():
            for s in range(seqs):
                mix_t[s] = masked_ref[s].T.astype(BF)
            wgrad[...] = jnp.zeros_like(wgrad)
            dn[...] = jnp.zeros_like(dn)

        def part(mat):
            gm = dot_nt(ga_ref[...], mat(3))
            sig = sg_ref[...].astype(F32)
            rat = ratio_ref[...].astype(F32)
            scaled = gm * sig
            gq = (scaled * rat * (1.0 - sig)).astype(BF)
            gq_ref[...] = gq
            gnum_f = scaled * rden_ref[...].astype(F32)
            gnum = gnum_f.astype(BF)
            gden = (-gnum_f * rat).astype(BF)
            wq, wk, wv = mat(0), mat(1), mat(2)
            dn[rows:] += dot_nn(gq, wq)
            for r in range(2):
                for s in range(seqs):
                    here = slice(s * block, (s + 1) * block)
                    there = slice(r * rows + s * block, r * rows + (s + 1) * block)
                    cols = slice(r * window, r * window + block)
                    ke = wsum_ref[there].astype(F32)
                    gcar = dot_nn(mix_t[s, cols], gnum[here])
                    gsum = dot_nn(mix_t[s, cols], gden[here])
                    gv = (gcar * ke).astype(BF)
                    gk = ((gcar * v_ref[there].astype(F32) + gsum) * ke).astype(BF)
                    gk_ref[there] = gk
                    gv_ref[there] = gv
                    wgrad[s, :, cols] += dot_nt(gnum[here], car_ref[there]) + dot_nt(gden[here], wsum_ref[there])
                    dn[there] += dot_nn(gk, wk) + dot_nn(gv, wv)

        by_third(step, w_refs, place_ref, part)

        @pl.when(step == THIRDS - 1)
        def _():
            total = wgrad[0] * masked_ref[0]
            for s in range(1, seqs):
                total = total + wgrad[s] * masked_ref[s]
            lane_row = lax.broadcasted_iota(jnp.int32, (block, keys), 0) + 1
            bit = 1
            while bit <= block:
                rolled = pltpu.roll(total, keys - bit, axis=1)
                total = jnp.where((lane_row & bit) != 0, rolled, total)
                bit *= 2
            band_ref[...] = reverse_lanes(total[:, :window])
            halo_ref[...] = dn[:rows].astype(BF)
            own_ref[...] = dn[rows:]

    def col(n):
        return pl.BlockSpec((n, third), lambda i, *_: (0, i))

    return call(
        order,
        body,
        (THIRDS,),
        [whole((rows, width))]
        + attn_specs(weights)
        + [col(rows)] * 3 + [col(2 * rows)] * 3 + [whole((seqs, block, keys))],
        [col(rows), col(2 * rows), col(2 * rows), whole((block, window)), whole((rows, width)), whole((rows, width))],
        [
            shape_of((rows, width), BF),
            shape_of((2 * rows, width), BF),
            shape_of((2 * rows, width), BF),
            shape_of((block, window), F32),
            shape_of((rows, width), F32),
            shape_of((rows, width), BF),
        ],
        [
            pltpu.VMEM((seqs, keys, block), BF),
            pltpu.VMEM((seqs, block, keys), F32),
            pltpu.VMEM((2 * rows, width), F32),
        ],
        prefetch=1,
        name="attn_bwd",
        limit=46 * 1024 * 1024,
        near_in=(0,),
        near_out=(0, 1, 2, 3, 4, 5),
    )(place, grad_low, *weights, sg, ratio, rden, v, wsum, carried, masked)


def attn_weight_grads(order, place, gq, gk, gv, mixed, normed, halo, grad_low, band, mp, mixed_rows, riding):
    rows, width = gq.shape
    half = width // 2
    quarter = half // 2
    piece = quarter // mp
    window = band.shape[1]
    share = 2 * RIDERS
    def body(place_ref, gq_ref, gk_ref, gv_ref, mixed_ref, n_ref, h_ref, ga_ref, band_ref, *out_refs):
        def part(outs, core):
            if riding:
                for p in range(4):
                    owner = 2 * (place_ref[2] ^ p) + (place_ref[3] ^ core)
                    start = pl.multiple_of(owner * share, share)
                    rows_here = band_ref[pl.ds(start, share)].astype(BF)
                    outs[0][p, quarter:] = jnp.concatenate(
                        [rows_here[:RIDERS], rows_here[RIDERS:], jnp.zeros((RIDERS, width - 2 * window), BF)], axis=1
                    )

            def put(m, value):
                low = value.astype(BF)
                spot = place_ref[0] ^ m
                if not mixed_rows:
                    outs[0][spot, :quarter] = low[:quarter]
                    outs[1][spot] = low[quarter:]
                    return
                for z in range(mp):
                    for k in range(2):
                        outs[k][spot, z * piece : (z + 1) * piece] = low[
                            (2 * z + k) * piece : (2 * z + k + 1) * piece
                        ]

            put(0, dot_tn(gq_ref[...], n_ref[...]))
            for m, ref in ((1, gk_ref), (2, gv_ref)):
                put(m, dot_tn(ref[:rows], h_ref[...]) + dot_tn(ref[rows:], n_ref[...]))
            put(3, dot_tn(mixed_ref[...], ga_ref[...]))

        pl.when(pl.program_id(0) == 0)(lambda: part(out_refs[:2], 0))
        pl.when(pl.program_id(0) == 1)(lambda: part(out_refs[2:], 1))

    def col(n):
        return pl.BlockSpec((n, half), lambda i, *_: (0, i))

    shapes = [(4, quarter + (RIDERS if riding else 0), width), (4, quarter, width)] * 2
    return call(
        order,
        body,
        (2,),
        [col(rows), col(2 * rows), col(2 * rows), col(rows)] + [whole((rows, width))] * 3 + [whole(band.shape)],
        [whole(shape) for shape in shapes],
        [shape_of(shape, BF) for shape in shapes],
        prefetch=1,
        name="attn_wgrad",
        limit=36 * 1024 * 1024,
        near_in=(0, 1, 2, 6, 7),
    )(place, gq, gk, gv, mixed, normed, halo, grad_low, band)


def leave_attn(order, x, grad, own, back, gain):
    rows, width = x.shape

    def body(x_ref, g_ref, o_ref, b_ref, gain_ref, out_ref, gg_ref, gs_ref):
        normal, inv = normalize(x_ref[...])
        total = o_ref[...] + b_ref[...].astype(F32)
        out_ref[...] = g_ref[...] + norm_back(total, normal, inv, gain_ref[...])
        gg_ref[...] = jnp.sum(total * normal, axis=0, keepdims=True)
        gs_ref[...] = jnp.sum(total, axis=0, keepdims=True)

    return call(
        order,
        body,
        (1,),
        [whole((rows, width))] * 4 + [whole((1, width))],
        [whole((rows, width)), whole((1, width)), whole((1, width))],
        [shape_of((rows, width), F32)] + [shape_of((1, width), F32)] * 2,
        name="leave",
    )(x, grad, own, back, gain)


def finish_layer(order, layer, layers, place, parts, channels, hidden, mp, window, norm_rows, previous):
    width = parts[0].shape[-1]
    total = 4 * channels
    single = len(parts) == 1
    groups = len(parts) // 4
    dp = parts[0].shape[0] if single else 2 * groups
    piece = total // dp
    share = 2 * RIDERS
    block = dp * share

    def body(place_ref, *rest):
        p_refs, rest = rest[: len(parts)], rest[len(parts) :]
        qkv_ref, out_ref, up_ref, down_ref, band_ref = rest[:5]
        up = rest[-1]

        def put(owner, rows_of, ff_rows_of, bands):
            start = pl.multiple_of(owner * piece, piece)
            mat = owner * piece // channels
            inner = pl.multiple_of(owner * piece - mat * channels, piece)
            value = rows_of(0, piece).astype(F32)

            @pl.when(mat < 3)
            def _():
                qkv_ref[0, jnp.minimum(mat, 2), pl.ds(inner, piece)] = value

            @pl.when(mat == 3)
            def _():
                out_ref[0, pl.ds(inner, piece)] = value

            up[pl.ds(start, piece)] = ff_rows_of(0, piece).astype(F32)
            down_ref[0, pl.ds(start, piece)] = ff_rows_of(piece, piece).astype(F32)
            for p in range(mp):
                band = rows_of(bands + p * RIDERS, RIDERS).astype(F32)
                first = pl.multiple_of((place_ref[1] ^ p) * block + owner * share, share)
                band_ref[0, pl.ds(first, RIDERS)] = band[:, :window]
                band_ref[0, pl.ds(first + RIDERS, RIDERS)] = band[:, window : 2 * window]

        if single:
            for owner in range(dp):
                put(
                    jnp.int32(owner),
                    lambda start, count, owner=owner: p_refs[0][owner, start : start + count],
                    lambda start, count, owner=owner: p_refs[0][owner, piece + start : piece + start + count],
                    3 * piece,
                )
        else:
            for core in range(2):
                for p in range(groups):
                    ref, ff_ref = p_refs[core * groups + p], p_refs[(2 + core) * groups + p]
                    owner = 2 * (place_ref[2] ^ p) + (place_ref[3] ^ core)
                    put(
                        owner,
                        lambda start, count, ref=ref: ref[start : start + count],
                        lambda start, count, ref=ff_ref: ref[start : start + count],
                        piece + norm_rows,
                    )
        up_ref[0] = up[...].T
        if norm_rows:
            half = norm_rows // 2
            sums = []
            for p in range(groups):
                for core in range(2):
                    rows = p_refs[core * groups + p][piece : piece + norm_rows].astype(F32)
                    sums.append(rows[:half] + rows[half:])
            while len(sums) > 1:
                sums = [sums[k] + sums[k + 1] for k in range(0, len(sums), 2)]
            rest[5][...] = sums[0]

    shapes = [
        (layers, 3, channels, width),
        (layers, channels, width),
        (layers, width, hidden),
        (layers, hidden, width),
        (layers, mp * block, window),
    ]

    def here(shape):
        return pl.BlockSpec((1,) + shape[1:], lambda i, *_: (layer,) + (0,) * (len(shape) - 1))

    extra = list(previous) if previous is not None else []
    anywhere = pl.BlockSpec(memory_space=pl.ANY)
    return call(
        order,
        lambda *refs: body(*refs[: 1 + len(parts)], *refs[1 + len(parts) + len(extra) :]),
        (1,),
        [whole(part.shape) for part in parts] + [anywhere] * len(extra),
        [here(shape) for shape in shapes] + ([whole((norm_rows // 2, width))] if norm_rows else []),
        [shape_of(shape, F32) for shape in shapes]
        + ([shape_of((norm_rows // 2, width), F32)] if norm_rows else []),
        [pltpu.VMEM((total, width), F32)],
        prefetch=1,
        name="finish",
        aliases={1 + len(parts) + k: k for k in range(len(extra))},
    )(place, *parts, *extra)


DP = ("g", "c")


class Order:
    def __init__(self):
        self.token = jnp.zeros(TOKEN, jnp.int32)

    def pin(self, *arrays):
        *arrays, self.token = tie(*arrays, self.token)
        return arrays


class Links:
    def __init__(self, order, dp, mp):
        self.order = order
        self.dp = dp
        self.mp = mp
        bits = [1 << k for k in range(1, dp.bit_length() - 1)]
        self.routes = (bits, bits[::-1])

    def swap(self, value, axis, bit):
        size = self.dp if axis == DP else self.mp
        return lax.ppermute(value, axis, [(i, i ^ bit) for i in range(size)])


class Spread:
    def __init__(self, links, values):
        self.links = links
        self.values = list(values)
        self.phase = 0
        self.have = [[], []]

    def start(self):
        self.values = self.links.order.pin(*self.values)
        self.coming = [
            self.links.swap(value, DP, route[self.phase])
            for value, route in zip(self.values, self.links.routes)
        ]

    def wait(self):
        coming = self.links.order.pin(*self.coming)
        for k in range(2):
            bit = self.links.routes[k][self.phase]
            place = sum(1 for other in self.have[k] if other > bit)
            self.values[k] = jnp.stack([self.values[k], coming[k]], axis=place)
            self.have[k].append(bit)
        self.phase += 1

    def wait_all(self):
        self.wait()
        while self.phase < len(self.links.routes[0]):
            self.start()
            self.wait()

    def start_cores(self):
        self.values = self.links.order.pin(*self.values)
        self.coming = [self.links.swap(value, DP, 1) for value in self.values]

    def wait_cores(self):
        return self.values + self.links.order.pin(*self.coming)


class Gather(Spread):
    def __init__(self, links, piece_a, piece_b):
        super().__init__(links, ())
        self.cut = piece_a.shape[0]
        self.piece = jnp.concatenate([piece_a, piece_b], axis=0)

    def start_mp(self):
        (self.piece,) = self.links.order.pin(self.piece)
        self.coming_mp = [self.links.swap(self.piece, "mp", p) for p in range(1, self.links.mp)]

    def wait_mp(self):
        parts = [self.piece] + self.links.order.pin(*self.coming_mp)
        self.values = [
            jnp.stack([part[: self.cut] for part in parts]),
            jnp.stack([part[self.cut :] for part in parts]),
        ]


class Reduce:
    def __init__(self, links, halves):
        self.links = links
        self.halves = halves
        self.phase = 0

    def start_cores(self):
        others = self.links.order.pin(*self.halves[2:])
        self.coming = [self.links.swap(other, DP, 1) for other in others]

    def wait_cores(self):
        coming = self.links.order.pin(*self.coming)
        mp = self.links.mp
        self.have = [sorted(route, reverse=True) for route in self.links.routes]
        lead = (2,) * len(self.have[0])
        self.terms = []
        for own, other in zip(self.halves[:2], coming):
            shape = lead + (-1, own.shape[-1])
            self.terms.append([own.reshape(shape), other.reshape(shape)])

    def start(self):
        sends = []
        for k in range(2):
            place = self.have[k].index(self.links.routes[1 - k][self.phase])
            sends.append(
                sum(lax.index_in_dim(term, 1, place, keepdims=False).astype(F32) for term in self.terms[k]).astype(BF)
            )
            self.terms[k] = [lax.index_in_dim(term, 0, place, keepdims=False) for term in self.terms[k]]
        sends = self.links.order.pin(*sends)
        self.coming = [
            self.links.swap(sends[k], DP, self.links.routes[1 - k][self.phase]) for k in range(2)
        ]

    def wait(self):
        coming = self.links.order.pin(*self.coming)
        for k in range(2):
            self.terms[k].append(coming[k])
            self.have[k].remove(self.links.routes[1 - k][self.phase])
        self.phase += 1

    def wait_all(self):
        self.wait()
        while self.phase < len(self.links.routes[0]):
            self.start()
            self.wait()
        sums = [sum(term.astype(F32) for term in terms).astype(BF) for terms in self.terms]
        count = sums[1].shape[0]
        mp = self.links.mp
        riders = sums[0][count:]
        return [value[:count].reshape(mp, count // mp, -1) for value in sums], riders


class ReduceWide:
    def __init__(self, links, grads):
        self.links = links
        (grads,) = links.order.pin(grads.reshape((links.dp,) + grads.shape[2:]))
        self.sums = lax.psum_scatter(grads, DP, scatter_dimension=0, tiled=True)

    def wait(self):
        (sums,) = self.links.order.pin(self.sums)
        sums = sums.reshape(2, self.links.mp, -1, sums.shape[-1])
        return [sums[0], sums[1]]


class ReduceMp:
    def __init__(self, links, arrays, index, riders):
        self.links = links
        joined = jnp.concatenate(arrays, axis=1)
        self.count = joined.shape[1]
        if index is None:
            blocks = [joined[p] for p in range(links.mp)]
        else:
            blocks = [
                lax.dynamic_index_in_dim(joined, jnp.bitwise_xor(index, p), 0, keepdims=False)
                for p in range(links.mp)
            ]
        if riders is not None:
            blocks = [jnp.concatenate([block, riders], axis=0) for block in blocks]
        self.kept, *sends = links.order.pin(*blocks)
        self.coming = [links.swap(send, "mp", p + 1) for p, send in enumerate(sends)]

    def wait(self):
        parts = [self.kept] + self.links.order.pin(*self.coming)
        total = sum(part[: self.count].astype(F32) for part in parts)
        return total.astype(BF), [part[self.count :] for part in parts]


def make_shards(dp, mp):
    def shards(
        tokens,
        segments,
        qkv_weight,
        out_weight,
        up_weight,
        down_projection_weight,
        norm_gain,
        norm_bias,
        pos_bias,
        cotangent,
    ):
        seqs, block, width = tokens.shape
        layers = qkv_weight.shape[0]
        window = pos_bias.shape[2]
        channels = qkv_weight.shape[-1]
        hidden = up_weight.shape[-1]
        rows = seqs * block
        group = lax.axis_index("g")
        core = lax.axis_index("c")
        dp_index = group * 2 + core
        mp_index = lax.axis_index("mp")
        order = Order()
        links = Links(order, dp, mp)
        attn_rows = 4 * channels // dp
        ff_rows = hidden // dp
        groups = dp // 2
        per = max(1, width // (mp * ff_rows))
        place = jnp.stack([group // (groups // 4), mp_index, group, core, group // per, group % per]).astype(jnp.int32)

        def picks(count, offset, length):
            return (
                lax.broadcasted_iota(jnp.int32, (count, length), 0) + offset
                == lax.broadcasted_iota(jnp.int32, (count, length), 1)
            ).astype(BF)

        ff_pick = picks(ff_rows, dp_index * ff_rows, hidden)

        def attn_piece(layer):
            by_channel = jnp.transpose(qkv_weight[layer], (0, 2, 1)).reshape(3 * channels, width)
            start = dp_index * attn_rows
            inner = start - 3 * channels
            return jnp.where(
                inner < 0,
                lax.dynamic_slice_in_dim(by_channel, jnp.minimum(start, 3 * channels - attn_rows), attn_rows),
                lax.dynamic_slice_in_dim(out_weight[layer], jnp.maximum(inner, 0), attn_rows),
            )

        def ff_pieces(layer):
            return (
                dot_nt(ff_pick, up_weight[layer]).astype(BF),
                dot_nn(ff_pick, down_projection_weight[layer]).astype(BF),
            )

        def attn_mats(parts):
            return [part.reshape(4, -1, width) for part in parts]

        def ff_mats(parts):
            flat = [part.reshape(-1, width) for part in parts]
            return (flat[0], flat[2]), (flat[1], flat[3])

        def relative(gathered):
            by_dp = jnp.take(gathered, jnp.bitwise_xor(jnp.arange(dp), dp_index), axis=0)
            both = jnp.take(by_dp, jnp.bitwise_xor(jnp.arange(mp), mp_index), axis=1)
            both = both.reshape((dp // 2, 2) + gathered.shape[1:])
            return both[:, 0], both[:, 1]

        def forward_halo(value):
            return lax.ppermute(value, "mp", [(i, i + 1) for i in range(mp - 1)])

        def backward_halo(value):
            return lax.ppermute(value, "mp", [(i + 1, i) for i in range(mp - 1)])

        gains = norm_gain.reshape(layers, 2, 1, width)
        shifts = norm_bias.reshape(layers, 2, 1, width)
        middle = attn_rows // 2
        in_blocks = (
            middle % 16 == 0 and groups == 4 and block == 2 * RIDERS * dp and width == 3 * window
        )

        piece = attn_piece(0)
        attn0 = Gather(links, piece[:middle], piece[middle:])
        attn0.start_mp()
        ff0 = Gather(links, *ff_pieces(0))
        ff0.start_mp()
        later = jnp.concatenate((attn_piece(1),) + ff_pieces(1), axis=0)
        x, normed = enter_kernel(order, tokens.reshape(rows, width), gains[0, 0], shifts[0, 0])
        (normed,) = order.pin(normed)
        halo = forward_halo(normed)

        seg_pad = jnp.concatenate([jnp.full((seqs, window), -1, segments.dtype), segments], axis=1)
        seg_keys = lax.dynamic_slice_in_dim(seg_pad, mp_index * block, block + window, axis=1)
        seg_q = seg_keys[:, window:].reshape(seqs, block, 1)
        seg_k = seg_keys.reshape(seqs, 1, block + window)

        attn0.wait_mp()
        attn0.start()
        attn0.wait()
        attn0.start()
        ff0.wait_mp()
        ff0.start()
        (later,) = order.pin(later)
        later = lax.all_gather(later, ("g", "c", "mp"), axis=0, tiled=False)
        (halo,) = order.pin(halo)
        attn0.wait_all()
        ff0.wait()
        ff0.start()
        attn0.start_cores()
        w_attn0 = attn_mats(attn0.wait_cores())

        def attn(layer, x, normed, halo, w_attn):
            sg, ratio, rden, v, wsum, carried, mixed, masked, x1, normed_b = attn_forward(
                order, layer, place, x, normed, halo, w_attn, pos_bias, seg_q, seg_k,
                gains[layer, 1], shifts[layer, 1],
            )
            return x1, normed_b, (sg, ratio, rden, v, wsum, carried, masked), (mixed, normed, halo)

        x1_0, normed_b0, saved0, rows0 = attn(0, x, normed, halo, w_attn0)
        ff0.wait_all()
        ff0.start_cores()
        own_up, own_down = [value.reshape(-1, width) for value in ff0.values]
        act0, slope0, x_half = ff_forward(order, x1_0, normed_b0, own_up, own_down, None, None)
        ups0, downs0 = ff_mats(ff0.wait_cores())
        act0o, slope0o, x2, normed2 = ff_forward(
            order, x_half, normed_b0, ups0[1], downs0[1], gains[1, 0], shifts[1, 0]
        )
        (normed2,) = order.pin(normed2)
        halo2 = forward_halo(normed2)
        (later,) = order.pin(later)
        if in_blocks:
            w_attn1 = w_ff1 = [later.reshape((groups, 2, mp) + later.shape[1:])]
        else:
            own, other = relative(later.reshape((dp, mp) + later.shape[1:]))
            cuts = [middle, attn_rows, attn_rows + ff_rows]
            own_a, own_b, own_up, own_down = jnp.split(own, cuts, axis=2)
            other_a, other_b, other_up, other_down = jnp.split(other, cuts, axis=2)
            w_attn1 = attn_mats([own_a, own_b, other_a, other_b])
            w_ff1 = sum(ff_mats([own_up, own_down, other_up, other_down]), ())
        (halo2,) = order.pin(halo2)
        x1_1, normed_b1, saved1, rows1 = attn(1, x2, normed2, halo2, w_attn1)

        wide1, grad1, grad1_low, gain_b1, shift_b1, output = ff_backward(
            order, place, x1_1, normed_b1, w_ff1, groups, cotangent.reshape(rows, width), gains[1, 1], None
        )
        wide1 = ReduceWide(links, wide1)
        gq, gk, gv, band1, dn_own1, back1 = attn_backward(order, place, grad1_low, w_attn1, *saved1)
        (back1,) = order.pin(back1)
        back1 = backward_halo(back1)
        r_attn1 = Reduce(
            links, attn_weight_grads(order, place, gq, gk, gv, *rows1, grad1_low, band1, mp, in_blocks, in_blocks)
        )
        (back1,) = order.pin(back1)
        r_attn1.start_cores()
        grad2, gain_a1, shift_a1 = leave_attn(order, x2, grad1, dn_own1, back1, gains[1, 0])
        r_attn1.wait_cores()
        r_attn1.start()
        wide0, grad3, grad3_low, gain_b0, shift_b0 = ff_backward(
            order, place, x1_0, normed_b0, ups0 + downs0, groups, grad2, gains[0, 1],
            (act0, slope0, act0o, slope0o),
        )
        r_attn1.wait()
        wide0 = ReduceWide(links, wide0)
        r_attn1.start()
        z_of_1 = mp_index if in_blocks else None
        attn1_sum, riders1 = r_attn1.wait_all()
        z_ff1 = ReduceMp(links, wide1.wait(), z_of_1, None)
        gq, gk, gv, band0, dn_own0, back0 = attn_backward(order, place, grad3_low, w_attn0, *saved0)
        r_attn0 = Reduce(
            links, attn_weight_grads(order, place, gq, gk, gv, *rows0, grad3_low, band0, mp, False, in_blocks)
        )
        sum1_ff, _ = z_ff1.wait()
        r_attn0.start_cores()
        z_attn1 = ReduceMp(links, attn1_sum, z_of_1, riders1)
        r_attn0.wait_cores()
        sum1, riders1 = z_attn1.wait()
        r_attn0.start()
        (back0,) = order.pin(back0)
        back0 = backward_halo(back0)
        (full1,) = order.pin(jnp.concatenate([sum1, sum1_ff] + riders1, axis=0))
        full1 = lax.all_gather(full1, DP, axis=0, tiled=False)
        r_attn0.wait()
        (back0,) = order.pin(back0)
        ff0_sum = wide0.wait()
        r_attn0.start()
        z_ff0 = ReduceMp(links, ff0_sum, None, None)
        grad4, gain_a0, shift_a0 = leave_attn(order, x, grad3, dn_own0, back0, gains[0, 0])
        norms = jnp.concatenate(
            [gain_a0, gain_b0, shift_a0, shift_b0, gain_a1, gain_b1, shift_a1, shift_b1], axis=0
        )

        def two_parts(value):
            high = value.astype(BF)
            return jnp.concatenate([high, (value - high.astype(F32)).astype(BF)], axis=0)

        def one_part(value):
            count = value.shape[0] // 2
            return value[:count].astype(F32) + value[count:].astype(F32)

        attn0_sum, riders0 = r_attn0.wait_all()

        def regather(value):
            (value,) = order.pin(value)
            return [value] + [links.swap(value, DP, 2 * p) for p in range(1, groups)], [links.swap(value, DP, 1)]

        def regather_cores(parts):
            same, other = parts
            other[0], *same[1:] = order.pin(other[0], *same[1:])
            same[1:] = order.pin(*same[1:])
            return same, other + [links.swap(part, DP, 1) for part in same[1:]]

        def regather_wait(parts):
            same, other = parts
            return same + other[:1] + order.pin(*other[1:])

        ff0_sum, _ = z_ff0.wait()
        z_attn0 = ReduceMp(links, attn0_sum, None, jnp.concatenate([two_parts(norms), riders0], axis=0))
        ff0_parts = regather(ff0_sum)
        (full1,) = order.pin(full1)

        cut = 2 * norms.shape[0]

        def finish(layer, full, previous):
            if in_blocks:
                norm_rows = 0 if layer else cut
                return finish_layer(
                    order, layer, layers, place, full, channels, hidden, mp, window, norm_rows, previous
                )
            if len(full) == 1:
                owner = jnp.arange(dp)
                joined = full[0]
            else:
                owner = jnp.bitwise_xor(jnp.arange(dp), dp_index)
                joined = jnp.concatenate(
                    [jnp.stack(full[: 2 * groups])[:, :attn_rows], jnp.stack(full[2 * groups :])], axis=1
                ).reshape(2, groups, -1, width)
                joined = jnp.swapaxes(joined, 0, 1).reshape(dp, -1, width)
            joined = joined[:, : attn_rows + 2 * ff_rows]
            attn_part, up_part, down_part = jnp.split(joined, [attn_rows, attn_rows + ff_rows], axis=1)

            def rows_of(value):
                return value.reshape(-1, width)

            def place_of(count):
                spots = (owner[:, None] * count + jnp.arange(count)[None, :]).reshape(-1, 1)
                return (spots == jnp.arange(dp * count)[None, :]).astype(BF)

            attn_place = place_of(attn_rows).reshape(-1, 4, channels)
            ff_place = place_of(ff_rows)
            values = (
                jnp.einsum("pd,pmc->mcd", rows_of(attn_part), attn_place[:, :3], preferred_element_type=F32),
                dot_tn(attn_place[:, 3], rows_of(attn_part)),
                dot_tn(rows_of(up_part), ff_place),
                dot_tn(ff_place, rows_of(down_part)),
            )
            if previous is None:
                previous = [jnp.zeros((layers,) + value.shape, F32) for value in values]
            return [
                lax.dynamic_update_index_in_dim(kept, value, layer, 0)
                for kept, value in zip(previous, values)
            ]

        big = finish(1, [full1], None)
        sum0, riders0 = z_attn0.wait()
        norms = [one_part(part[:cut]) for part in riders0]
        while len(norms) > 1:
            norms = [norms[k] + norms[k + 1] for k in range(0, len(norms), 2)]
        sum0 = jnp.concatenate([sum0, two_parts(norms[0])] + [part[cut:] for part in riders0], axis=0)
        ff0_parts = regather_cores(ff0_parts)
        attn0_parts = regather(sum0)
        ff0_parts = regather_wait(ff0_parts)
        attn0_parts = regather_wait(regather_cores(attn0_parts))
        qkv_out, out_out, up_out, down_out, *small = finish(0, attn0_parts + ff0_parts, big)
        if in_blocks:
            band_sum, norm_sum = small
        else:
            sums = [one_part(attn0_parts[p + k][attn_rows : attn_rows + cut]) for p in range(groups) for k in (0, groups)]
            while len(sums) > 1:
                sums = [sums[k] + sums[k + 1] for k in range(0, len(sums), 2)]
            norm_sum = sums[0]
            band_sum = lax.all_gather(
                lax.psum(jnp.stack([band0, band1]), DP), "mp", axis=1, tiled=True
            )
        norm_sum = norm_sum.reshape(layers, 4, width)
        return (
            output.reshape(tokens.shape),
            grad4.reshape(tokens.shape),
            jnp.transpose(qkv_out, (0, 1, 3, 2)),
            out_out,
            up_out,
            down_out,
            norm_sum[:, :2],
            norm_sum[:, 2:],
            band_sum,
        )

    return shards


def solution(mesh):
    dp, mp = mesh.shape["dp"], mesh.shape["mp"]
    inner = Mesh(mesh.devices.reshape(dp // 2, 2, mp), DP + ("mp",))
    placed = (
        P(DP, "mp", None),
        P(DP, None),
        P(None, None, None, "mp"),
        P(None, "mp", None),
        P(None, None, "mp"),
        P(None, "mp", None),
        P(),
        P(),
        P(),
        P(DP, "mp", None),
    )
    return jax.shard_map(
        make_shards(dp, mp),
        mesh=inner,
        in_specs=placed,
        out_specs=(
            P(DP, "mp", None),
            P(DP, "mp", None),
            P(None, None, None, "mp"),
            P(None, "mp", None),
            P(None, None, "mp"),
            P(None, "mp", None),
            P(),
            P(),
            P(),
        ),
        check_vma=False,
    )
```

```python
import functools

import jax
import jax.numpy as jnp
from jax import lax
from jax.experimental import pallas as pl
from jax.experimental.pallas import tpu as pltpu
from jax.sharding import Mesh, PartitionSpec as P

BF = jnp.bfloat16
F32 = jnp.float32
VMEM_LIMIT = 58 * 1024 * 1024
TOKEN = (8, 128)
SUB = 256
RIDERS = 16
GELU_A = 0.7978845608028654
GELU_B = 0.044715


def dot_nt(lhs, rhs):
    return lax.dot_general(lhs, rhs, (((1,), (1,)), ((), ())), preferred_element_type=F32)


def dot_nn(lhs, rhs):
    return lax.dot_general(lhs, rhs, (((1,), (0,)), ((), ())), preferred_element_type=F32)


def dot_tn(lhs, rhs):
    return lax.dot_general(lhs, rhs, (((0,), (0,)), ((), ())), preferred_element_type=F32)


def normalize(values):
    center = values - jnp.mean(values, axis=-1, keepdims=True)
    inv_std = lax.rsqrt(jnp.mean(center * center, axis=-1, keepdims=True) + 1e-05)
    return center * inv_std, inv_std


def norm_back(grad_out, normal, inv_std, gain):
    grad_normal = grad_out * gain
    mean_one = jnp.mean(grad_normal, axis=-1, keepdims=True)
    mean_two = jnp.mean(grad_normal * normal, axis=-1, keepdims=True)
    return inv_std * (grad_normal - mean_one - normal * mean_two)


def whole(shape):
    return pl.BlockSpec(shape, lambda *_: (0,) * len(shape))


def call(
    order, body, grid, in_specs, out_specs, out_shape, scratch=(), prefetch=0, name=None, aliases=None,
    limit=None, near_in=(), near_out=(),
):
    first = prefetch + len(in_specs)
    second = first + 1 + len(out_specs)
    anywhere = pl.BlockSpec(memory_space=pl.ANY)

    def with_token(*refs):
        return body(*refs[:first], *refs[first + 1 : second], *refs[second + 1 :])

    kernel = pl.pallas_call(
        with_token,
        grid_spec=pltpu.PrefetchScalarGridSpec(
            num_scalar_prefetch=prefetch,
            grid=grid,
            in_specs=list(in_specs) + [anywhere],
            out_specs=list(out_specs) + [anywhere],
            scratch_shapes=list(scratch),
        ),
        out_shape=[
            shape if limit is None or k in near_out else pltpu.HBM(shape.shape, shape.dtype)
            for k, shape in enumerate(out_shape)
        ]
        + [shape_of(TOKEN, jnp.int32)],
        input_output_aliases={**(aliases or {}), first: len(out_specs)},
        compiler_params=pltpu.CompilerParams(
            dimension_semantics=("arbitrary",) * len(grid), vmem_limit_bytes=limit or VMEM_LIMIT
        ),
        cost_estimate=pl.CostEstimate(flops=0, bytes_accessed=0, transcendentals=0),
        name=name,
    )

    def run(*operands):
        placed = [
            operand
            if limit is None or k < prefetch or k - prefetch in near_in
            else pltpu.with_memory_space_constraint(operand, pltpu.HBM)
            for k, operand in enumerate(operands)
        ]
        *results, order.token = kernel(*placed, order.token)
        return results

    return run


def shape_of(shape, dtype):
    return jax.ShapeDtypeStruct(shape, dtype)


def tie(*arrays):
    count = len(arrays)
    return pl.pallas_call(
        lambda *refs: None,
        out_shape=[shape_of(a.shape, a.dtype) for a in arrays],
        in_specs=[pl.BlockSpec(memory_space=pl.ANY)] * count,
        out_specs=[pl.BlockSpec(memory_space=pl.ANY)] * count,
        input_output_aliases={i: i for i in range(count)},
        cost_estimate=pl.CostEstimate(flops=0, bytes_accessed=0, transcendentals=0),
        name="tie",
    )(*arrays)


def enter_kernel(order, tokens, gain, shift):
    rows, width = tokens.shape

    def body(t_ref, g_ref, s_ref, x_ref, n_ref):
        x = t_ref[...].astype(F32)
        x_ref[...] = x
        normal, _ = normalize(x)
        n_ref[...] = (normal * g_ref[...] + s_ref[...]).astype(BF)

    return call(
        order,
        body,
        (1,),
        [whole((rows, width)), whole((1, width)), whole((1, width))],
        [whole((rows, width)), whole((rows, width))],
        [shape_of((rows, width), F32), shape_of((rows, width), BF)],
        name="enter",
    )(tokens, gain, shift)


def reverse_lanes(values):
    count = values.shape[1]
    flip = (
        lax.broadcasted_iota(jnp.int32, (count, count), 0)
        + lax.broadcasted_iota(jnp.int32, (count, count), 1)
        == count - 1
    ).astype(BF)
    high = values.astype(BF)
    rest = values - high.astype(F32)
    middle = rest.astype(BF)
    last = (rest - middle.astype(F32)).astype(BF)
    return (dot_nn(high, flip) + dot_nn(middle, flip)) + dot_nn(last, flip)


THIRDS = 3


def attn_specs(weights):
    if len(weights) == 4:
        return [whole(w.shape) for w in weights]
    groups, two, mp, count, width = weights[0].shape
    return [pl.BlockSpec((groups, two, mp, count // 3, width), lambda i, place: (0, 0, 0, 0, 0))]


def by_third(step, refs, place_ref, part):
    def pieces(m):
        if len(refs) == 4:
            for ref in refs:
                yield lambda here, ref=ref: ref[place_ref[0] ^ m, here], ref.shape[1]
            return
        for half in range(2):
            for z in range(refs[0].shape[2]):
                yield lambda here, half=half, z=z: refs[0][m, place_ref[3] ^ half, z, here], refs[0].shape[3]

    def mat(m, third):
        count = sum(length for _, length in pieces(m)) // THIRDS
        first, last, at, out = third * count, (third + 1) * count, 0, []
        for read, length in pieces(m):
            low, high = max(first - at, 0), min(last - at, length)
            if low < high:
                out.append(read(slice(low, high)))
            at += length
        return jnp.concatenate(out, axis=0)

    for third in range(THIRDS):
        pl.when(step == third)(functools.partial(part, functools.partial(mat, third=third)))


def attn_forward(order, layer, place, x, normed, halo, weights, pos_bias, seg_q, seg_k, gain, shift):
    rows, width = x.shape
    seqs, block, _ = seg_q.shape
    keys = seg_k.shape[2]
    window = keys - block
    third = width // THIRDS

    def body(place_ref, x_ref, n_ref, h_ref, *rest):
        w_refs, rest = rest[: len(weights)], rest[len(weights) :]
        (band_ref, sq_ref, sk_ref, g_ref, s_ref, sg_ref, ratio_ref, rden_ref, v_ref, wsum_ref, car_ref, mixed_ref,
         masked_ref, x1_ref, nb_ref, mix) = rest
        step = pl.program_id(0)

        @pl.when(step == 0)
        def _():
            band = reverse_lanes(jnp.exp(band_ref[0]))
            band = jnp.concatenate([band, jnp.zeros((block, block), F32)], axis=1)
            spread = pltpu.roll(band, 1, axis=1, stride=1, stride_axis=0)
            for s in range(seqs):
                masked = jnp.where(sq_ref[s] == sk_ref[s], spread, 0.0)
                masked_ref[s] = masked
                mix[s] = masked.astype(BF)
            x1_ref[...] = x_ref[...]

        def part(mat):
            wq, wk, wv = mat(0), mat(1), mat(2)
            q = dot_nt(n_ref[...], wq)
            sg = jax.nn.sigmoid(q)
            sg_ref[...] = sg.astype(BF)
            carried, wsum = [], []
            for r, source in enumerate((h_ref, n_ref)):
                here = slice(r * rows, (r + 1) * rows)
                kexp = jnp.exp(dot_nt(source[...], wk))
                v = dot_nt(source[...], wv)
                v_ref[here] = v.astype(BF)
                wsum.append(kexp.astype(BF))
                carried.append((kexp * v).astype(BF))
                wsum_ref[here] = wsum[r]
                car_ref[here] = carried[r]
            mixed = []
            for s in range(seqs):
                here = slice(s * block, (s + 1) * block)
                num = dot_nn(mix[s, :, :window], carried[0][here]) + dot_nn(mix[s, :, window:], carried[1][here])
                den = dot_nn(mix[s, :, :window], wsum[0][here]) + dot_nn(mix[s, :, window:], wsum[1][here])
                rden = 1.0 / den
                ratio = num / den
                rden_ref[here] = rden.astype(BF)
                ratio_ref[here] = ratio.astype(BF)
                mixed.append((sg[here] * ratio).astype(BF))
            mixed = jnp.concatenate(mixed, axis=0)
            mixed_ref[...] = mixed
            x1_ref[...] += dot_nn(mixed, mat(3))

        by_third(step, w_refs, place_ref, part)

        @pl.when(step == THIRDS - 1)
        def _():
            normal, _ = normalize(x1_ref[...])
            nb_ref[...] = (normal * g_ref[...] + s_ref[...]).astype(BF)

    def col(n):
        return pl.BlockSpec((n, third), lambda i, *_: (0, i))

    return call(
        order,
        body,
        (THIRDS,),
        [whole((rows, width))] * 3
        + attn_specs(weights)
        + [pl.BlockSpec((1, block, window), lambda i, place: (layer, place[1], 0))]
        + [whole((seqs, block, 1)), whole((seqs, 1, keys)), whole((1, width)), whole((1, width))],
        [col(rows)] * 3 + [col(2 * rows)] * 3 + [col(rows)]
        + [whole((seqs, block, keys)), whole((rows, width)), whole((rows, width))],
        [shape_of((rows, width), BF)] * 3
        + [shape_of((2 * rows, width), BF)] * 3
        + [
            shape_of((rows, width), BF),
            shape_of((seqs, block, keys), F32),
            shape_of((rows, width), F32),
            shape_of((rows, width), BF),
        ],
        [pltpu.VMEM((seqs, block, keys), BF)],
        prefetch=1,
        name="attn_fwd",
    )(place, x, normed, halo, *weights, pos_bias, seg_q, seg_k, gain, shift)


def gelu_both(pre):
    square = pre * pre
    upper = 0.5 + 0.5 * jnp.tanh(pre * (GELU_A + (GELU_A * GELU_B) * square))
    act = pre * upper
    return act, upper + act * (1.0 - upper) * (2.0 * GELU_A + (6.0 * GELU_A * GELU_B) * square)


def chunk_specs(chunk, width, per_half):
    own = pl.BlockSpec((chunk, width), lambda i, *_: (jnp.minimum(i, per_half - 1), 0))
    other = pl.BlockSpec((chunk, width), lambda i, *_: (jnp.maximum(i - per_half, 0), 0))
    return own, other


def ff_forward(order, x1, normed, up, down, gain, shift):
    rows, width = x1.shape
    half = up.shape[0]
    chunk = width
    steps = half // chunk
    last = gain is not None

    def body(x_ref, n_ref, u, d, *rest):
        if last:
            g_ref, s_ref, act_ref, slope_ref, x2_ref, next_ref = rest
        else:
            act_ref, slope_ref, x2_ref = rest
        step = pl.program_id(0)

        @pl.when(step == 0)
        def _():
            x2_ref[...] = x_ref[...]

        for k in range(chunk // SUB):
            here = slice(k * SUB, (k + 1) * SUB)
            act, slope = gelu_both(dot_nt(n_ref[...], u[here]))
            act_ref[:, here] = act.astype(BF)
            slope_ref[:, here] = slope.astype(BF)
        x2_ref[...] += dot_nn(act_ref[...], d[...])

        if last:

            @pl.when(step == steps - 1)
            def _():
                normal, _ = normalize(x2_ref[...])
                next_ref[...] = (normal * g_ref[...] + s_ref[...]).astype(BF)

    full = whole((rows, width))
    weight = pl.BlockSpec((chunk, width), lambda i: (i, 0))
    col = pl.BlockSpec((rows, chunk), lambda i: (0, i))
    return call(
        order,
        body,
        (steps,),
        [full, full, weight, weight] + [whole((1, width))] * (2 if last else 0),
        [col, col, full] + ([full] if last else []),
        [shape_of((rows, half), BF)] * 2 + [shape_of((rows, width), F32)] + ([shape_of((rows, width), BF)] if last else []),
        name="ff_fwd",
    )(x1, normed, up, down, *((gain, shift) if last else ()))


def ff_specs(weights, chunk):
    if len(weights) == 4:
        half, width = weights[0].shape
        own, other = chunk_specs(chunk, width, half // chunk)
        return list(weights), [own, other, own, other]
    groups, _, mp, count, width = weights[0].shape
    rows = count // 3
    per = chunk // (mp * rows)
    steps = groups // per

    def spec(which):
        return pl.BlockSpec(
            (per, 1, mp, rows, width), lambda i, place: (i % steps, place[3] ^ (i // steps), 0, which, 0)
        )

    return [weights[0], weights[0]], [spec(1), spec(2)]


def ff_backward(order, place, x1, normed, weights, groups, grad, gain, saved):
    rows, width = x1.shape
    chunk = width
    half = 2 * width
    per_half = half // chunk
    steps = 2 * per_half
    operands, w_specs = ff_specs(weights, chunk)
    group_rows = half // groups
    per = chunk // group_rows
    fresh = saved is None
    relative = len(weights) == 4

    def body(place_ref, x_ref, n_ref, *rest):
        rest = list(rest)
        w_refs = [rest.pop(0) for _ in operands]
        grad_ref, g_ref = rest.pop(0), rest.pop(0)
        kept = [] if fresh else [rest.pop(0) for _ in range(4)]
        wg_ref = rest.pop(0)
        g1_ref, ga_ref, gg_ref, gs_ref = rest[:4]
        out_ref = rest[4] if fresh else None
        low, dn, pre_grads = rest[5:8] if fresh else rest[4:7]
        acts, x2 = rest[8:] if fresh else (None, None)
        step = pl.program_id(0)

        @pl.when(step == 0)
        def _():
            low[...] = grad_ref[...].astype(BF)
            dn[...] = jnp.zeros_like(dn)
            if fresh:
                x2[...] = x_ref[...]

        def part(u_ref, d_ref, act_ref, slope_ref):
            u = u_ref[...].reshape(chunk, width)
            d = d_ref[...].reshape(chunk, width)
            for k in range(chunk // SUB):
                here = slice(k * SUB, (k + 1) * SUB)
                if fresh:
                    act, slope = gelu_both(dot_nt(n_ref[...], u[here]))
                    acts[:, here] = act.astype(BF)
                else:
                    slope = slope_ref[:, here].astype(F32)
                pre_grads[:, here] = (dot_nt(low[...], d[here]) * slope).astype(BF)
            pre_grad = pre_grads[...]
            act = acts[...] if fresh else act_ref[...]
            if fresh:
                x2[...] += dot_nn(act, d)
            dn[...] += dot_nn(pre_grad, u)
            for which, value in ((0, dot_tn(pre_grad, n_ref[...])), (1, dot_tn(act, low[...]))):
                value = value.astype(BF)
                for k in range(per):
                    spot = (place_ref[5] ^ k) if relative else k
                    wg_ref[spot, 0, which] = value[k * group_rows : (k + 1) * group_rows]

        own_w, other_w = (w_refs[::2], w_refs[1::2]) if relative else (w_refs, w_refs)
        if fresh:
            pl.when(step < per_half)(lambda: part(*own_w, None, None))
            pl.when(step >= per_half)(lambda: part(*other_w, None, None))
        else:
            pl.when(step < per_half)(lambda: part(*own_w, *kept[:2]))
            pl.when(step >= per_half)(lambda: part(*other_w, *kept[2:]))

        @pl.when(step == steps - 1)
        def _():
            if fresh:
                out_ref[...] = x2[...].astype(BF)
            normal, inv = normalize(x_ref[...])
            total = dn[...]
            g1 = grad_ref[...] + norm_back(total, normal, inv, g_ref[...])
            g1_ref[...] = g1
            ga_ref[...] = g1.astype(BF)
            gg_ref[...] = jnp.sum(total * normal, axis=0, keepdims=True)
            gs_ref[...] = jnp.sum(total, axis=0, keepdims=True)

    full = whole((rows, width))
    def own_index(i):
        return jnp.minimum(i, per_half - 1)

    def other_index(i):
        return jnp.maximum(i - per_half, 0)

    wg_specs = [
        pl.BlockSpec(
            (per, 1, 2, group_rows, width),
            lambda i, place: (
                (place[4] ^ (i % per_half)) if relative else i % per_half, place[3] ^ (i // per_half), 0, 0, 0,
            ),
        )
    ]
    wg_shapes = [shape_of((groups, 2, 2, group_rows, width), BF)]
    kept_specs = [
        pl.BlockSpec((rows, chunk), lambda i, *_, index=index: (0, index(i)))
        for index in (() if fresh else (own_index, own_index, other_index, other_index))
    ]
    return call(
        order,
        body,
        (steps,),
        [full, full] + w_specs + [full, whole((1, width))] + kept_specs,
        wg_specs + [full, full, whole((1, width)), whole((1, width))] + ([full] if fresh else []),
        wg_shapes
        + [
            shape_of((rows, width), F32),
            shape_of((rows, width), BF),
            shape_of((1, width), F32),
            shape_of((1, width), F32),
        ]
        + ([shape_of((rows, width), BF)] if fresh else []),
        [pltpu.VMEM((rows, width), BF), pltpu.VMEM((rows, width), F32), pltpu.VMEM((rows, chunk), BF)]
        + ([pltpu.VMEM((rows, chunk), BF), pltpu.VMEM((rows, width), F32)] if fresh else []),
        prefetch=1,
        name="ff_bwd",
    )(place, x1, normed, *operands, grad, gain, *(() if fresh else saved))


def attn_backward(order, place, grad_low, weights, sg, ratio, rden, v, wsum, carried, masked):
    rows, width = grad_low.shape
    seqs, block, keys = masked.shape
    window = keys - block
    third = width // THIRDS

    def body(place_ref, ga_ref, *rest):
        w_refs, rest = rest[: len(weights)], rest[len(weights) :]
        (sg_ref, ratio_ref, rden_ref, v_ref, wsum_ref, car_ref, masked_ref,
         gq_ref, gk_ref, gv_ref, band_ref, own_ref, halo_ref, mix_t, wgrad, dn) = rest
        step = pl.program_id(0)

        @pl.when(step == 0)
        def _():
            for s in range(seqs):
                mix_t[s] = masked_ref[s].T.astype(BF)
            wgrad[...] = jnp.zeros_like(wgrad)
            dn[...] = jnp.zeros_like(dn)

        def part(mat):
            gm = dot_nt(ga_ref[...], mat(3))
            sig = sg_ref[...].astype(F32)
            rat = ratio_ref[...].astype(F32)
            scaled = gm * sig
            gq = (scaled * rat * (1.0 - sig)).astype(BF)
            gq_ref[...] = gq
            gnum_f = scaled * rden_ref[...].astype(F32)
            gnum = gnum_f.astype(BF)
            gden = (-gnum_f * rat).astype(BF)
            wq, wk, wv = mat(0), mat(1), mat(2)
            dn[rows:] += dot_nn(gq, wq)
            for r in range(2):
                for s in range(seqs):
                    here = slice(s * block, (s + 1) * block)
                    there = slice(r * rows + s * block, r * rows + (s + 1) * block)
                    cols = slice(r * window, r * window + block)
                    ke = wsum_ref[there].astype(F32)
                    gcar = dot_nn(mix_t[s, cols], gnum[here])
                    gsum = dot_nn(mix_t[s, cols], gden[here])
                    gv = (gcar * ke).astype(BF)
                    gk = ((gcar * v_ref[there].astype(F32) + gsum) * ke).astype(BF)
                    gk_ref[there] = gk
                    gv_ref[there] = gv
                    wgrad[s, :, cols] += dot_nt(gnum[here], car_ref[there]) + dot_nt(gden[here], wsum_ref[there])
                    dn[there] += dot_nn(gk, wk) + dot_nn(gv, wv)

        by_third(step, w_refs, place_ref, part)

        @pl.when(step == THIRDS - 1)
        def _():
            total = wgrad[0] * masked_ref[0]
            for s in range(1, seqs):
                total = total + wgrad[s] * masked_ref[s]
            lane_row = lax.broadcasted_iota(jnp.int32, (block, keys), 0) + 1
            bit = 1
            while bit <= block:
                rolled = pltpu.roll(total, keys - bit, axis=1)
                total = jnp.where((lane_row & bit) != 0, rolled, total)
                bit *= 2
            band_ref[...] = reverse_lanes(total[:, :window])
            halo_ref[...] = dn[:rows].astype(BF)
            own_ref[...] = dn[rows:]

    def col(n):
        return pl.BlockSpec((n, third), lambda i, *_: (0, i))

    return call(
        order,
        body,
        (THIRDS,),
        [whole((rows, width))]
        + attn_specs(weights)
        + [col(rows)] * 3 + [col(2 * rows)] * 3 + [whole((seqs, block, keys))],
        [col(rows), col(2 * rows), col(2 * rows), whole((block, window)), whole((rows, width)), whole((rows, width))],
        [
            shape_of((rows, width), BF),
            shape_of((2 * rows, width), BF),
            shape_of((2 * rows, width), BF),
            shape_of((block, window), F32),
            shape_of((rows, width), F32),
            shape_of((rows, width), BF),
        ],
        [
            pltpu.VMEM((seqs, keys, block), BF),
            pltpu.VMEM((seqs, block, keys), F32),
            pltpu.VMEM((2 * rows, width), F32),
        ],
        prefetch=1,
        name="attn_bwd",
        limit=46 * 1024 * 1024,
        near_in=(0,),
        near_out=(0, 1, 2, 3, 4, 5),
    )(place, grad_low, *weights, sg, ratio, rden, v, wsum, carried, masked)


def attn_weight_grads(order, place, gq, gk, gv, mixed, normed, halo, grad_low, band, mp, mixed_rows, riding):
    rows, width = gq.shape
    half = width // 2
    quarter = half // 2
    piece = quarter // mp
    window = band.shape[1]
    share = 2 * RIDERS
    def body(place_ref, gq_ref, gk_ref, gv_ref, mixed_ref, n_ref, h_ref, ga_ref, band_ref, *out_refs):
        def part(outs, core):
            if riding:
                for p in range(4):
                    owner = 2 * (place_ref[2] ^ p) + (place_ref[3] ^ core)
                    start = pl.multiple_of(owner * share, share)
                    rows_here = band_ref[pl.ds(start, share)].astype(BF)
                    outs[0][p, quarter:] = jnp.concatenate(
                        [rows_here[:RIDERS], rows_here[RIDERS:], jnp.zeros((RIDERS, width - 2 * window), BF)], axis=1
                    )

            def put(m, value):
                low = value.astype(BF)
                spot = place_ref[0] ^ m
                if not mixed_rows:
                    outs[0][spot, :quarter] = low[:quarter]
                    outs[1][spot] = low[quarter:]
                    return
                for z in range(mp):
                    for k in range(2):
                        outs[k][spot, z * piece : (z + 1) * piece] = low[
                            (2 * z + k) * piece : (2 * z + k + 1) * piece
                        ]

            put(0, dot_tn(gq_ref[...], n_ref[...]))
            for m, ref in ((1, gk_ref), (2, gv_ref)):
                put(m, dot_tn(ref[:rows], h_ref[...]) + dot_tn(ref[rows:], n_ref[...]))
            put(3, dot_tn(mixed_ref[...], ga_ref[...]))

        pl.when(pl.program_id(0) == 0)(lambda: part(out_refs[:2], 0))
        pl.when(pl.program_id(0) == 1)(lambda: part(out_refs[2:], 1))

    def col(n):
        return pl.BlockSpec((n, half), lambda i, *_: (0, i))

    shapes = [(4, quarter + (RIDERS if riding else 0), width), (4, quarter, width)] * 2
    return call(
        order,
        body,
        (2,),
        [col(rows), col(2 * rows), col(2 * rows), col(rows)] + [whole((rows, width))] * 3 + [whole(band.shape)],
        [whole(shape) for shape in shapes],
        [shape_of(shape, BF) for shape in shapes],
        prefetch=1,
        name="attn_wgrad",
        limit=36 * 1024 * 1024,
        near_in=(0, 1, 2, 6, 7),
    )(place, gq, gk, gv, mixed, normed, halo, grad_low, band)


def leave_attn(order, x, grad, own, back, gain):
    rows, width = x.shape

    def body(x_ref, g_ref, o_ref, b_ref, gain_ref, out_ref, gg_ref, gs_ref):
        normal, inv = normalize(x_ref[...])
        total = o_ref[...] + b_ref[...].astype(F32)
        out_ref[...] = g_ref[...] + norm_back(total, normal, inv, gain_ref[...])
        gg_ref[...] = jnp.sum(total * normal, axis=0, keepdims=True)
        gs_ref[...] = jnp.sum(total, axis=0, keepdims=True)

    return call(
        order,
        body,
        (1,),
        [whole((rows, width))] * 4 + [whole((1, width))],
        [whole((rows, width)), whole((1, width)), whole((1, width))],
        [shape_of((rows, width), F32)] + [shape_of((1, width), F32)] * 2,
        name="leave",
    )(x, grad, own, back, gain)


def finish_layer(order, layer, layers, place, parts, channels, hidden, mp, window, norm_rows, previous):
    width = parts[0].shape[-1]
    total = 4 * channels
    single = len(parts) == 1
    groups = len(parts) // 4
    dp = parts[0].shape[0] if single else 2 * groups
    piece = total // dp
    share = 2 * RIDERS
    block = dp * share

    def body(place_ref, *rest):
        p_refs, rest = rest[: len(parts)], rest[len(parts) :]
        qkv_ref, out_ref, up_ref, down_ref, band_ref = rest[:5]
        up = rest[-1]

        def put(owner, rows_of, ff_rows_of, bands):
            start = pl.multiple_of(owner * piece, piece)
            mat = owner * piece // channels
            inner = pl.multiple_of(owner * piece - mat * channels, piece)
            value = rows_of(0, piece).astype(F32)

            @pl.when(mat < 3)
            def _():
                qkv_ref[0, jnp.minimum(mat, 2), pl.ds(inner, piece)] = value

            @pl.when(mat == 3)
            def _():
                out_ref[0, pl.ds(inner, piece)] = value

            up[pl.ds(start, piece)] = ff_rows_of(0, piece).astype(F32)
            down_ref[0, pl.ds(start, piece)] = ff_rows_of(piece, piece).astype(F32)
            for p in range(mp):
                band = rows_of(bands + p * RIDERS, RIDERS).astype(F32)
                first = pl.multiple_of((place_ref[1] ^ p) * block + owner * share, share)
                band_ref[0, pl.ds(first, RIDERS)] = band[:, :window]
                band_ref[0, pl.ds(first + RIDERS, RIDERS)] = band[:, window : 2 * window]

        if single:
            for owner in range(dp):
                put(
                    jnp.int32(owner),
                    lambda start, count, owner=owner: p_refs[0][owner, start : start + count],
                    lambda start, count, owner=owner: p_refs[0][owner, piece + start : piece + start + count],
                    3 * piece,
                )
        else:
            for core in range(2):
                for p in range(groups):
                    ref, ff_ref = p_refs[core * groups + p], p_refs[(2 + core) * groups + p]
                    owner = 2 * (place_ref[2] ^ p) + (place_ref[3] ^ core)
                    put(
                        owner,
                        lambda start, count, ref=ref: ref[start : start + count],
                        lambda start, count, ref=ff_ref: ref[start : start + count],
                        piece + norm_rows,
                    )
        up_ref[0] = up[...].T
        if norm_rows:
            half = norm_rows // 2
            sums = []
            for p in range(groups):
                for core in range(2):
                    rows = p_refs[core * groups + p][piece : piece + norm_rows].astype(F32)
                    sums.append(rows[:half] + rows[half:])
            while len(sums) > 1:
                sums = [sums[k] + sums[k + 1] for k in range(0, len(sums), 2)]
            rest[5][...] = sums[0]

    shapes = [
        (layers, 3, channels, width),
        (layers, channels, width),
        (layers, width, hidden),
        (layers, hidden, width),
        (layers, mp * block, window),
    ]

    def here(shape):
        return pl.BlockSpec((1,) + shape[1:], lambda i, *_: (layer,) + (0,) * (len(shape) - 1))

    extra = list(previous) if previous is not None else []
    anywhere = pl.BlockSpec(memory_space=pl.ANY)
    return call(
        order,
        lambda *refs: body(*refs[: 1 + len(parts)], *refs[1 + len(parts) + len(extra) :]),
        (1,),
        [whole(part.shape) for part in parts] + [anywhere] * len(extra),
        [here(shape) for shape in shapes] + ([whole((norm_rows // 2, width))] if norm_rows else []),
        [shape_of(shape, F32) for shape in shapes]
        + ([shape_of((norm_rows // 2, width), F32)] if norm_rows else []),
        [pltpu.VMEM((total, width), F32)],
        prefetch=1,
        name="finish",
        aliases={1 + len(parts) + k: k for k in range(len(extra))},
    )(place, *parts, *extra)


DP = ("g", "c")


class Order:
    def __init__(self):
        self.token = jnp.zeros(TOKEN, jnp.int32)

    def pin(self, *arrays):
        *arrays, self.token = tie(*arrays, self.token)
        return arrays


class Links:
    def __init__(self, order, dp, mp):
        self.order = order
        self.dp = dp
        self.mp = mp
        bits = [1 << k for k in range(1, dp.bit_length() - 1)]
        self.routes = (bits, bits[::-1])

    def swap(self, value, axis, bit):
        size = self.dp if axis == DP else self.mp
        return lax.ppermute(value, axis, [(i, i ^ bit) for i in range(size)])


class Spread:
    def __init__(self, links, values):
        self.links = links
        self.values = list(values)
        self.phase = 0
        self.have = [[], []]

    def start(self):
        self.values = self.links.order.pin(*self.values)
        self.coming = [
            self.links.swap(value, DP, route[self.phase])
            for value, route in zip(self.values, self.links.routes)
        ]

    def wait(self):
        coming = self.links.order.pin(*self.coming)
        for k in range(2):
            bit = self.links.routes[k][self.phase]
            place = sum(1 for other in self.have[k] if other > bit)
            self.values[k] = jnp.stack([self.values[k], coming[k]], axis=place)
            self.have[k].append(bit)
        self.phase += 1

    def wait_all(self):
        self.wait()
        while self.phase < len(self.links.routes[0]):
            self.start()
            self.wait()

    def start_cores(self):
        self.values = self.links.order.pin(*self.values)
        self.coming = [self.links.swap(value, DP, 1) for value in self.values]

    def wait_cores(self):
        return self.values + self.links.order.pin(*self.coming)


class Gather(Spread):
    def __init__(self, links, piece_a, piece_b):
        super().__init__(links, ())
        self.cut = piece_a.shape[0]
        self.piece = jnp.concatenate([piece_a, piece_b], axis=0)

    def start_mp(self):
        (self.piece,) = self.links.order.pin(self.piece)
        self.coming_mp = [self.links.swap(self.piece, "mp", p) for p in range(1, self.links.mp)]

    def wait_mp(self):
        parts = [self.piece] + self.links.order.pin(*self.coming_mp)
        self.values = [
            jnp.stack([part[: self.cut] for part in parts]),
            jnp.stack([part[self.cut :] for part in parts]),
        ]


class Reduce:
    def __init__(self, links, halves):
        self.links = links
        self.halves = halves
        self.phase = 0

    def start_cores(self):
        others = self.links.order.pin(*self.halves[2:])
        self.coming = [self.links.swap(other, DP, 1) for other in others]

    def wait_cores(self):
        coming = self.links.order.pin(*self.coming)
        mp = self.links.mp
        self.have = [sorted(route, reverse=True) for route in self.links.routes]
        lead = (2,) * len(self.have[0])
        self.terms = []
        for own, other in zip(self.halves[:2], coming):
            shape = lead + (-1, own.shape[-1])
            self.terms.append([own.reshape(shape), other.reshape(shape)])

    def start(self):
        sends = []
        for k in range(2):
            place = self.have[k].index(self.links.routes[1 - k][self.phase])
            sends.append(
                sum(lax.index_in_dim(term, 1, place, keepdims=False).astype(F32) for term in self.terms[k]).astype(BF)
            )
            self.terms[k] = [lax.index_in_dim(term, 0, place, keepdims=False) for term in self.terms[k]]
        sends = self.links.order.pin(*sends)
        self.coming = [
            self.links.swap(sends[k], DP, self.links.routes[1 - k][self.phase]) for k in range(2)
        ]

    def wait(self):
        coming = self.links.order.pin(*self.coming)
        for k in range(2):
            self.terms[k].append(coming[k])
            self.have[k].remove(self.links.routes[1 - k][self.phase])
        self.phase += 1

    def wait_all(self):
        self.wait()
        while self.phase < len(self.links.routes[0]):
            self.start()
            self.wait()
        sums = [sum(term.astype(F32) for term in terms).astype(BF) for terms in self.terms]
        count = sums[1].shape[0]
        mp = self.links.mp
        riders = sums[0][count:]
        return [value[:count].reshape(mp, count // mp, -1) for value in sums], riders


class ReduceWide:
    def __init__(self, links, grads):
        self.links = links
        (grads,) = links.order.pin(grads.reshape((links.dp,) + grads.shape[2:]))
        self.sums = lax.psum_scatter(grads, DP, scatter_dimension=0, tiled=True)

    def wait(self):
        (sums,) = self.links.order.pin(self.sums)
        sums = sums.reshape(2, self.links.mp, -1, sums.shape[-1])
        return [sums[0], sums[1]]


class ReduceMp:
    def __init__(self, links, arrays, index, riders):
        self.links = links
        joined = jnp.concatenate(arrays, axis=1)
        self.count = joined.shape[1]
        if index is None:
            blocks = [joined[p] for p in range(links.mp)]
        else:
            blocks = [
                lax.dynamic_index_in_dim(joined, jnp.bitwise_xor(index, p), 0, keepdims=False)
                for p in range(links.mp)
            ]
        if riders is not None:
            blocks = [jnp.concatenate([block, riders], axis=0) for block in blocks]
        self.kept, *sends = links.order.pin(*blocks)
        self.coming = [links.swap(send, "mp", p + 1) for p, send in enumerate(sends)]

    def wait(self):
        parts = [self.kept] + self.links.order.pin(*self.coming)
        total = sum(part[: self.count].astype(F32) for part in parts)
        return total.astype(BF), [part[self.count :] for part in parts]


def make_shards(dp, mp):
    def shards(
        tokens,
        segments,
        qkv_weight,
        out_weight,
        up_weight,
        down_projection_weight,
        norm_gain,
        norm_bias,
        pos_bias,
        cotangent,
    ):
        seqs, block, width = tokens.shape
        layers = qkv_weight.shape[0]
        window = pos_bias.shape[2]
        channels = qkv_weight.shape[-1]
        hidden = up_weight.shape[-1]
        rows = seqs * block
        group = lax.axis_index("g")
        core = lax.axis_index("c")
        dp_index = group * 2 + core
        mp_index = lax.axis_index("mp")
        order = Order()
        links = Links(order, dp, mp)
        attn_rows = 4 * channels // dp
        ff_rows = hidden // dp
        groups = dp // 2
        per = max(1, width // (mp * ff_rows))
        place = jnp.stack([group // (groups // 4), mp_index, group, core, group // per, group % per]).astype(jnp.int32)

        def picks(count, offset, length):
            return (
                lax.broadcasted_iota(jnp.int32, (count, length), 0) + offset
                == lax.broadcasted_iota(jnp.int32, (count, length), 1)
            ).astype(BF)

        ff_pick = picks(ff_rows, dp_index * ff_rows, hidden)

        def attn_piece(layer):
            by_channel = jnp.transpose(qkv_weight[layer], (0, 2, 1)).reshape(3 * channels, width)
            start = dp_index * attn_rows
            inner = start - 3 * channels
            return jnp.where(
                inner < 0,
                lax.dynamic_slice_in_dim(by_channel, jnp.minimum(start, 3 * channels - attn_rows), attn_rows),
                lax.dynamic_slice_in_dim(out_weight[layer], jnp.maximum(inner, 0), attn_rows),
            )

        def ff_pieces(layer):
            return (
                dot_nt(ff_pick, up_weight[layer]).astype(BF),
                dot_nn(ff_pick, down_projection_weight[layer]).astype(BF),
            )

        def attn_mats(parts):
            return [part.reshape(4, -1, width) for part in parts]

        def ff_mats(parts):
            flat = [part.reshape(-1, width) for part in parts]
            return (flat[0], flat[2]), (flat[1], flat[3])

        def relative(gathered):
            by_dp = jnp.take(gathered, jnp.bitwise_xor(jnp.arange(dp), dp_index), axis=0)
            both = jnp.take(by_dp, jnp.bitwise_xor(jnp.arange(mp), mp_index), axis=1)
            both = both.reshape((dp // 2, 2) + gathered.shape[1:])
            return both[:, 0], both[:, 1]

        def forward_halo(value):
            return lax.ppermute(value, "mp", [(i, i + 1) for i in range(mp - 1)])

        def backward_halo(value):
            return lax.ppermute(value, "mp", [(i + 1, i) for i in range(mp - 1)])

        gains = norm_gain.reshape(layers, 2, 1, width)
        shifts = norm_bias.reshape(layers, 2, 1, width)
        middle = attn_rows // 2
        in_blocks = (
            middle % 16 == 0 and groups == 4 and block == 2 * RIDERS * dp and width == 3 * window
        )

        piece = attn_piece(0)
        attn0 = Gather(links, piece[:middle], piece[middle:])
        attn0.start_mp()
        ff0 = Gather(links, *ff_pieces(0))
        ff0.start_mp()
        later = jnp.concatenate((attn_piece(1),) + ff_pieces(1), axis=0)
        x, normed = enter_kernel(order, tokens.reshape(rows, width), gains[0, 0], shifts[0, 0])
        (normed,) = order.pin(normed)
        halo = forward_halo(normed)

        seg_pad = jnp.concatenate([jnp.full((seqs, window), -1, segments.dtype), segments], axis=1)
        seg_keys = lax.dynamic_slice_in_dim(seg_pad, mp_index * block, block + window, axis=1)
        seg_q = seg_keys[:, window:].reshape(seqs, block, 1)
        seg_k = seg_keys.reshape(seqs, 1, block + window)

        attn0.wait_mp()
        attn0.start()
        attn0.wait()
        attn0.start()
        ff0.wait_mp()
        ff0.start()
        (later,) = order.pin(later)
        later = lax.all_gather(later, ("g", "c", "mp"), axis=0, tiled=False)
        (halo,) = order.pin(halo)
        attn0.wait_all()
        ff0.wait()
        ff0.start()
        attn0.start_cores()
        w_attn0 = attn_mats(attn0.wait_cores())

        def attn(layer, x, normed, halo, w_attn):
            sg, ratio, rden, v, wsum, carried, mixed, masked, x1, normed_b = attn_forward(
                order, layer, place, x, normed, halo, w_attn, pos_bias, seg_q, seg_k,
                gains[layer, 1], shifts[layer, 1],
            )
            return x1, normed_b, (sg, ratio, rden, v, wsum, carried, masked), (mixed, normed, halo)

        x1_0, normed_b0, saved0, rows0 = attn(0, x, normed, halo, w_attn0)
        ff0.wait_all()
        ff0.start_cores()
        own_up, own_down = [value.reshape(-1, width) for value in ff0.values]
        act0, slope0, x_half = ff_forward(order, x1_0, normed_b0, own_up, own_down, None, None)
        ups0, downs0 = ff_mats(ff0.wait_cores())
        act0o, slope0o, x2, normed2 = ff_forward(
            order, x_half, normed_b0, ups0[1], downs0[1], gains[1, 0], shifts[1, 0]
        )
        (normed2,) = order.pin(normed2)
        halo2 = forward_halo(normed2)
        (later,) = order.pin(later)
        if in_blocks:
            w_attn1 = w_ff1 = [later.reshape((groups, 2, mp) + later.shape[1:])]
        else:
            own, other = relative(later.reshape((dp, mp) + later.shape[1:]))
            cuts = [middle, attn_rows, attn_rows + ff_rows]
            own_a, own_b, own_up, own_down = jnp.split(own, cuts, axis=2)
            other_a, other_b, other_up, other_down = jnp.split(other, cuts, axis=2)
            w_attn1 = attn_mats([own_a, own_b, other_a, other_b])
            w_ff1 = sum(ff_mats([own_up, own_down, other_up, other_down]), ())
        (halo2,) = order.pin(halo2)
        x1_1, normed_b1, saved1, rows1 = attn(1, x2, normed2, halo2, w_attn1)

        wide1, grad1, grad1_low, gain_b1, shift_b1, output = ff_backward(
            order, place, x1_1, normed_b1, w_ff1, groups, cotangent.reshape(rows, width), gains[1, 1], None
        )
        wide1 = ReduceWide(links, wide1)
        gq, gk, gv, band1, dn_own1, back1 = attn_backward(order, place, grad1_low, w_attn1, *saved1)
        (back1,) = order.pin(back1)
        back1 = backward_halo(back1)
        r_attn1 = Reduce(
            links, attn_weight_grads(order, place, gq, gk, gv, *rows1, grad1_low, band1, mp, in_blocks, in_blocks)
        )
        (back1,) = order.pin(back1)
        r_attn1.start_cores()
        grad2, gain_a1, shift_a1 = leave_attn(order, x2, grad1, dn_own1, back1, gains[1, 0])
        r_attn1.wait_cores()
        r_attn1.start()
        wide0, grad3, grad3_low, gain_b0, shift_b0 = ff_backward(
            order, place, x1_0, normed_b0, ups0 + downs0, groups, grad2, gains[0, 1],
            (act0, slope0, act0o, slope0o),
        )
        r_attn1.wait()
        wide0 = ReduceWide(links, wide0)
        r_attn1.start()
        z_of_1 = mp_index if in_blocks else None
        z_ff1 = ReduceMp(links, wide1.wait(), z_of_1, None)
        gq, gk, gv, band0, dn_own0, back0 = attn_backward(order, place, grad3_low, w_attn0, *saved0)
        r_attn0 = Reduce(
            links, attn_weight_grads(order, place, gq, gk, gv, *rows0, grad3_low, band0, mp, False, in_blocks)
        )
        attn1_sum, riders1 = r_attn1.wait_all()
        sum1_ff, _ = z_ff1.wait()
        r_attn0.start_cores()
        z_attn1 = ReduceMp(links, attn1_sum, z_of_1, riders1)
        r_attn0.wait_cores()
        sum1, riders1 = z_attn1.wait()
        r_attn0.start()
        (back0,) = order.pin(back0)
        back0 = backward_halo(back0)
        (full1,) = order.pin(jnp.concatenate([sum1, sum1_ff] + riders1, axis=0))
        full1 = lax.all_gather(full1, DP, axis=0, tiled=False)
        r_attn0.wait()
        (back0,) = order.pin(back0)
        ff0_sum = wide0.wait()
        r_attn0.start()
        z_ff0 = ReduceMp(links, ff0_sum, None, None)
        grad4, gain_a0, shift_a0 = leave_attn(order, x, grad3, dn_own0, back0, gains[0, 0])
        norms = jnp.concatenate(
            [gain_a0, gain_b0, shift_a0, shift_b0, gain_a1, gain_b1, shift_a1, shift_b1], axis=0
        )

        def two_parts(value):
            high = value.astype(BF)
            return jnp.concatenate([high, (value - high.astype(F32)).astype(BF)], axis=0)

        def one_part(value):
            count = value.shape[0] // 2
            return value[:count].astype(F32) + value[count:].astype(F32)

        attn0_sum, riders0 = r_attn0.wait_all()

        def regather(value):
            (value,) = order.pin(value)
            return [value] + [links.swap(value, DP, 2 * p) for p in range(1, groups)], [links.swap(value, DP, 1)]

        def regather_cores(parts):
            same, other = parts
            other[0], *same[1:] = order.pin(other[0], *same[1:])
            same[1:] = order.pin(*same[1:])
            return same, other + [links.swap(part, DP, 1) for part in same[1:]]

        def regather_wait(parts):
            same, other = parts
            return same + other[:1] + order.pin(*other[1:])

        ff0_sum, _ = z_ff0.wait()
        z_attn0 = ReduceMp(links, attn0_sum, None, jnp.concatenate([two_parts(norms), riders0], axis=0))
        ff0_parts = regather(ff0_sum)
        (full1,) = order.pin(full1)

        cut = 2 * norms.shape[0]

        def finish(layer, full, previous):
            if in_blocks:
                norm_rows = 0 if layer else cut
                return finish_layer(
                    order, layer, layers, place, full, channels, hidden, mp, window, norm_rows, previous
                )
            if len(full) == 1:
                owner = jnp.arange(dp)
                joined = full[0]
            else:
                owner = jnp.bitwise_xor(jnp.arange(dp), dp_index)
                joined = jnp.concatenate(
                    [jnp.stack(full[: 2 * groups])[:, :attn_rows], jnp.stack(full[2 * groups :])], axis=1
                ).reshape(2, groups, -1, width)
                joined = jnp.swapaxes(joined, 0, 1).reshape(dp, -1, width)
            joined = joined[:, : attn_rows + 2 * ff_rows]
            attn_part, up_part, down_part = jnp.split(joined, [attn_rows, attn_rows + ff_rows], axis=1)

            def rows_of(value):
                return value.reshape(-1, width)

            def place_of(count):
                spots = (owner[:, None] * count + jnp.arange(count)[None, :]).reshape(-1, 1)
                return (spots == jnp.arange(dp * count)[None, :]).astype(BF)

            attn_place = place_of(attn_rows).reshape(-1, 4, channels)
            ff_place = place_of(ff_rows)
            values = (
                jnp.einsum("pd,pmc->mcd", rows_of(attn_part), attn_place[:, :3], preferred_element_type=F32),
                dot_tn(attn_place[:, 3], rows_of(attn_part)),
                dot_tn(rows_of(up_part), ff_place),
                dot_tn(ff_place, rows_of(down_part)),
            )
            if previous is None:
                previous = [jnp.zeros((layers,) + value.shape, F32) for value in values]
            return [
                lax.dynamic_update_index_in_dim(kept, value, layer, 0)
                for kept, value in zip(previous, values)
            ]

        big = finish(1, [full1], None)
        sum0, riders0 = z_attn0.wait()
        norms = [one_part(part[:cut]) for part in riders0]
        while len(norms) > 1:
            norms = [norms[k] + norms[k + 1] for k in range(0, len(norms), 2)]
        sum0 = jnp.concatenate([sum0, two_parts(norms[0])] + [part[cut:] for part in riders0], axis=0)
        ff0_parts = regather_cores(ff0_parts)
        attn0_parts = regather(sum0)
        ff0_parts = regather_wait(ff0_parts)
        attn0_parts = regather_wait(regather_cores(attn0_parts))
        qkv_out, out_out, up_out, down_out, *small = finish(0, attn0_parts + ff0_parts, big)
        if in_blocks:
            band_sum, norm_sum = small
        else:
            sums = [one_part(attn0_parts[p + k][attn_rows : attn_rows + cut]) for p in range(groups) for k in (0, groups)]
            while len(sums) > 1:
                sums = [sums[k] + sums[k + 1] for k in range(0, len(sums), 2)]
            norm_sum = sums[0]
            band_sum = lax.all_gather(
                lax.psum(jnp.stack([band0, band1]), DP), "mp", axis=1, tiled=True
            )
        norm_sum = norm_sum.reshape(layers, 4, width)
        return (
            output.reshape(tokens.shape),
            grad4.reshape(tokens.shape),
            jnp.transpose(qkv_out, (0, 1, 3, 2)),
            out_out,
            up_out,
            down_out,
            norm_sum[:, :2],
            norm_sum[:, 2:],
            band_sum,
        )

    return shards


def solution(mesh):
    dp, mp = mesh.shape["dp"], mesh.shape["mp"]
    inner = Mesh(mesh.devices.reshape(dp // 2, 2, mp), DP + ("mp",))
    placed = (
        P(DP, "mp", None),
        P(DP, None),
        P(None, None, None, "mp"),
        P(None, "mp", None),
        P(None, None, "mp"),
        P(None, "mp", None),
        P(),
        P(),
        P(),
        P(DP, "mp", None),
    )
    return jax.shard_map(
        make_shards(dp, mp),
        mesh=inner,
        in_specs=placed,
        out_specs=(
            P(DP, "mp", None),
            P(DP, "mp", None),
            P(None, None, None, "mp"),
            P(None, "mp", None),
            P(None, None, "mp"),
            P(None, "mp", None),
            P(),
            P(),
            P(),
        ),
        check_vma=False,
    )
```
